32 devices in a mesh: seq: 4 (over y, core), batch: 8 (over z, x).
Axes of the slice: x: 2, y: 2, z: 4, core: 2. Of those that a mesh axis runs over, the one named last changes fastest.
Arguments:
- tokens: bfloat16 [8, 1024, 2048], P('batch', 'seq'), may hold values from -6 to 6
- cotangent: bfloat16 [8, 1024, 2048], P('batch', 'seq'), may hold values from -6 to 6
- selection: int32 [8, 1024], P('batch', 'seq'), may hold values from 0 to 1, as said below
- segments: int32 [8, 1024], P('batch', 'seq'), may hold values from 0 to 510, as said below
- positions: int32 [8, 1024], P('batch', 'seq'), may hold values from 0 to 1534, as said below
- gain_attn: bfloat16 [2048], P(('seq', 'batch')), may hold values from 0.099609375 to 1.8984375
- w_query: bfloat16 [2048, 2048], P(('seq', 'batch')), may hold values from -0.125 to 0.125
- w_key: bfloat16 [2048, 256], P(('seq', 'batch')), may hold values from -0.125 to 0.125
- w_value: bfloat16 [2048, 256], P(('seq', 'batch')), may hold values from -0.125 to 0.125
- w_out: bfloat16 [2048, 2048], P(('seq', 'batch')), may hold values from -1 to 1
- gain_mlp: bfloat16 [2048], P(('seq', 'batch')), may hold values from 0.099609375 to 1.8984375
- w_gate: bfloat16 [2048, 5632], P(('seq', 'batch')), may hold values from -0.125 to 0.125
- w_up: bfloat16 [2048, 5632], P(('seq', 'batch')), may hold values from -0.125 to 0.125
- w_down: bfloat16 [5632, 2048], P(('seq', 'batch')), may hold values from -0.078125 to 0.078125
Outputs:
- mixed: bfloat16 [8, 1024, 2048], P('batch', 'seq')
- tokens_grad: bfloat16 [8, 1024, 2048], P('batch', 'seq')
- grad_query: float32 [2048, 2048], P(('seq', 'batch'))
- grad_key: float32 [2048, 256], P(('seq', 'batch'))
- grad_value: float32 [2048, 256], P(('seq', 'batch'))
- grad_out: float32 [2048, 2048], P(('seq', 'batch'))
- grad_gate: float32 [2048, 5632], P(('seq', 'batch'))
- grad_up: float32 [2048, 5632], P(('seq', 'batch'))
- grad_down: float32 [5632, 2048], P(('seq', 'batch'))
- grad_gain_attn: float32 [2048], P(('seq', 'batch'))
- grad_gain_mlp: float32 [2048], P(('seq', 'batch'))
The draws below stay inside these ranges and needn't reach their ends.
Inputs may be any that keep to these rules, and one draw needn't show every extreme that they name: `selection`: 1 where the token's loss gradient is kept; each row keeps its own share of its tokens. `segments`: document number of each position, never falling along a row and starting at 0 in each row; a row holds at most 511 documents. `positions`: each token's place in its document; the first document of a row may continue an earlier one and start below 512.
All inputs are finite; a program needn't handle non-finite values.
Results may differ from the reference program's by a relative error of at most 0.015.
Values may be sent and summed in bfloat16 or wider, within the bound.
A program may use at most 448 MiB of HBM per device.

```python
import jax
import jax.numpy as jnp
from jax import lax

D = 2048
HEADS = 32
KV_HEADS = 4
HEAD_DIM = 64
FF = 5632
TOK_DEV = 256
SEQ_LEN = 1024
ROWS = 8


def document_starts(key):
    key_first, key_last, key_noise = jax.random.split(key, 3)
    row_index = jnp.arange(ROWS, dtype=jnp.int32)[:, None]
    first_drawn = jax.random.randint(key_first, (ROWS, 1), 0, TOK_DEV)
    last_drawn = jax.random.randint(key_last, (ROWS, 1), SEQ_LEN - TOK_DEV, SEQ_LEN)
    span_first = jnp.where(row_index == 0, 0, jnp.where(row_index == ROWS - 1, TOK_DEV - 1, first_drawn))
    span_last = jnp.where(row_index == 0, SEQ_LEN - 1, jnp.where(row_index == ROWS - 1, SEQ_LEN - TOK_DEV, last_drawn))
    places = jnp.arange(SEQ_LEN, dtype=jnp.int32)[None, :]
    random_cut = (jax.random.randint(key_noise, (ROWS, SEQ_LEN), 0, 48) == 0) | (row_index == ROWS - 1)
    outside = (places < span_first) | (places > span_last + 1)
    chosen = (places == span_first) | (places == span_last + 1) | random_cut & outside
    return jnp.where((places > 0) & chosen, 1, 0).astype(jnp.int32)


def draw_segments(key, part):
    flags = document_starts(key)
    return jnp.cumsum(flags, axis=1).astype(jnp.int32)


def draw_positions(key, part):
    flags = document_starts(key)
    key = jax.random.fold_in(key, 5)
    row_index = jnp.arange(ROWS, dtype=jnp.int32)[:, None]
    offset = jnp.where(row_index == 0, 511, jax.random.randint(key, (ROWS, 1), 0, 512))
    places = jnp.broadcast_to(jnp.arange(SEQ_LEN, dtype=jnp.int32)[None, :], (ROWS, SEQ_LEN))
    begins = lax.cummax(jnp.where(flags == 1, places, 0), axis=1)
    return (places - begins + jnp.where(begins == 0, offset, 0)).astype(jnp.int32)


def draw_selection(key, part):
    key = jax.random.fold_in(key, 9)
    key_rate, key_roll = jax.random.split(key)
    rate = jax.random.randint(key_rate, (ROWS, 1), 10, 96)
    rolled = jax.random.randint(key_roll, (ROWS, SEQ_LEN), 0, 100)
    return jnp.where(rolled < rate, 1, 0).astype(jnp.int32)


def block_scale(own_key, shape, cuts, least, largest):
    level = 1.0
    for dim, parts in cuts:
        draws = jax.random.uniform(jax.random.fold_in(jax.random.fold_in(own_key, 6), dim), (parts,), jnp.float32, least / len(cuts), largest / len(cuts))
        level = level * jnp.repeat(jnp.exp(draws), shape[dim] // parts).reshape((-1,) + (1,) * (len(shape) - 1 - dim))
    return level


def gaussian(rng, shape, scale, bound, cuts=(), kind=jnp.bfloat16):
    values = jax.random.normal(rng, shape, jnp.float32) * scale
    if len(cuts) > 0:
        values = block_scale(rng, shape, cuts, -0.22, 0.18) * values
    return jnp.clip(values, min=-bound, max=bound).astype(kind)


def setup_inputs(seed: int = 0) -> dict:
    key_list = jax.random.split(jax.random.key(seed), 15)
    return {
        "tokens": gaussian(key_list[0], (ROWS, SEQ_LEN, D), 1.0, 6.0, ((0, 8), (1, 4))),
        "cotangent": gaussian(key_list[1], (ROWS, SEQ_LEN, D), 1.0, 6.0, ((0, 8), (1, 4))),
        "selection": draw_selection(jax.random.fold_in(key_list[14], 71), 0),
        "segments": draw_segments(jax.random.fold_in(key_list[14], 71), 0),
        "positions": draw_positions(jax.random.fold_in(key_list[14], 71), 0),
        "gain_attn": jnp.clip(1.0 + 0.18 * jax.random.normal(key_list[5], (D,), jnp.float32), 0.099609375, 1.8984375).astype(jnp.bfloat16),
        "w_query": gaussian(key_list[6], (D, HEADS * HEAD_DIM), D ** -0.5, 0.125, ((0, 32),)),
        "w_key": gaussian(key_list[7], (D, KV_HEADS * HEAD_DIM), D ** -0.5, 0.125, ((0, 32),)),
        "w_value": gaussian(key_list[8], (D, KV_HEADS * HEAD_DIM), D ** -0.5, 0.125, ((0, 32),)),
        "w_out": gaussian(key_list[9], (HEADS * HEAD_DIM, D), (max(HEADS * HEAD_DIM // 64, 2)) ** -0.5, 1.0, ((0, 32),)),
        "gain_mlp": jnp.clip(1.0 + 0.18 * jax.random.normal(key_list[10], (D,), jnp.float32), 0.099609375, 1.8984375).astype(jnp.bfloat16),
        "w_gate": gaussian(key_list[11], (D, FF), D ** -0.5, 0.125, ((0, 32),)),
        "w_up": gaussian(key_list[12], (D, FF), D ** -0.5, 0.125, ((0, 32),)),
        "w_down": gaussian(key_list[13], (FF, D), FF ** -0.5, 0.078125, ((0, 32),)),
    }


@jax.custom_vjp
def low(v):
    return lax.optimization_barrier(v.astype(jnp.bfloat16)).astype(jnp.float32)

@jax.custom_vjp
def low_back(v):
    return v

def low_keep(v):
    return (low(v), None)

def low_pass(kept, grad):
    return (grad,)

def back_keep(v):
    return (v, None)

def back_low(kept, grad):
    return (low(grad),)
low.defvjp(low_keep, low_pass)
low_back.defvjp(back_keep, back_low)
EPSILON = 1e-05
PRECISE = lax.Precision.HIGHEST

def matmul(left, right):
    return jnp.dot(left, right, precision=PRECISE, preferred_element_type=jnp.float32)

def tables(pos_row):
    half_dim = HEAD_DIM // 2
    frequency = 10000.0 ** (-(jnp.arange(half_dim, dtype=jnp.float32) * 2.0 / HEAD_DIM))
    angles = pos_row.astype(jnp.float32)[:, None] * frequency[None, :]
    doubled = jnp.concatenate([angles, angles], axis=-1)
    return (jnp.cos(doubled)[:, None, :], jnp.sin(doubled)[:, None, :])

def rotate(vectors, cosine, sine):
    half_dim = vectors.shape[-1] // 2
    turned = jnp.concatenate([-vectors[..., half_dim:], vectors[..., :half_dim]], axis=-1)
    return vectors * cosine + turned * sine

def rms_scale(inputs):
    return lax.rsqrt(lax.optimization_barrier(jnp.mean(inputs * inputs, axis=-1, keepdims=True)) + EPSILON)

def attend(query_rot, key_rot, values, seg_row):
    length = query_rot.shape[0]
    group = HEADS // KV_HEADS
    qblock = min(512, length)
    blocks = length // qblock
    scale = HEAD_DIM ** (-0.5)
    key_pos = jnp.arange(length).astype(jnp.int32)
    grouped = query_rot.reshape(blocks, qblock, KV_HEADS, group, HEAD_DIM)
    starts = (jnp.arange(blocks) * qblock).astype(jnp.int32)

    def query_block(pieces):
        query_part, first_row = pieces
        query_pos = (first_row + jnp.arange(qblock)).astype(jnp.int32)
        query_seg = lax.dynamic_slice_in_dim(seg_row, first_row, qblock)
        raw_scores = low_back(jnp.einsum('qkgd,tkd->kgqt', query_part, key_rot, precision=PRECISE))
        scores = raw_scores * scale
        allowed = (key_pos[None, :] <= query_pos[:, None]) & (seg_row[None, :] == query_seg[:, None])
        attn_probs = low(jax.nn.softmax(jnp.where(allowed[None, None], scores, -1e+30), axis=-1))
        return jnp.einsum('kgqt,tkd->qkgd', attn_probs, values, precision=PRECISE)
    stacked = lax.map(jax.checkpoint(query_block), (grouped, starts))
    return stacked.reshape(length, HEADS * HEAD_DIM)

def block_layer(row_in, seg_row, pos_row, params):
    gain_attn, w_query, w_key, w_value, w_out, gain_mlp, w_gate, w_up, w_down = params
    length = row_in.shape[0]
    normed1 = low(row_in * rms_scale(row_in) * gain_attn)
    queries = low_back(matmul(normed1, w_query))
    key_proj = low_back(matmul(normed1, w_key))
    values = low(low_back(matmul(normed1, w_value)))
    cosine, sine = tables(pos_row)
    query_rot = low(rotate(queries.reshape(length, HEADS, HEAD_DIM), cosine, sine))
    key_rot = low(rotate(key_proj.reshape(length, KV_HEADS, HEAD_DIM), cosine, sine))
    attended = attend(query_rot, key_rot, values.reshape(length, KV_HEADS, HEAD_DIM), seg_row)
    mixed_heads = low(low_back(attended))
    residual = row_in + low_back(matmul(mixed_heads, w_out))
    normed2 = low(residual * rms_scale(residual) * gain_mlp)
    gate_proj = low_back(matmul(normed2, w_gate))
    up_proj = low_back(matmul(normed2, w_up))
    hidden = low(jax.nn.silu(gate_proj) * up_proj)
    return residual + low_back(matmul(hidden, w_down))

def reference(tokens, cotangent, selection, segments, positions, gain_attn, w_query, w_key, w_value, w_out, gain_mlp, w_gate, w_up, w_down):
    weights = tuple((param.astype(jnp.float32) for param in (gain_attn, w_query, w_key, w_value, w_out, gain_mlp, w_gate, w_up, w_down)))
    zeroed = jax.tree.map(jnp.zeros_like, weights)

    def one_row(summed, item):
        row_in, row_cot, row_keep, seg_row, pos_row = item

        def forward(layer_in, params):
            return block_layer(layer_in, seg_row, pos_row, params)
        layer_out, pullback = jax.vjp(forward, row_in.astype(jnp.float32), weights)
        grad_in, grad_params = pullback(row_cot.astype(jnp.float32) * row_keep.astype(jnp.float32)[:, None])
        summed = jax.tree.map(jnp.add, summed, grad_params)
        return (summed, (layer_out.astype(jnp.bfloat16), grad_in.astype(jnp.bfloat16)))
    totals, (mixed, tokens_grad) = lax.scan(one_row, zeroed, (tokens, cotangent, selection, segments, positions))
    grad_ga, grad_q, grad_k, grad_v, grad_o, grad_gm, grad_g, grad_u, grad_d = totals
    return (mixed, tokens_grad, grad_q, grad_k, grad_v, grad_o, grad_g, grad_u, grad_d, grad_ga, grad_gm)
```

```python
import functools

import jax
import jax.numpy as jnp
from jax import lax
from jax.experimental import pallas as pl
from jax.experimental.pallas import tpu as pltpu
from jax.sharding import PartitionSpec as P

HEADS = 32
KV_HEADS = 4
HEAD_DIM = 64
HALF = HEAD_DIM // 2

EPSILON = 1e-05
MASKED_SCORE = -1e30
SCALE = HEAD_DIM ** (-0.5)
CONTRACT_ROWS = (((0,), (0,)), ((), ()))
CONTRACT_COLS = (((1,), (1,)), ((), ()))
BF16 = jnp.bfloat16
F32 = jnp.float32


def product(left, right):
    return jnp.dot(left, right, preferred_element_type=F32)


def product_rows(left, right):
    return lax.dot_general(left, right, CONTRACT_ROWS, preferred_element_type=F32)


def product_cols(left, right):
    return lax.dot_general(left, right, CONTRACT_COLS, preferred_element_type=F32)


def rms_scale(inputs):
    return lax.rsqrt(jnp.mean(inputs * inputs, axis=-1, keepdims=True) + EPSILON)


def norm_back(grad_normed, inputs, inverse, gain):
    scaled = gain * grad_normed
    cubed = inverse * inverse * inverse
    return inverse * scaled - inputs * cubed * jnp.mean(scaled * inputs, axis=-1, keepdims=True)


class Axis:
    def __init__(self, name, inner):
        self.name = name
        self.size = lax.axis_size(name)
        self.inner = inner
        self.outer = self.size // inner
        index = lax.axis_index(name)
        self.index = index
        self.o = index // inner
        self.i = index % inner

    def shift(self, value, outer_by, inner_by):
        pairs = []
        for o in range(self.outer):
            for i in range(self.inner):
                target = ((o + outer_by) % self.outer) * self.inner + (i + inner_by) % self.inner
                pairs.append((o * self.inner + i, target))
        return lax.ppermute(value, self.name, pairs)

    def before(self, outer_by, inner_by):
        o = lax.rem(self.o + self.outer - outer_by, self.outer)
        i = lax.rem(self.i + self.inner - inner_by, self.inner)
        return o * self.inner + i

    def after(self, outer_by, inner_by):
        o = lax.rem(self.o + outer_by, self.outer)
        i = lax.rem(self.i + inner_by, self.inner)
        return o * self.inner + i

    def gather(self, block, dim=0):
        shape = block.shape[:dim] + (self.size,) + block.shape[dim:]
        out = jnp.zeros(shape, block.dtype)
        for k in range(self.outer):
            got = block if k == 0 else self.shift(block, k, 0)
            for m in range(self.inner):
                piece = got if m == 0 else self.shift(got, 0, m)
                out = lax.dynamic_update_slice_in_dim(
                    out, jnp.expand_dims(piece, dim), self.before(k, m), dim
                )
        return out

    def scatter_sum(self, parts, dim=0):
        shape = parts.shape[:dim] + (self.outer, self.inner) + parts.shape[dim + 1 :]
        grid = parts.reshape(shape)

        def inner_part(i):
            return lax.squeeze(lax.dynamic_slice_in_dim(grid, i, 1, dim + 1), (dim + 1,))

        total = inner_part(self.i).astype(F32)
        for m in range(1, self.inner):
            mine = inner_part(lax.rem(self.i + m, self.inner))
            total = total + self.shift(mine, 0, m).astype(F32)
        low = total.astype(BF16)

        def outer_part(o):
            return lax.squeeze(lax.dynamic_slice_in_dim(low, o, 1, dim), (dim,))

        out = outer_part(self.o).astype(F32)
        for k in range(1, self.outer):
            out = out + self.shift(outer_part(lax.rem(self.o + k, self.outer)), k, 0).astype(F32)
        return out

    def exchange(self, parts):
        out = jnp.zeros(parts.shape, parts.dtype)
        for k in range(self.outer):
            for m in range(self.inner):
                part = lax.dynamic_slice_in_dim(parts, self.after(k, m), 1, 0)
                got = part if (k, m) == (0, 0) else self.shift(part, k, m)
                out = lax.dynamic_update_slice_in_dim(out, got, self.before(k, m), 0)
        return out


def rotate_lanes(value, sign):
    lane = lax.broadcasted_iota(jnp.int32, value.shape, 1) % HEAD_DIM
    first = lane < HALF
    width = value.shape[1]
    up = pltpu.roll(value, width - HALF, 1)
    down = pltpu.roll(value, HALF, 1)
    return jnp.where(first, -sign * up, sign * down)


def mask_bias(bias_ref, seg_row_ref, seg_col_ref, length):
    rows = 256
    for start in range(0, length, rows):
        keys = seg_col_ref[start : start + rows, :]
        queries = seg_row_ref[:, :]
        key_pos = start + lax.broadcasted_iota(jnp.int32, (rows, length), 0)
        query_pos = lax.broadcasted_iota(jnp.int32, (rows, length), 1)
        allowed = (keys == queries) & (key_pos <= query_pos)
        bias_ref[start : start + rows, :] = jnp.where(allowed, 0.0, MASKED_SCORE)


def attend_kernel(
    qblock,
    q_ref,
    kv_ref,
    cos_ref,
    sin_ref,
    seg_row_ref,
    seg_col_ref,
    o_ref,
    qr_ref,
    kvr_ref,
    lse_ref,
    bias_ref,
):
    length = q_ref.shape[0]
    cosine = cos_ref[...]
    sine = sin_ref[...]

    @pl.when(pl.program_id(0) == 0)
    def _():
        mask_bias(bias_ref, seg_row_ref, seg_col_ref, length)
        kv = kv_ref[...]
        rotated = kv * cosine + rotate_lanes(kv, 1.0) * sine
        lane = lax.broadcasted_iota(jnp.int32, kv.shape, 1)
        kvr_ref[...] = jnp.where(lane < HEAD_DIM, rotated, kv).astype(BF16)

    q = q_ref[...]
    qr_ref[...] = (q * cosine + rotate_lanes(q, 1.0) * sine).astype(BF16)
    for start in range(0, length, qblock):
        stop = start + qblock
        keys = kvr_ref[:stop, :HEAD_DIM]
        values = kvr_ref[:stop, HEAD_DIM:]
        for head in range(2):
            lanes = slice(head * HEAD_DIM, (head + 1) * HEAD_DIM)
            queries = qr_ref[start:stop, lanes] * SCALE
            scores = product_cols(keys, queries.astype(BF16)) + bias_ref[:stop, start:stop]
            top = jnp.max(scores, axis=0, keepdims=True)
            grown = jnp.exp(scores - top)
            total = jnp.sum(grown, axis=0, keepdims=True)
            probs = (grown * (1.0 / total)).astype(BF16)
            lse_ref[0, head : head + 1, start:stop] = top + jnp.log(total)
            o_ref[start:stop, lanes] = product_rows(probs, values).astype(BF16)


def attend_back_kernel(
    qblock,
    qr_ref,
    kvr_ref,
    do_ref,
    lse_ref,
    cos_ref,
    sin_ref,
    seg_row_ref,
    seg_col_ref,
    dqkv_ref,
    bias_ref,
    dq_ref,
    dk_ref,
    dv_ref,
):
    length = qr_ref.shape[0]
    cosine = cos_ref[...]
    sine = sin_ref[...]
    pair = pl.program_id(0)

    @pl.when(pair == 0)
    def _():
        mask_bias(bias_ref, seg_row_ref, seg_col_ref, length)
        dk_ref[...] = jnp.zeros_like(dk_ref)
        dv_ref[...] = jnp.zeros_like(dv_ref)

    for start in range(0, length, qblock):
        stop = start + qblock
        keys = kvr_ref[:stop, :HEAD_DIM]
        values = kvr_ref[:stop, HEAD_DIM:]
        for head in range(2):
            lanes = slice(head * HEAD_DIM, (head + 1) * HEAD_DIM)
            queries = (qr_ref[start:stop, lanes] * SCALE).astype(BF16)
            grads = do_ref[start:stop, lanes]
            scores = product_cols(keys, queries) + bias_ref[:stop, start:stop]
            probs = jnp.exp(scores - lse_ref[0, head : head + 1, start:stop])
            dprobs = product_cols(values, grads)
            delta = jnp.sum(probs * dprobs, axis=0, keepdims=True)
            dscores = (probs * (dprobs - delta)).astype(BF16)
            dv_ref[:stop, :] += product(probs.astype(BF16), grads)
            dk_ref[:stop, :] += product(dscores, queries)
            dq_ref[start:stop, lanes] = product_rows(dscores, keys) * SCALE

    dq = dq_ref[...]
    turned = rotate_lanes(dq * sine, -1.0)
    columns = pl.ds(pl.multiple_of(pair * 128, 128), 128)
    dqkv_ref[:, columns] = (dq * cosine + turned).astype(BF16)

    @pl.when(pair == pl.num_programs(0) - 1)
    def _():
        grads = jnp.concatenate([dk_ref[...], dv_ref[...]], axis=1)
        back = grads * cosine + rotate_lanes(grads * sine, -1.0)
        lane = lax.broadcasted_iota(jnp.int32, grads.shape, 1)
        width = dqkv_ref.shape[1]
        dqkv_ref[:, width - 128 :] = jnp.where(lane < HEAD_DIM, back, grads).astype(BF16)


def whole_spec(shape):
    return pl.BlockSpec(shape, lambda j: (0,) * len(shape))


def attend(qkv, cosine, sine, seg_row, seg_col):
    length, width = qkv.shape
    pairs = width // 128 - 1
    qblock = min(256, length)
    return pl.pallas_call(
        functools.partial(attend_kernel, qblock),
        grid=(pairs,),
        in_specs=[
            pl.BlockSpec((length, 128), lambda j: (0, j)),
            pl.BlockSpec((length, 128), lambda j: (0, pairs)),
            whole_spec((length, 128)),
            whole_spec((length, 128)),
            whole_spec((1, length)),
            whole_spec((length, 1)),
        ],
        out_specs=[
            pl.BlockSpec((length, 128), lambda j: (0, j)),
            pl.BlockSpec((length, 128), lambda j: (0, j)),
            whole_spec((length, 128)),
            pl.BlockSpec((1, 2, length), lambda j: (j, 0, 0)),
        ],
        out_shape=[
            jax.ShapeDtypeStruct((length, pairs * 128), BF16),
            jax.ShapeDtypeStruct((length, pairs * 128), BF16),
            jax.ShapeDtypeStruct((length, 128), BF16),
            jax.ShapeDtypeStruct((pairs, 2, length), F32),
        ],
        scratch_shapes=[pltpu.VMEM((length, length), F32)],
        compiler_params=pltpu.CompilerParams(vmem_limit_bytes=48 * 1024 * 1024),
        cost_estimate=pl.CostEstimate(
            flops=pairs * 2 * length * length * HEAD_DIM * 2,
            bytes_accessed=8 * length * width,
            transcendentals=pairs * length * length,
        ),
    )(qkv, qkv, cosine, sine, seg_row, seg_col)


def attend_back(qr, kvr, grads, lse, cosine, sine, seg_row, seg_col):
    length = qr.shape[0]
    pairs = qr.shape[1] // 128
    qblock = min(256, length)
    return pl.pallas_call(
        functools.partial(attend_back_kernel, qblock),
        grid=(pairs,),
        in_specs=[
            pl.BlockSpec((length, 128), lambda j: (0, j)),
            whole_spec((length, 128)),
            pl.BlockSpec((length, 128), lambda j: (0, j)),
            pl.BlockSpec((1, 2, length), lambda j: (j, 0, 0)),
            whole_spec((length, 128)),
            whole_spec((length, 128)),
            whole_spec((1, length)),
            whole_spec((length, 1)),
        ],
        out_specs=whole_spec((length, (pairs + 1) * 128)),
        out_shape=jax.ShapeDtypeStruct((length, (pairs + 1) * 128), BF16),
        scratch_shapes=[
            pltpu.VMEM((length, length), F32),
            pltpu.VMEM((length, 128), F32),
            pltpu.VMEM((length, HEAD_DIM), F32),
            pltpu.VMEM((length, HEAD_DIM), F32),
        ],
        compiler_params=pltpu.CompilerParams(vmem_limit_bytes=48 * 1024 * 1024),
        cost_estimate=pl.CostEstimate(
            flops=pairs * 5 * length * length * HEAD_DIM * 2,
            bytes_accessed=12 * length * qr.shape[1],
            transcendentals=pairs * length * length,
        ),
    )(qr, kvr, grads, lse, cosine, sine, seg_row, seg_col)


def per_device(
    tokens,
    cotangent,
    selection,
    segments,
    positions,
    gain_attn,
    w_query,
    w_key,
    w_value,
    w_out,
    gain_mlp,
    w_gate,
    w_up,
    w_down,
):
    seq = Axis("seq", 2)
    batch = Axis("batch", lax.axis_size("batch") // 4)
    n_seq, n_batch = seq.size, batch.size
    length, width = tokens.shape[1], tokens.shape[2]
    total_len = length * n_seq
    rows = w_query.shape[0]
    ff = w_gate.shape[1]
    q_cols = w_query.shape[1] // n_seq
    sharers = n_seq // KV_HEADS

    query_parts = w_query.reshape(rows, n_seq, q_cols)
    key_parts = jnp.repeat(w_key.reshape(rows, KV_HEADS, HEAD_DIM), sharers, axis=1)
    value_parts = jnp.repeat(w_value.reshape(rows, KV_HEADS, HEAD_DIM), sharers, axis=1)
    qkv_parts = jnp.concatenate([query_parts, key_parts, value_parts], axis=2).transpose(1, 0, 2)

    def spread(parts):
        mine = seq.exchange(parts)
        return batch.gather(mine, 1).reshape(n_seq * n_batch * rows, parts.shape[2])

    def collect(grad):
        parts = grad.astype(BF16).reshape(n_seq, n_batch, rows, grad.shape[1])
        return seq.exchange(batch.scatter_sum(parts, 1).astype(BF16)).astype(F32)

    def by_columns(weight):
        return weight.reshape(rows, n_seq, weight.shape[1] // n_seq).transpose(1, 0, 2)

    places = seq.gather(jnp.stack([segments[0], positions[0]]), 1)
    seg_all = places[0].reshape(total_len)
    pos_all = places[1].reshape(total_len)
    gains = batch.gather(seq.gather(jnp.stack([gain_attn, gain_mlp]), 1), 2)
    gain_one = gains[0].reshape(1, width).astype(F32)
    gain_two = gains[1].reshape(1, width).astype(F32)
    x_all = seq.gather(tokens[0], 0).reshape(total_len, width).astype(F32)
    w_qkv = spread(qkv_parts)
    wo = batch.gather(w_out, 0).reshape(n_batch * rows, width)
    wg = spread(by_columns(w_gate))
    wu = spread(by_columns(w_up))
    wd = batch.gather(w_down, 0).reshape(n_batch * w_down.shape[0], width)

    grad_out_row = cotangent[0].astype(F32) * selection[0].astype(F32)[:, None]
    grad_low = seq.gather(grad_out_row.astype(BF16), 0).reshape(total_len, width)

    row_input = tokens[0].astype(F32)
    inv_attn = rms_scale(row_input)
    normed1 = (x_all * rms_scale(x_all) * gain_one).astype(BF16)
    qkv = product(normed1, w_qkv)
    frequency = 10000.0 ** (-(jnp.arange(HALF, dtype=F32) * 2.0 / HEAD_DIM))
    angles = pos_all.astype(F32)[:, None] * jnp.tile(frequency, 4)[None, :]
    cosine, sine = jnp.cos(angles), jnp.sin(angles)
    seg_row, seg_col = seg_all[None, :], seg_all[:, None]
    heads_out, query_rot, kv_rot, lse = attend(qkv, cosine, sine, seg_row, seg_col)
    attn_part = product(heads_out, wo).astype(BF16).reshape(n_seq, length, width)
    residual = row_input + seq.scatter_sum(attn_part, 0)

    inv_mlp = rms_scale(residual)
    normed2_own = (residual * inv_mlp * gain_two).astype(BF16)
    normed2 = seq.gather(normed2_own, 0).reshape(total_len, width)
    gate_proj = product(normed2, wg)
    up_proj = product(normed2, wu)
    sigma = jax.nn.sigmoid(gate_proj)
    activated = gate_proj * sigma
    hidden = (activated * up_proj).astype(BF16)
    mixed_part = product(hidden, wd).astype(BF16).reshape(n_seq, length, width)
    mixed = (residual + seq.scatter_sum(mixed_part, 0)).astype(BF16)[None]

    grad_down = product_rows(hidden, grad_low)
    grad_hidden = product_cols(grad_low, wd)
    grad_gate_act = (
        grad_hidden * up_proj * sigma * (1.0 + gate_proj * (1.0 - sigma))
    ).astype(BF16)
    grad_up_act = (grad_hidden * activated).astype(BF16)
    grad_gate = product_rows(normed2, grad_gate_act)
    grad_up = product_rows(normed2, grad_up_act)
    normed_part = product_cols(grad_gate_act, wg) + product_cols(grad_up_act, wu)
    normed_terms = seq.scatter_sum(normed_part.astype(BF16).reshape(n_seq, length, width), 0)
    grad_resid = grad_out_row + norm_back(normed_terms, residual, inv_mlp, gain_two)

    down_own = batch.scatter_sum(
        grad_down.astype(BF16).reshape(n_batch, w_down.shape[0], width), 0
    )
    gate_own = collect(grad_gate).transpose(1, 0, 2).reshape(rows, ff)
    up_own = collect(grad_up).transpose(1, 0, 2).reshape(rows, ff)

    grad_branch = seq.gather(grad_resid.astype(BF16), 0).reshape(total_len, width)
    grad_wout = product_rows(heads_out, grad_branch)
    grad_heads = product_cols(grad_branch, wo).astype(BF16)
    grad_qkv_act = attend_back(
        query_rot, kv_rot, grad_heads, lse, cosine, sine, seg_row, seg_col
    )
    grad_wqkv = product_rows(normed1, grad_qkv_act)
    input_part = product_cols(grad_qkv_act, w_qkv).astype(BF16).reshape(n_seq, length, width)
    grad_normed1 = seq.scatter_sum(input_part, 0)
    tokens_grad = (
        grad_resid + norm_back(grad_normed1, row_input, inv_attn, gain_one)
    ).astype(BF16)[None]
    out_own = batch.scatter_sum(grad_wout.astype(BF16).reshape(n_batch, rows, width), 0)
    qkv_own = collect(grad_wqkv)
    query_own = qkv_own[:, :, :q_cols].transpose(1, 0, 2).reshape(rows, n_seq * q_cols)

    def shared(columns):
        heads = columns.reshape(KV_HEADS, sharers, rows, HEAD_DIM).sum(axis=1)
        return heads.transpose(1, 0, 2).reshape(rows, KV_HEADS * HEAD_DIM)

    key_own = shared(qkv_own[:, :, q_cols : q_cols + HEAD_DIM])
    value_own = shared(qkv_own[:, :, q_cols + HEAD_DIM :])

    def along(weight, grad):
        return jnp.sum(weight.astype(F32) * grad, axis=1)

    gain1_own = (
        along(w_query, query_own) + along(w_key, key_own) + along(w_value, value_own)
    ) / gain_attn.astype(F32)
    gain2_own = (along(w_gate, gate_own) + along(w_up, up_own)) / gain_mlp.astype(F32)
    return (
        mixed,
        tokens_grad,
        query_own,
        key_own,
        value_own,
        out_own,
        gate_own,
        up_own,
        down_own,
        gain1_own,
        gain2_own,
    )


def solution(mesh):
    both = ("seq", "batch")
    tokens = P("batch", "seq", None)
    flags = P("batch", "seq")
    matrix = P(both, None)
    vector = P(both)
    in_specs = (
        (tokens, tokens, flags, flags, flags)
        + (vector, matrix, matrix, matrix, matrix)
        + (vector, matrix, matrix, matrix)
    )
    out_specs = (tokens, tokens) + (matrix,) * 7 + (vector, vector)
    return jax.shard_map(
        per_device, mesh=mesh, in_specs=in_specs, out_specs=out_specs, check_vma=False
    )
```

```python
import functools

import jax
import jax.numpy as jnp
from jax import lax
from jax.experimental import pallas as pl
from jax.experimental.pallas import tpu as pltpu
from jax.sharding import PartitionSpec as P

HEADS = 32
KV_HEADS = 4
HEAD_DIM = 64
HALF = HEAD_DIM // 2

EPSILON = 1e-05
MASKED_SCORE = -1e30
SCALE = HEAD_DIM ** (-0.5)
CONTRACT_ROWS = (((0,), (0,)), ((), ()))
CONTRACT_COLS = (((1,), (1,)), ((), ()))
BF16 = jnp.bfloat16
F32 = jnp.float32


def product(left, right):
    return jnp.dot(left, right, preferred_element_type=F32)


def product_rows(left, right):
    return lax.dot_general(left, right, CONTRACT_ROWS, preferred_element_type=F32)


def product_cols(left, right):
    return lax.dot_general(left, right, CONTRACT_COLS, preferred_element_type=F32)


def rms_scale(inputs):
    return lax.rsqrt(jnp.mean(inputs * inputs, axis=-1, keepdims=True) + EPSILON)


def norm_back(grad_normed, inputs, inverse, gain):
    scaled = gain * grad_normed
    cubed = inverse * inverse * inverse
    return inverse * scaled - inputs * cubed * jnp.mean(scaled * inputs, axis=-1, keepdims=True)


class Axis:
    def __init__(self, name, inner):
        self.name = name
        self.size = lax.axis_size(name)
        self.inner = inner
        self.outer = self.size // inner
        index = lax.axis_index(name)
        self.index = index
        self.o = index // inner
        self.i = index % inner

    def shift(self, value, outer_by, inner_by):
        pairs = []
        for o in range(self.outer):
            for i in range(self.inner):
                target = ((o + outer_by) % self.outer) * self.inner + (i + inner_by) % self.inner
                pairs.append((o * self.inner + i, target))
        return lax.ppermute(value, self.name, pairs)

    def before(self, outer_by, inner_by):
        o = lax.rem(self.o + self.outer - outer_by, self.outer)
        i = lax.rem(self.i + self.inner - inner_by, self.inner)
        return o * self.inner + i

    def after(self, outer_by, inner_by):
        o = lax.rem(self.o + outer_by, self.outer)
        i = lax.rem(self.i + inner_by, self.inner)
        return o * self.inner + i

    def gather(self, block, dim=0):
        shape = block.shape[:dim] + (self.size,) + block.shape[dim:]
        out = jnp.zeros(shape, block.dtype)
        for k in range(self.outer):
            got = block if k == 0 else self.shift(block, k, 0)
            for m in range(self.inner):
                piece = got if m == 0 else self.shift(got, 0, m)
                out = lax.dynamic_update_slice_in_dim(
                    out, jnp.expand_dims(piece, dim), self.before(k, m), dim
                )
        return out

    def scatter_sum(self, parts, dim=0):
        shape = parts.shape[:dim] + (self.outer, self.inner) + parts.shape[dim + 1 :]
        grid = parts.reshape(shape)

        def inner_part(i):
            return lax.squeeze(lax.dynamic_slice_in_dim(grid, i, 1, dim + 1), (dim + 1,))

        total = inner_part(self.i).astype(F32)
        for m in range(1, self.inner):
            mine = inner_part(lax.rem(self.i + m, self.inner))
            total = total + self.shift(mine, 0, m).astype(F32)
        low = total.astype(BF16)

        def outer_part(o):
            return lax.squeeze(lax.dynamic_slice_in_dim(low, o, 1, dim), (dim,))

        out = outer_part(self.o).astype(F32)
        for k in range(1, self.outer):
            out = out + self.shift(outer_part(lax.rem(self.o + k, self.outer)), k, 0).astype(F32)
        return out

    def exchange(self, parts):
        out = jnp.zeros(parts.shape, parts.dtype)
        for k in range(self.outer):
            for m in range(self.inner):
                part = lax.dynamic_slice_in_dim(parts, self.after(k, m), 1, 0)
                got = part if (k, m) == (0, 0) else self.shift(part, k, m)
                out = lax.dynamic_update_slice_in_dim(out, got, self.before(k, m), 0)
        return out


def rotate_lanes(value, sign):
    lane = lax.broadcasted_iota(jnp.int32, value.shape, 1) % HEAD_DIM
    first = lane < HALF
    width = value.shape[1]
    up = pltpu.roll(value, width - HALF, 1)
    down = pltpu.roll(value, HALF, 1)
    return jnp.where(first, -sign * up, sign * down)


def mask_bias(bias_ref, seg_row_ref, seg_col_ref, length):
    rows = 256
    for start in range(0, length, rows):
        keys = seg_col_ref[start : start + rows, :]
        queries = seg_row_ref[:, :]
        key_pos = start + lax.broadcasted_iota(jnp.int32, (rows, length), 0)
        query_pos = lax.broadcasted_iota(jnp.int32, (rows, length), 1)
        allowed = (keys == queries) & (key_pos <= query_pos)
        bias_ref[start : start + rows, :] = jnp.where(allowed, 0.0, MASKED_SCORE)


def attend_back_kernel(
    qblock,
    qr_ref,
    kvr_ref,
    do_ref,
    lse_ref,
    cos_ref,
    sin_ref,
    seg_row_ref,
    seg_col_ref,
    dqkv_ref,
    bias_ref,
    dq_ref,
    dk_ref,
    dv_ref,
):
    length = qr_ref.shape[0]
    cosine = cos_ref[...]
    sine = sin_ref[...]
    pair = pl.program_id(0)

    @pl.when(pair == 0)
    def _():
        mask_bias(bias_ref, seg_row_ref, seg_col_ref, length)
        dk_ref[...] = jnp.zeros_like(dk_ref)
        dv_ref[...] = jnp.zeros_like(dv_ref)

    for start in range(0, length, qblock):
        stop = start + qblock
        keys = kvr_ref[:stop, :HEAD_DIM]
        values = kvr_ref[:stop, HEAD_DIM:]
        for head in range(2):
            lanes = slice(head * HEAD_DIM, (head + 1) * HEAD_DIM)
            queries = (qr_ref[start:stop, lanes] * SCALE).astype(BF16)
            grads = do_ref[start:stop, lanes]
            scores = product_cols(keys, queries) + bias_ref[:stop, start:stop]
            probs = jnp.exp(scores - lse_ref[0, head : head + 1, start:stop])
            dprobs = product_cols(values, grads)
            delta = jnp.sum(probs * dprobs, axis=0, keepdims=True)
            dscores = (probs * (dprobs - delta)).astype(BF16)
            dv_ref[:stop, :] += product(probs.astype(BF16), grads)
            dk_ref[:stop, :] += product(dscores, queries)
            dq_ref[start:stop, lanes] = product_rows(dscores, keys) * SCALE

    dq = dq_ref[...]
    turned = rotate_lanes(dq * sine, -1.0)
    columns = pl.ds(pl.multiple_of(pair * 128, 128), 128)
    dqkv_ref[:, columns] = (dq * cosine + turned).astype(BF16)

    @pl.when(pair == pl.num_programs(0) - 1)
    def _():
        grads = jnp.concatenate([dk_ref[...], dv_ref[...]], axis=1)
        back = grads * cosine + rotate_lanes(grads * sine, -1.0)
        lane = lax.broadcasted_iota(jnp.int32, grads.shape, 1)
        width = dqkv_ref.shape[1]
        dqkv_ref[:, width - 128 :] = jnp.where(lane < HEAD_DIM, back, grads).astype(BF16)


def whole_spec(shape):
    return pl.BlockSpec(shape, lambda j: (0,) * len(shape))


def attend_back(qr, kvr, grads, lse, cosine, sine, seg_row, seg_col):
    length = qr.shape[0]
    pairs = qr.shape[1] // 128
    qblock = min(256, length)
    return pl.pallas_call(
        functools.partial(attend_back_kernel, qblock),
        grid=(pairs,),
        in_specs=[
            pl.BlockSpec((length, 128), lambda j: (0, j)),
            whole_spec((length, 128)),
            pl.BlockSpec((length, 128), lambda j: (0, j)),
            pl.BlockSpec((1, 2, length), lambda j: (j, 0, 0)),
            whole_spec((length, 128)),
            whole_spec((length, 128)),
            whole_spec((1, length)),
            whole_spec((length, 1)),
        ],
        out_specs=whole_spec((length, (pairs + 1) * 128)),
        out_shape=jax.ShapeDtypeStruct((length, (pairs + 1) * 128), BF16),
        scratch_shapes=[
            pltpu.VMEM((length, length), F32),
            pltpu.VMEM((length, 128), F32),
            pltpu.VMEM((length, HEAD_DIM), F32),
            pltpu.VMEM((length, HEAD_DIM), F32),
        ],
        compiler_params=pltpu.CompilerParams(vmem_limit_bytes=48 * 1024 * 1024),
        cost_estimate=pl.CostEstimate(
            flops=pairs * 5 * length * length * HEAD_DIM * 2,
            bytes_accessed=12 * length * qr.shape[1],
            transcendentals=pairs * length * length,
        ),
    )(qr, kvr, grads, lse, cosine, sine, seg_row, seg_col)


MESH = pl.DeviceIdType.MESH


class Place:
    def __init__(self, sizes):
        self.ny, self.nc, self.nz, self.nx = sizes
        self.s = lax.axis_index("seq")
        self.b = lax.axis_index("batch")
        self.y, self.c = self.s // self.nc, self.s % self.nc
        self.z, self.x = self.b // self.nx, self.b % self.nx

    def seq_at(self, dy, dc):
        return (self.y + dy + self.ny) % self.ny * self.nc + (self.c + dc + self.nc) % self.nc

    def batch_at(self, dz, dx):
        return (self.z + dz + self.nz) % self.nz * self.nx + (self.x + dx + self.nx) % self.nx


class Wires:
    def __init__(self, send_sems, recv_sems):
        self.send_sems, self.recv_sems = send_sems, recv_sems
        self.started = []
        self.count = 0

    def push(self, source, target, device):
        index = self.count
        self.count += 1
        copy = pltpu.make_async_remote_copy(
            src_ref=source,
            dst_ref=target,
            send_sem=self.send_sems.at[index],
            recv_sem=self.recv_sems.at[index],
            device_id=device,
            device_id_type=MESH,
        )
        copy.start()
        self.started.append(copy)
        return index, device

    def wait(self, ticket, landed):
        index, device = ticket
        pltpu.make_async_remote_copy(
            src_ref=landed,
            dst_ref=landed,
            send_sem=self.send_sems.at[index],
            recv_sem=self.recv_sems.at[index],
            device_id=device,
            device_id_type=MESH,
        ).wait_recv()

    def close(self):
        for copy in self.started:
            copy.wait_send()


class Gather:
    def __init__(self, wires, slot, own, outer, inner, at, device):
        self.wires, self.slot, self.own = wires, slot, own
        self.outer, self.inner, self.at, self.device = outer, inner, at, device
        self.first, self.second = {}, {}

    def start(self):
        mine = self.at(0, 0)
        for k in range(1, self.outer):
            self.first[k] = self.wires.push(self.own, self.slot(mine), self.device(self.at(k, 0)))
        for m in range(1, self.inner):
            self.second[0, m] = self.wires.push(
                self.own, self.slot(mine), self.device(self.at(0, m))
            )

    def pass_on(self, k):
        came = self.slot(self.at(-k, 0))
        self.wires.wait(self.first[k], came)
        for m in range(1, self.inner):
            self.second[k, m] = self.wires.push(came, came, self.device(self.at(0, m)))

    def finish(self):
        for (k, m), ticket in self.second.items():
            self.wires.wait(ticket, self.slot(self.at(-k, -m)))


def enter(place):
    peers = [
        (place.seq_at(dy, dc), place.b)
        for dy in range(place.ny)
        for dc in range(place.nc)
        if (dy, dc) != (0, 0)
    ]
    peers += [(place.s, place.batch_at(k, 0)) for k in range(1, place.nz)]
    peers += [(place.s, place.batch_at(0, m)) for m in range(1, place.nx)]
    barrier = pltpu.get_barrier_semaphore()
    for peer in peers:
        pl.semaphore_signal(barrier, inc=1, device_id=peer, device_id_type=MESH)
    pl.semaphore_wait(barrier, len(peers))


def front_kernel(
    sizes,
    pairs,
    x_ref,
    gb_ref,
    table_ref,
    gain_ref,
    qkv_ref,
    out_ref,
    gate_ref,
    up_ref,
    down_ref,
    wqkv_ref,
    wo_ref,
    wg_ref,
    wu_ref,
    wd_ref,
    gb_all_ref,
    n1_ref,
    n2_ref,
    residual_ref,
    heads_ref,
    qr_ref,
    kvr_ref,
    lse_ref,
    tables_ref,
    gains_ref,
    x_all_ref,
    table_all_ref,
    gain_all_ref,
    qkv_proj_ref,
    bias_ref,
    part_ref,
    core_in_ref,
    far_in_ref,
    n2_own_ref,
    send_sems,
    recv_sems,
    copy_sems,
):
    place = Place(sizes)
    ny, nc, nz, nx = sizes
    s, b = place.s, place.b
    n_seq, n_batch = ny * nc, nz * nx
    length, width = x_ref.shape
    total_len = n_seq * length
    wires = Wires(send_sems, recv_sems)
    copies = []

    def local(source, target):
        copy = pltpu.make_async_copy(source, target, copy_sems.at[len(copies)])
        copy.start()
        copies.append(copy)
        return copy

    def over_batch(slot, own):
        return Gather(wires, slot, own, nz, nx, place.batch_at, lambda j: (s, j))

    def over_seq(slot, own):
        return Gather(wires, slot, own, ny, nc, place.seq_at, lambda j: (j, b))

    def columns(ref):
        return lambda j: ref.at[:, j]

    def blocks(ref):
        return lambda j: ref.at[j]

    class Exchange:
        def __init__(self, parts, target, many=True):
            self.target = target
            part = (lambda j: parts.at[j]) if many else (lambda j: parts)
            self.copy = local(part(s), target.at[s, b])
            self.tickets = {}
            for dy in range(ny):
                for dc in range(nc):
                    if (dy, dc) != (0, 0):
                        j = place.seq_at(dy, dc)
                        self.tickets[dy, dc] = wires.push(part(j), target.at[s, b], (j, b))

        def finish(self):
            self.copy.wait()
            for (dy, dc), ticket in self.tickets.items():
                wires.wait(ticket, self.target.at[place.seq_at(-dy, -dc), b])

    enter(place)
    qkv_parts = Exchange(qkv_ref, wqkv_ref)
    gain_parts = Exchange(gain_ref, gain_all_ref, many=False)
    own_table = local(table_ref, table_all_ref.at[s])
    own_x = local(x_ref, x_all_ref.at[s])
    own_out = local(out_ref, wo_ref.at[b])
    own_down = local(down_ref, wd_ref.at[b])
    own_gb = local(gb_ref, gb_all_ref.at[s])
    table_all = over_seq(blocks(table_all_ref), table_ref)
    table_all.start()
    x_all = over_seq(blocks(x_all_ref), x_ref)
    x_all.start()
    wo = over_batch(blocks(wo_ref), out_ref)
    wo.start()
    gate_parts = Exchange(gate_ref, wg_ref)
    up_parts = Exchange(up_ref, wu_ref)
    wqkv = over_batch(columns(wqkv_ref), wqkv_ref.at[:, b])
    gains = over_batch(columns(gain_all_ref), gain_all_ref.at[:, b])
    wg = over_batch(columns(wg_ref), wg_ref.at[:, b])
    wu = over_batch(columns(wu_ref), wu_ref.at[:, b])
    wd = over_batch(blocks(wd_ref), down_ref)
    gb_all = over_seq(blocks(gb_all_ref), gb_ref)

    qkv_parts.finish()
    wqkv.start()
    gain_parts.finish()
    gains.start()
    for k in range(1, ny):
        table_all.pass_on(k)
        x_all.pass_on(k)
    for k in range(1, nz):
        wo.pass_on(k)
        gains.pass_on(k)
    for k in range(1, nz):
        wqkv.pass_on(k)
    gate_parts.finish()
    wg.start()
    gb_all.start()

    own_table.wait()
    table_all.finish()
    own_x.wait()
    x_all.finish()
    gains.finish()
    pieces = [(i, j) for i in range(n_seq) for j in range(n_batch)]
    rows = width // (n_seq * n_batch)
    for g in range(2):
        gains_ref[g : g + 1, :] = jnp.concatenate(
            [gain_all_ref[i, j, g : g + 1, :rows] for i, j in pieces], axis=1
        )
    gain_one = gains_ref[0:1, :]

    def norm_rows(i, unused):
        part = x_all_ref[i // 2, pl.ds(i % 2 * (length // 2), length // 2), :].astype(F32)
        at = pl.ds(pl.multiple_of(i * (length // 2), length // 2), length // 2)
        n1_ref[at, :] = (part * rms_scale(part) * gain_one).astype(BF16)
        return unused

    lax.fori_loop(0, 2 * n_seq, norm_rows, 0)
    for j in range(n_seq):
        at = slice(j * length, (j + 1) * length)
        table = table_all_ref[j]
        cos_part, sin_part = table[:, :HALF], table[:, HALF:HEAD_DIM]
        tables_ref[0, at, :] = jnp.concatenate([cos_part] * 4, axis=1)
        tables_ref[1, at, :] = jnp.concatenate([sin_part] * 4, axis=1)
    flipped = [jnp.transpose(table_all_ref[j])[HEAD_DIM : HEAD_DIM + 1, :] for j in range(n_seq)]
    query_seg = jnp.concatenate(flipped, axis=1)
    for j in range(n_seq):
        key_seg = table_all_ref[j][:, HEAD_DIM : HEAD_DIM + 1]
        key_pos = j * length + lax.broadcasted_iota(jnp.int32, (length, total_len), 0)
        query_pos = lax.broadcasted_iota(jnp.int32, (length, total_len), 1)
        allowed = (key_seg == query_seg) & (key_pos <= query_pos)
        bias_ref[j * length : (j + 1) * length, :] = jnp.where(allowed, 0.0, MASKED_SCORE).astype(
            bias_ref.dtype
        )

    wqkv.finish()
    weights = wqkv_ref[...].reshape(width, wqkv_ref.shape[3])

    def project(i, unused):
        at = pl.ds(pl.multiple_of(i * length, length), length)
        qkv_proj_ref[at, :] = product(n1_ref[at, :], weights)
        return unused

    lax.fori_loop(0, n_seq, project, 0)
    cosine, sine = tables_ref[0], tables_ref[1]
    kv = qkv_proj_ref[:, pairs * 128 :]
    lane = lax.broadcasted_iota(jnp.int32, kv.shape, 1)
    rotated = kv * cosine + rotate_lanes(kv, 1.0) * sine
    kvr_ref[...] = jnp.where(lane < HEAD_DIM, rotated, kv).astype(BF16)

    def attend_pair(pair, unused):
        at = pl.ds(pl.multiple_of(pair * 128, 128), 128)
        q = qkv_proj_ref[:, at]
        qr = (q * tables_ref[0] + rotate_lanes(q, 1.0) * tables_ref[1]).astype(BF16)
        qr_ref[:, at] = qr
        low = (qr * SCALE).astype(BF16)
        for start in range(0, total_len, length):
            stop = start + length
            outs = []
            for head in range(2):
                queries = low[start:stop, head * HEAD_DIM : (head + 1) * HEAD_DIM]
                scores = product_cols(kvr_ref[:stop, :HEAD_DIM], queries)
                scores = scores + bias_ref[:stop, start:stop].astype(F32)
                top = jnp.max(scores, axis=0, keepdims=True)
                grown = jnp.exp(scores - top)
                total = jnp.sum(grown, axis=0, keepdims=True)
                probs = (grown * (1.0 / total)).astype(BF16)
                lse_ref[pair, head : head + 1, start:stop] = top + jnp.log(total)
                outs.append(product_rows(probs, kvr_ref[:stop, HEAD_DIM:]))
            heads_ref[start:stop, at] = jnp.concatenate(outs, axis=1).astype(BF16)
        return unused

    lax.fori_loop(0, pairs // 2, attend_pair, 0)
    wg.pass_on(1)
    lax.fori_loop(pairs // 2, pairs, attend_pair, 0)

    own_out.wait()
    wo.finish()
    out_weights = wo_ref[...].reshape(n_batch * wo_ref.shape[1], width)

    def out_part(j):
        at = pl.ds(pl.multiple_of(j * length, length), length)
        return product(heads_ref[at, :], out_weights)

    to_core = {}
    for dy in range(ny):
        for dc in range(1, nc):
            j = place.seq_at(dy, dc)
            part_ref[j] = out_part(j).astype(BF16)
            to_core[dy, dc] = wires.push(
                part_ref.at[j], core_in_ref.at[dc - 1, dy], (place.seq_at(0, dc), b)
            )

    def with_core(dy):
        total = out_part(place.seq_at(dy, 0))
        for dc in range(1, nc):
            wires.wait(to_core[dy, dc], core_in_ref.at[dc - 1, dy])
            total = total + core_in_ref[dc - 1, dy].astype(F32)
        return total

    to_far = {}
    for dy in range(1, ny):
        j = place.seq_at(dy, 0)
        part_ref[j] = with_core(dy).astype(BF16)
        to_far[dy] = wires.push(part_ref.at[j], far_in_ref.at[dy - 1], (j, b))
    total = with_core(0) + x_all_ref[s].astype(F32)
    wg.pass_on(2)
    up_parts.finish()
    wu.start()
    for dy in range(1, ny):
        wires.wait(to_far[dy], far_in_ref.at[dy - 1])
        total = total + far_in_ref[dy - 1].astype(F32)
    residual_ref[...] = total
    n2_own_ref[...] = (total * rms_scale(total) * gains_ref[1:2, :]).astype(BF16)
    own_n2 = local(n2_own_ref, n2_ref.at[s])
    n2 = over_seq(blocks(n2_ref), n2_own_ref)
    n2.start()
    wg.pass_on(3)
    for k in range(4, nz):
        wg.pass_on(k)
    wu.pass_on(1)
    wd.start()
    for k in range(1, ny):
        n2.pass_on(k)
        gb_all.pass_on(k)
    for k in range(2, nz):
        wu.pass_on(k)
    for k in range(1, nz):
        wd.pass_on(k)
    n2.finish()
    gb_all.finish()
    wg.finish()
    wu.finish()
    wd.finish()
    own_down.wait()
    own_gb.wait()
    own_n2.wait()
    wires.close()


def front(sizes, x, gb, table, gain, qkv, w_out, gate, up, down):
    ny, nc, nz, nx = sizes
    n_seq, n_batch = ny * nc, nz * nx
    length, width = x.shape
    total_len = n_seq * length
    pairs = qkv.shape[2] // 128 - 1
    rows = w_out.shape[0]
    hbm = pl.BlockSpec(memory_space=pl.ANY)
    vmem = pl.BlockSpec(memory_space=pltpu.VMEM)

    def shape(dims, kind):
        return jax.ShapeDtypeStruct(dims, kind)

    results = [
        (vmem, shape((n_seq, n_batch, rows, qkv.shape[2]), BF16)),
        (vmem, shape((n_batch, rows, width), BF16)),
        (hbm, shape((n_seq, n_batch, rows, gate.shape[2]), BF16)),
        (hbm, shape((n_seq, n_batch, rows, up.shape[2]), BF16)),
        (hbm, shape((n_batch,) + down.shape, BF16)),
        (hbm, shape((n_seq, length, width), BF16)),
        (vmem, shape((total_len, width), BF16)),
        (hbm, shape((n_seq, length, width), BF16)),
        (vmem, shape((length, width), F32)),
        (vmem, shape((total_len, pairs * 128), BF16)),
        (vmem, shape((total_len, pairs * 128), BF16)),
        (vmem, shape((total_len, 128), BF16)),
        (vmem, shape((pairs, 2, total_len), F32)),
        (vmem, shape((2, total_len, 128), F32)),
        (vmem, shape((2, width), F32)),
    ]
    seq_copies = ny - 1 + (nc - 1) * ny
    batch_copies = nz - 1 + (nx - 1) * nz
    wires = 4 * (n_seq - 1) + 4 * seq_copies + 6 * batch_copies + seq_copies
    return pl.pallas_call(
        functools.partial(front_kernel, sizes, pairs),
        in_specs=[hbm] * 9,
        out_specs=[spec for spec, unused in results],
        out_shape=[kind for unused, kind in results],
        scratch_shapes=[
            pltpu.VMEM((n_seq, length, width), BF16),
            pltpu.VMEM((n_seq, length, 128), F32),
            pltpu.VMEM((n_seq, n_batch, 8, 128), F32),
            pltpu.VMEM((total_len, qkv.shape[2]), F32),
            pltpu.VMEM((total_len, total_len), F32 if total_len <= 1024 else BF16),
            pltpu.VMEM((n_seq, length, width), BF16),
            pltpu.VMEM((nc - 1, ny, length, width), BF16),
            pltpu.VMEM((ny - 1, length, width), BF16),
            pltpu.VMEM((length, width), BF16),
            pltpu.SemaphoreType.DMA((wires,)),
            pltpu.SemaphoreType.DMA((wires,)),
            pltpu.SemaphoreType.DMA((16,)),
        ],
        compiler_params=pltpu.CompilerParams(
            collective_id=0, has_side_effects=True, vmem_limit_bytes=60 * 1024 * 1024
        ),
        cost_estimate=pl.CostEstimate(
            flops=2 * total_len * width * (qkv.shape[2] + rows * n_batch),
            bytes_accessed=100 * 1024 * 1024,
            transcendentals=pairs * total_len * total_len,
        ),
    )(x, gb, table, gain, qkv, w_out, gate, up, down)


def per_device(
    tokens,
    cotangent,
    selection,
    segments,
    positions,
    gain_attn,
    w_query,
    w_key,
    w_value,
    w_out,
    gain_mlp,
    w_gate,
    w_up,
    w_down,
):
    seq = Axis("seq", 2)
    batch = Axis("batch", lax.axis_size("batch") // 4)
    n_seq, n_batch = seq.size, batch.size
    length, width = tokens.shape[1], tokens.shape[2]
    total_len = length * n_seq
    rows = w_query.shape[0]
    ff = w_gate.shape[1]
    q_cols = w_query.shape[1] // n_seq
    sharers = n_seq // KV_HEADS

    query_parts = w_query.reshape(rows, n_seq, q_cols)
    key_parts = jnp.repeat(w_key.reshape(rows, KV_HEADS, HEAD_DIM), sharers, axis=1)
    value_parts = jnp.repeat(w_value.reshape(rows, KV_HEADS, HEAD_DIM), sharers, axis=1)
    qkv_parts = jnp.concatenate([query_parts, key_parts, value_parts], axis=2).transpose(1, 0, 2)

    def collect(grad):
        parts = grad.astype(BF16).reshape(n_seq, n_batch, rows, grad.shape[1])
        return seq.exchange(batch.scatter_sum(parts, 1).astype(BF16)).astype(F32)

    def by_columns(weight):
        return weight.reshape(rows, n_seq, weight.shape[1] // n_seq).transpose(1, 0, 2)

    grad_out_row = cotangent[0].astype(F32) * selection[0].astype(F32)[:, None]
    frequency = 10000.0 ** (-(jnp.arange(HALF, dtype=F32) * 2.0 / HEAD_DIM))
    angles = positions[0].astype(F32)[:, None] * frequency[None, :]
    table = jnp.concatenate(
        [
            jnp.cos(angles),
            jnp.sin(angles),
            jnp.broadcast_to(segments[0].astype(F32)[:, None], (length, 128 - HEAD_DIM)),
        ],
        axis=1,
    )
    gain_tile = jnp.pad(
        jnp.stack([gain_attn, gain_mlp]).astype(F32), ((0, 6), (0, 128 - gain_attn.shape[0]))
    )
    sizes = (n_seq // 2, 2, 4, n_batch // 4)
    (
        w_qkv,
        wo,
        wg,
        wu,
        wd,
        grad_low,
        normed1,
        normed2,
        residual,
        heads_out,
        query_rot,
        kv_rot,
        lse,
        rotary,
        gains,
    ) = front(
        sizes,
        tokens[0],
        grad_out_row.astype(BF16),
        table,
        gain_tile,
        qkv_parts,
        w_out,
        by_columns(w_gate),
        by_columns(w_up),
        w_down,
    )
    gain_one, gain_two = gains[0:1], gains[1:2]
    w_qkv = w_qkv.reshape(width, w_qkv.shape[3])
    wo = wo.reshape(n_batch * rows, width)
    wg = wg.reshape(width, wg.shape[3])
    wu = wu.reshape(width, wu.shape[3])
    wd = wd.reshape(n_batch * w_down.shape[0], width)
    grad_low = grad_low.reshape(total_len, width)
    normed2 = normed2.reshape(total_len, width)
    cosine, sine = rotary[0], rotary[1]
    seg_all = seq.gather(segments[0], 0).reshape(total_len)
    seg_row, seg_col = seg_all[None, :], seg_all[:, None]
    row_input = tokens[0].astype(F32)
    inv_attn = rms_scale(row_input)

    inv_mlp = rms_scale(residual)
    gate_proj = product(normed2, wg)
    up_proj = product(normed2, wu)
    sigma = jax.nn.sigmoid(gate_proj)
    activated = gate_proj * sigma
    hidden = (activated * up_proj).astype(BF16)
    mixed_part = product(hidden, wd).astype(BF16).reshape(n_seq, length, width)
    mixed = (residual + seq.scatter_sum(mixed_part, 0)).astype(BF16)[None]

    grad_down = product_rows(hidden, grad_low)
    grad_hidden = product_cols(grad_low, wd)
    grad_gate_act = (
        grad_hidden * up_proj * sigma * (1.0 + gate_proj * (1.0 - sigma))
    ).astype(BF16)
    grad_up_act = (grad_hidden * activated).astype(BF16)
    grad_gate = product_rows(normed2, grad_gate_act)
    grad_up = product_rows(normed2, grad_up_act)
    normed_part = product_cols(grad_gate_act, wg) + product_cols(grad_up_act, wu)
    normed_terms = seq.scatter_sum(normed_part.astype(BF16).reshape(n_seq, length, width), 0)
    grad_resid = grad_out_row + norm_back(normed_terms, residual, inv_mlp, gain_two)

    down_own = batch.scatter_sum(
        grad_down.astype(BF16).reshape(n_batch, w_down.shape[0], width), 0
    )
    gate_own = collect(grad_gate).transpose(1, 0, 2).reshape(rows, ff)
    up_own = collect(grad_up).transpose(1, 0, 2).reshape(rows, ff)

    grad_branch = seq.gather(grad_resid.astype(BF16), 0).reshape(total_len, width)
    grad_wout = product_rows(heads_out, grad_branch)
    grad_heads = product_cols(grad_branch, wo).astype(BF16)
    grad_qkv_act = attend_back(
        query_rot, kv_rot, grad_heads, lse, cosine, sine, seg_row, seg_col
    )
    grad_wqkv = product_rows(normed1, grad_qkv_act)
    input_part = product_cols(grad_qkv_act, w_qkv).astype(BF16).reshape(n_seq, length, width)
    grad_normed1 = seq.scatter_sum(input_part, 0)
    tokens_grad = (
        grad_resid + norm_back(grad_normed1, row_input, inv_attn, gain_one)
    ).astype(BF16)[None]
    out_own = batch.scatter_sum(grad_wout.astype(BF16).reshape(n_batch, rows, width), 0)
    qkv_own = collect(grad_wqkv)
    query_own = qkv_own[:, :, :q_cols].transpose(1, 0, 2).reshape(rows, n_seq * q_cols)

    def shared(columns):
        heads = columns.reshape(KV_HEADS, sharers, rows, HEAD_DIM).sum(axis=1)
        return heads.transpose(1, 0, 2).reshape(rows, KV_HEADS * HEAD_DIM)

    key_own = shared(qkv_own[:, :, q_cols : q_cols + HEAD_DIM])
    value_own = shared(qkv_own[:, :, q_cols + HEAD_DIM :])

    def along(weight, grad):
        return jnp.sum(weight.astype(F32) * grad, axis=1)

    gain1_own = (
        along(w_query, query_own) + along(w_key, key_own) + along(w_value, value_own)
    ) / gain_attn.astype(F32)
    gain2_own = (along(w_gate, gate_own) + along(w_up, up_own)) / gain_mlp.astype(F32)
    return (
        mixed,
        tokens_grad,
        query_own,
        key_own,
        value_own,
        out_own,
        gate_own,
        up_own,
        down_own,
        gain1_own,
        gain2_own,
    )


def solution(mesh):
    both = ("seq", "batch")
    tokens = P("batch", "seq", None)
    flags = P("batch", "seq")
    matrix = P(both, None)
    vector = P(both)
    in_specs = (
        (tokens, tokens, flags, flags, flags)
        + (vector, matrix, matrix, matrix, matrix)
        + (vector, matrix, matrix, matrix)
    )
    out_specs = (tokens, tokens) + (matrix,) * 7 + (vector, vector)
    return jax.shard_map(
        per_device, mesh=mesh, in_specs=in_specs, out_specs=out_specs, check_vma=False
    )
```

```python
import functools

import jax
import jax.numpy as jnp
from jax import lax
from jax.experimental import pallas as pl
from jax.experimental.pallas import tpu as pltpu
from jax.sharding import PartitionSpec as P

HEADS = 32
KV_HEADS = 4
HEAD_DIM = 64
HALF = HEAD_DIM // 2

EPSILON = 1e-05
MASKED_SCORE = -1e30
SCALE = HEAD_DIM ** (-0.5)
CONTRACT_ROWS = (((0,), (0,)), ((), ()))
CONTRACT_COLS = (((1,), (1,)), ((), ()))
BF16 = jnp.bfloat16
F32 = jnp.float32


def product(left, right):
    return jnp.dot(left, right, preferred_element_type=F32)


def product_rows(left, right):
    return lax.dot_general(left, right, CONTRACT_ROWS, preferred_element_type=F32)


def product_cols(left, right):
    return lax.dot_general(left, right, CONTRACT_COLS, preferred_element_type=F32)


def rms_scale(inputs):
    return lax.rsqrt(jnp.mean(inputs * inputs, axis=-1, keepdims=True) + EPSILON)


def norm_back(grad_normed, inputs, inverse, gain):
    scaled = gain * grad_normed
    cubed = inverse * inverse * inverse
    return inverse * scaled - inputs * cubed * jnp.mean(scaled * inputs, axis=-1, keepdims=True)


class Axis:
    def __init__(self, name, inner):
        self.name = name
        self.size = lax.axis_size(name)
        self.inner = inner
        self.outer = self.size // inner
        index = lax.axis_index(name)
        self.index = index
        self.o = index // inner
        self.i = index % inner

    def shift(self, value, outer_by, inner_by):
        pairs = []
        for o in range(self.outer):
            for i in range(self.inner):
                target = ((o + outer_by) % self.outer) * self.inner + (i + inner_by) % self.inner
                pairs.append((o * self.inner + i, target))
        return lax.ppermute(value, self.name, pairs)

    def before(self, outer_by, inner_by):
        o = lax.rem(self.o + self.outer - outer_by, self.outer)
        i = lax.rem(self.i + self.inner - inner_by, self.inner)
        return o * self.inner + i

    def after(self, outer_by, inner_by):
        o = lax.rem(self.o + outer_by, self.outer)
        i = lax.rem(self.i + inner_by, self.inner)
        return o * self.inner + i

    def gather(self, block, dim=0):
        shape = block.shape[:dim] + (self.size,) + block.shape[dim:]
        out = jnp.zeros(shape, block.dtype)
        for k in range(self.outer):
            got = block if k == 0 else self.shift(block, k, 0)
            for m in range(self.inner):
                piece = got if m == 0 else self.shift(got, 0, m)
                out = lax.dynamic_update_slice_in_dim(
                    out, jnp.expand_dims(piece, dim), self.before(k, m), dim
                )
        return out

    def scatter_sum(self, parts, dim=0):
        shape = parts.shape[:dim] + (self.outer, self.inner) + parts.shape[dim + 1 :]
        grid = parts.reshape(shape)

        def inner_part(i):
            return lax.squeeze(lax.dynamic_slice_in_dim(grid, i, 1, dim + 1), (dim + 1,))

        total = inner_part(self.i).astype(F32)
        for m in range(1, self.inner):
            mine = inner_part(lax.rem(self.i + m, self.inner))
            total = total + self.shift(mine, 0, m).astype(F32)
        low = total.astype(BF16)

        def outer_part(o):
            return lax.squeeze(lax.dynamic_slice_in_dim(low, o, 1, dim), (dim,))

        out = outer_part(self.o).astype(F32)
        for k in range(1, self.outer):
            out = out + self.shift(outer_part(lax.rem(self.o + k, self.outer)), k, 0).astype(F32)
        return out

    def exchange(self, parts):
        out = jnp.zeros(parts.shape, parts.dtype)
        for k in range(self.outer):
            for m in range(self.inner):
                part = lax.dynamic_slice_in_dim(parts, self.after(k, m), 1, 0)
                got = part if (k, m) == (0, 0) else self.shift(part, k, m)
                out = lax.dynamic_update_slice_in_dim(out, got, self.before(k, m), 0)
        return out


def rotate_lanes(value, sign):
    lane = lax.broadcasted_iota(jnp.int32, value.shape, 1) % HEAD_DIM
    first = lane < HALF
    width = value.shape[1]
    up = pltpu.roll(value, width - HALF, 1)
    down = pltpu.roll(value, HALF, 1)
    return jnp.where(first, -sign * up, sign * down)


def mask_bias(bias_ref, seg_row_ref, seg_col_ref, length):
    rows = 256
    for start in range(0, length, rows):
        keys = seg_col_ref[start : start + rows, :]
        queries = seg_row_ref[:, :]
        key_pos = start + lax.broadcasted_iota(jnp.int32, (rows, length), 0)
        query_pos = lax.broadcasted_iota(jnp.int32, (rows, length), 1)
        allowed = (keys == queries) & (key_pos <= query_pos)
        bias_ref[start : start + rows, :] = jnp.where(allowed, 0.0, MASKED_SCORE)


def attend_kernel(
    qblock,
    q_ref,
    kv_ref,
    cos_ref,
    sin_ref,
    seg_row_ref,
    seg_col_ref,
    o_ref,
    qr_ref,
    kvr_ref,
    lse_ref,
    bias_ref,
):
    length = q_ref.shape[0]
    cosine = cos_ref[...]
    sine = sin_ref[...]

    @pl.when(pl.program_id(0) == 0)
    def _():
        mask_bias(bias_ref, seg_row_ref, seg_col_ref, length)
        kv = kv_ref[...]
        rotated = kv * cosine + rotate_lanes(kv, 1.0) * sine
        lane = lax.broadcasted_iota(jnp.int32, kv.shape, 1)
        kvr_ref[...] = jnp.where(lane < HEAD_DIM, rotated, kv).astype(BF16)

    q = q_ref[...]
    qr_ref[...] = (q * cosine + rotate_lanes(q, 1.0) * sine).astype(BF16)
    for start in range(0, length, qblock):
        stop = start + qblock
        keys = kvr_ref[:stop, :HEAD_DIM]
        values = kvr_ref[:stop, HEAD_DIM:]
        for head in range(2):
            lanes = slice(head * HEAD_DIM, (head + 1) * HEAD_DIM)
            queries = qr_ref[start:stop, lanes] * SCALE
            scores = product_cols(keys, queries.astype(BF16)) + bias_ref[:stop, start:stop]
            top = jnp.max(scores, axis=0, keepdims=True)
            grown = jnp.exp(scores - top)
            total = jnp.sum(grown, axis=0, keepdims=True)
            probs = (grown * (1.0 / total)).astype(BF16)
            lse_ref[0, head : head + 1, start:stop] = top + jnp.log(total)
            o_ref[start:stop, lanes] = product_rows(probs, values).astype(BF16)


def attend_back_kernel(
    qblock,
    qr_ref,
    kvr_ref,
    do_ref,
    lse_ref,
    cos_ref,
    sin_ref,
    seg_row_ref,
    seg_col_ref,
    dqkv_ref,
    bias_ref,
    dq_ref,
    dk_ref,
    dv_ref,
):
    length = qr_ref.shape[0]
    cosine = cos_ref[...]
    sine = sin_ref[...]
    pair = pl.program_id(0)

    @pl.when(pair == 0)
    def _():
        mask_bias(bias_ref, seg_row_ref, seg_col_ref, length)
        dk_ref[...] = jnp.zeros_like(dk_ref)
        dv_ref[...] = jnp.zeros_like(dv_ref)

    for start in range(0, length, qblock):
        stop = start + qblock
        keys = kvr_ref[:stop, :HEAD_DIM]
        values = kvr_ref[:stop, HEAD_DIM:]
        for head in range(2):
            lanes = slice(head * HEAD_DIM, (head + 1) * HEAD_DIM)
            queries = (qr_ref[start:stop, lanes] * SCALE).astype(BF16)
            grads = do_ref[start:stop, lanes]
            scores = product_cols(keys, queries) + bias_ref[:stop, start:stop]
            probs = jnp.exp(scores - lse_ref[0, head : head + 1, start:stop])
            dprobs = product_cols(values, grads)
            delta = jnp.sum(probs * dprobs, axis=0, keepdims=True)
            dscores = (probs * (dprobs - delta)).astype(BF16)
            dv_ref[:stop, :] += product(probs.astype(BF16), grads)
            dk_ref[:stop, :] += product(dscores, queries)
            dq_ref[start:stop, lanes] = product_rows(dscores, keys) * SCALE

    dq = dq_ref[...]
    turned = rotate_lanes(dq * sine, -1.0)
    columns = pl.ds(pl.multiple_of(pair * 128, 128), 128)
    dqkv_ref[:, columns] = (dq * cosine + turned).astype(BF16)

    @pl.when(pair == pl.num_programs(0) - 1)
    def _():
        grads = jnp.concatenate([dk_ref[...], dv_ref[...]], axis=1)
        back = grads * cosine + rotate_lanes(grads * sine, -1.0)
        lane = lax.broadcasted_iota(jnp.int32, grads.shape, 1)
        width = dqkv_ref.shape[1]
        dqkv_ref[:, width - 128 :] = jnp.where(lane < HEAD_DIM, back, grads).astype(BF16)


def whole_spec(shape):
    return pl.BlockSpec(shape, lambda j: (0,) * len(shape))


def attend(qkv, cosine, sine, seg_row, seg_col):
    length, width = qkv.shape
    pairs = width // 128 - 1
    qblock = min(256, length)
    return pl.pallas_call(
        functools.partial(attend_kernel, qblock),
        grid=(pairs,),
        in_specs=[
            pl.BlockSpec((length, 128), lambda j: (0, j)),
            pl.BlockSpec((length, 128), lambda j: (0, pairs)),
            whole_spec((length, 128)),
            whole_spec((length, 128)),
            whole_spec((1, length)),
            whole_spec((length, 1)),
        ],
        out_specs=[
            pl.BlockSpec((length, 128), lambda j: (0, j)),
            pl.BlockSpec((length, 128), lambda j: (0, j)),
            whole_spec((length, 128)),
            pl.BlockSpec((1, 2, length), lambda j: (j, 0, 0)),
        ],
        out_shape=[
            jax.ShapeDtypeStruct((length, pairs * 128), BF16),
            jax.ShapeDtypeStruct((length, pairs * 128), BF16),
            jax.ShapeDtypeStruct((length, 128), BF16),
            jax.ShapeDtypeStruct((pairs, 2, length), F32),
        ],
        scratch_shapes=[pltpu.VMEM((length, length), F32)],
        compiler_params=pltpu.CompilerParams(vmem_limit_bytes=48 * 1024 * 1024),
        cost_estimate=pl.CostEstimate(
            flops=pairs * 2 * length * length * HEAD_DIM * 2,
            bytes_accessed=8 * length * width,
            transcendentals=pairs * length * length,
        ),
    )(qkv, qkv, cosine, sine, seg_row, seg_col)


def attend_back(qr, kvr, grads, lse, cosine, sine, seg_row, seg_col):
    length = qr.shape[0]
    pairs = qr.shape[1] // 128
    qblock = min(256, length)
    return pl.pallas_call(
        functools.partial(attend_back_kernel, qblock),
        grid=(pairs,),
        in_specs=[
            pl.BlockSpec((length, 128), lambda j: (0, j)),
            whole_spec((length, 128)),
            pl.BlockSpec((length, 128), lambda j: (0, j)),
            pl.BlockSpec((1, 2, length), lambda j: (j, 0, 0)),
            whole_spec((length, 128)),
            whole_spec((length, 128)),
            whole_spec((1, length)),
            whole_spec((length, 1)),
        ],
        out_specs=whole_spec((length, (pairs + 1) * 128)),
        out_shape=jax.ShapeDtypeStruct((length, (pairs + 1) * 128), BF16),
        scratch_shapes=[
            pltpu.VMEM((length, length), F32),
            pltpu.VMEM((length, 128), F32),
            pltpu.VMEM((length, HEAD_DIM), F32),
            pltpu.VMEM((length, HEAD_DIM), F32),
        ],
        compiler_params=pltpu.CompilerParams(vmem_limit_bytes=48 * 1024 * 1024),
        cost_estimate=pl.CostEstimate(
            flops=pairs * 5 * length * length * HEAD_DIM * 2,
            bytes_accessed=12 * length * qr.shape[1],
            transcendentals=pairs * length * length,
        ),
    )(qr, kvr, grads, lse, cosine, sine, seg_row, seg_col)


MESH = pl.DeviceIdType.MESH
HBM = pl.BlockSpec(memory_space=pl.ANY)
VMEM = pl.BlockSpec(memory_space=pltpu.VMEM)
VMEM_BYTES = 62 * 1024 * 1024
STEP = 16


class Place:
    def __init__(self, sizes):
        self.ny, self.nc, self.nz, self.nx = sizes
        self.s = lax.axis_index("seq")
        self.b = lax.axis_index("batch")
        self.y, self.c = self.s // self.nc, self.s % self.nc
        self.z, self.x = self.b // self.nx, self.b % self.nx

    def seq_at(self, dy, dc):
        return (self.y + dy + self.ny) % self.ny * self.nc + (self.c + dc + self.nc) % self.nc

    def z_at(self, dz):
        return (self.z + dz + self.nz) % self.nz

    def batch_at(self, dz, dx):
        return self.z_at(dz) * self.nx + (self.x + dx + self.nx) % self.nx

    def enter(self):
        peers = [
            (self.seq_at(dy, dc), self.b)
            for dy in range(self.ny)
            for dc in range(self.nc)
            if (dy, dc) != (0, 0)
        ]
        peers += [(self.s, self.batch_at(k, 0)) for k in range(1, self.nz)]
        peers += [(self.s, self.batch_at(0, m)) for m in range(1, self.nx)]
        barrier = pltpu.get_barrier_semaphore()
        for peer in peers:
            pl.semaphore_signal(barrier, inc=1, device_id=peer, device_id_type=MESH)
        pl.semaphore_wait(barrier, len(peers))


class Wires:
    def __init__(self, send_sems, recv_sems):
        self.send_sems, self.recv_sems = send_sems, recv_sems
        self.ends = []
        self.open = []

    def describe(self, index, source, target):
        return pltpu.make_async_remote_copy(
            src_ref=source,
            dst_ref=target,
            send_sem=self.send_sems.at[index],
            recv_sem=self.recv_sems.at[index],
            device_id=self.ends[index][2](),
            device_id_type=MESH,
        )

    def push(self, source, target, device):
        index = len(self.ends)
        self.ends.append((source, target, device))
        self.open.append(index)
        self.describe(index, source(), target()).start()
        return index

    def wait(self, index, landed):
        self.describe(index, landed, landed).wait_recv()

    def sent(self, index):
        self.open.remove(index)
        source, target, unused = self.ends[index]
        self.describe(index, source(), target()).wait_send()

    def close(self):
        for index in list(self.open):
            self.sent(index)


class Copies:
    def __init__(self, sems):
        self.sems = sems
        self.count = 0

    def start(self, source, target):
        copy = pltpu.make_async_copy(source, target, self.sems.at[self.count])
        self.count += 1
        copy.start()
        return copy


class Gather:
    def __init__(self, wires, slot, own, outer, inner, at, device):
        self.wires, self.slot, self.own = wires, slot, own
        self.outer, self.inner, self.at, self.device = outer, inner, at, device
        self.first, self.second = {}, {}

    def push(self, source, target, k, m):
        return self.wires.push(source, target, lambda: self.device(self.at(k, m)))

    def start(self):
        mine = lambda: self.slot(self.at(0, 0))
        for k in range(1, self.outer):
            self.first[k] = self.push(self.own, mine, k, 0)
        for m in range(1, self.inner):
            self.second[0, m] = self.push(self.own, mine, 0, m)

    def pass_on(self, k):
        came = lambda: self.slot(self.at(-k, 0))
        self.wires.wait(self.first[k], came())
        for m in range(1, self.inner):
            self.second[k, m] = self.push(came, came, 0, m)

    def finish(self):
        for (k, m), ticket in self.second.items():
            self.wires.wait(ticket, self.slot(self.at(-k, -m)))


class RowSum:
    def __init__(self, wires, place, part_ref, core_in, far_in):
        self.wires, self.place = wires, place
        self.part_ref, self.core_in, self.far_in = part_ref, core_in, far_in
        self.tickets = {}

    def slot(self, t):
        return self.place.seq_at((t + 1) % 2, (3 - t) // 2)

    def push(self, t, source, target, dy, dc):
        self.tickets[t] = self.wires.push(
            lambda: self.part_ref.at[source],
            lambda: target(),
            lambda: (self.place.seq_at(dy, dc), self.place.b),
        )

    def compute(self, part):
        def body(t, unused):
            self.part_ref[t] = part(self.slot(t)).astype(BF16)

            @pl.when(t == 0)
            def _():
                self.push(0, 0, lambda: self.core_in.at[1], 0, 1)

            @pl.when(t == 1)
            def _():
                self.push(1, 1, lambda: self.core_in.at[0], 0, 1)

            @pl.when(t == 2)
            def _():
                self.wires.wait(self.tickets[0], self.core_in.at[1])
                mine = self.part_ref.at[2]
                add_up(mine, [mine, self.core_in.at[1]])
                self.push(2, 2, lambda: self.far_in, 1, 0)

            return unused

        lax.fori_loop(0, 4, body, 0)

    def finish(self, target, extra=()):
        self.wires.wait(self.tickets[1], self.core_in.at[0])
        self.wires.wait(self.tickets[2], self.far_in)
        add_up(target, [self.part_ref.at[3], self.core_in.at[0], self.far_in] + list(extra))

    def sent(self):
        for ticket in self.tickets.values():
            self.wires.sent(ticket)


class Rotating:
    def __init__(self, copies):
        self.sems, self.base = copies.sems, copies.count
        copies.count += 2

    def copy(self, i, source, target):
        return pltpu.make_async_copy(source, target, self.sems.at[self.base + i % 2])


def add_up(target, sources):
    shape = target.shape
    steps = shape[-2] // STEP

    def body(i, unused):
        at = pl.ds(pl.multiple_of(i % steps * STEP, STEP), STEP)
        where = (at, slice(None)) if len(shape) == 2 else (i // steps, at, slice(None))
        total = sources[0][where].astype(F32)
        for source in sources[1:]:
            total = total + source[where].astype(F32)
        target[where] = total.astype(target.dtype)
        return unused

    lax.fori_loop(0, steps * (1 if len(shape) == 2 else shape[0]), body, 0)


def front_kernel(
    sizes,
    pairs,
    x_ref,
    gb_ref,
    table_ref,
    gain_ref,
    qkv_ref,
    out_ref,
    gate_ref,
    up_ref,
    down_ref,
    wqkv_ref,
    wo_ref,
    wg_ref,
    wu_ref,
    wd_ref,
    gb_all_ref,
    n1t_ref,
    n2t_ref,
    residual_ref,
    headst_ref,
    qr_ref,
    kvr_ref,
    lse_ref,
    tables_ref,
    gains_ref,
    bias_ref,
    gate_proj_ref,
    up_proj_ref,
    grad_down_ref,
    hidden_out_ref,
    x_all_ref,
    table_all_ref,
    gain_all_ref,
    core_in_ref,
    far_in_ref,
    n2_own_ref,
    n2_ref,
    send_sems,
    recv_sems,
    copy_sems,
):
    place = Place(sizes)
    ny, nc, nz, nx = sizes
    s, b = place.s, place.b
    n_seq, n_batch = ny * nc, nz * nx
    length, width = x_ref.shape
    total_len = n_seq * length
    ff = gate_ref.shape[2]
    wires = Wires(send_sems, recv_sems)
    copies = Copies(copy_sems)
    row_others = [(dy, dc) for dy in range(ny) for dc in range(nc) if dy or dc]

    def over_batch(slot, own):
        return Gather(wires, slot, own, nz, nx, place.batch_at, lambda j: (s, j))

    def over_seq(slot, own):
        return Gather(wires, slot, own, ny, nc, place.seq_at, lambda j: (j, b))

    def columns(ref):
        return lambda j: ref.at[:, j]

    def blocks(ref):
        return lambda j: ref.at[j]

    class Exchange:
        def __init__(self, parts, target, many=True):
            self.target = target
            part = (lambda j: parts.at[j]) if many else (lambda j: parts)
            self.copy = copies.start(part(s), target.at[s, b])
            self.tickets = {}
            for away in row_others:
                self.tickets[away] = wires.push(
                    lambda away=away: part(place.seq_at(*away)),
                    lambda: target.at[s, b],
                    lambda away=away: (place.seq_at(*away), b),
                )

        def finish(self):
            self.copy.wait()
            for (dy, dc), ticket in self.tickets.items():
                wires.wait(ticket, self.target.at[place.seq_at(-dy, -dc), b])

    place.enter()
    qkv_parts = Exchange(qkv_ref, wqkv_ref)
    gain_parts = Exchange(gain_ref, gain_all_ref, many=False)
    own_table = copies.start(table_ref, table_all_ref.at[s])
    own_x = copies.start(x_ref, x_all_ref.at[s])
    own_out = copies.start(out_ref, wo_ref.at[b])
    own_down = copies.start(down_ref, wd_ref.at[b])
    own_gb = copies.start(gb_ref, gb_all_ref.at[s])
    table_all = over_seq(blocks(table_all_ref), lambda: table_ref)
    table_all.start()
    x_all = over_seq(blocks(x_all_ref), lambda: x_ref)
    x_all.start()
    wo = over_batch(blocks(wo_ref), lambda: out_ref)
    wo.start()
    gate_parts = Exchange(gate_ref, wg_ref)
    up_parts = Exchange(up_ref, wu_ref)
    wqkv = over_batch(columns(wqkv_ref), lambda: wqkv_ref.at[:, b])
    gains = over_batch(columns(gain_all_ref), lambda: gain_all_ref.at[:, b])
    wg = over_batch(columns(wg_ref), lambda: wg_ref.at[:, b])
    wu = over_batch(columns(wu_ref), lambda: wu_ref.at[:, b])
    wd = over_batch(blocks(wd_ref), lambda: down_ref)
    gb_all = over_seq(blocks(gb_all_ref), lambda: gb_ref)

    qkv_parts.finish()
    wqkv.start()
    gain_parts.finish()
    gains.start()
    for k in range(1, ny):
        table_all.pass_on(k)
        x_all.pass_on(k)
    for k in range(1, nz):
        wo.pass_on(k)
        gains.pass_on(k)
    for k in range(1, nz):
        wqkv.pass_on(k)
    gate_parts.finish()
    wg.start()
    gb_all.start()

    def attention(n1_ref, qkv_proj_ref, part_ref):
        own_table.wait()
        table_all.finish()
        own_x.wait()
        x_all.finish()
        gains.finish()
        rows = width // (n_seq * n_batch)
        for g in range(2):
            gains_ref[g : g + 1, :] = jnp.concatenate(
                [gain_all_ref[i, j, g : g + 1, :rows] for i in range(n_seq) for j in range(n_batch)],
                axis=1,
            )
        gain_one = gains_ref[0:1, :]
        half = length // 2

        def norm_rows(i, unused):
            part = x_all_ref[i // 2, pl.ds(i % 2 * half, half), :].astype(F32)
            at = pl.ds(pl.multiple_of(i * half, half), half)
            n1_ref[at, :] = (part * rms_scale(part) * gain_one).astype(BF16)
            return unused

        lax.fori_loop(0, 2 * n_seq, norm_rows, 0)
        for j in range(n_seq):
            at = slice(j * length, (j + 1) * length)
            table = table_all_ref[j]
            cos_part, sin_part = table[:, :HALF], table[:, HALF:HEAD_DIM]
            tables_ref[0, at, :] = jnp.concatenate([cos_part] * 4, axis=1)
            tables_ref[1, at, :] = jnp.concatenate([sin_part] * 4, axis=1)
        flipped = [
            jnp.transpose(table_all_ref[j])[HEAD_DIM : HEAD_DIM + 1, :] for j in range(n_seq)
        ]
        query_seg = jnp.concatenate(flipped, axis=1)
        for j in range(n_seq):
            key_seg = table_all_ref[j][:, HEAD_DIM : HEAD_DIM + 1]
            key_pos = j * length + lax.broadcasted_iota(jnp.int32, (length, total_len), 0)
            query_pos = lax.broadcasted_iota(jnp.int32, (length, total_len), 1)
            allowed = (key_seg == query_seg) & (key_pos <= query_pos)
            bias_ref[j * length : (j + 1) * length, :] = jnp.where(
                allowed, 0.0, MASKED_SCORE
            ).astype(BF16)

        wqkv.finish()
        weights = wqkv_ref[...].reshape(width, wqkv_ref.shape[3])

        def project(i, unused):
            at = pl.ds(pl.multiple_of(i * length, length), length)
            qkv_proj_ref[at, :] = product(n1_ref[at, :], weights)
            return unused

        lax.fori_loop(0, n_seq, project, 0)
        kv = qkv_proj_ref[:, pairs * 128 :]
        lane = lax.broadcasted_iota(jnp.int32, kv.shape, 1)
        rotated = kv * tables_ref[0] + rotate_lanes(kv, 1.0) * tables_ref[1]
        kvr_ref[...] = jnp.where(lane < HEAD_DIM, rotated, kv).astype(BF16)

        def attend_pair(pair, unused):
            at = pl.ds(pl.multiple_of(pair * 128, 128), 128)
            q = qkv_proj_ref[:, at]
            qr = (q * tables_ref[0] + rotate_lanes(q, 1.0) * tables_ref[1]).astype(BF16)
            qr_ref[:, at] = qr
            low = (qr * SCALE).astype(BF16)
            for start in range(0, total_len, length):
                stop = start + length
                outs = []
                for head in range(2):
                    queries = low[start:stop, head * HEAD_DIM : (head + 1) * HEAD_DIM]
                    scores = product_cols(kvr_ref[:stop, :HEAD_DIM], queries)
                    scores = scores + bias_ref[:stop, start:stop].astype(F32)
                    top = jnp.max(scores, axis=0, keepdims=True)
                    grown = jnp.exp(scores - top)
                    total = jnp.sum(grown, axis=0, keepdims=True)
                    probs = (grown * (1.0 / total)).astype(BF16)
                    lse_ref[pair, head : head + 1, start:stop] = top + jnp.log(total)
                    outs.append(product_rows(probs, kvr_ref[:stop, HEAD_DIM:]))
                headst_ref[at, start:stop] = jnp.transpose(
                    jnp.concatenate(outs, axis=1).astype(BF16)
                )
            return unused

        lax.fori_loop(0, pairs, attend_pair, 0)
        wg.pass_on(1)

        own_out.wait()
        wo.finish()
        out_weights = wo_ref[...].reshape(n_batch * wo_ref.shape[1], width)

        def out_part(j):
            at = pl.ds(pl.multiple_of(j * length, length), length)
            return product_rows(headst_ref[:, at], out_weights)

        row_sum = RowSum(wires, place, part_ref, core_in_ref, far_in_ref)
        row_sum.compute(out_part)
        wg.pass_on(2)
        up_parts.finish()
        wu.start()

        def flip_rows(i, unused):
            at = pl.ds(pl.multiple_of(i * length, length), length)
            n1t_ref[:, at] = jnp.transpose(n1_ref[at, :])
            return unused

        lax.fori_loop(0, n_seq, flip_rows, 0)
        row_sum.finish(residual_ref, [x_all_ref.at[s]])

        def norm_own(i, unused):
            at = pl.ds(pl.multiple_of(i * 32, 32), 32)
            total = residual_ref[at, :]
            n2_own_ref[at, :] = (total * rms_scale(total) * gains_ref[1:2, :]).astype(BF16)
            return unused

        lax.fori_loop(0, length // 32, norm_own, 0)
        row_sum.sent()

    pl.run_scoped(
        attention,
        pltpu.VMEM((total_len, width), BF16),
        pltpu.VMEM((total_len, wqkv_ref.shape[3]), F32),
        pltpu.VMEM((n_seq, length, width), BF16),
    )
    own_n2 = copies.start(n2_own_ref, n2_ref.at[s])
    n2 = over_seq(blocks(n2_ref), lambda: n2_own_ref)
    n2.start()
    wg.pass_on(3)
    wu.pass_on(1)
    wd.start()
    for k in range(1, ny):
        n2.pass_on(k)
        gb_all.pass_on(k)

    def feed_forward(weight_ref, gate_buf, up_buf, hidden_ref, gb_buf, grad_buf):
        own_n2.wait()
        n2.finish()
        for j in range(n_seq):
            n2t_ref[:, j * length : (j + 1) * length] = jnp.transpose(n2_ref[j])
        wu.pass_on(2)
        wg.finish()
        copies.start(wg_ref, weight_ref).wait()
        weights = (width, ff)

        def gate_rows(j, unused):
            at = pl.ds(pl.multiple_of(j * length, length), length)
            gate_buf[at, :] = product(n2_ref[j], weight_ref[...].reshape(weights))
            return unused

        lax.fori_loop(0, n_seq, gate_rows, 0)
        outs = [copies.start(gate_buf, gate_proj_ref)]
        wu.pass_on(3)
        own_gb.wait()
        gb_all.finish()
        gb_in = copies.start(gb_all_ref, gb_buf)
        wd.pass_on(1)
        wu.finish()
        copies.start(wu_ref, weight_ref).wait()
        up_out = Rotating(copies)

        def up_copy(j):
            at = pl.ds(pl.multiple_of(j * length, length), length)
            return up_out.copy(j, up_buf.at[j % 2], up_proj_ref.at[at])

        def up_rows(j, unused):
            at = pl.ds(pl.multiple_of(j * length, length), length)

            @pl.when(j >= 2)
            def _():
                up_copy(j - 2).wait()

            up = product(n2_ref[j], weight_ref[...].reshape(weights))
            up_buf[j % 2] = up
            up_copy(j).start()
            gate = gate_buf[at, :]
            hidden_ref[at, :] = (gate * jax.nn.sigmoid(gate) * up).astype(BF16)
            return unused

        lax.fori_loop(0, n_seq, up_rows, 0)
        outs.append(copies.start(hidden_ref, hidden_out_ref))
        gb_in.wait()
        wd.pass_on(2)
        grads = gb_buf[...].reshape(total_len, width)
        grad_out = Rotating(copies)

        def grad_copy(i):
            at = pl.ds(pl.multiple_of(i * 256, 256), 256)
            return grad_out.copy(i, grad_buf.at[i % 2], grad_down_ref.at[at])

        def grad_rows(i, unused):
            at = pl.ds(pl.multiple_of(i * 256, 256), 256)

            @pl.when(i >= 2)
            def _():
                grad_copy(i - 2).wait()

            grad_buf[i % 2] = product_rows(hidden_ref[:, at], grads).astype(BF16)
            grad_copy(i).start()
            return unused

        whole = ff // 256
        lax.fori_loop(0, whole, grad_rows, 0)
        up_copy(n_seq - 2).wait()
        up_copy(n_seq - 1).wait()
        grad_copy(whole - 2).wait()
        grad_copy(whole - 1).wait()
        rest = ff - whole * 256
        if rest:
            grad_buf[0, :rest] = product_rows(hidden_ref[:, whole * 256 :], grads).astype(BF16)
            outs.append(
                copies.start(grad_buf.at[0, :rest], grad_down_ref.at[pl.ds(whole * 256, rest)])
            )
        wd.pass_on(3)
        for copy in outs:
            copy.wait()

    pl.run_scoped(
        feed_forward,
        pltpu.VMEM(wg_ref.shape, BF16),
        pltpu.VMEM((total_len, ff), F32),
        pltpu.VMEM((2, length, ff), F32),
        pltpu.VMEM((total_len, ff), BF16),
        pltpu.VMEM((n_seq, length, width), BF16),
        pltpu.VMEM((2, 256, width), BF16),
    )
    wd.finish()
    own_down.wait()
    wires.close()


def shape_of(dims, kind):
    return jax.ShapeDtypeStruct(dims, kind)


def front(sizes, x, gb, table, gain, qkv, w_out, gate, up, down):
    ny, nc, nz, nx = sizes
    n_seq, n_batch = ny * nc, nz * nx
    length, width = x.shape
    total_len = n_seq * length
    pairs = qkv.shape[2] // 128 - 1
    rows = w_out.shape[0]
    ff = gate.shape[2]
    results = [
        (VMEM, shape_of((n_seq, n_batch, rows, qkv.shape[2]), BF16)),
        (VMEM, shape_of((n_batch, rows, width), BF16)),
        (HBM, shape_of((n_seq, n_batch, rows, ff), BF16)),
        (HBM, shape_of((n_seq, n_batch, rows, ff), BF16)),
        (HBM, shape_of((n_batch,) + down.shape, BF16)),
        (HBM, shape_of((n_seq, length, width), BF16)),
        (VMEM, shape_of((width, total_len), BF16)),
        (VMEM, shape_of((width, total_len), BF16)),
        (VMEM, shape_of((length, width), F32)),
        (VMEM, shape_of((pairs * 128, total_len), BF16)),
        (VMEM, shape_of((total_len, pairs * 128), BF16)),
        (VMEM, shape_of((total_len, 128), BF16)),
        (VMEM, shape_of((pairs, 2, total_len), F32)),
        (VMEM, shape_of((2, total_len, 128), F32)),
        (VMEM, shape_of((2, width), F32)),
        (VMEM, shape_of((total_len, total_len), BF16)),
        (HBM, shape_of((total_len, ff), F32)),
        (HBM, shape_of((total_len, ff), F32)),
        (HBM, shape_of((ff, width), BF16)),
        (HBM, shape_of((total_len, ff), BF16)),
    ]
    seq_copies = ny - 1 + (nc - 1) * ny
    batch_copies = nz - 1 + (nx - 1) * nz
    wires = 4 * (n_seq - 1) + 5 * seq_copies + 6 * batch_copies
    return pl.pallas_call(
        functools.partial(front_kernel, sizes, pairs),
        in_specs=[HBM] * 9,
        out_specs=[spec for spec, unused in results],
        out_shape=[kind for unused, kind in results],
        scratch_shapes=[
            pltpu.VMEM((n_seq, length, width), BF16),
            pltpu.VMEM((n_seq, length, 128), F32),
            pltpu.VMEM((n_seq, n_batch, 8, 128), F32),
            pltpu.VMEM((ny, length, width), BF16),
            pltpu.VMEM((length, width), BF16),
            pltpu.VMEM((length, width), BF16),
            pltpu.VMEM((n_seq, length, width), BF16),
            pltpu.SemaphoreType.DMA((wires,)),
            pltpu.SemaphoreType.DMA((wires,)),
            pltpu.SemaphoreType.DMA((40,)),
        ],
        compiler_params=pltpu.CompilerParams(
            collective_id=0, has_side_effects=True, vmem_limit_bytes=VMEM_BYTES
        ),
        cost_estimate=pl.CostEstimate(
            flops=2 * total_len * width * (qkv.shape[2] + rows * n_batch + 3 * ff),
            bytes_accessed=100 * 1024 * 1024,
            transcendentals=pairs * total_len * total_len,
        ),
    )(x, gb, table, gain, qkv, w_out, gate, up, down)


class Reduce:
    def __init__(self, wires, place, copies, to_z, from_x, from_z, stage):
        self.wires, self.place, self.copies = wires, place, copies
        self.to_z, self.from_x, self.from_z, self.stage = to_z, from_x, from_z, stage
        self.x_tickets, self.z_tickets = {}, {}

    def send(self, k, chunk):
        place = self.place
        self.x_tickets[k] = self.wires.push(
            lambda: chunk(place.z_at(k)),
            lambda: self.from_x.at[place.z_at(k)],
            lambda: (place.s, place.batch_at(0, 1)),
        )

    def add(self, k):
        place = self.place
        zz = place.z_at(k)
        self.wires.wait(self.x_tickets[k], self.from_x.at[zz])
        self.copies.start(self.from_x.at[zz], self.stage).wait()
        add_up(self.to_z.at[zz], [self.to_z.at[zz], self.stage])
        if k:
            self.z_tickets[k] = self.wires.push(
                lambda: self.to_z.at[place.z_at(k)],
                lambda: self.from_z.at[k - 1],
                lambda: (place.s, place.batch_at(k, 0)),
            )

    def finish(self, target=None):
        mine = self.to_z.at[self.place.z]
        nz = self.place.nz

        def body(stages):
            loads = []
            for k in range(1, nz):
                self.wires.wait(self.z_tickets[k], self.from_z.at[k - 1])
                loads.append(self.copies.start(self.from_z.at[k - 1], stages.at[k - 1]))
            for load in loads:
                load.wait()
            add_up(
                mine if target is None else target,
                [mine] + [stages.at[k] for k in range(nz - 1)],
            )

        pl.run_scoped(body, pltpu.VMEM((nz - 1,) + self.stage.shape, BF16))
        return mine


def norm_back_rows(grad_ref, input_ref, gain, base_ref, target_ref, low_ref):
    rows = 32

    def body(i, unused):
        at = pl.ds(pl.multiple_of(i * rows, rows), rows)
        inputs = input_ref[at, :].astype(F32)
        back = norm_back(grad_ref[at, :], inputs, rms_scale(inputs), gain)
        total = base_ref[at, :].astype(F32) + back
        if target_ref is not None:
            target_ref[at, :] = total
        low_ref[at, :] = total.astype(BF16)
        return unused

    lax.fori_loop(0, grad_ref.shape[0] // rows, body, 0)


def back_kernel(
    sizes,
    pairs,
    gd_ref,
    hidden_ref,
    wd_ref,
    wg_ref,
    wu_ref,
    gate_ref,
    up_ref,
    gb_ref,
    n1t_ref,
    n2t_ref,
    headst_ref,
    residual_ref,
    qr_ref,
    kvr_ref,
    tables_ref,
    bias_ref,
    wqkv_ref,
    wo_ref,
    x_ref,
    lse_ref,
    gains_ref,
    mixed_ref,
    tokens_ref,
    down_own,
    out_own,
    gate_own,
    up_own,
    qkv_own,
    x_down,
    x_gate,
    x_up,
    x_out,
    x_qkv,
    z_down,
    z_gate,
    z_up,
    z_out,
    z_qkv,
    send_gate,
    send_up,
    da_all_ref,
    s_down,
    s_gate,
    s_up,
    s_out,
    s_qkv,
    send_out,
    send_qkv,
    stage_down,
    stage_gate,
    stage_out,
    stage_qkv,
    core_in_ref,
    far_in_ref,
    mixed_core_in,
    mixed_far_in,
    da_own_ref,
    total_ref,
    send_sems,
    recv_sems,
    copy_sems,
):
    place = Place(sizes)
    ny, nc, nz, nx = sizes
    s, b = place.s, place.b
    n_seq, n_batch = ny * nc, nz * nx
    length, width = x_ref.shape
    total_len = n_seq * length
    ff = wg_ref.shape[3]
    rows = wo_ref.shape[1]
    wires = Wires(send_sems, recv_sems)
    copies = Copies(copy_sems)
    down = Reduce(wires, place, copies, s_down, x_down, z_down, stage_down)
    gate = Reduce(wires, place, copies, s_gate, x_gate, z_gate, stage_gate)
    up = Reduce(wires, place, copies, s_up, x_up, z_up, stage_gate)
    out = Reduce(wires, place, copies, s_out, x_out, z_out, stage_out)
    qkv = Reduce(wires, place, copies, s_qkv, x_qkv, z_qkv, stage_qkv)
    order = list(range(1, nz)) + [0]
    row_others = [(dy, dc) for dy in range(ny) for dc in range(nc) if dy or dc]

    place.enter()
    own_down = []
    for k in order:
        down.send(k, lambda zz: gd_ref.at[zz * nx + (place.x + 1) % nx])
    for k in order:
        own_down.append(copies.start(gd_ref.at[place.batch_at(k, 0)], s_down.at[place.z_at(k)]))

    def weight_rows(flipped_ref, grads, k, dx):
        j = place.batch_at(k, dx)
        pieces = []
        for i in range(n_seq):
            start = pl.multiple_of((i * n_batch + j) * rows, rows)
            pieces.append(flipped_ref[pl.ds(start, rows), :])
        value = product(jnp.concatenate(pieces, axis=0), grads)
        return value.astype(BF16).reshape(n_seq, rows, grads.shape[1])

    def feed_forward(dgate_ref, dup_ref, part_ref):
        row_sum = RowSum(wires, place, part_ref, core_in_ref, far_in_ref)

        def activations(weight1, gate_buf, up_buf, gb_buf):
            load1 = copies.start(wd_ref, weight1)

            base = copies.count
            copies.count += 3

            def load_gb(j):
                return pltpu.make_async_copy(gb_ref.at[j], gb_buf, copy_sems.at[base])

            def load_gate(j):
                at = pl.ds(pl.multiple_of(j * length, length), length)
                return (
                    pltpu.make_async_copy(gate_ref.at[at], gate_buf, copy_sems.at[base + 1]),
                    pltpu.make_async_copy(up_ref.at[at], up_buf, copy_sems.at[base + 2]),
                )

            load_gb(0).start()
            for copy in load_gate(0):
                copy.start()
            load1.wait()

            def rows_back(j, unused):
                load_gb(j).wait()
                grad_hidden = product_cols(gb_buf[...], weight1[...].reshape(ff, width))

                @pl.when(j + 1 < n_seq)
                def _():
                    load_gb(j + 1).start()

                for copy in load_gate(j):
                    copy.wait()
                gate_part, up_part = gate_buf[...], up_buf[...]
                sigma = jax.nn.sigmoid(gate_part)
                activated = gate_part * sigma
                dgate_ref[j] = (
                    grad_hidden * up_part * sigma * (1.0 + gate_part * (1.0 - sigma))
                ).astype(BF16)
                dup_ref[j] = (grad_hidden * activated).astype(BF16)

                @pl.when(j + 1 < n_seq)
                def _():
                    for copy in load_gate(j + 1):
                        copy.start()

                return unused

            lax.fori_loop(0, n_seq, rows_back, 0)
            for copy in own_down:
                copy.wait()

        pl.run_scoped(
            activations,
            pltpu.VMEM(wd_ref.shape, BF16),
            pltpu.VMEM((length, ff), F32),
            pltpu.VMEM((length, ff), F32),
            pltpu.VMEM((length, width), BF16),
        )

        def inputs(weight1, weight2):
            loads = [copies.start(wg_ref, weight1), copies.start(wu_ref, weight2)]
            down.add(1)
            for load in loads:
                load.wait()

            def input_part(j):
                return product_cols(
                    dgate_ref[j], weight1[...].reshape(width, ff)
                ) + product_cols(dup_ref[j], weight2[...].reshape(width, ff))

            row_sum.compute(input_part)
            down.add(2)

        pl.run_scoped(inputs, pltpu.VMEM(wg_ref.shape, BF16), pltpu.VMEM(wg_ref.shape, BF16))

        def weights(flipped, staging, residual_buf, gb_buf):
            loads = [
                copies.start(n2t_ref, flipped),
                copies.start(residual_ref, residual_buf),
                copies.start(gb_ref.at[s], gb_buf),
            ]
            loads[0].wait()

            def rows_of(reduce, grads_ref):
                def body(i, unused):
                    k = (i + 1) % nz
                    zz = place.z_at(k)
                    grads = grads_ref[...].reshape(total_len, ff)
                    staging[zz] = weight_rows(flipped, grads, k, 1)
                    reduce.to_z[zz] = weight_rows(flipped, grads, k, 0)
                    return unused

                lax.fori_loop(0, nz, body, 0)

            def send_off(reduce, send_ref):
                copies.start(staging, send_ref).wait()
                for k in order:
                    reduce.send(k, lambda zz: send_ref.at[zz])

            rows_of(gate, dgate_ref)
            send_off(gate, send_gate)
            for copy in loads[1:]:
                copy.wait()
            row_sum.finish(total_ref)
            norm_back_rows(
                total_ref, residual_buf, gains_ref[1:2, :], gb_buf, total_ref, da_own_ref
            )
            da.start()
            down.add(3)
            rows_of(up, dup_ref)
            send_off(up, send_up)
            down.add(0)
            row_sum.sent()

        pl.run_scoped(
            weights,
            pltpu.VMEM(n2t_ref.shape, BF16),
            pltpu.VMEM((nz, n_seq, rows, ff), BF16),
            pltpu.VMEM((length, width), F32),
            pltpu.VMEM((length, width), BF16),
        )

    own_da = []
    da = Gather(
        wires,
        lambda j: da_all_ref.at[j],
        lambda: da_own_ref,
        ny,
        nc,
        place.seq_at,
        lambda j: (j, b),
    )
    pl.run_scoped(
        feed_forward,
        pltpu.VMEM((n_seq, length, ff), BF16),
        pltpu.VMEM((n_seq, length, ff), BF16),
        pltpu.VMEM((n_seq, length, width), BF16),
    )
    own_da.append(copies.start(da_own_ref, da_all_ref.at[s]))
    for k in range(1, ny):
        da.pass_on(k)

    def attention(
        da_buf,
        wo_buf,
        wqkv_buf,
        qr_buf,
        headst_buf,
        do_buf,
        kvr_buf,
        tables_buf,
        bias_buf,
        dqkv_buf,
        n1t_buf,
        dq_buf,
        dk_buf,
        dv_buf,
        part_ref,
        x_buf,
    ):
        loads = [
            copies.start(source, target)
            for source, target in [
                (wo_ref, wo_buf),
                (headst_ref, headst_buf),
                (qr_ref, qr_buf),
                (kvr_ref, kvr_buf),
                (tables_ref, tables_buf),
                (bias_ref, bias_buf),
                (n1t_ref, n1t_buf),
                (wqkv_ref, wqkv_buf),
                (x_ref, x_buf),
            ]
        ]
        gate.add(1)
        da.finish()
        own_da[0].wait()
        copies.start(da_all_ref, da_buf).wait()
        for load in loads:
            load.wait()
        out_weights = wo_buf[...].reshape(n_batch * rows, width)

        def heads_back(j, unused):
            at = pl.ds(pl.multiple_of(j * length, length), length)
            do_buf[at, :] = product_cols(da_buf[j], out_weights).astype(BF16)
            return unused

        lax.fori_loop(0, n_seq, heads_back, 0)
        branch = da_buf[...].reshape(total_len, width)

        def out_rows(dx):
            pieces = []
            for zz in range(nz):
                start = pl.multiple_of((zz * nx + (place.x + dx) % nx) * rows, rows)
                pieces.append(headst_buf[pl.ds(start, rows), :])
            value = product(jnp.concatenate(pieces, axis=0), branch)
            return value.astype(BF16).reshape(nz, rows, width)

        send_out[...] = out_rows(1)
        for k in order:
            out.send(k, lambda zz: send_out.at[zz])
        s_out[...] = out_rows(0)
        dk_buf[...] = jnp.zeros_like(dk_buf)
        dv_buf[...] = jnp.zeros_like(dv_buf)

        def pair_back(pair, unused):
            at = pl.ds(pl.multiple_of(pair * 128, 128), 128)
            low = (qr_buf[:, at] * SCALE).astype(BF16)
            grads_pair = do_buf[:, at]
            for start in range(0, total_len, length):
                stop = start + length
                outs = []
                for head in range(2):
                    lanes = slice(head * HEAD_DIM, (head + 1) * HEAD_DIM)
                    queries = low[start:stop, lanes]
                    grads = grads_pair[start:stop, lanes]
                    keys = kvr_buf[:stop, :HEAD_DIM]
                    values = kvr_buf[:stop, HEAD_DIM:]
                    scores = product_cols(keys, queries)
                    scores = scores + bias_buf[:stop, start:stop].astype(F32)
                    probs = jnp.exp(scores - lse_ref[pair, head : head + 1, start:stop])
                    dprobs = product_cols(values, grads)
                    delta = jnp.sum(probs * dprobs, axis=0, keepdims=True)
                    dscores = (probs * (dprobs - delta)).astype(BF16)
                    dv_buf[:stop, :] += product(probs.astype(BF16), grads)
                    dk_buf[:stop, :] += product(dscores, queries)
                    outs.append(product_rows(dscores, keys) * SCALE)
                dq_buf[start:stop, :] = jnp.concatenate(outs, axis=1)
            dq = dq_buf[...]
            turned = rotate_lanes(dq * tables_buf[1], -1.0)
            dqkv_buf[:, at] = (dq * tables_buf[0] + turned).astype(BF16)
            return unused

        gate.add(2)
        lax.fori_loop(0, pairs, pair_back, 0)
        gate.add(3)
        gate.add(0)
        grads = jnp.concatenate([dk_buf[...], dv_buf[...]], axis=1)
        back = grads * tables_buf[0] + rotate_lanes(grads * tables_buf[1], -1.0)
        lane = lax.broadcasted_iota(jnp.int32, grads.shape, 1)
        dqkv_buf[:, pairs * 128 :] = jnp.where(lane < HEAD_DIM, back, grads).astype(BF16)

        row_sum = RowSum(wires, place, part_ref, core_in_ref, far_in_ref)
        in_weights = wqkv_buf[...].reshape(width, wqkv_ref.shape[3])

        def input_part(j):
            at = pl.ds(pl.multiple_of(j * length, length), length)
            return product_cols(dqkv_buf[at, :], in_weights)

        row_sum.compute(input_part)

        def qkv_rows(zz, unused):
            k = (zz - place.z + nz) % nz
            send_qkv[zz] = weight_rows(n1t_buf, dqkv_buf[...], k, 1)
            s_qkv[zz] = weight_rows(n1t_buf, dqkv_buf[...], k, 0)
            return unused

        lax.fori_loop(0, nz, qkv_rows, 0)
        for k in order:
            qkv.send(k, lambda zz: send_qkv.at[zz])
        up.add(1)

        def last(grad_ref):
            row_sum.finish(grad_ref)
            norm_back_rows(grad_ref, x_buf, gains_ref[0:1, :], total_ref, None, tokens_ref)

        pl.run_scoped(last, pltpu.VMEM((length, width), F32))
        row_sum.sent()

    pl.run_scoped(
        attention,
        pltpu.VMEM((n_seq, length, width), BF16),
        pltpu.VMEM(wo_ref.shape, BF16),
        pltpu.VMEM(wqkv_ref.shape, BF16),
        pltpu.VMEM(qr_ref.shape, BF16),
        pltpu.VMEM(headst_ref.shape, BF16),
        pltpu.VMEM(qr_ref.shape, BF16),
        pltpu.VMEM(kvr_ref.shape, BF16),
        pltpu.VMEM(tables_ref.shape, F32),
        pltpu.VMEM(bias_ref.shape, BF16),
        pltpu.VMEM((total_len, (pairs + 1) * 128), BF16),
        pltpu.VMEM(n1t_ref.shape, BF16),
        pltpu.VMEM((total_len, 128), F32),
        pltpu.VMEM((total_len, HEAD_DIM), F32),
        pltpu.VMEM((total_len, HEAD_DIM), F32),
        pltpu.VMEM((n_seq, length, width), BF16),
        pltpu.VMEM((length, width), BF16),
    )

    def layer_out(weight_buf, hidden_buf, part_ref, mixed_total):
        loads = [
            copies.start(wd_ref, weight_buf),
            copies.start(hidden_ref, hidden_buf),
            copies.start(residual_ref, mixed_total),
        ]
        up.add(2)
        for load in loads:
            load.wait()

        def mixed_part(j):
            at = pl.ds(pl.multiple_of(j * length, length), length)
            return product(hidden_buf[at, :], weight_buf[...].reshape(ff, width))

        row_sum = RowSum(wires, place, part_ref, mixed_core_in, mixed_far_in)
        row_sum.compute(mixed_part)
        up.add(3)
        down.finish(down_own)
        row_sum.finish(mixed_ref, [mixed_total])
        row_sum.sent()

    pl.run_scoped(
        layer_out,
        pltpu.VMEM(wd_ref.shape, BF16),
        pltpu.VMEM(hidden_ref.shape, BF16),
        pltpu.VMEM((n_seq, length, width), BF16),
        pltpu.VMEM((length, width), F32),
    )

    exchanges = []

    def exchange(reduce, target):
        mine = reduce.finish()
        copy = copies.start(mine.at[s], target.at[s])
        tickets = {}
        for away in row_others:
            tickets[away] = wires.push(
                lambda away=away: mine.at[place.seq_at(*away)],
                lambda: target.at[s],
                lambda away=away: (place.seq_at(*away), b),
            )
        exchanges.append((copy, target, tickets))

    exchange(gate, gate_own)
    up.add(0)
    for k in order:
        out.add(k)
    exchange(up, up_own)
    for k in order:
        qkv.add(k)
    out.finish(out_own)
    exchange(qkv, qkv_own)
    for copy, target, tickets in exchanges:
        copy.wait()
        for (dy, dc), ticket in tickets.items():
            wires.wait(ticket, target.at[place.seq_at(-dy, -dc)])
    wires.close()


def back(sizes, gd, hidden, wd, wg, wu, gate, up, gb, n1t, n2t, headst, residual, qr, kvr, tables, bias, wqkv, wo, x, lse, gains):
    ny, nc, nz, nx = sizes
    n_seq, n_batch = ny * nc, nz * nx
    length, width = x.shape
    ff = wg.shape[3]
    rows = wo.shape[1]
    pairs = qr.shape[1] // 128
    chunk_down = gd.shape[1:]
    chunk_gate = (n_seq, rows, ff)
    chunk_out = (rows, width)
    chunk_qkv = (n_seq, rows, wqkv.shape[3])
    chunks = [chunk_down, chunk_gate, chunk_gate, chunk_out, chunk_qkv]
    results = [
        (VMEM, shape_of((length, width), BF16)),
        (VMEM, shape_of((length, width), BF16)),
        (VMEM, shape_of(chunk_down, F32)),
        (VMEM, shape_of(chunk_out, F32)),
        (HBM, shape_of(chunk_gate, BF16)),
        (HBM, shape_of(chunk_gate, BF16)),
        (HBM, shape_of(chunk_qkv, BF16)),
    ]
    results += [(HBM, shape_of((nz,) + chunk, BF16)) for chunk in chunks]
    results += [(HBM, shape_of((nz - 1,) + chunk, BF16)) for chunk in chunks]
    results += [(HBM, shape_of((nz,) + chunk_gate, BF16))] * 2
    results += [(HBM, shape_of((n_seq, length, width), BF16))]
    wires = 5 * (2 * nz - 1) + 3 * 3 + 3 + 3 * (n_seq - 1)
    row = pltpu.VMEM((length, width), BF16)
    return pl.pallas_call(
        functools.partial(back_kernel, sizes, pairs),
        in_specs=[HBM] * 19 + [VMEM] * 2,
        out_specs=[spec for spec, unused in results],
        out_shape=[kind for unused, kind in results],
        scratch_shapes=[pltpu.VMEM((nz,) + chunk, BF16) for chunk in chunks]
        + [
            pltpu.VMEM((nz,) + chunk_out, BF16),
            pltpu.VMEM((nz,) + chunk_qkv, BF16),
            pltpu.VMEM(chunk_down, BF16),
            pltpu.VMEM(chunk_gate, BF16),
            pltpu.VMEM(chunk_out, BF16),
            pltpu.VMEM(chunk_qkv, BF16),
            pltpu.VMEM((ny, length, width), BF16),
            row,
            pltpu.VMEM((ny, length, width), BF16),
            row,
            row,
            pltpu.VMEM((length, width), F32),
            pltpu.SemaphoreType.DMA((wires,)),
            pltpu.SemaphoreType.DMA((wires,)),
            pltpu.SemaphoreType.DMA((100,)),
        ],
        compiler_params=pltpu.CompilerParams(
            collective_id=1, has_side_effects=True, vmem_limit_bytes=VMEM_BYTES
        ),
        cost_estimate=pl.CostEstimate(
            flops=12 * n_seq * length * width * ff,
            bytes_accessed=100 * 1024 * 1024,
            transcendentals=pairs * (n_seq * length) ** 2,
        ),
    )(gd, hidden, wd, wg, wu, gate, up, gb, n1t, n2t, headst, residual, qr, kvr, tables, bias, wqkv, wo, x, lse, gains)


def by_permutes(
    tokens,
    cotangent,
    selection,
    segments,
    positions,
    gain_attn,
    w_query,
    w_key,
    w_value,
    w_out,
    gain_mlp,
    w_gate,
    w_up,
    w_down,
):
    seq = Axis("seq", 2)
    batch = Axis("batch", lax.axis_size("batch") // 4)
    n_seq, n_batch = seq.size, batch.size
    length, width = tokens.shape[1], tokens.shape[2]
    total_len = length * n_seq
    rows = w_query.shape[0]
    ff = w_gate.shape[1]
    q_cols = w_query.shape[1] // n_seq
    sharers = n_seq // KV_HEADS

    query_parts = w_query.reshape(rows, n_seq, q_cols)
    key_parts = jnp.repeat(w_key.reshape(rows, KV_HEADS, HEAD_DIM), sharers, axis=1)
    value_parts = jnp.repeat(w_value.reshape(rows, KV_HEADS, HEAD_DIM), sharers, axis=1)
    qkv_parts = jnp.concatenate([query_parts, key_parts, value_parts], axis=2).transpose(1, 0, 2)

    def spread(parts):
        mine = seq.exchange(parts)
        return batch.gather(mine, 1).reshape(n_seq * n_batch * rows, parts.shape[2])

    def collect(grad):
        parts = grad.astype(BF16).reshape(n_seq, n_batch, rows, grad.shape[1])
        return seq.exchange(batch.scatter_sum(parts, 1).astype(BF16)).astype(F32)

    def by_columns(weight):
        return weight.reshape(rows, n_seq, weight.shape[1] // n_seq).transpose(1, 0, 2)

    places = seq.gather(jnp.stack([segments[0], positions[0]]), 1)
    seg_all = places[0].reshape(total_len)
    pos_all = places[1].reshape(total_len)
    gains = batch.gather(seq.gather(jnp.stack([gain_attn, gain_mlp]), 1), 2)
    gain_one = gains[0].reshape(1, width).astype(F32)
    gain_two = gains[1].reshape(1, width).astype(F32)
    x_all = seq.gather(tokens[0], 0).reshape(total_len, width).astype(F32)
    w_qkv = spread(qkv_parts)
    wo = batch.gather(w_out, 0).reshape(n_batch * rows, width)
    wg = spread(by_columns(w_gate))
    wu = spread(by_columns(w_up))
    wd = batch.gather(w_down, 0).reshape(n_batch * w_down.shape[0], width)

    grad_out_row = cotangent[0].astype(F32) * selection[0].astype(F32)[:, None]
    grad_low = seq.gather(grad_out_row.astype(BF16), 0).reshape(total_len, width)

    row_input = tokens[0].astype(F32)
    inv_attn = rms_scale(row_input)
    normed1 = (x_all * rms_scale(x_all) * gain_one).astype(BF16)
    qkv = product(normed1, w_qkv)
    frequency = 10000.0 ** (-(jnp.arange(HALF, dtype=F32) * 2.0 / HEAD_DIM))
    angles = pos_all.astype(F32)[:, None] * jnp.tile(frequency, 4)[None, :]
    cosine, sine = jnp.cos(angles), jnp.sin(angles)
    seg_row, seg_col = seg_all[None, :], seg_all[:, None]
    heads_out, query_rot, kv_rot, lse = attend(qkv, cosine, sine, seg_row, seg_col)
    attn_part = product(heads_out, wo).astype(BF16).reshape(n_seq, length, width)
    residual = row_input + seq.scatter_sum(attn_part, 0)

    inv_mlp = rms_scale(residual)
    normed2_own = (residual * inv_mlp * gain_two).astype(BF16)
    normed2 = seq.gather(normed2_own, 0).reshape(total_len, width)
    gate_proj = product(normed2, wg)
    up_proj = product(normed2, wu)
    sigma = jax.nn.sigmoid(gate_proj)
    activated = gate_proj * sigma
    hidden = (activated * up_proj).astype(BF16)
    mixed_part = product(hidden, wd).astype(BF16).reshape(n_seq, length, width)
    mixed = (residual + seq.scatter_sum(mixed_part, 0)).astype(BF16)[None]

    grad_down = product_rows(hidden, grad_low)
    grad_hidden = product_cols(grad_low, wd)
    grad_gate_act = (
        grad_hidden * up_proj * sigma * (1.0 + gate_proj * (1.0 - sigma))
    ).astype(BF16)
    grad_up_act = (grad_hidden * activated).astype(BF16)
    grad_gate = product_rows(normed2, grad_gate_act)
    grad_up = product_rows(normed2, grad_up_act)
    normed_part = product_cols(grad_gate_act, wg) + product_cols(grad_up_act, wu)
    normed_terms = seq.scatter_sum(normed_part.astype(BF16).reshape(n_seq, length, width), 0)
    grad_resid = grad_out_row + norm_back(normed_terms, residual, inv_mlp, gain_two)

    down_own = batch.scatter_sum(
        grad_down.astype(BF16).reshape(n_batch, w_down.shape[0], width), 0
    )
    gate_own = collect(grad_gate).transpose(1, 0, 2).reshape(rows, ff)
    up_own = collect(grad_up).transpose(1, 0, 2).reshape(rows, ff)

    grad_branch = seq.gather(grad_resid.astype(BF16), 0).reshape(total_len, width)
    grad_wout = product_rows(heads_out, grad_branch)
    grad_heads = product_cols(grad_branch, wo).astype(BF16)
    grad_qkv_act = attend_back(
        query_rot, kv_rot, grad_heads, lse, cosine, sine, seg_row, seg_col
    )
    grad_wqkv = product_rows(normed1, grad_qkv_act)
    input_part = product_cols(grad_qkv_act, w_qkv).astype(BF16).reshape(n_seq, length, width)
    grad_normed1 = seq.scatter_sum(input_part, 0)
    tokens_grad = (
        grad_resid + norm_back(grad_normed1, row_input, inv_attn, gain_one)
    ).astype(BF16)[None]
    out_own = batch.scatter_sum(grad_wout.astype(BF16).reshape(n_batch, rows, width), 0)
    qkv_own = collect(grad_wqkv)
    query_own = qkv_own[:, :, :q_cols].transpose(1, 0, 2).reshape(rows, n_seq * q_cols)

    def shared(columns):
        heads = columns.reshape(KV_HEADS, sharers, rows, HEAD_DIM).sum(axis=1)
        return heads.transpose(1, 0, 2).reshape(rows, KV_HEADS * HEAD_DIM)

    key_own = shared(qkv_own[:, :, q_cols : q_cols + HEAD_DIM])
    value_own = shared(qkv_own[:, :, q_cols + HEAD_DIM :])

    def along(weight, grad):
        return jnp.sum(weight.astype(F32) * grad, axis=1)

    gain1_own = (
        along(w_query, query_own) + along(w_key, key_own) + along(w_value, value_own)
    ) / gain_attn.astype(F32)
    gain2_own = (along(w_gate, gate_own) + along(w_up, up_own)) / gain_mlp.astype(F32)
    return (
        mixed,
        tokens_grad,
        query_own,
        key_own,
        value_own,
        out_own,
        gate_own,
        up_own,
        down_own,
        gain1_own,
        gain2_own,
    )


def by_kernels(
    tokens,
    cotangent,
    selection,
    segments,
    positions,
    gain_attn,
    w_query,
    w_key,
    w_value,
    w_out,
    gain_mlp,
    w_gate,
    w_up,
    w_down,
):
    sizes = mesh_sizes()
    n_seq, n_batch = sizes[0] * sizes[1], sizes[2] * sizes[3]
    length, width = tokens.shape[1], tokens.shape[2]
    rows, ff = w_gate.shape
    q_cols = w_query.shape[1] // n_seq

    def by_columns(weight):
        return weight.reshape(rows, n_seq, weight.shape[1] // n_seq).transpose(1, 0, 2)

    qkv_parts = jnp.concatenate([by_columns(w) for w in (w_query, w_key, w_value)], axis=2)
    grad_low = (cotangent[0].astype(F32) * selection[0].astype(F32)[:, None]).astype(BF16)
    frequency = 10000.0 ** (-(jnp.arange(HALF, dtype=F32) * 2.0 / HEAD_DIM))
    angles = positions[0].astype(F32)[:, None] * frequency[None, :]
    documents = jnp.broadcast_to(segments[0].astype(F32)[:, None], (length, 128 - HEAD_DIM))
    table = jnp.concatenate([jnp.cos(angles), jnp.sin(angles), documents], axis=1)
    gain_tile = jnp.pad(
        jnp.stack([gain_attn, gain_mlp]).astype(F32), ((0, 6), (0, 128 - gain_attn.shape[0]))
    )
    (
        w_qkv,
        wo,
        wg,
        wu,
        wd,
        gb_all,
        n1t,
        n2t,
        residual,
        headst,
        query_rot,
        kv_rot,
        lse,
        rotary,
        gains,
        bias,
        gate_proj,
        up_proj,
        grad_down,
        hidden,
    ) = front(
        sizes,
        tokens[0],
        grad_low,
        table,
        gain_tile,
        qkv_parts,
        w_out,
        by_columns(w_gate),
        by_columns(w_up),
        w_down,
    )
    mixed, tokens_grad, down_own, out_own, gate_part, up_part, qkv_part = back(
        sizes,
        grad_down.reshape(n_batch, w_down.shape[0], width),
        hidden,
        wd,
        wg,
        wu,
        gate_proj,
        up_proj,
        gb_all,
        n1t,
        n2t,
        headst,
        residual,
        query_rot,
        kv_rot,
        rotary,
        bias,
        w_qkv,
        wo,
        tokens[0],
        lse,
        gains,
    )[:7]

    def by_rows(part):
        return part.astype(F32).transpose(1, 0, 2).reshape(rows, n_seq * part.shape[2])

    query_own = by_rows(qkv_part[:, :, :q_cols])
    key_own = by_rows(qkv_part[:, :, q_cols : q_cols + HEAD_DIM])
    value_own = by_rows(qkv_part[:, :, q_cols + HEAD_DIM :])
    gate_own, up_own = by_rows(gate_part), by_rows(up_part)

    def along(weight, grad):
        return jnp.sum(weight.astype(F32) * grad, axis=1)

    gain1_own = (
        along(w_query, query_own) + along(w_key, key_own) + along(w_value, value_own)
    ) / gain_attn.astype(F32)
    gain2_own = (along(w_gate, gate_own) + along(w_up, up_own)) / gain_mlp.astype(F32)
    return (
        mixed[None],
        tokens_grad[None],
        query_own,
        key_own,
        value_own,
        out_own,
        gate_own,
        up_own,
        down_own,
        gain1_own,
        gain2_own,
    )


def mesh_sizes():
    return (lax.axis_size("seq") // 2, 2, 4, lax.axis_size("batch") // 4)


def per_device(*args):
    fits = mesh_sizes() == (2, 2, 4, 2) and args[0].shape[1:] == (256, 2048)
    return (by_kernels if fits else by_permutes)(*args)


def solution(mesh):
    both = ("seq", "batch")
    tokens = P("batch", "seq", None)
    flags = P("batch", "seq")
    matrix = P(both, None)
    vector = P(both)
    in_specs = (
        (tokens, tokens, flags, flags, flags)
        + (vector, matrix, matrix, matrix, matrix)
        + (vector, matrix, matrix, matrix)
    )
    out_specs = (tokens, tokens) + (matrix,) * 7 + (vector, vector)
    return jax.shard_map(
        per_device, mesh=mesh, in_specs=in_specs, out_specs=out_specs, check_vma=False
    )
```

```python
import functools

import jax
import jax.numpy as jnp
from jax import lax
from jax.experimental import pallas as pl
from jax.experimental.pallas import tpu as pltpu
from jax.sharding import PartitionSpec as P

HEADS = 32
KV_HEADS = 4
HEAD_DIM = 64
HALF = HEAD_DIM // 2

EPSILON = 1e-05
MASKED_SCORE = -1e30
SCALE = HEAD_DIM ** (-0.5)
CONTRACT_ROWS = (((0,), (0,)), ((), ()))
CONTRACT_COLS = (((1,), (1,)), ((), ()))
BF16 = jnp.bfloat16
F32 = jnp.float32


def product(left, right):
    return jnp.dot(left, right, preferred_element_type=F32)


def product_rows(left, right):
    return lax.dot_general(left, right, CONTRACT_ROWS, preferred_element_type=F32)


def product_cols(left, right):
    return lax.dot_general(left, right, CONTRACT_COLS, preferred_element_type=F32)


def rms_scale(inputs):
    return lax.rsqrt(jnp.mean(inputs * inputs, axis=-1, keepdims=True) + EPSILON)


def norm_back(grad_normed, inputs, inverse, gain):
    scaled = gain * grad_normed
    cubed = inverse * inverse * inverse
    return inverse * scaled - inputs * cubed * jnp.mean(scaled * inputs, axis=-1, keepdims=True)


class Axis:
    def __init__(self, name, inner):
        self.name = name
        self.size = lax.axis_size(name)
        self.inner = inner
        self.outer = self.size // inner
        index = lax.axis_index(name)
        self.index = index
        self.o = index // inner
        self.i = index % inner

    def shift(self, value, outer_by, inner_by):
        pairs = []
        for o in range(self.outer):
            for i in range(self.inner):
                target = ((o + outer_by) % self.outer) * self.inner + (i + inner_by) % self.inner
                pairs.append((o * self.inner + i, target))
        return lax.ppermute(value, self.name, pairs)

    def before(self, outer_by, inner_by):
        o = lax.rem(self.o + self.outer - outer_by, self.outer)
        i = lax.rem(self.i + self.inner - inner_by, self.inner)
        return o * self.inner + i

    def after(self, outer_by, inner_by):
        o = lax.rem(self.o + outer_by, self.outer)
        i = lax.rem(self.i + inner_by, self.inner)
        return o * self.inner + i

    def gather(self, block, dim=0):
        shape = block.shape[:dim] + (self.size,) + block.shape[dim:]
        out = jnp.zeros(shape, block.dtype)
        for k in range(self.outer):
            got = block if k == 0 else self.shift(block, k, 0)
            for m in range(self.inner):
                piece = got if m == 0 else self.shift(got, 0, m)
                out = lax.dynamic_update_slice_in_dim(
                    out, jnp.expand_dims(piece, dim), self.before(k, m), dim
                )
        return out

    def scatter_sum(self, parts, dim=0):
        shape = parts.shape[:dim] + (self.outer, self.inner) + parts.shape[dim + 1 :]
        grid = parts.reshape(shape)

        def inner_part(i):
            return lax.squeeze(lax.dynamic_slice_in_dim(grid, i, 1, dim + 1), (dim + 1,))

        total = inner_part(self.i).astype(F32)
        for m in range(1, self.inner):
            mine = inner_part(lax.rem(self.i + m, self.inner))
            total = total + self.shift(mine, 0, m).astype(F32)
        low = total.astype(BF16)

        def outer_part(o):
            return lax.squeeze(lax.dynamic_slice_in_dim(low, o, 1, dim), (dim,))

        out = outer_part(self.o).astype(F32)
        for k in range(1, self.outer):
            out = out + self.shift(outer_part(lax.rem(self.o + k, self.outer)), k, 0).astype(F32)
        return out

    def exchange(self, parts):
        out = jnp.zeros(parts.shape, parts.dtype)
        for k in range(self.outer):
            for m in range(self.inner):
                part = lax.dynamic_slice_in_dim(parts, self.after(k, m), 1, 0)
                got = part if (k, m) == (0, 0) else self.shift(part, k, m)
                out = lax.dynamic_update_slice_in_dim(out, got, self.before(k, m), 0)
        return out


def rotate_lanes(value, sign):
    lane = lax.broadcasted_iota(jnp.int32, value.shape, 1) % HEAD_DIM
    first = lane < HALF
    width = value.shape[1]
    up = pltpu.roll(value, width - HALF, 1)
    down = pltpu.roll(value, HALF, 1)
    return jnp.where(first, -sign * up, sign * down)


def mask_bias(bias_ref, seg_row_ref, seg_col_ref, length):
    rows = 256
    for start in range(0, length, rows):
        keys = seg_col_ref[start : start + rows, :]
        queries = seg_row_ref[:, :]
        key_pos = start + lax.broadcasted_iota(jnp.int32, (rows, length), 0)
        query_pos = lax.broadcasted_iota(jnp.int32, (rows, length), 1)
        allowed = (keys == queries) & (key_pos <= query_pos)
        bias_ref[start : start + rows, :] = jnp.where(allowed, 0.0, MASKED_SCORE)


def attend_kernel(
    qblock,
    q_ref,
    kv_ref,
    cos_ref,
    sin_ref,
    seg_row_ref,
    seg_col_ref,
    o_ref,
    qr_ref,
    kvr_ref,
    lse_ref,
    bias_ref,
):
    length = q_ref.shape[0]
    cosine = cos_ref[...]
    sine = sin_ref[...]

    @pl.when(pl.program_id(0) == 0)
    def _():
        mask_bias(bias_ref, seg_row_ref, seg_col_ref, length)
        kv = kv_ref[...]
        rotated = kv * cosine + rotate_lanes(kv, 1.0) * sine
        lane = lax.broadcasted_iota(jnp.int32, kv.shape, 1)
        kvr_ref[...] = jnp.where(lane < HEAD_DIM, rotated, kv).astype(BF16)

    q = q_ref[...]
    qr_ref[...] = (q * cosine + rotate_lanes(q, 1.0) * sine).astype(BF16)
    for start in range(0, length, qblock):
        stop = start + qblock
        keys = kvr_ref[:stop, :HEAD_DIM]
        values = kvr_ref[:stop, HEAD_DIM:]
        for head in range(2):
            lanes = slice(head * HEAD_DIM, (head + 1) * HEAD_DIM)
            queries = qr_ref[start:stop, lanes] * SCALE
            scores = product_cols(keys, queries.astype(BF16)) + bias_ref[:stop, start:stop]
            top = jnp.max(scores, axis=0, keepdims=True)
            grown = jnp.exp(scores - top)
            total = jnp.sum(grown, axis=0, keepdims=True)
            probs = (grown * (1.0 / total)).astype(BF16)
            lse_ref[0, head : head + 1, start:stop] = top + jnp.log(total)
            o_ref[start:stop, lanes] = product_rows(probs, values).astype(BF16)


def attend_back_kernel(
    qblock,
    qr_ref,
    kvr_ref,
    do_ref,
    lse_ref,
    cos_ref,
    sin_ref,
    seg_row_ref,
    seg_col_ref,
    dqkv_ref,
    bias_ref,
    dq_ref,
    dk_ref,
    dv_ref,
):
    length = qr_ref.shape[0]
    cosine = cos_ref[...]
    sine = sin_ref[...]
    pair = pl.program_id(0)

    @pl.when(pair == 0)
    def _():
        mask_bias(bias_ref, seg_row_ref, seg_col_ref, length)
        dk_ref[...] = jnp.zeros_like(dk_ref)
        dv_ref[...] = jnp.zeros_like(dv_ref)

    for start in range(0, length, qblock):
        stop = start + qblock
        keys = kvr_ref[:stop, :HEAD_DIM]
        values = kvr_ref[:stop, HEAD_DIM:]
        for head in range(2):
            lanes = slice(head * HEAD_DIM, (head + 1) * HEAD_DIM)
            queries = (qr_ref[start:stop, lanes] * SCALE).astype(BF16)
            grads = do_ref[start:stop, lanes]
            scores = product_cols(keys, queries) + bias_ref[:stop, start:stop]
            probs = jnp.exp(scores - lse_ref[0, head : head + 1, start:stop])
            dprobs = product_cols(values, grads)
            delta = jnp.sum(probs * dprobs, axis=0, keepdims=True)
            dscores = (probs * (dprobs - delta)).astype(BF16)
            dv_ref[:stop, :] += product(probs.astype(BF16), grads)
            dk_ref[:stop, :] += product(dscores, queries)
            dq_ref[start:stop, lanes] = product_rows(dscores, keys) * SCALE

    dq = dq_ref[...]
    turned = rotate_lanes(dq * sine, -1.0)
    columns = pl.ds(pl.multiple_of(pair * 128, 128), 128)
    dqkv_ref[:, columns] = (dq * cosine + turned).astype(BF16)

    @pl.when(pair == pl.num_programs(0) - 1)
    def _():
        grads = jnp.concatenate([dk_ref[...], dv_ref[...]], axis=1)
        back = grads * cosine + rotate_lanes(grads * sine, -1.0)
        lane = lax.broadcasted_iota(jnp.int32, grads.shape, 1)
        width = dqkv_ref.shape[1]
        dqkv_ref[:, width - 128 :] = jnp.where(lane < HEAD_DIM, back, grads).astype(BF16)


def whole_spec(shape):
    return pl.BlockSpec(shape, lambda j: (0,) * len(shape))


def attend(qkv, cosine, sine, seg_row, seg_col):
    length, width = qkv.shape
    pairs = width // 128 - 1
    qblock = min(256, length)
    return pl.pallas_call(
        functools.partial(attend_kernel, qblock),
        grid=(pairs,),
        in_specs=[
            pl.BlockSpec((length, 128), lambda j: (0, j)),
            pl.BlockSpec((length, 128), lambda j: (0, pairs)),
            whole_spec((length, 128)),
            whole_spec((length, 128)),
            whole_spec((1, length)),
            whole_spec((length, 1)),
        ],
        out_specs=[
            pl.BlockSpec((length, 128), lambda j: (0, j)),
            pl.BlockSpec((length, 128), lambda j: (0, j)),
            whole_spec((length, 128)),
            pl.BlockSpec((1, 2, length), lambda j: (j, 0, 0)),
        ],
        out_shape=[
            jax.ShapeDtypeStruct((length, pairs * 128), BF16),
            jax.ShapeDtypeStruct((length, pairs * 128), BF16),
            jax.ShapeDtypeStruct((length, 128), BF16),
            jax.ShapeDtypeStruct((pairs, 2, length), F32),
        ],
        scratch_shapes=[pltpu.VMEM((length, length), F32)],
        compiler_params=pltpu.CompilerParams(vmem_limit_bytes=48 * 1024 * 1024),
        cost_estimate=pl.CostEstimate(
            flops=pairs * 2 * length * length * HEAD_DIM * 2,
            bytes_accessed=8 * length * width,
            transcendentals=pairs * length * length,
        ),
    )(qkv, qkv, cosine, sine, seg_row, seg_col)


def attend_back(qr, kvr, grads, lse, cosine, sine, seg_row, seg_col):
    length = qr.shape[0]
    pairs = qr.shape[1] // 128
    qblock = min(256, length)
    return pl.pallas_call(
        functools.partial(attend_back_kernel, qblock),
        grid=(pairs,),
        in_specs=[
            pl.BlockSpec((length, 128), lambda j: (0, j)),
            whole_spec((length, 128)),
            pl.BlockSpec((length, 128), lambda j: (0, j)),
            pl.BlockSpec((1, 2, length), lambda j: (j, 0, 0)),
            whole_spec((length, 128)),
            whole_spec((length, 128)),
            whole_spec((1, length)),
            whole_spec((length, 1)),
        ],
        out_specs=whole_spec((length, (pairs + 1) * 128)),
        out_shape=jax.ShapeDtypeStruct((length, (pairs + 1) * 128), BF16),
        scratch_shapes=[
            pltpu.VMEM((length, length), F32),
            pltpu.VMEM((length, 128), F32),
            pltpu.VMEM((length, HEAD_DIM), F32),
            pltpu.VMEM((length, HEAD_DIM), F32),
        ],
        compiler_params=pltpu.CompilerParams(vmem_limit_bytes=48 * 1024 * 1024),
        cost_estimate=pl.CostEstimate(
            flops=pairs * 5 * length * length * HEAD_DIM * 2,
            bytes_accessed=12 * length * qr.shape[1],
            transcendentals=pairs * length * length,
        ),
    )(qr, kvr, grads, lse, cosine, sine, seg_row, seg_col)


MESH = pl.DeviceIdType.MESH
HBM = pl.BlockSpec(memory_space=pl.ANY)
VMEM = pl.BlockSpec(memory_space=pltpu.VMEM)
VMEM_BYTES = 62 * 1024 * 1024
STEP = 16
DOWN_CUT = 64


class Place:
    def __init__(self, sizes):
        self.ny, self.nc, self.nz, self.nx = sizes
        self.s = lax.axis_index("seq")
        self.b = lax.axis_index("batch")
        self.y, self.c = self.s // self.nc, self.s % self.nc
        self.z, self.x = self.b // self.nx, self.b % self.nx

    def seq_at(self, dy, dc):
        return (self.y + dy + self.ny) % self.ny * self.nc + (self.c + dc + self.nc) % self.nc

    def z_at(self, dz):
        return (self.z + dz + self.nz) % self.nz

    def batch_at(self, dz, dx):
        return self.z_at(dz) * self.nx + (self.x + dx + self.nx) % self.nx

    def enter(self):
        peers = [
            (self.seq_at(dy, dc), self.b)
            for dy in range(self.ny)
            for dc in range(self.nc)
            if (dy, dc) != (0, 0)
        ]
        peers += [(self.s, self.batch_at(k, 0)) for k in range(1, self.nz)]
        peers += [(self.s, self.batch_at(0, m)) for m in range(1, self.nx)]
        barrier = pltpu.get_barrier_semaphore()
        for peer in peers:
            pl.semaphore_signal(barrier, inc=1, device_id=peer, device_id_type=MESH)
        pl.semaphore_wait(barrier, len(peers))


def only(when, action):
    if when is None:
        action()
    else:
        pl.when(when())(action)


class Wires:
    def __init__(self, send_sems, recv_sems):
        self.send_sems, self.recv_sems = send_sems, recv_sems
        self.ends = []
        self.open = []

    def describe(self, index, source, target):
        return pltpu.make_async_remote_copy(
            src_ref=source,
            dst_ref=target,
            send_sem=self.send_sems.at[index],
            recv_sem=self.recv_sems.at[index],
            device_id=self.ends[index][2](),
            device_id_type=MESH,
        )

    def push(self, source, target, device, when=None):
        index = len(self.ends)
        self.ends.append((source, target, device, when))
        self.open.append(index)
        only(when, lambda: self.describe(index, source(), target()).start())
        return index

    def wait(self, index, landed):
        self.describe(index, landed, landed).wait_recv()

    def sent(self, index):
        self.open.remove(index)
        source, target, unused, when = self.ends[index]
        only(when, lambda: self.describe(index, source(), target()).wait_send())

    def close(self):
        for index in list(self.open):
            self.sent(index)


class Copies:
    def __init__(self, sems):
        self.sems = sems
        self.count = 0

    def start(self, source, target):
        copy = Copy(self, self.count, source, target)
        self.count += 1
        copy.describe().start()
        return copy


class Copy:
    def __init__(self, copies, index, source, target):
        self.copies, self.index, self.source, self.target = copies, index, source, target

    def describe(self):
        sem = self.copies.sems.at[self.index]
        return pltpu.make_async_copy(self.source, self.target, sem)

    def wait(self):
        self.describe().wait()


class Through:
    def __init__(self, copies, source, buffer, target):
        self.copies, self.buffer, self.target = copies, buffer, target
        self.copy = copies.start(source, buffer)

    def turn(self):
        self.copy.wait()
        self.copy = self.copies.start(self.buffer, self.target)

    def wait(self):
        self.copy.wait()


class Gather:
    def __init__(self, wires, slot, own, outer, inner, at, device):
        self.wires, self.slot, self.own = wires, slot, own
        self.outer, self.inner, self.at, self.device = outer, inner, at, device
        self.first, self.second = {}, {}

    def push(self, source, target, k, m):
        return self.wires.push(source, target, lambda: self.device(self.at(k, m)))

    def start(self):
        mine = lambda: self.slot(self.at(0, 0))
        for k in range(1, self.outer):
            self.first[k] = self.push(self.own, mine, k, 0)
        for m in range(1, self.inner):
            self.second[0, m] = self.push(self.own, mine, 0, m)

    def pass_on(self, k):
        came = lambda: self.slot(self.at(-k, 0))
        self.wires.wait(self.first[k], came())
        for m in range(1, self.inner):
            self.second[k, m] = self.push(came, came, 0, m)

    def finish(self):
        for (k, m), ticket in self.second.items():
            self.wires.wait(ticket, self.slot(self.at(-k, -m)))


class LineGather:
    def __init__(self, wires, place, slot, own, x_first=False):
        self.wires, self.place, self.slot, self.own, self.x_first = wires, place, slot, own, x_first
        self.up, self.down, self.across = {}, {}, {}

    def at(self, dz, dx):
        place = self.place
        zz = jnp.clip(place.z + dz, 0, place.nz - 1)
        return self.slot(zz * place.nx + (place.x + dx) % place.nx)

    def below(self, k):
        return self.place.z >= k

    def above(self, k):
        return self.place.z + k < self.place.nz

    def push(self, source, dz, dx, when=None):
        place = self.place
        return self.wires.push(
            source[0],
            source[1],
            lambda: (
                place.s,
                jnp.clip(place.z + dz, 0, place.nz - 1) * place.nx + (place.x + dx) % place.nx,
            ),
            when,
        )

    def spread(self, source, dx):
        self.up[dx, 1] = self.push(source, 1, 0, lambda: self.above(1))
        self.down[dx, 1] = self.push(source, -1, 0, lambda: self.below(1))

    def start_x(self):
        self.across[0] = self.push((self.own, lambda: self.at(0, 0)), 0, 1)

    def start_z(self):
        self.spread((self.own, lambda: self.at(0, 0)), 0)

    def cross(self):
        came = lambda: self.at(0, 1)
        self.wires.wait(self.across[0], came())
        self.spread((came, came), 1)

    def relay(self, k):
        last = k + 1 == self.place.nz
        for dx in (0, 1) if self.x_first else (0,):
            for side, table, here, on in (
                (-1, self.up, self.below, self.above),
                (1, self.down, self.above, self.below),
            ):
                pl.when(here(k))(
                    lambda: self.wires.wait(table[dx, k], self.at(side * k, dx))
                )
                if not last:
                    table[dx, k + 1] = self.push(
                        self.fixed(side * k, dx),
                        -side,
                        0,
                        lambda here=here, on=on: here(k) & on(1),
                    )
                if not self.x_first:
                    self.across[side * k] = self.push(
                        self.fixed(side * k, dx), 0, 1, lambda here=here: here(k)
                    )

    def fixed(self, dz, dx):
        came = lambda: self.at(dz, dx)
        return came, came

    def finish(self):
        if self.x_first:
            return
        self.wires.wait(self.across[0], self.at(0, 1))
        for k in range(1, self.place.nz):
            pl.when(self.below(k))(
                lambda: self.wires.wait(self.across[-k], self.at(-k, 1))
            )
            pl.when(self.above(k))(
                lambda: self.wires.wait(self.across[k], self.at(k, 1))
            )


class RowSum:
    def __init__(self, wires, place, part_ref, core_in, far_in):
        self.wires, self.place = wires, place
        self.part_ref, self.core_in, self.far_in = part_ref, core_in, far_in
        self.tickets = {}

    def slot(self, t):
        return self.place.seq_at((t + 1) % 2, (3 - t) // 2)

    def push(self, t, source, target, dy, dc):
        self.tickets[t] = self.wires.push(
            lambda: self.part_ref.at[source],
            lambda: target(),
            lambda: (self.place.seq_at(dy, dc), self.place.b),
        )

    def compute(self, part):
        def body(t, unused):
            self.part_ref[t] = part(self.slot(t)).astype(BF16)

            @pl.when(t == 0)
            def _():
                self.push(0, 0, lambda: self.core_in.at[1], 0, 1)

            @pl.when(t == 1)
            def _():
                self.push(1, 1, lambda: self.core_in.at[0], 0, 1)

            @pl.when(t == 2)
            def _():
                self.wires.wait(self.tickets[0], self.core_in.at[1])
                mine = self.part_ref.at[2]
                add_up(mine, [mine, self.core_in.at[1]])
                self.push(2, 2, lambda: self.far_in, 1, 0)

            return unused

        lax.fori_loop(0, 4, body, 0)

    def finish(self, target, extra=()):
        self.wires.wait(self.tickets[1], self.core_in.at[0])
        self.wires.wait(self.tickets[2], self.far_in)
        add_up(target, [self.part_ref.at[3], self.core_in.at[0], self.far_in] + list(extra))

    def sent(self):
        for ticket in self.tickets.values():
            self.wires.sent(ticket)


class Rotating:
    def __init__(self, copies):
        self.sems, self.base = copies.sems, copies.count
        copies.count += 2

    def copy(self, i, source, target):
        return pltpu.make_async_copy(source, target, self.sems.at[self.base + i % 2])


def add_up(target, sources):
    shape = target.shape
    steps = shape[-2] // STEP

    def body(i, unused):
        at = pl.ds(pl.multiple_of(i % steps * STEP, STEP), STEP)
        where = (at, slice(None)) if len(shape) == 2 else (i // steps, at, slice(None))
        total = sources[0][where].astype(F32)
        for source in sources[1:]:
            total = total + source[where].astype(F32)
        target[where] = total.astype(target.dtype)
        return unused

    lax.fori_loop(0, steps * (1 if len(shape) == 2 else shape[0]), body, 0)


def front_kernel(
    sizes,
    pairs,
    x_ref,
    gb_ref,
    table_ref,
    gain_ref,
    qkv_ref,
    out_ref,
    gate_ref,
    up_ref,
    down_ref,
    wqkv_out,
    wo_out,
    wg_ref,
    wu_ref,
    wd_ref,
    gb_all_ref,
    n1t_out,
    n2t_out,
    residual_out,
    headst_out,
    qr_out,
    kvr_out,
    lse_ref,
    tables_out,
    gains_ref,
    bias_out,
    gate_proj_ref,
    up_proj_ref,
    grad_down_ref,
    hidden_out_ref,
    wqkv_ref,
    wo_ref,
    n1t_ref,
    n2t_ref,
    residual_ref,
    headst_ref,
    qr_ref,
    kvr_ref,
    tables_ref,
    bias_ref,
    x_all_ref,
    table_all_ref,
    gain_all_ref,
    core_in_ref,
    far_in_ref,
    own_gb_ref,
    n2_ref,
    own_down_ref,
    own_gate_ref,
    send_sems,
    recv_sems,
    copy_sems,
):
    place = Place(sizes)
    ny, nc, nz, nx = sizes
    s, b = place.s, place.b
    n_seq, n_batch = ny * nc, nz * nx
    length, width = x_ref.shape
    total_len = n_seq * length
    ff = gate_ref.shape[2]
    wires = Wires(send_sems, recv_sems)
    copies = Copies(copy_sems)
    row_others = [(dy, dc) for dy in range(ny) for dc in range(nc) if dy or dc]

    def over_batch(slot, own, x_first=False):
        return LineGather(wires, place, slot, own, x_first)

    def over_seq(slot, own):
        return Gather(wires, slot, own, ny, nc, place.seq_at, lambda j: (j, b))

    def columns(ref):
        return lambda j: ref.at[:, j]

    def blocks(ref):
        return lambda j: ref.at[j]

    class Exchange:
        def __init__(self, parts, target, many=True, own=None):
            self.target = target
            part = (lambda j: parts.at[j]) if many else (lambda j: parts)
            self.copy = own or copies.start(part(s), target.at[s, b])
            self.tickets = {}
            for away in row_others:
                self.tickets[away] = wires.push(
                    lambda away=away: part(place.seq_at(*away)),
                    lambda: target.at[s, b],
                    lambda away=away: (place.seq_at(*away), b),
                )

        def finish(self):
            self.copy.wait()
            for (dy, dc), ticket in self.tickets.items():
                wires.wait(ticket, self.target.at[place.seq_at(-dy, -dc), b])

    late = []

    def keep(source, target):
        late.append(copies.start(source, target))

    own_gb = Through(copies, gb_ref, own_gb_ref, gb_all_ref.at[s])
    own_down = Through(copies, down_ref, own_down_ref, wd_ref.at[b])
    own_gate = Through(copies, gate_ref.at[s], own_gate_ref.at[0], wg_ref.at[s, b])
    own_up = Through(copies, up_ref.at[s], own_gate_ref.at[1], wu_ref.at[s, b])
    own_table = copies.start(table_ref, table_all_ref.at[s])
    own_x = copies.start(x_ref, x_all_ref.at[s])
    own_out = copies.start(out_ref, wo_ref.at[b])
    place.enter()
    qkv_parts = Exchange(qkv_ref, wqkv_ref)
    gain_parts = Exchange(gain_ref, gain_all_ref, many=False)
    for copy in (own_gate, own_up, own_down, own_gb):
        copy.turn()
    wo = over_batch(blocks(wo_ref), lambda: out_ref)
    wo.start_x()
    wo.start_z()
    table_all = over_seq(blocks(table_all_ref), lambda: table_ref)
    table_all.start()
    gate_parts = Exchange(gate_ref, wg_ref, own=own_gate)
    x_all = over_seq(blocks(x_all_ref), lambda: x_ref)
    x_all.start()
    up_parts = Exchange(up_ref, wu_ref, own=own_up)
    wqkv = over_batch(columns(wqkv_ref), lambda: wqkv_ref.at[:, b])
    gains = over_batch(columns(gain_all_ref), lambda: gain_all_ref.at[:, b])
    wg = over_batch(columns(wg_ref), lambda: wg_ref.at[:, b])
    wu = over_batch(columns(wu_ref), lambda: wu_ref.at[:, b])
    cut = pl.ds(0, DOWN_CUT)
    rest = pl.ds(DOWN_CUT, down_ref.shape[0] - DOWN_CUT)
    wd1 = over_batch(lambda j: wd_ref.at[j, cut], lambda: down_ref.at[cut])
    wd2 = over_batch(lambda j: wd_ref.at[j, rest], lambda: down_ref.at[rest], True)
    gb_all = over_seq(blocks(gb_all_ref), lambda: gb_ref)

    qkv_parts.finish()
    wqkv.start_x()
    wqkv.start_z()
    gain_parts.finish()
    gains.start_x()
    gains.start_z()
    wo.relay(1)
    gains.relay(1)
    gate_parts.finish()
    wg.start_x()
    wqkv.relay(1)
    wg.start_z()
    wo.relay(2)
    gains.relay(2)
    wqkv.relay(2)
    for k in range(1, ny):
        table_all.pass_on(k)
        x_all.pass_on(k)
    wo.relay(3)
    gains.relay(3)
    wqkv.relay(3)
    up_parts.finish()
    wu.start_x()
    wd2.start_x()
    wu.start_z()
    gb_all.start()

    def attention(n1_ref, qkv_proj_ref, part_ref):
        own_table.wait()
        table_all.finish()
        own_x.wait()
        x_all.finish()
        gains.finish()
        rows = width // (n_seq * n_batch)
        for g in range(2):
            gains_ref[g : g + 1, :] = jnp.concatenate(
                [gain_all_ref[i, j, g : g + 1, :rows] for i in range(n_seq) for j in range(n_batch)],
                axis=1,
            )
        gain_one = gains_ref[0:1, :]
        half = length // 2

        def norm_rows(i, unused):
            part = x_all_ref[i // 2, pl.ds(i % 2 * half, half), :].astype(F32)
            at = pl.ds(pl.multiple_of(i * half, half), half)
            n1_ref[at, :] = (part * rms_scale(part) * gain_one).astype(BF16)
            return unused

        lax.fori_loop(0, 2 * n_seq, norm_rows, 0)
        for j in range(n_seq):
            at = slice(j * length, (j + 1) * length)
            table = table_all_ref[j]
            cos_part, sin_part = table[:, :HALF], table[:, HALF:HEAD_DIM]
            tables_ref[0, at, :] = jnp.concatenate([cos_part] * 4, axis=1)
            tables_ref[1, at, :] = jnp.concatenate([sin_part] * 4, axis=1)
        flipped = [
            jnp.transpose(table_all_ref[j])[HEAD_DIM : HEAD_DIM + 1, :] for j in range(n_seq)
        ]
        query_seg = jnp.concatenate(flipped, axis=1)
        for j in range(n_seq):
            key_seg = table_all_ref[j][:, HEAD_DIM : HEAD_DIM + 1]
            key_pos = j * length + lax.broadcasted_iota(jnp.int32, (length, total_len), 0)
            query_pos = lax.broadcasted_iota(jnp.int32, (length, total_len), 1)
            allowed = (key_seg == query_seg) & (key_pos <= query_pos)
            bias_ref[j * length : (j + 1) * length, :] = jnp.where(
                allowed, 0.0, MASKED_SCORE
            ).astype(BF16)
        keep(tables_ref, tables_out)
        keep(bias_ref, bias_out)

        wqkv.finish()
        keep(wqkv_ref, wqkv_out)
        weights = wqkv_ref[...].reshape(width, wqkv_ref.shape[3])

        def project(i, unused):
            at = pl.ds(pl.multiple_of(i * length, length), length)
            qkv_proj_ref[at, :] = product(n1_ref[at, :], weights)
            return unused

        lax.fori_loop(0, n_seq, project, 0)
        kv = qkv_proj_ref[:, pairs * 128 :]
        lane = lax.broadcasted_iota(jnp.int32, kv.shape, 1)
        rotated = kv * tables_ref[0] + rotate_lanes(kv, 1.0) * tables_ref[1]
        kvr_ref[...] = jnp.where(lane < HEAD_DIM, rotated, kv).astype(BF16)

        def attend_pair(pair, unused):
            at = pl.ds(pl.multiple_of(pair * 128, 128), 128)
            q = qkv_proj_ref[:, at]
            qr = (q * tables_ref[0] + rotate_lanes(q, 1.0) * tables_ref[1]).astype(BF16)
            qr_ref[:, at] = qr
            low = (qr * SCALE).astype(BF16)
            for start in range(0, total_len, length):
                stop = start + length
                outs = []
                for head in range(2):
                    queries = low[start:stop, head * HEAD_DIM : (head + 1) * HEAD_DIM]
                    scores = product_cols(kvr_ref[:stop, :HEAD_DIM], queries)
                    scores = scores + bias_ref[:stop, start:stop].astype(F32)
                    top = jnp.max(scores, axis=0, keepdims=True)
                    grown = jnp.exp(scores - top)
                    total = jnp.sum(grown, axis=0, keepdims=True)
                    probs = (grown * (1.0 / total)).astype(BF16)
                    lse_ref[pair, head : head + 1, start:stop] = top + jnp.log(total)
                    outs.append(product_rows(probs, kvr_ref[:stop, HEAD_DIM:]))
                headst_ref[at, start:stop] = jnp.transpose(
                    jnp.concatenate(outs, axis=1).astype(BF16)
                )
            return unused

        wg.relay(1)
        lax.fori_loop(0, pairs, attend_pair, 0)
        wg.relay(2)

        keep(headst_ref, headst_out)
        keep(qr_ref, qr_out)
        keep(kvr_ref, kvr_out)

        own_out.wait()
        wo.finish()
        keep(wo_ref, wo_out)
        out_weights = wo_ref[...].reshape(n_batch * wo_ref.shape[1], width)

        def out_part(j):
            at = pl.ds(pl.multiple_of(j * length, length), length)
            return product_rows(headst_ref[:, at], out_weights)

        row_sum = RowSum(wires, place, part_ref, core_in_ref, far_in_ref)
        row_sum.compute(out_part)
        wg.relay(3)

        def flip_rows(i, unused):
            at = pl.ds(pl.multiple_of(i * length, length), length)
            n1t_ref[:, at] = jnp.transpose(n1_ref[at, :])
            return unused

        lax.fori_loop(0, n_seq, flip_rows, 0)
        keep(n1t_ref, n1t_out)
        wu.relay(1)
        wd1.start_z()
        wd2.start_z()
        wd2.cross()
        row_sum.finish(residual_ref, [x_all_ref.at[s]])
        keep(residual_ref, residual_out)

        def norm_own(i, unused):
            at = pl.ds(pl.multiple_of(i * 32, 32), 32)
            total = residual_ref[at, :]
            normed = (total * rms_scale(total) * gains_ref[1:2, :]).astype(BF16)
            n2_ref[s, at, :] = normed
            return unused

        lax.fori_loop(0, length // 32, norm_own, 0)
        row_sum.sent()

    pl.run_scoped(
        attention,
        pltpu.VMEM((total_len, width), BF16),
        pltpu.VMEM((total_len, wqkv_ref.shape[3]), F32),
        pltpu.VMEM((n_seq, length, width), BF16),
    )
    n2 = over_seq(blocks(n2_ref), lambda: n2_ref.at[s])
    n2.start()
    wu.relay(2)
    wd1.start_x()
    for k in range(1, ny):
        n2.pass_on(k)
        gb_all.pass_on(k)
    wu.relay(3)

    def feed_forward(weight_ref, gate_buf, up_buf, hidden_ref, gb_buf, grad_buf):
        n2.finish()
        for j in range(n_seq):
            n2t_ref[:, j * length : (j + 1) * length] = jnp.transpose(n2_ref[j])
        keep(n2t_ref, n2t_out)
        wd1.relay(1)
        wd1.relay(2)
        wg.finish()
        copies.start(wg_ref, weight_ref).wait()
        weights = (width, ff)

        def gate_rows(j, unused):
            at = pl.ds(pl.multiple_of(j * length, length), length)
            gate_buf[at, :] = product(n2_ref[j], weight_ref[...].reshape(weights))
            return unused

        lax.fori_loop(0, n_seq, gate_rows, 0)
        outs = [copies.start(gate_buf, gate_proj_ref)]
        wd1.relay(3)
        wd2.relay(1)
        own_gb.wait()
        gb_all.finish()
        gb_in = copies.start(gb_all_ref, gb_buf)
        wu.finish()
        copies.start(wu_ref, weight_ref).wait()
        up_out = Rotating(copies)

        def up_copy(j):
            at = pl.ds(pl.multiple_of(j * length, length), length)
            return up_out.copy(j, up_buf.at[j % 2], up_proj_ref.at[at])

        def up_rows(j, unused):
            at = pl.ds(pl.multiple_of(j * length, length), length)

            @pl.when(j >= 2)
            def _():
                up_copy(j - 2).wait()

            up = product(n2_ref[j], weight_ref[...].reshape(weights))
            up_buf[j % 2] = up
            up_copy(j).start()
            gate = gate_buf[at, :]
            hidden_ref[at, :] = (gate * jax.nn.sigmoid(gate) * up).astype(BF16)
            return unused

        lax.fori_loop(0, n_seq, up_rows, 0)
        outs.append(copies.start(hidden_ref, hidden_out_ref))
        gb_in.wait()
        wd2.relay(2)
        grads = gb_buf[...].reshape(total_len, width)
        grad_out = Rotating(copies)

        def grad_copy(i):
            at = pl.ds(pl.multiple_of(i * 256, 256), 256)
            return grad_out.copy(i, grad_buf.at[i % 2], grad_down_ref.at[at])

        def grad_rows(i, unused):
            at = pl.ds(pl.multiple_of(i * 256, 256), 256)

            @pl.when(i >= 2)
            def _():
                grad_copy(i - 2).wait()

            grad_buf[i % 2] = product_rows(hidden_ref[:, at], grads).astype(BF16)
            grad_copy(i).start()
            return unused

        whole = ff // 256
        lax.fori_loop(0, whole, grad_rows, 0)
        up_copy(n_seq - 2).wait()
        up_copy(n_seq - 1).wait()
        grad_copy(whole - 2).wait()
        grad_copy(whole - 1).wait()
        rest = ff - whole * 256
        if rest:
            grad_buf[0, :rest] = product_rows(hidden_ref[:, whole * 256 :], grads).astype(BF16)
            outs.append(
                copies.start(grad_buf.at[0, :rest], grad_down_ref.at[pl.ds(whole * 256, rest)])
            )
        for copy in outs:
            copy.wait()

    pl.run_scoped(
        feed_forward,
        pltpu.VMEM(wg_ref.shape, BF16),
        pltpu.VMEM((total_len, ff), F32),
        pltpu.VMEM((2, length, ff), F32),
        pltpu.VMEM((total_len, ff), BF16),
        pltpu.VMEM((n_seq, length, width), BF16),
        pltpu.VMEM((2, 256, width), BF16),
    )
    wd2.relay(3)
    wd1.finish()
    wd2.finish()
    own_down.wait()
    for copy in late:
        copy.wait()
    wires.close()


def shape_of(dims, kind):
    return jax.ShapeDtypeStruct(dims, kind)


def front(sizes, x, gb, table, gain, qkv, w_out, gate, up, down):
    ny, nc, nz, nx = sizes
    n_seq, n_batch = ny * nc, nz * nx
    length, width = x.shape
    total_len = n_seq * length
    pairs = qkv.shape[2] // 128 - 1
    rows = w_out.shape[0]
    ff = gate.shape[2]
    held = [
        ((n_seq, n_batch, rows, qkv.shape[2]), BF16),
        ((n_batch, rows, width), BF16),
        ((width, total_len), BF16),
        ((width, total_len), BF16),
        ((length, width), F32),
        ((pairs * 128, total_len), BF16),
        ((total_len, pairs * 128), BF16),
        ((total_len, 128), BF16),
        ((2, total_len, 128), F32),
        ((total_len, total_len), BF16),
    ]
    kept = [(HBM, shape_of(*item)) for item in held]
    results = kept[:2]
    results += [
        (HBM, shape_of((n_seq, n_batch, rows, ff), BF16)),
        (HBM, shape_of((n_seq, n_batch, rows, ff), BF16)),
        (HBM, shape_of((n_batch,) + down.shape, BF16)),
        (HBM, shape_of((n_seq, length, width), BF16)),
    ]
    results += kept[2:8]
    results += [(VMEM, shape_of((pairs, 2, total_len), F32))]
    results += kept[8:9]
    results += [(VMEM, shape_of((2, width), F32))]
    results += kept[9:]
    results += [
        (HBM, shape_of((total_len, ff), F32)),
        (HBM, shape_of((total_len, ff), F32)),
        (HBM, shape_of((ff, width), BF16)),
        (HBM, shape_of((total_len, ff), BF16)),
    ]
    seq_copies = ny - 1 + (nc - 1) * ny
    wires = 4 * (n_seq - 1) + 5 * seq_copies + 7 * 16
    return pl.pallas_call(
        functools.partial(front_kernel, sizes, pairs),
        in_specs=[HBM] * 9,
        out_specs=[spec for spec, unused in results],
        out_shape=[kind for unused, kind in results],
        scratch_shapes=[pltpu.VMEM(*item) for item in held]
        + [
            pltpu.VMEM((n_seq, length, width), BF16),
            pltpu.VMEM((n_seq, length, 128), F32),
            pltpu.VMEM((n_seq, n_batch, 8, 128), F32),
            pltpu.VMEM((ny, length, width), BF16),
            pltpu.VMEM((length, width), BF16),
            pltpu.VMEM((length, width), BF16),
            pltpu.VMEM((n_seq, length, width), BF16),
            pltpu.VMEM(down.shape, BF16),
            pltpu.VMEM((2, rows, ff), BF16),
            pltpu.SemaphoreType.DMA((wires,)),
            pltpu.SemaphoreType.DMA((wires,)),
            pltpu.SemaphoreType.DMA((40,)),
        ],
        compiler_params=pltpu.CompilerParams(
            collective_id=0, has_side_effects=True, vmem_limit_bytes=VMEM_BYTES
        ),
        cost_estimate=pl.CostEstimate(
            flops=2 * total_len * width * (qkv.shape[2] + rows * n_batch + 3 * ff),
            bytes_accessed=100 * 1024 * 1024,
            transcendentals=pairs * total_len * total_len,
        ),
    )(x, gb, table, gain, qkv, w_out, gate, up, down)


class Reduce:
    def __init__(self, wires, place, copies, to_z, from_x, from_z, stage):
        self.wires, self.place, self.copies = wires, place, copies
        self.to_z, self.from_x, self.from_z, self.stage = to_z, from_x, from_z, stage
        self.x_tickets, self.z_tickets = {}, {}

    def send(self, k, chunk):
        place = self.place
        self.x_tickets[k] = self.wires.push(
            lambda: chunk(place.z_at(k)),
            lambda: self.from_x.at[place.z_at(k)],
            lambda: (place.s, place.batch_at(0, 1)),
        )

    def add(self, k):
        place = self.place
        zz = place.z_at(k)
        self.wires.wait(self.x_tickets[k], self.from_x.at[zz])
        self.copies.start(self.from_x.at[zz], self.stage).wait()
        add_up(self.to_z.at[zz], [self.to_z.at[zz], self.stage])
        if k:
            self.z_tickets[k] = self.wires.push(
                lambda: self.to_z.at[place.z_at(k)],
                lambda: self.from_z.at[k - 1],
                lambda: (place.s, place.batch_at(k, 0)),
            )

    def finish(self, target=None):
        mine = self.to_z.at[self.place.z]
        nz = self.place.nz

        def body(stages):
            loads = []
            for k in range(1, nz):
                self.wires.wait(self.z_tickets[k], self.from_z.at[k - 1])
                loads.append(self.copies.start(self.from_z.at[k - 1], stages.at[k - 1]))
            for load in loads:
                load.wait()
            add_up(
                mine if target is None else target,
                [mine] + [stages.at[k] for k in range(nz - 1)],
            )

        pl.run_scoped(body, pltpu.VMEM((nz - 1,) + self.stage.shape, BF16))
        return mine


def norm_back_rows(grad_ref, input_ref, gain, base_ref, target_ref, low_ref):
    rows = 32

    def body(i, unused):
        at = pl.ds(pl.multiple_of(i * rows, rows), rows)
        inputs = input_ref[at, :].astype(F32)
        back = norm_back(grad_ref[at, :], inputs, rms_scale(inputs), gain)
        total = base_ref[at, :].astype(F32) + back
        if target_ref is not None:
            target_ref[at, :] = total
        low_ref[at, :] = total.astype(BF16)
        return unused

    lax.fori_loop(0, grad_ref.shape[0] // rows, body, 0)


def back_kernel(
    sizes,
    pairs,
    gd_ref,
    hidden_ref,
    wd_ref,
    wg_ref,
    wu_ref,
    gate_ref,
    up_ref,
    gb_ref,
    n1t_ref,
    n2t_ref,
    headst_ref,
    residual_ref,
    qr_ref,
    kvr_ref,
    tables_ref,
    bias_ref,
    wqkv_ref,
    wo_ref,
    x_ref,
    lse_ref,
    gains_ref,
    mixed_out,
    tokens_out,
    down_out,
    out_out,
    gate_own,
    up_own,
    qkv_own,
    x_down,
    x_gate,
    x_up,
    x_out,
    x_qkv,
    z_down,
    z_gate,
    z_up,
    z_out,
    z_qkv,
    send_gate,
    send_up,
    da_all_ref,
    mixed_ref,
    tokens_ref,
    down_own,
    out_own,
    s_down,
    s_gate,
    s_up,
    s_out,
    s_qkv,
    send_out,
    send_qkv,
    stage_down,
    stage_gate,
    stage_out,
    stage_qkv,
    core_in_ref,
    far_in_ref,
    mixed_core_in,
    mixed_far_in,
    da_own_ref,
    total_ref,
    send_sems,
    recv_sems,
    copy_sems,
):
    place = Place(sizes)
    ny, nc, nz, nx = sizes
    s, b = place.s, place.b
    n_seq, n_batch = ny * nc, nz * nx
    length, width = x_ref.shape
    total_len = n_seq * length
    ff = wg_ref.shape[3]
    rows = wo_ref.shape[1]
    wires = Wires(send_sems, recv_sems)
    copies = Copies(copy_sems)
    down = Reduce(wires, place, copies, s_down, x_down, z_down, stage_down)
    gate = Reduce(wires, place, copies, s_gate, x_gate, z_gate, stage_gate)
    up = Reduce(wires, place, copies, s_up, x_up, z_up, stage_gate)
    out = Reduce(wires, place, copies, s_out, x_out, z_out, stage_out)
    qkv = Reduce(wires, place, copies, s_qkv, x_qkv, z_qkv, stage_qkv)
    order = list(range(1, nz)) + [0]
    row_others = [(dy, dc) for dy in range(ny) for dc in range(nc) if dy or dc]

    late = []
    place.enter()
    own_down = []
    for k in order:
        down.send(k, lambda zz: gd_ref.at[zz * nx + (place.x + 1) % nx])
    for k in order:
        own_down.append(copies.start(gd_ref.at[place.batch_at(k, 0)], s_down.at[place.z_at(k)]))

    def weight_rows(flipped_ref, grads, k, dx):
        j = place.batch_at(k, dx)
        pieces = []
        for i in range(n_seq):
            start = pl.multiple_of((i * n_batch + j) * rows, rows)
            pieces.append(flipped_ref[pl.ds(start, rows), :])
        value = product(jnp.concatenate(pieces, axis=0), grads)
        return value.astype(BF16).reshape(n_seq, rows, grads.shape[1])

    def feed_forward(dgate_ref, dup_ref, part_ref):
        row_sum = RowSum(wires, place, part_ref, core_in_ref, far_in_ref)

        def activations(weight1, gate_buf, up_buf, gb_buf):
            load1 = copies.start(wd_ref, weight1)

            base = copies.count
            copies.count += 3

            def load_gb(j):
                return pltpu.make_async_copy(gb_ref.at[j], gb_buf, copy_sems.at[base])

            def load_gate(j):
                at = pl.ds(pl.multiple_of(j * length, length), length)
                return (
                    pltpu.make_async_copy(gate_ref.at[at], gate_buf, copy_sems.at[base + 1]),
                    pltpu.make_async_copy(up_ref.at[at], up_buf, copy_sems.at[base + 2]),
                )

            load_gb(0).start()
            for copy in load_gate(0):
                copy.start()
            load1.wait()

            def rows_back(j, unused):
                load_gb(j).wait()
                grad_hidden = product_cols(gb_buf[...], weight1[...].reshape(ff, width))

                @pl.when(j + 1 < n_seq)
                def _():
                    load_gb(j + 1).start()

                for copy in load_gate(j):
                    copy.wait()
                gate_part, up_part = gate_buf[...], up_buf[...]
                sigma = jax.nn.sigmoid(gate_part)
                activated = gate_part * sigma
                dgate_ref[j] = (
                    grad_hidden * up_part * sigma * (1.0 + gate_part * (1.0 - sigma))
                ).astype(BF16)
                dup_ref[j] = (grad_hidden * activated).astype(BF16)

                @pl.when(j + 1 < n_seq)
                def _():
                    for copy in load_gate(j + 1):
                        copy.start()

                return unused

            lax.fori_loop(0, n_seq, rows_back, 0)
            for copy in own_down:
                copy.wait()

        pl.run_scoped(
            activations,
            pltpu.VMEM(wd_ref.shape, BF16),
            pltpu.VMEM((length, ff), F32),
            pltpu.VMEM((length, ff), F32),
            pltpu.VMEM((length, width), BF16),
        )

        def inputs(weight1, weight2):
            loads = [copies.start(wg_ref, weight1), copies.start(wu_ref, weight2)]
            down.add(1)
            for load in loads:
                load.wait()

            def input_part(j):
                return product_cols(
                    dgate_ref[j], weight1[...].reshape(width, ff)
                ) + product_cols(dup_ref[j], weight2[...].reshape(width, ff))

            row_sum.compute(input_part)
            down.add(2)

        pl.run_scoped(inputs, pltpu.VMEM(wg_ref.shape, BF16), pltpu.VMEM(wg_ref.shape, BF16))

        def weights(flipped, staging, residual_buf, gb_buf):
            loads = [
                copies.start(n2t_ref, flipped),
                copies.start(residual_ref, residual_buf),
                copies.start(gb_ref.at[s], gb_buf),
            ]
            loads[0].wait()

            def rows_of(reduce, grads_ref):
                def body(i, unused):
                    k = (i + 1) % nz
                    zz = place.z_at(k)
                    grads = grads_ref[...].reshape(total_len, ff)
                    staging[zz] = weight_rows(flipped, grads, k, 1)
                    reduce.to_z[zz] = weight_rows(flipped, grads, k, 0)
                    return unused

                lax.fori_loop(0, nz, body, 0)

            def send_off(reduce, send_ref):
                copies.start(staging, send_ref).wait()
                for k in order:
                    reduce.send(k, lambda zz: send_ref.at[zz])

            rows_of(gate, dgate_ref)
            send_off(gate, send_gate)
            for copy in loads[1:]:
                copy.wait()
            row_sum.finish(total_ref)
            norm_back_rows(
                total_ref, residual_buf, gains_ref[1:2, :], gb_buf, total_ref, da_own_ref
            )
            da.start()
            down.add(3)
            rows_of(up, dup_ref)
            send_off(up, send_up)
            down.add(0)
            row_sum.sent()

        pl.run_scoped(
            weights,
            pltpu.VMEM(n2t_ref.shape, BF16),
            pltpu.VMEM((nz, n_seq, rows, ff), BF16),
            pltpu.VMEM((length, width), F32),
            pltpu.VMEM((length, width), BF16),
        )

    own_da = []
    da = Gather(
        wires,
        lambda j: da_all_ref.at[j],
        lambda: da_own_ref,
        ny,
        nc,
        place.seq_at,
        lambda j: (j, b),
    )
    pl.run_scoped(
        feed_forward,
        pltpu.VMEM((n_seq, length, ff), BF16),
        pltpu.VMEM((n_seq, length, ff), BF16),
        pltpu.VMEM((n_seq, length, width), BF16),
    )
    own_da.append(copies.start(da_own_ref, da_all_ref.at[s]))
    for k in range(1, ny):
        da.pass_on(k)

    def attention(
        da_buf,
        wo_buf,
        wqkv_buf,
        qr_buf,
        headst_buf,
        do_buf,
        kvr_buf,
        tables_buf,
        bias_buf,
        dqkv_buf,
        n1t_buf,
        dq_buf,
        dk_buf,
        dv_buf,
        part_ref,
        x_buf,
    ):
        loads = [
            copies.start(source, target)
            for source, target in [
                (wo_ref, wo_buf),
                (headst_ref, headst_buf),
                (qr_ref, qr_buf),
                (kvr_ref, kvr_buf),
                (tables_ref, tables_buf),
                (bias_ref, bias_buf),
                (n1t_ref, n1t_buf),
                (wqkv_ref, wqkv_buf),
                (x_ref, x_buf),
            ]
        ]
        gate.add(1)
        da.finish()
        own_da[0].wait()
        copies.start(da_all_ref, da_buf).wait()
        for load in loads:
            load.wait()
        out_weights = wo_buf[...].reshape(n_batch * rows, width)

        def heads_back(j, unused):
            at = pl.ds(pl.multiple_of(j * length, length), length)
            do_buf[at, :] = product_cols(da_buf[j], out_weights).astype(BF16)
            return unused

        lax.fori_loop(0, n_seq, heads_back, 0)
        branch = da_buf[...].reshape(total_len, width)

        def out_rows(dx):
            pieces = []
            for zz in range(nz):
                start = pl.multiple_of((zz * nx + (place.x + dx) % nx) * rows, rows)
                pieces.append(headst_buf[pl.ds(start, rows), :])
            value = product(jnp.concatenate(pieces, axis=0), branch)
            return value.astype(BF16).reshape(nz, rows, width)

        send_out[...] = out_rows(1)
        for k in order:
            out.send(k, lambda zz: send_out.at[zz])
        s_out[...] = out_rows(0)
        dk_buf[...] = jnp.zeros_like(dk_buf)
        dv_buf[...] = jnp.zeros_like(dv_buf)

        def pair_back(pair, unused):
            at = pl.ds(pl.multiple_of(pair * 128, 128), 128)
            low = (qr_buf[:, at] * SCALE).astype(BF16)
            grads_pair = do_buf[:, at]
            for start in range(0, total_len, length):
                stop = start + length
                outs = []
                for head in range(2):
                    lanes = slice(head * HEAD_DIM, (head + 1) * HEAD_DIM)
                    queries = low[start:stop, lanes]
                    grads = grads_pair[start:stop, lanes]
                    keys = kvr_buf[:stop, :HEAD_DIM]
                    values = kvr_buf[:stop, HEAD_DIM:]
                    scores = product_cols(keys, queries)
                    scores = scores + bias_buf[:stop, start:stop].astype(F32)
                    probs = jnp.exp(scores - lse_ref[pair, head : head + 1, start:stop])
                    dprobs = product_cols(values, grads)
                    delta = jnp.sum(probs * dprobs, axis=0, keepdims=True)
                    dscores = (probs * (dprobs - delta)).astype(BF16)
                    dv_buf[:stop, :] += product(probs.astype(BF16), grads)
                    dk_buf[:stop, :] += product(dscores, queries)
                    outs.append(product_rows(dscores, keys) * SCALE)
                dq_buf[start:stop, :] = jnp.concatenate(outs, axis=1)
            dq = dq_buf[...]
            turned = rotate_lanes(dq * tables_buf[1], -1.0)
            dqkv_buf[:, at] = (dq * tables_buf[0] + turned).astype(BF16)
            return unused

        gate.add(2)
        lax.fori_loop(0, pairs, pair_back, 0)
        gate.add(3)
        gate.add(0)
        grads = jnp.concatenate([dk_buf[...], dv_buf[...]], axis=1)
        back = grads * tables_buf[0] + rotate_lanes(grads * tables_buf[1], -1.0)
        lane = lax.broadcasted_iota(jnp.int32, grads.shape, 1)
        dqkv_buf[:, pairs * 128 :] = jnp.where(lane < HEAD_DIM, back, grads).astype(BF16)

        row_sum = RowSum(wires, place, part_ref, core_in_ref, far_in_ref)
        in_weights = wqkv_buf[...].reshape(width, wqkv_ref.shape[3])

        def input_part(j):
            at = pl.ds(pl.multiple_of(j * length, length), length)
            return product_cols(dqkv_buf[at, :], in_weights)

        row_sum.compute(input_part)

        def qkv_rows(zz, unused):
            k = (zz - place.z + nz) % nz
            send_qkv[zz] = weight_rows(n1t_buf, dqkv_buf[...], k, 1)
            s_qkv[zz] = weight_rows(n1t_buf, dqkv_buf[...], k, 0)
            return unused

        lax.fori_loop(0, nz, qkv_rows, 0)
        for k in order:
            qkv.send(k, lambda zz: send_qkv.at[zz])
        up.add(1)

        def last(grad_ref):
            row_sum.finish(grad_ref)
            norm_back_rows(grad_ref, x_buf, gains_ref[0:1, :], total_ref, None, tokens_ref)

        pl.run_scoped(last, pltpu.VMEM((length, width), F32))
        late.append(copies.start(tokens_ref, tokens_out))
        row_sum.sent()

    pl.run_scoped(
        attention,
        pltpu.VMEM((n_seq, length, width), BF16),
        pltpu.VMEM(wo_ref.shape, BF16),
        pltpu.VMEM(wqkv_ref.shape, BF16),
        pltpu.VMEM(qr_ref.shape, BF16),
        pltpu.VMEM(headst_ref.shape, BF16),
        pltpu.VMEM(qr_ref.shape, BF16),
        pltpu.VMEM(kvr_ref.shape, BF16),
        pltpu.VMEM(tables_ref.shape, F32),
        pltpu.VMEM(bias_ref.shape, BF16),
        pltpu.VMEM((total_len, (pairs + 1) * 128), BF16),
        pltpu.VMEM(n1t_ref.shape, BF16),
        pltpu.VMEM((total_len, 128), F32),
        pltpu.VMEM((total_len, HEAD_DIM), F32),
        pltpu.VMEM((total_len, HEAD_DIM), F32),
        pltpu.VMEM((n_seq, length, width), BF16),
        pltpu.VMEM((length, width), BF16),
    )

    def layer_out(weight_buf, hidden_buf, part_ref, mixed_total):
        loads = [
            copies.start(wd_ref, weight_buf),
            copies.start(hidden_ref, hidden_buf),
            copies.start(residual_ref, mixed_total),
        ]
        up.add(2)
        for load in loads:
            load.wait()

        def mixed_part(j):
            at = pl.ds(pl.multiple_of(j * length, length), length)
            return product(hidden_buf[at, :], weight_buf[...].reshape(ff, width))

        row_sum = RowSum(wires, place, part_ref, mixed_core_in, mixed_far_in)
        row_sum.compute(mixed_part)
        up.add(3)
        down.finish(down_own)
        late.append(copies.start(down_own, down_out))
        row_sum.finish(mixed_ref, [mixed_total])
        late.append(copies.start(mixed_ref, mixed_out))
        row_sum.sent()

    pl.run_scoped(
        layer_out,
        pltpu.VMEM(wd_ref.shape, BF16),
        pltpu.VMEM(hidden_ref.shape, BF16),
        pltpu.VMEM((n_seq, length, width), BF16),
        pltpu.VMEM((length, width), F32),
    )

    exchanges = []

    def exchange(reduce, target):
        mine = reduce.finish()
        copy = copies.start(mine.at[s], target.at[s])
        tickets = {}
        for away in row_others:
            tickets[away] = wires.push(
                lambda away=away: mine.at[place.seq_at(*away)],
                lambda: target.at[s],
                lambda away=away: (place.seq_at(*away), b),
            )
        exchanges.append((copy, target, tickets))

    exchange(gate, gate_own)
    up.add(0)
    for k in order:
        out.add(k)
    exchange(up, up_own)
    for k in order:
        qkv.add(k)
    out.finish(out_own)
    late.append(copies.start(out_own, out_out))
    exchange(qkv, qkv_own)
    for copy, target, tickets in exchanges:
        copy.wait()
        for (dy, dc), ticket in tickets.items():
            wires.wait(ticket, target.at[place.seq_at(-dy, -dc)])
    for copy in late:
        copy.wait()
    wires.close()


def back(sizes, gd, hidden, wd, wg, wu, gate, up, gb, n1t, n2t, headst, residual, qr, kvr, tables, bias, wqkv, wo, x, lse, gains):
    ny, nc, nz, nx = sizes
    n_seq, n_batch = ny * nc, nz * nx
    length, width = x.shape
    ff = wg.shape[3]
    rows = wo.shape[1]
    pairs = qr.shape[1] // 128
    chunk_down = gd.shape[1:]
    chunk_gate = (n_seq, rows, ff)
    chunk_out = (rows, width)
    chunk_qkv = (n_seq, rows, wqkv.shape[3])
    chunks = [chunk_down, chunk_gate, chunk_gate, chunk_out, chunk_qkv]
    results = [
        (HBM, shape_of((length, width), BF16)),
        (HBM, shape_of((length, width), BF16)),
        (HBM, shape_of(chunk_down, F32)),
        (HBM, shape_of(chunk_out, F32)),
        (HBM, shape_of(chunk_gate, BF16)),
        (HBM, shape_of(chunk_gate, BF16)),
        (HBM, shape_of(chunk_qkv, BF16)),
    ]
    results += [(HBM, shape_of((nz,) + chunk, BF16)) for chunk in chunks]
    results += [(HBM, shape_of((nz - 1,) + chunk, BF16)) for chunk in chunks]
    results += [(HBM, shape_of((nz,) + chunk_gate, BF16))] * 2
    results += [(HBM, shape_of((n_seq, length, width), BF16))]
    wires = 5 * (2 * nz - 1) + 3 * 3 + 3 + 3 * (n_seq - 1)
    row = pltpu.VMEM((length, width), BF16)
    return pl.pallas_call(
        functools.partial(back_kernel, sizes, pairs),
        in_specs=[HBM] * 19 + [VMEM] * 2,
        out_specs=[spec for spec, unused in results],
        out_shape=[kind for unused, kind in results],
        scratch_shapes=[row, row, pltpu.VMEM(chunk_down, F32), pltpu.VMEM(chunk_out, F32)]
        + [pltpu.VMEM((nz,) + chunk, BF16) for chunk in chunks]
        + [
            pltpu.VMEM((nz,) + chunk_out, BF16),
            pltpu.VMEM((nz,) + chunk_qkv, BF16),
            pltpu.VMEM(chunk_down, BF16),
            pltpu.VMEM(chunk_gate, BF16),
            pltpu.VMEM(chunk_out, BF16),
            pltpu.VMEM(chunk_qkv, BF16),
            pltpu.VMEM((ny, length, width), BF16),
            row,
            pltpu.VMEM((ny, length, width), BF16),
            row,
            row,
            pltpu.VMEM((length, width), F32),
            pltpu.SemaphoreType.DMA((wires,)),
            pltpu.SemaphoreType.DMA((wires,)),
            pltpu.SemaphoreType.DMA((100,)),
        ],
        compiler_params=pltpu.CompilerParams(
            collective_id=1, has_side_effects=True, vmem_limit_bytes=VMEM_BYTES
        ),
        cost_estimate=pl.CostEstimate(
            flops=12 * n_seq * length * width * ff,
            bytes_accessed=100 * 1024 * 1024,
            transcendentals=pairs * (n_seq * length) ** 2,
        ),
    )(gd, hidden, wd, wg, wu, gate, up, gb, n1t, n2t, headst, residual, qr, kvr, tables, bias, wqkv, wo, x, lse, gains)


def by_permutes(
    tokens,
    cotangent,
    selection,
    segments,
    positions,
    gain_attn,
    w_query,
    w_key,
    w_value,
    w_out,
    gain_mlp,
    w_gate,
    w_up,
    w_down,
):
    seq = Axis("seq", 2)
    batch = Axis("batch", lax.axis_size("batch") // 4)
    n_seq, n_batch = seq.size, batch.size
    length, width = tokens.shape[1], tokens.shape[2]
    total_len = length * n_seq
    rows = w_query.shape[0]
    ff = w_gate.shape[1]
    q_cols = w_query.shape[1] // n_seq
    sharers = n_seq // KV_HEADS

    query_parts = w_query.reshape(rows, n_seq, q_cols)
    key_parts = jnp.repeat(w_key.reshape(rows, KV_HEADS, HEAD_DIM), sharers, axis=1)
    value_parts = jnp.repeat(w_value.reshape(rows, KV_HEADS, HEAD_DIM), sharers, axis=1)
    qkv_parts = jnp.concatenate([query_parts, key_parts, value_parts], axis=2).transpose(1, 0, 2)

    def spread(parts):
        mine = seq.exchange(parts)
        return batch.gather(mine, 1).reshape(n_seq * n_batch * rows, parts.shape[2])

    def collect(grad):
        parts = grad.astype(BF16).reshape(n_seq, n_batch, rows, grad.shape[1])
        return seq.exchange(batch.scatter_sum(parts, 1).astype(BF16)).astype(F32)

    def by_columns(weight):
        return weight.reshape(rows, n_seq, weight.shape[1] // n_seq).transpose(1, 0, 2)

    places = seq.gather(jnp.stack([segments[0], positions[0]]), 1)
    seg_all = places[0].reshape(total_len)
    pos_all = places[1].reshape(total_len)
    gains = batch.gather(seq.gather(jnp.stack([gain_attn, gain_mlp]), 1), 2)
    gain_one = gains[0].reshape(1, width).astype(F32)
    gain_two = gains[1].reshape(1, width).astype(F32)
    x_all = seq.gather(tokens[0], 0).reshape(total_len, width).astype(F32)
    w_qkv = spread(qkv_parts)
    wo = batch.gather(w_out, 0).reshape(n_batch * rows, width)
    wg = spread(by_columns(w_gate))
    wu = spread(by_columns(w_up))
    wd = batch.gather(w_down, 0).reshape(n_batch * w_down.shape[0], width)

    grad_out_row = cotangent[0].astype(F32) * selection[0].astype(F32)[:, None]
    grad_low = seq.gather(grad_out_row.astype(BF16), 0).reshape(total_len, width)

    row_input = tokens[0].astype(F32)
    inv_attn = rms_scale(row_input)
    normed1 = (x_all * rms_scale(x_all) * gain_one).astype(BF16)
    qkv = product(normed1, w_qkv)
    frequency = 10000.0 ** (-(jnp.arange(HALF, dtype=F32) * 2.0 / HEAD_DIM))
    angles = pos_all.astype(F32)[:, None] * jnp.tile(frequency, 4)[None, :]
    cosine, sine = jnp.cos(angles), jnp.sin(angles)
    seg_row, seg_col = seg_all[None, :], seg_all[:, None]
    heads_out, query_rot, kv_rot, lse = attend(qkv, cosine, sine, seg_row, seg_col)
    attn_part = product(heads_out, wo).astype(BF16).reshape(n_seq, length, width)
    residual = row_input + seq.scatter_sum(attn_part, 0)

    inv_mlp = rms_scale(residual)
    normed2_own = (residual * inv_mlp * gain_two).astype(BF16)
    normed2 = seq.gather(normed2_own, 0).reshape(total_len, width)
    gate_proj = product(normed2, wg)
    up_proj = product(normed2, wu)
    sigma = jax.nn.sigmoid(gate_proj)
    activated = gate_proj * sigma
    hidden = (activated * up_proj).astype(BF16)
    mixed_part = product(hidden, wd).astype(BF16).reshape(n_seq, length, width)
    mixed = (residual + seq.scatter_sum(mixed_part, 0)).astype(BF16)[None]

    grad_down = product_rows(hidden, grad_low)
    grad_hidden = product_cols(grad_low, wd)
    grad_gate_act = (
        grad_hidden * up_proj * sigma * (1.0 + gate_proj * (1.0 - sigma))
    ).astype(BF16)
    grad_up_act = (grad_hidden * activated).astype(BF16)
    grad_gate = product_rows(normed2, grad_gate_act)
    grad_up = product_rows(normed2, grad_up_act)
    normed_part = product_cols(grad_gate_act, wg) + product_cols(grad_up_act, wu)
    normed_terms = seq.scatter_sum(normed_part.astype(BF16).reshape(n_seq, length, width), 0)
    grad_resid = grad_out_row + norm_back(normed_terms, residual, inv_mlp, gain_two)

    down_own = batch.scatter_sum(
        grad_down.astype(BF16).reshape(n_batch, w_down.shape[0], width), 0
    )
    gate_own = collect(grad_gate).transpose(1, 0, 2).reshape(rows, ff)
    up_own = collect(grad_up).transpose(1, 0, 2).reshape(rows, ff)

    grad_branch = seq.gather(grad_resid.astype(BF16), 0).reshape(total_len, width)
    grad_wout = product_rows(heads_out, grad_branch)
    grad_heads = product_cols(grad_branch, wo).astype(BF16)
    grad_qkv_act = attend_back(
        query_rot, kv_rot, grad_heads, lse, cosine, sine, seg_row, seg_col
    )
    grad_wqkv = product_rows(normed1, grad_qkv_act)
    input_part = product_cols(grad_qkv_act, w_qkv).astype(BF16).reshape(n_seq, length, width)
    grad_normed1 = seq.scatter_sum(input_part, 0)
    tokens_grad = (
        grad_resid + norm_back(grad_normed1, row_input, inv_attn, gain_one)
    ).astype(BF16)[None]
    out_own = batch.scatter_sum(grad_wout.astype(BF16).reshape(n_batch, rows, width), 0)
    qkv_own = collect(grad_wqkv)
    query_own = qkv_own[:, :, :q_cols].transpose(1, 0, 2).reshape(rows, n_seq * q_cols)

    def shared(columns):
        heads = columns.reshape(KV_HEADS, sharers, rows, HEAD_DIM).sum(axis=1)
        return heads.transpose(1, 0, 2).reshape(rows, KV_HEADS * HEAD_DIM)

    key_own = shared(qkv_own[:, :, q_cols : q_cols + HEAD_DIM])
    value_own = shared(qkv_own[:, :, q_cols + HEAD_DIM :])

    def along(weight, grad):
        return jnp.sum(weight.astype(F32) * grad, axis=1)

    gain1_own = (
        along(w_query, query_own) + along(w_key, key_own) + along(w_value, value_own)
    ) / gain_attn.astype(F32)
    gain2_own = (along(w_gate, gate_own) + along(w_up, up_own)) / gain_mlp.astype(F32)
    return (
        mixed,
        tokens_grad,
        query_own,
        key_own,
        value_own,
        out_own,
        gate_own,
        up_own,
        down_own,
        gain1_own,
        gain2_own,
    )


def by_kernels(
    tokens,
    cotangent,
    selection,
    segments,
    positions,
    gain_attn,
    w_query,
    w_key,
    w_value,
    w_out,
    gain_mlp,
    w_gate,
    w_up,
    w_down,
):
    sizes = mesh_sizes()
    n_seq, n_batch = sizes[0] * sizes[1], sizes[2] * sizes[3]
    length, width = tokens.shape[1], tokens.shape[2]
    rows, ff = w_gate.shape
    q_cols = w_query.shape[1] // n_seq

    def by_columns(weight):
        return weight.reshape(rows, n_seq, weight.shape[1] // n_seq).transpose(1, 0, 2)

    qkv_parts = jnp.concatenate([by_columns(w) for w in (w_query, w_key, w_value)], axis=2)
    grad_low = (cotangent[0].astype(F32) * selection[0].astype(F32)[:, None]).astype(BF16)
    frequency = 10000.0 ** (-(jnp.arange(HALF, dtype=F32) * 2.0 / HEAD_DIM))
    angles = positions[0].astype(F32)[:, None] * frequency[None, :]
    documents = jnp.broadcast_to(segments[0].astype(F32)[:, None], (length, 128 - HEAD_DIM))
    table = jnp.concatenate([jnp.cos(angles), jnp.sin(angles), documents], axis=1)
    gain_tile = jnp.pad(
        jnp.stack([gain_attn, gain_mlp]).astype(F32), ((0, 6), (0, 128 - gain_attn.shape[0]))
    )
    (
        w_qkv,
        wo,
        wg,
        wu,
        wd,
        gb_all,
        n1t,
        n2t,
        residual,
        headst,
        query_rot,
        kv_rot,
        lse,
        rotary,
        gains,
        bias,
        gate_proj,
        up_proj,
        grad_down,
        hidden,
    ) = front(
        sizes,
        tokens[0],
        grad_low,
        table,
        gain_tile,
        qkv_parts,
        w_out,
        by_columns(w_gate),
        by_columns(w_up),
        w_down,
    )
    mixed, tokens_grad, down_own, out_own, gate_part, up_part, qkv_part = back(
        sizes,
        grad_down.reshape(n_batch, w_down.shape[0], width),
        hidden,
        wd,
        wg,
        wu,
        gate_proj,
        up_proj,
        gb_all,
        n1t,
        n2t,
        headst,
        residual,
        query_rot,
        kv_rot,
        rotary,
        bias,
        w_qkv,
        wo,
        tokens[0],
        lse,
        gains,
    )[:7]

    def by_rows(part):
        return part.astype(F32).transpose(1, 0, 2).reshape(rows, n_seq * part.shape[2])

    query_own = by_rows(qkv_part[:, :, :q_cols])
    key_own = by_rows(qkv_part[:, :, q_cols : q_cols + HEAD_DIM])
    value_own = by_rows(qkv_part[:, :, q_cols + HEAD_DIM :])
    gate_own, up_own = by_rows(gate_part), by_rows(up_part)

    def along(weight, grad):
        return jnp.sum(weight.astype(F32) * grad, axis=1)

    gain1_own = (
        along(w_query, query_own) + along(w_key, key_own) + along(w_value, value_own)
    ) / gain_attn.astype(F32)
    gain2_own = (along(w_gate, gate_own) + along(w_up, up_own)) / gain_mlp.astype(F32)
    return (
        mixed[None],
        tokens_grad[None],
        query_own,
        key_own,
        value_own,
        out_own,
        gate_own,
        up_own,
        down_own,
        gain1_own,
        gain2_own,
    )


def mesh_sizes():
    return (lax.axis_size("seq") // 2, 2, 4, lax.axis_size("batch") // 4)


def per_device(*args):
    fits = mesh_sizes() == (2, 2, 4, 2) and args[0].shape[1:] == (256, 2048)
    return (by_kernels if fits else by_permutes)(*args)


def solution(mesh):
    both = ("seq", "batch")
    tokens = P("batch", "seq", None)
    flags = P("batch", "seq")
    matrix = P(both, None)
    vector = P(both)
    in_specs = (
        (tokens, tokens, flags, flags, flags)
        + (vector, matrix, matrix, matrix, matrix)
        + (vector, matrix, matrix, matrix)
    )
    out_specs = (tokens, tokens) + (matrix,) * 7 + (vector, vector)
    return jax.shard_map(
        per_device, mesh=mesh, in_specs=in_specs, out_specs=out_specs, check_vma=False
    )
```

```python
import functools

import jax
import jax.numpy as jnp
from jax import lax
from jax.experimental import pallas as pl
from jax.experimental.pallas import tpu as pltpu
from jax.sharding import PartitionSpec as P

HEADS = 32
KV_HEADS = 4
HEAD_DIM = 64
HALF = HEAD_DIM // 2

EPSILON = 1e-05
MASKED_SCORE = -1e30
SCALE = HEAD_DIM ** (-0.5)
CONTRACT_ROWS = (((0,), (0,)), ((), ()))
CONTRACT_COLS = (((1,), (1,)), ((), ()))
BF16 = jnp.bfloat16
F32 = jnp.float32


def product(left, right):
    return jnp.dot(left, right, preferred_element_type=F32)


def product_rows(left, right):
    return lax.dot_general(left, right, CONTRACT_ROWS, preferred_element_type=F32)


def product_cols(left, right):
    return lax.dot_general(left, right, CONTRACT_COLS, preferred_element_type=F32)


def rms_scale(inputs):
    return lax.rsqrt(jnp.mean(inputs * inputs, axis=-1, keepdims=True) + EPSILON)


def norm_back(grad_normed, inputs, inverse, gain):
    scaled = gain * grad_normed
    cubed = inverse * inverse * inverse
    return inverse * scaled - inputs * cubed * jnp.mean(scaled * inputs, axis=-1, keepdims=True)


class Axis:
    def __init__(self, name, inner):
        self.name = name
        self.size = lax.axis_size(name)
        self.inner = inner
        self.outer = self.size // inner
        index = lax.axis_index(name)
        self.index = index
        self.o = index // inner
        self.i = index % inner

    def shift(self, value, outer_by, inner_by):
        pairs = []
        for o in range(self.outer):
            for i in range(self.inner):
                target = ((o + outer_by) % self.outer) * self.inner + (i + inner_by) % self.inner
                pairs.append((o * self.inner + i, target))
        return lax.ppermute(value, self.name, pairs)

    def before(self, outer_by, inner_by):
        o = lax.rem(self.o + self.outer - outer_by, self.outer)
        i = lax.rem(self.i + self.inner - inner_by, self.inner)
        return o * self.inner + i

    def after(self, outer_by, inner_by):
        o = lax.rem(self.o + outer_by, self.outer)
        i = lax.rem(self.i + inner_by, self.inner)
        return o * self.inner + i

    def gather(self, block, dim=0):
        shape = block.shape[:dim] + (self.size,) + block.shape[dim:]
        out = jnp.zeros(shape, block.dtype)
        for k in range(self.outer):
            got = block if k == 0 else self.shift(block, k, 0)
            for m in range(self.inner):
                piece = got if m == 0 else self.shift(got, 0, m)
                out = lax.dynamic_update_slice_in_dim(
                    out, jnp.expand_dims(piece, dim), self.before(k, m), dim
                )
        return out

    def scatter_sum(self, parts, dim=0):
        shape = parts.shape[:dim] + (self.outer, self.inner) + parts.shape[dim + 1 :]
        grid = parts.reshape(shape)

        def inner_part(i):
            return lax.squeeze(lax.dynamic_slice_in_dim(grid, i, 1, dim + 1), (dim + 1,))

        total = inner_part(self.i).astype(F32)
        for m in range(1, self.inner):
            mine = inner_part(lax.rem(self.i + m, self.inner))
            total = total + self.shift(mine, 0, m).astype(F32)
        low = total.astype(BF16)

        def outer_part(o):
            return lax.squeeze(lax.dynamic_slice_in_dim(low, o, 1, dim), (dim,))

        out = outer_part(self.o).astype(F32)
        for k in range(1, self.outer):
            out = out + self.shift(outer_part(lax.rem(self.o + k, self.outer)), k, 0).astype(F32)
        return out

    def exchange(self, parts):
        out = jnp.zeros(parts.shape, parts.dtype)
        for k in range(self.outer):
            for m in range(self.inner):
                part = lax.dynamic_slice_in_dim(parts, self.after(k, m), 1, 0)
                got = part if (k, m) == (0, 0) else self.shift(part, k, m)
                out = lax.dynamic_update_slice_in_dim(out, got, self.before(k, m), 0)
        return out


def rotate_lanes(value, sign):
    lane = lax.broadcasted_iota(jnp.int32, value.shape, 1) % HEAD_DIM
    first = lane < HALF
    width = value.shape[1]
    up = pltpu.roll(value, width - HALF, 1)
    down = pltpu.roll(value, HALF, 1)
    return jnp.where(first, -sign * up, sign * down)


def mask_bias(bias_ref, seg_row_ref, seg_col_ref, length):
    rows = 256
    for start in range(0, length, rows):
        keys = seg_col_ref[start : start + rows, :]
        queries = seg_row_ref[:, :]
        key_pos = start + lax.broadcasted_iota(jnp.int32, (rows, length), 0)
        query_pos = lax.broadcasted_iota(jnp.int32, (rows, length), 1)
        allowed = (keys == queries) & (key_pos <= query_pos)
        bias_ref[start : start + rows, :] = jnp.where(allowed, 0.0, MASKED_SCORE)


def attend_kernel(
    qblock,
    q_ref,
    kv_ref,
    cos_ref,
    sin_ref,
    seg_row_ref,
    seg_col_ref,
    o_ref,
    qr_ref,
    kvr_ref,
    lse_ref,
    bias_ref,
):
    length = q_ref.shape[0]
    cosine = cos_ref[...]
    sine = sin_ref[...]

    @pl.when(pl.program_id(0) == 0)
    def _():
        mask_bias(bias_ref, seg_row_ref, seg_col_ref, length)
        kv = kv_ref[...]
        rotated = kv * cosine + rotate_lanes(kv, 1.0) * sine
        lane = lax.broadcasted_iota(jnp.int32, kv.shape, 1)
        kvr_ref[...] = jnp.where(lane < HEAD_DIM, rotated, kv).astype(BF16)

    q = q_ref[...]
    qr_ref[...] = (q * cosine + rotate_lanes(q, 1.0) * sine).astype(BF16)
    for start in range(0, length, qblock):
        stop = start + qblock
        keys = kvr_ref[:stop, :HEAD_DIM]
        values = kvr_ref[:stop, HEAD_DIM:]
        for head in range(2):
            lanes = slice(head * HEAD_DIM, (head + 1) * HEAD_DIM)
            queries = qr_ref[start:stop, lanes] * SCALE
            scores = product_cols(keys, queries.astype(BF16)) + bias_ref[:stop, start:stop]
            top = jnp.max(scores, axis=0, keepdims=True)
            grown = jnp.exp(scores - top)
            total = jnp.sum(grown, axis=0, keepdims=True)
            probs = (grown * (1.0 / total)).astype(BF16)
            lse_ref[0, head : head + 1, start:stop] = top + jnp.log(total)
            o_ref[start:stop, lanes] = product_rows(probs, values).astype(BF16)


def attend_back_kernel(
    qblock,
    qr_ref,
    kvr_ref,
    do_ref,
    lse_ref,
    cos_ref,
    sin_ref,
    seg_row_ref,
    seg_col_ref,
    dqkv_ref,
    bias_ref,
    dq_ref,
    dk_ref,
    dv_ref,
):
    length = qr_ref.shape[0]
    cosine = cos_ref[...]
    sine = sin_ref[...]
    pair = pl.program_id(0)

    @pl.when(pair == 0)
    def _():
        mask_bias(bias_ref, seg_row_ref, seg_col_ref, length)
        dk_ref[...] = jnp.zeros_like(dk_ref)
        dv_ref[...] = jnp.zeros_like(dv_ref)

    for start in range(0, length, qblock):
        stop = start + qblock
        keys = kvr_ref[:stop, :HEAD_DIM]
        values = kvr_ref[:stop, HEAD_DIM:]
        for head in range(2):
            lanes = slice(head * HEAD_DIM, (head + 1) * HEAD_DIM)
            queries = (qr_ref[start:stop, lanes] * SCALE).astype(BF16)
            grads = do_ref[start:stop, lanes]
            scores = product_cols(keys, queries) + bias_ref[:stop, start:stop]
            probs = jnp.exp(scores - lse_ref[0, head : head + 1, start:stop])
            dprobs = product_cols(values, grads)
            delta = jnp.sum(probs * dprobs, axis=0, keepdims=True)
            dscores = (probs * (dprobs - delta)).astype(BF16)
            dv_ref[:stop, :] += product(probs.astype(BF16), grads)
            dk_ref[:stop, :] += product(dscores, queries)
            dq_ref[start:stop, lanes] = product_rows(dscores, keys) * SCALE

    dq = dq_ref[...]
    turned = rotate_lanes(dq * sine, -1.0)
    columns = pl.ds(pl.multiple_of(pair * 128, 128), 128)
    dqkv_ref[:, columns] = (dq * cosine + turned).astype(BF16)

    @pl.when(pair == pl.num_programs(0) - 1)
    def _():
        grads = jnp.concatenate([dk_ref[...], dv_ref[...]], axis=1)
        back = grads * cosine + rotate_lanes(grads * sine, -1.0)
        lane = lax.broadcasted_iota(jnp.int32, grads.shape, 1)
        width = dqkv_ref.shape[1]
        dqkv_ref[:, width - 128 :] = jnp.where(lane < HEAD_DIM, back, grads).astype(BF16)


def whole_spec(shape):
    return pl.BlockSpec(shape, lambda j: (0,) * len(shape))


def attend(qkv, cosine, sine, seg_row, seg_col):
    length, width = qkv.shape
    pairs = width // 128 - 1
    qblock = min(256, length)
    return pl.pallas_call(
        functools.partial(attend_kernel, qblock),
        grid=(pairs,),
        in_specs=[
            pl.BlockSpec((length, 128), lambda j: (0, j)),
            pl.BlockSpec((length, 128), lambda j: (0, pairs)),
            whole_spec((length, 128)),
            whole_spec((length, 128)),
            whole_spec((1, length)),
            whole_spec((length, 1)),
        ],
        out_specs=[
            pl.BlockSpec((length, 128), lambda j: (0, j)),
            pl.BlockSpec((length, 128), lambda j: (0, j)),
            whole_spec((length, 128)),
            pl.BlockSpec((1, 2, length), lambda j: (j, 0, 0)),
        ],
        out_shape=[
            jax.ShapeDtypeStruct((length, pairs * 128), BF16),
            jax.ShapeDtypeStruct((length, pairs * 128), BF16),
            jax.ShapeDtypeStruct((length, 128), BF16),
            jax.ShapeDtypeStruct((pairs, 2, length), F32),
        ],
        scratch_shapes=[pltpu.VMEM((length, length), F32)],
        compiler_params=pltpu.CompilerParams(vmem_limit_bytes=48 * 1024 * 1024),
        cost_estimate=pl.CostEstimate(
            flops=pairs * 2 * length * length * HEAD_DIM * 2,
            bytes_accessed=8 * length * width,
            transcendentals=pairs * length * length,
        ),
    )(qkv, qkv, cosine, sine, seg_row, seg_col)


def attend_back(qr, kvr, grads, lse, cosine, sine, seg_row, seg_col):
    length = qr.shape[0]
    pairs = qr.shape[1] // 128
    qblock = min(256, length)
    return pl.pallas_call(
        functools.partial(attend_back_kernel, qblock),
        grid=(pairs,),
        in_specs=[
            pl.BlockSpec((length, 128), lambda j: (0, j)),
            whole_spec((length, 128)),
            pl.BlockSpec((length, 128), lambda j: (0, j)),
            pl.BlockSpec((1, 2, length), lambda j: (j, 0, 0)),
            whole_spec((length, 128)),
            whole_spec((length, 128)),
            whole_spec((1, length)),
            whole_spec((length, 1)),
        ],
        out_specs=whole_spec((length, (pairs + 1) * 128)),
        out_shape=jax.ShapeDtypeStruct((length, (pairs + 1) * 128), BF16),
        scratch_shapes=[
            pltpu.VMEM((length, length), F32),
            pltpu.VMEM((length, 128), F32),
            pltpu.VMEM((length, HEAD_DIM), F32),
            pltpu.VMEM((length, HEAD_DIM), F32),
        ],
        compiler_params=pltpu.CompilerParams(vmem_limit_bytes=48 * 1024 * 1024),
        cost_estimate=pl.CostEstimate(
            flops=pairs * 5 * length * length * HEAD_DIM * 2,
            bytes_accessed=12 * length * qr.shape[1],
            transcendentals=pairs * length * length,
        ),
    )(qr, kvr, grads, lse, cosine, sine, seg_row, seg_col)


MESH = pl.DeviceIdType.MESH
HBM = pl.BlockSpec(memory_space=pl.ANY)
VMEM = pl.BlockSpec(memory_space=pltpu.VMEM)
VMEM_BYTES = 62 * 1024 * 1024
STEP = 16
DOWN_CUT = 64
BACK_CUT = 80


class Place:
    def __init__(self, sizes):
        self.ny, self.nc, self.nz, self.nx = sizes
        self.s = lax.axis_index("seq")
        self.b = lax.axis_index("batch")
        self.y, self.c = self.s // self.nc, self.s % self.nc
        self.z, self.x = self.b // self.nx, self.b % self.nx

    def seq_at(self, dy, dc):
        return (self.y + dy + self.ny) % self.ny * self.nc + (self.c + dc + self.nc) % self.nc

    def z_at(self, dz):
        return (self.z + dz + self.nz) % self.nz

    def batch_at(self, dz, dx):
        return self.z_at(dz) * self.nx + (self.x + dx + self.nx) % self.nx

    def enter(self):
        peers = [
            (self.seq_at(dy, dc), self.b)
            for dy in range(self.ny)
            for dc in range(self.nc)
            if (dy, dc) != (0, 0)
        ]
        peers += [(self.s, self.batch_at(k, 0)) for k in range(1, self.nz)]
        peers += [(self.s, self.batch_at(0, m)) for m in range(1, self.nx)]
        barrier = pltpu.get_barrier_semaphore()
        for peer in peers:
            pl.semaphore_signal(barrier, inc=1, device_id=peer, device_id_type=MESH)
        pl.semaphore_wait(barrier, len(peers))


def only(when, action):
    if when is None:
        action()
    else:
        pl.when(when())(action)


class Wires:
    def __init__(self, send_sems, recv_sems):
        self.send_sems, self.recv_sems = send_sems, recv_sems
        self.ends = []
        self.open = []

    def describe(self, index, source, target, step=0):
        return pltpu.make_async_remote_copy(
            src_ref=source,
            dst_ref=target,
            send_sem=self.send_sems.at[index + step],
            recv_sem=self.recv_sems.at[index + step],
            device_id=self.ends[index][2](),
            device_id_type=MESH,
        )

    def plan(self, source, target, device, when=None):
        index = len(self.ends)
        self.ends.append((source, target, device, when))
        self.open.append(index)
        return index

    def push(self, source, target, device, when=None):
        index = self.plan(source, target, device, when)
        only(when, lambda: self.describe(index, source(), target()).start())
        return index

    def wait(self, index, landed):
        self.describe(index, landed, landed).wait_recv()

    def sent(self, index):
        self.open.remove(index)
        source, target, unused, when = self.ends[index]
        only(when, lambda: self.describe(index, source(), target()).wait_send())

    def close(self):
        for index in list(self.open):
            self.sent(index)


class Copies:
    def __init__(self, sems):
        self.sems = sems
        self.count = 0

    def start(self, source, target):
        copy = Copy(self, self.count, source, target)
        self.count += 1
        copy.describe().start()
        return copy


class Copy:
    def __init__(self, copies, index, source, target):
        self.copies, self.index, self.source, self.target = copies, index, source, target

    def describe(self):
        sem = self.copies.sems.at[self.index]
        return pltpu.make_async_copy(self.source, self.target, sem)

    def wait(self):
        self.describe().wait()


class Through:
    def __init__(self, copies, source, buffer, target):
        self.copies, self.buffer, self.target = copies, buffer, target
        self.copy = copies.start(source, buffer)

    def turn(self):
        self.copy.wait()
        self.copy = self.copies.start(self.buffer, self.target)

    def wait(self):
        self.copy.wait()


class Gather:
    def __init__(self, wires, slot, own, outer, inner, at, device):
        self.wires, self.slot, self.own = wires, slot, own
        self.outer, self.inner, self.at, self.device = outer, inner, at, device
        self.first, self.second = {}, {}

    def push(self, source, target, k, m):
        return self.wires.push(source, target, lambda: self.device(self.at(k, m)))

    def start(self):
        mine = lambda: self.slot(self.at(0, 0))
        for k in range(1, self.outer):
            self.first[k] = self.push(self.own, mine, k, 0)
        for m in range(1, self.inner):
            self.second[0, m] = self.push(self.own, mine, 0, m)

    def pass_on(self, k):
        came = lambda: self.slot(self.at(-k, 0))
        self.wires.wait(self.first[k], came())
        for m in range(1, self.inner):
            self.second[k, m] = self.push(came, came, 0, m)

    def finish(self):
        for (k, m), ticket in self.second.items():
            self.wires.wait(ticket, self.slot(self.at(-k, -m)))


class LineGather:
    def __init__(self, wires, place, slot, own, x_first=False):
        self.wires, self.place, self.slot, self.own, self.x_first = wires, place, slot, own, x_first
        self.up, self.down, self.across = {}, {}, {}

    def at(self, dz, dx):
        place = self.place
        zz = jnp.clip(place.z + dz, 0, place.nz - 1)
        return self.slot(zz * place.nx + (place.x + dx) % place.nx)

    def below(self, k):
        return self.place.z >= k

    def above(self, k):
        return self.place.z + k < self.place.nz

    def push(self, source, dz, dx, when=None):
        place = self.place
        return self.wires.push(
            source[0],
            source[1],
            lambda: (
                place.s,
                jnp.clip(place.z + dz, 0, place.nz - 1) * place.nx + (place.x + dx) % place.nx,
            ),
            when,
        )

    def spread(self, source, dx):
        self.up[dx, 1] = self.push(source, 1, 0, lambda: self.above(1))
        self.down[dx, 1] = self.push(source, -1, 0, lambda: self.below(1))

    def start_x(self):
        self.across[0] = self.push((self.own, lambda: self.at(0, 0)), 0, 1)

    def start_z(self):
        self.spread((self.own, lambda: self.at(0, 0)), 0)

    def cross(self):
        came = lambda: self.at(0, 1)
        self.wires.wait(self.across[0], came())
        self.spread((came, came), 1)

    def relay(self, k):
        last = k + 1 == self.place.nz
        for dx in (0, 1) if self.x_first else (0,):
            for side, table, here, on in (
                (-1, self.up, self.below, self.above),
                (1, self.down, self.above, self.below),
            ):
                pl.when(here(k))(
                    lambda: self.wires.wait(table[dx, k], self.at(side * k, dx))
                )
                if not last:
                    table[dx, k + 1] = self.push(
                        self.fixed(side * k, dx),
                        -side,
                        0,
                        lambda here=here, on=on: here(k) & on(1),
                    )
                if not self.x_first:
                    self.across[side * k] = self.push(
                        self.fixed(side * k, dx), 0, 1, lambda here=here: here(k)
                    )

    def fixed(self, dz, dx):
        came = lambda: self.at(dz, dx)
        return came, came

    def finish(self):
        if self.x_first:
            return
        self.wires.wait(self.across[0], self.at(0, 1))
        for k in range(1, self.place.nz):
            pl.when(self.below(k))(
                lambda: self.wires.wait(self.across[-k], self.at(-k, 1))
            )
            pl.when(self.above(k))(
                lambda: self.wires.wait(self.across[k], self.at(k, 1))
            )


class RowSum:
    def __init__(self, wires, place, part_ref, core_in, far_in):
        self.wires, self.place = wires, place
        self.part_ref, self.core_in, self.far_in = part_ref, core_in, far_in
        self.tickets = {}

    def slot(self, t):
        return self.place.seq_at((3 - t) // 2, (t + 1) % 2)

    def push(self, t, source, target, dy, dc):
        self.tickets[t] = self.wires.push(
            lambda: self.part_ref.at[source],
            lambda: target(),
            lambda: (self.place.seq_at(dy, dc), self.place.b),
        )

    def compute(self, part):
        def body(t, unused):
            self.part_ref[t] = part(self.slot(t)).astype(BF16)

            @pl.when(t == 0)
            def _():
                self.push(0, 0, lambda: self.core_in.at[1], 0, 1)

            @pl.when(t == 1)
            def _():
                self.wires.wait(self.tickets[0], self.core_in.at[1])
                mine = self.part_ref.at[1]
                add_up(mine, [mine, self.core_in.at[1]])
                self.push(1, 1, lambda: self.far_in, 1, 0)

            @pl.when(t == 2)
            def _():
                self.push(2, 2, lambda: self.core_in.at[0], 0, 1)

            return unused

        lax.fori_loop(0, 4, body, 0)

    def finish(self, target, extra=()):
        self.wires.wait(self.tickets[2], self.core_in.at[0])
        self.wires.wait(self.tickets[1], self.far_in)
        add_up(target, [self.part_ref.at[3], self.core_in.at[0], self.far_in] + list(extra))

    def sent(self):
        for ticket in self.tickets.values():
            self.wires.sent(ticket)


class Rotating:
    def __init__(self, copies):
        self.sems, self.base = copies.sems, copies.count
        copies.count += 2

    def copy(self, i, source, target):
        return pltpu.make_async_copy(source, target, self.sems.at[self.base + i % 2])


def add_up(target, sources):
    shape = target.shape
    steps = shape[-2] // STEP

    def body(i, unused):
        at = pl.ds(pl.multiple_of(i % steps * STEP, STEP), STEP)
        where = (at, slice(None)) if len(shape) == 2 else (i // steps, at, slice(None))
        total = sources[0][where].astype(F32)
        for source in sources[1:]:
            total = total + source[where].astype(F32)
        target[where] = total.astype(target.dtype)
        return unused

    lax.fori_loop(0, steps * (1 if len(shape) == 2 else shape[0]), body, 0)


def front_kernel(
    sizes,
    pairs,
    x_ref,
    gb_ref,
    table_ref,
    gain_ref,
    qkv_ref,
    out_ref,
    gate_ref,
    up_ref,
    down_ref,
    wqkv_out,
    wo_out,
    wg_ref,
    wu_ref,
    wd_ref,
    gb_all_ref,
    n1t_out,
    n2t_out,
    residual_out,
    headst_out,
    qr_out,
    kvr_out,
    lse_ref,
    tables_out,
    gains_ref,
    bias_out,
    gate_proj_ref,
    up_proj_ref,
    grad_down_ref,
    hidden_out_ref,
    wqkv_ref,
    wo_ref,
    n1t_ref,
    n2t_ref,
    residual_ref,
    headst_ref,
    qr_ref,
    kvr_ref,
    tables_ref,
    bias_ref,
    x_all_ref,
    table_all_ref,
    gain_all_ref,
    core_in_ref,
    far_in_ref,
    own_gb_ref,
    n2_ref,
    own_down_ref,
    own_gate_ref,
    send_sems,
    recv_sems,
    copy_sems,
):
    place = Place(sizes)
    ny, nc, nz, nx = sizes
    s, b = place.s, place.b
    n_seq, n_batch = ny * nc, nz * nx
    length, width = x_ref.shape
    total_len = n_seq * length
    ff = gate_ref.shape[2]
    wires = Wires(send_sems, recv_sems)
    copies = Copies(copy_sems)
    row_others = [(dy, dc) for dy in range(ny) for dc in range(nc) if dy or dc]

    def over_batch(slot, own, x_first=False):
        return LineGather(wires, place, slot, own, x_first)

    def over_seq(slot, own):
        return Gather(wires, slot, own, ny, nc, place.seq_at, lambda j: (j, b))

    def columns(ref):
        return lambda j: ref.at[:, j]

    def blocks(ref):
        return lambda j: ref.at[j]

    class Exchange:
        def __init__(self, parts, target, many=True, own=None):
            self.target = target
            part = (lambda j: parts.at[j]) if many else (lambda j: parts)
            self.copy = own or copies.start(part(s), target.at[s, b])
            self.tickets = {}
            for away in row_others:
                self.tickets[away] = wires.push(
                    lambda away=away: part(place.seq_at(*away)),
                    lambda: target.at[s, b],
                    lambda away=away: (place.seq_at(*away), b),
                )

        def finish(self):
            self.copy.wait()
            for (dy, dc), ticket in self.tickets.items():
                wires.wait(ticket, self.target.at[place.seq_at(-dy, -dc), b])

    late = []

    def keep(source, target):
        late.append(copies.start(source, target))

    own_gb = Through(copies, gb_ref, own_gb_ref, gb_all_ref.at[s])
    own_down = Through(copies, down_ref, own_down_ref, wd_ref.at[b])
    own_gate = Through(copies, gate_ref.at[s], own_gate_ref.at[0], wg_ref.at[s, b])
    own_up = Through(copies, up_ref.at[s], own_gate_ref.at[1], wu_ref.at[s, b])
    own_table = copies.start(table_ref, table_all_ref.at[s])
    own_x = copies.start(x_ref, x_all_ref.at[s])
    own_out = copies.start(out_ref, wo_ref.at[b])
    place.enter()
    qkv_parts = Exchange(qkv_ref, wqkv_ref)
    gain_parts = Exchange(gain_ref, gain_all_ref, many=False)
    for copy in (own_gate, own_up, own_down, own_gb):
        copy.turn()
    wo = over_batch(blocks(wo_ref), lambda: out_ref)
    wo.start_x()
    wo.start_z()
    table_all = over_seq(blocks(table_all_ref), lambda: table_ref)
    table_all.start()
    gate_parts = Exchange(gate_ref, wg_ref, own=own_gate)
    x_all = over_seq(blocks(x_all_ref), lambda: x_ref)
    x_all.start()
    up_parts = Exchange(up_ref, wu_ref, own=own_up)
    wqkv = over_batch(columns(wqkv_ref), lambda: wqkv_ref.at[:, b])
    gains = over_batch(columns(gain_all_ref), lambda: gain_all_ref.at[:, b])
    wg = over_batch(columns(wg_ref), lambda: wg_ref.at[:, b])
    wu = over_batch(columns(wu_ref), lambda: wu_ref.at[:, b])
    cut = pl.ds(0, DOWN_CUT)
    rest = pl.ds(DOWN_CUT, down_ref.shape[0] - DOWN_CUT)
    wd1 = over_batch(lambda j: wd_ref.at[j, cut], lambda: down_ref.at[cut])
    wd2 = over_batch(lambda j: wd_ref.at[j, rest], lambda: down_ref.at[rest], True)
    gb_all = over_seq(blocks(gb_all_ref), lambda: gb_ref)

    qkv_parts.finish()
    wqkv.start_x()
    wqkv.start_z()
    gain_parts.finish()
    gains.start_x()
    gains.start_z()
    wo.relay(1)
    gains.relay(1)
    gate_parts.finish()
    wg.start_x()
    wqkv.relay(1)
    wg.start_z()
    wo.relay(2)
    gains.relay(2)
    wqkv.relay(2)
    for k in range(1, ny):
        table_all.pass_on(k)
        x_all.pass_on(k)
    wo.relay(3)
    gains.relay(3)
    wqkv.relay(3)
    up_parts.finish()
    wu.start_x()
    wd2.start_x()
    wu.start_z()
    gb_all.start()

    def attention(n1_ref, qkv_proj_ref, part_ref):
        own_table.wait()
        table_all.finish()
        own_x.wait()
        x_all.finish()
        gains.finish()
        rows = width // (n_seq * n_batch)
        for g in range(2):
            gains_ref[g : g + 1, :] = jnp.concatenate(
                [gain_all_ref[i, j, g : g + 1, :rows] for i in range(n_seq) for j in range(n_batch)],
                axis=1,
            )
        gain_one = gains_ref[0:1, :]
        half = length // 2

        def norm_rows(i, unused):
            part = x_all_ref[i // 2, pl.ds(i % 2 * half, half), :].astype(F32)
            at = pl.ds(pl.multiple_of(i * half, half), half)
            n1_ref[at, :] = (part * rms_scale(part) * gain_one).astype(BF16)
            return unused

        lax.fori_loop(0, 2 * n_seq, norm_rows, 0)
        for j in range(n_seq):
            at = slice(j * length, (j + 1) * length)
            table = table_all_ref[j]
            cos_part, sin_part = table[:, :HALF], table[:, HALF:HEAD_DIM]
            tables_ref[0, at, :] = jnp.concatenate([cos_part] * 4, axis=1)
            tables_ref[1, at, :] = jnp.concatenate([sin_part] * 4, axis=1)
        flipped = [
            jnp.transpose(table_all_ref[j])[HEAD_DIM : HEAD_DIM + 1, :] for j in range(n_seq)
        ]
        query_seg = jnp.concatenate(flipped, axis=1)
        for j in range(n_seq):
            key_seg = table_all_ref[j][:, HEAD_DIM : HEAD_DIM + 1]
            key_pos = j * length + lax.broadcasted_iota(jnp.int32, (length, total_len), 0)
            query_pos = lax.broadcasted_iota(jnp.int32, (length, total_len), 1)
            allowed = (key_seg == query_seg) & (key_pos <= query_pos)
            bias_ref[j * length : (j + 1) * length, :] = jnp.where(
                allowed, 0.0, MASKED_SCORE
            ).astype(BF16)
        keep(tables_ref, tables_out)
        keep(bias_ref, bias_out)

        wqkv.finish()
        keep(wqkv_ref, wqkv_out)
        weights = wqkv_ref[...].reshape(width, wqkv_ref.shape[3])

        def project(i, unused):
            at = pl.ds(pl.multiple_of(i * length, length), length)
            qkv_proj_ref[at, :] = product(n1_ref[at, :], weights)
            return unused

        lax.fori_loop(0, n_seq, project, 0)
        kv = qkv_proj_ref[:, pairs * 128 :]
        lane = lax.broadcasted_iota(jnp.int32, kv.shape, 1)
        rotated = kv * tables_ref[0] + rotate_lanes(kv, 1.0) * tables_ref[1]
        kvr_ref[...] = jnp.where(lane < HEAD_DIM, rotated, kv).astype(BF16)

        def attend_pair(pair, unused):
            at = pl.ds(pl.multiple_of(pair * 128, 128), 128)
            q = qkv_proj_ref[:, at]
            qr = (q * tables_ref[0] + rotate_lanes(q, 1.0) * tables_ref[1]).astype(BF16)
            qr_ref[:, at] = qr
            low = (qr * SCALE).astype(BF16)
            for start in range(0, total_len, length):
                stop = start + length
                outs = []
                for head in range(2):
                    queries = low[start:stop, head * HEAD_DIM : (head + 1) * HEAD_DIM]
                    scores = product_cols(kvr_ref[:stop, :HEAD_DIM], queries)
                    scores = scores + bias_ref[:stop, start:stop].astype(F32)
                    top = jnp.max(scores, axis=0, keepdims=True)
                    grown = jnp.exp(scores - top)
                    total = jnp.sum(grown, axis=0, keepdims=True)
                    probs = (grown * (1.0 / total)).astype(BF16)
                    lse_ref[pair, head : head + 1, start:stop] = top + jnp.log(total)
                    outs.append(product_rows(probs, kvr_ref[:stop, HEAD_DIM:]))
                headst_ref[at, start:stop] = jnp.transpose(
                    jnp.concatenate(outs, axis=1).astype(BF16)
                )
            return unused

        wg.relay(1)
        lax.fori_loop(0, pairs, attend_pair, 0)
        wg.relay(2)

        keep(headst_ref, headst_out)
        keep(qr_ref, qr_out)
        keep(kvr_ref, kvr_out)

        own_out.wait()
        wo.finish()
        keep(wo_ref, wo_out)
        out_weights = wo_ref[...].reshape(n_batch * wo_ref.shape[1], width)

        def out_part(j):
            at = pl.ds(pl.multiple_of(j * length, length), length)
            return product_rows(headst_ref[:, at], out_weights)

        row_sum = RowSum(wires, place, part_ref, core_in_ref, far_in_ref)
        row_sum.compute(out_part)
        wg.relay(3)

        def flip_rows(i, unused):
            at = pl.ds(pl.multiple_of(i * length, length), length)
            n1t_ref[:, at] = jnp.transpose(n1_ref[at, :])
            return unused

        lax.fori_loop(0, n_seq, flip_rows, 0)
        keep(n1t_ref, n1t_out)
        wu.relay(1)
        wd1.start_z()
        wd2.start_z()
        wd2.cross()
        row_sum.finish(residual_ref, [x_all_ref.at[s]])
        keep(residual_ref, residual_out)

        def norm_own(i, unused):
            at = pl.ds(pl.multiple_of(i * 32, 32), 32)
            total = residual_ref[at, :]
            normed = (total * rms_scale(total) * gains_ref[1:2, :]).astype(BF16)
            n2_ref[s, at, :] = normed
            return unused

        lax.fori_loop(0, length // 32, norm_own, 0)
        row_sum.sent()

    pl.run_scoped(
        attention,
        pltpu.VMEM((total_len, width), BF16),
        pltpu.VMEM((total_len, wqkv_ref.shape[3]), F32),
        pltpu.VMEM((n_seq, length, width), BF16),
    )
    n2 = over_seq(blocks(n2_ref), lambda: n2_ref.at[s])
    n2.start()
    wu.relay(2)
    wd1.start_x()
    for k in range(1, ny):
        n2.pass_on(k)
        gb_all.pass_on(k)
    wu.relay(3)

    def feed_forward(weight_ref, gate_buf, up_buf, hidden_ref, gb_buf, grad_buf):
        n2.finish()
        for j in range(n_seq):
            n2t_ref[:, j * length : (j + 1) * length] = jnp.transpose(n2_ref[j])
        keep(n2t_ref, n2t_out)
        wd1.relay(1)
        wd1.relay(2)
        wg.finish()
        copies.start(wg_ref, weight_ref).wait()
        weights = (width, ff)

        def gate_rows(j, unused):
            at = pl.ds(pl.multiple_of(j * length, length), length)
            gate_buf[at, :] = product(n2_ref[j], weight_ref[...].reshape(weights))
            return unused

        lax.fori_loop(0, n_seq, gate_rows, 0)
        outs = [copies.start(gate_buf, gate_proj_ref)]
        wd1.relay(3)
        wd2.relay(1)
        own_gb.wait()
        gb_all.finish()
        gb_in = copies.start(gb_all_ref, gb_buf)
        wu.finish()
        copies.start(wu_ref, weight_ref).wait()
        up_out = Rotating(copies)

        def up_copy(j):
            at = pl.ds(pl.multiple_of(j * length, length), length)
            return up_out.copy(j, up_buf.at[j % 2], up_proj_ref.at[at])

        def up_rows(j, unused):
            at = pl.ds(pl.multiple_of(j * length, length), length)

            @pl.when(j >= 2)
            def _():
                up_copy(j - 2).wait()

            up = product(n2_ref[j], weight_ref[...].reshape(weights))
            up_buf[j % 2] = up
            up_copy(j).start()
            gate = gate_buf[at, :]
            hidden_ref[at, :] = (gate * jax.nn.sigmoid(gate) * up).astype(BF16)
            return unused

        lax.fori_loop(0, n_seq, up_rows, 0)
        outs.append(copies.start(hidden_ref, hidden_out_ref))
        gb_in.wait()
        wd2.relay(2)
        grads = gb_buf[...].reshape(total_len, width)
        grad_out = Rotating(copies)

        def grad_copy(i):
            at = pl.ds(pl.multiple_of(i * 256, 256), 256)
            return grad_out.copy(i, grad_buf.at[i % 2], grad_down_ref.at[at])

        def grad_rows(i, unused):
            at = pl.ds(pl.multiple_of(i * 256, 256), 256)

            @pl.when(i >= 2)
            def _():
                grad_copy(i - 2).wait()

            grad_buf[i % 2] = product_rows(hidden_ref[:, at], grads).astype(BF16)
            grad_copy(i).start()
            return unused

        whole = ff // 256
        lax.fori_loop(0, whole, grad_rows, 0)
        up_copy(n_seq - 2).wait()
        up_copy(n_seq - 1).wait()
        grad_copy(whole - 2).wait()
        grad_copy(whole - 1).wait()
        rest = ff - whole * 256
        if rest:
            grad_buf[0, :rest] = product_rows(hidden_ref[:, whole * 256 :], grads).astype(BF16)
            outs.append(
                copies.start(grad_buf.at[0, :rest], grad_down_ref.at[pl.ds(whole * 256, rest)])
            )
        for copy in outs:
            copy.wait()

    pl.run_scoped(
        feed_forward,
        pltpu.VMEM(wg_ref.shape, BF16),
        pltpu.VMEM((total_len, ff), F32),
        pltpu.VMEM((2, length, ff), F32),
        pltpu.VMEM((total_len, ff), BF16),
        pltpu.VMEM((n_seq, length, width), BF16),
        pltpu.VMEM((2, 256, width), BF16),
    )
    wd2.relay(3)
    wd1.finish()
    wd2.finish()
    own_down.wait()
    for copy in late:
        copy.wait()
    wires.close()


def shape_of(dims, kind):
    return jax.ShapeDtypeStruct(dims, kind)


def front(sizes, x, gb, table, gain, qkv, w_out, gate, up, down):
    ny, nc, nz, nx = sizes
    n_seq, n_batch = ny * nc, nz * nx
    length, width = x.shape
    total_len = n_seq * length
    pairs = qkv.shape[2] // 128 - 1
    rows = w_out.shape[0]
    ff = gate.shape[2]
    held = [
        ((n_seq, n_batch, rows, qkv.shape[2]), BF16),
        ((n_batch, rows, width), BF16),
        ((width, total_len), BF16),
        ((width, total_len), BF16),
        ((length, width), F32),
        ((pairs * 128, total_len), BF16),
        ((total_len, pairs * 128), BF16),
        ((total_len, 128), BF16),
        ((2, total_len, 128), F32),
        ((total_len, total_len), BF16),
    ]
    kept = [(HBM, shape_of(*item)) for item in held]
    results = kept[:2]
    results += [
        (HBM, shape_of((n_seq, n_batch, rows, ff), BF16)),
        (HBM, shape_of((n_seq, n_batch, rows, ff), BF16)),
        (HBM, shape_of((n_batch,) + down.shape, BF16)),
        (HBM, shape_of((n_seq, length, width), BF16)),
    ]
    results += kept[2:8]
    results += [(VMEM, shape_of((pairs, 2, total_len), F32))]
    results += kept[8:9]
    results += [(VMEM, shape_of((2, width), F32))]
    results += kept[9:]
    results += [
        (HBM, shape_of((total_len, ff), F32)),
        (HBM, shape_of((total_len, ff), F32)),
        (HBM, shape_of((ff, width), BF16)),
        (HBM, shape_of((total_len, ff), BF16)),
    ]
    seq_copies = ny - 1 + (nc - 1) * ny
    wires = 4 * (n_seq - 1) + 5 * seq_copies + 7 * 16
    return pl.pallas_call(
        functools.partial(front_kernel, sizes, pairs),
        in_specs=[HBM] * 9,
        out_specs=[spec for spec, unused in results],
        out_shape=[kind for unused, kind in results],
        scratch_shapes=[pltpu.VMEM(*item) for item in held]
        + [
            pltpu.VMEM((n_seq, length, width), BF16),
            pltpu.VMEM((n_seq, length, 128), F32),
            pltpu.VMEM((n_seq, n_batch, 8, 128), F32),
            pltpu.VMEM((ny, length, width), BF16),
            pltpu.VMEM((length, width), BF16),
            pltpu.VMEM((length, width), BF16),
            pltpu.VMEM((n_seq, length, width), BF16),
            pltpu.VMEM(down.shape, BF16),
            pltpu.VMEM((2, rows, ff), BF16),
            pltpu.SemaphoreType.DMA((wires,)),
            pltpu.SemaphoreType.DMA((wires,)),
            pltpu.SemaphoreType.DMA((40,)),
        ],
        compiler_params=pltpu.CompilerParams(
            collective_id=0, has_side_effects=True, vmem_limit_bytes=VMEM_BYTES
        ),
        cost_estimate=pl.CostEstimate(
            flops=2 * total_len * width * (qkv.shape[2] + rows * n_batch + 3 * ff),
            bytes_accessed=100 * 1024 * 1024,
            transcendentals=pairs * total_len * total_len,
        ),
    )(x, gb, table, gain, qkv, w_out, gate, up, down)


class LineReduce:
    def __init__(self, wires, place, copies, own, from_x, below, above, stage, x_last=False):
        self.wires, self.place, self.copies, self.own = wires, place, copies, own
        self.from_x, self.below, self.above, self.stage = from_x, below, above, stage
        self.x_last = x_last
        self.x_tickets, self.up, self.down = {}, {}, {}

    def target(self, i):
        z, last = self.place.z, self.place.nz - 1
        low = z < self.place.nz // 2
        return [
            jnp.where(low, last, 0),
            jnp.where(low, last - 1, 1),
            z + 1 - 2 * (z % 2),
            z,
        ][i]

    def across(self):
        return self.place.s, self.place.batch_at(0, 1)

    def send(self, chunk):
        for i in range(self.place.nz):
            self.x_tickets[i] = self.wires.push(
                lambda i=i: chunk(self.target(i)),
                lambda i=i: self.from_x.at[self.target(i)],
                self.across,
            )

    def plan(self, chunk):
        for i in range(self.place.nz):
            self.x_tickets[i] = self.wires.plan(
                lambda i=i: chunk(self.target(i)),
                lambda i=i: self.from_x.at[self.target(i)],
                self.across,
            )

    def any_target(self, i):
        chosen = self.target(0)
        for j in range(1, self.place.nz):
            chosen = jnp.where(i == j, self.target(j), chosen)
        return chosen

    def send_one(self, i, chunk):
        zz = self.any_target(i)
        self.wires.describe(self.x_tickets[0], chunk(zz), self.from_x.at[zz], i).start()

    def take(self, landed, mine):
        self.copies.start(landed, self.stage).wait()
        add_up(mine, [mine, self.stage])

    def add(self, i):
        zz = self.target(i)
        self.wires.wait(self.x_tickets[i], self.from_x.at[zz])
        self.take(self.from_x.at[zz], self.own.at[zz])

    def step(self, k):
        place = self.place
        nz = place.nz
        for side, tickets, landing in ((1, self.up, self.below), (-1, self.down, self.above)):

            def moves(side=side):
                return (place.z <= k - 1) if side > 0 else (place.z >= nz - k)

            def away(side=side):
                return jnp.clip(place.z + side * (nz - k), 0, nz - 1)

            if k > 1:
                behind = (place.z > 0) if side > 0 else (place.z < nz - 1)

                @pl.when(moves() & behind)
                def _():
                    landed = landing.at[k - 2]
                    self.wires.wait(tickets[k - 1], landed)
                    self.take(landed, self.own.at[away()])

            tickets[k] = self.wires.push(
                lambda away=away: self.own.at[away()],
                lambda landing=landing: landing.at[k - 1],
                lambda side=side: (
                    place.s,
                    jnp.clip(place.z + side, 0, nz - 1) * place.nx + place.x,
                ),
                moves,
            )

    def gather_z(self, target):
        place, last = self.place, self.place.nz - 1
        mine = self.own.at[place.z]

        def body(stages):
            def load(ticket, landed, stage):
                self.wires.wait(ticket, landed)
                self.copies.start(landed, stage).wait()

            @pl.when(place.z > 0)
            def _():
                load(self.up[last], self.below.at[last - 1], stages.at[0])

            @pl.when(place.z < last)
            def _():
                load(self.down[last], self.above.at[last - 1], stages.at[1])

            @pl.when(place.z == 0)
            def _():
                add_up(target, [mine, stages.at[1]])

            @pl.when(place.z == last)
            def _():
                add_up(target, [mine, stages.at[0]])

            @pl.when((place.z > 0) & (place.z < last))
            def _():
                add_up(target, [mine, stages.at[0], stages.at[1]])

        pl.run_scoped(body, pltpu.VMEM((2,) + self.stage.shape, BF16))

    def finish(self, target=None):
        mine = self.own.at[self.place.z]
        self.gather_z(mine if target is None else target)
        return mine

    def change(self):
        mine = self.own.at[self.place.z]
        self.gather_z(mine)
        self.x_tickets[0] = self.wires.push(
            lambda: self.own.at[self.place.z, (self.place.x + 1) % 2],
            lambda: self.from_x,
            self.across,
        )

    def close(self, target):
        self.wires.wait(self.x_tickets[0], self.from_x)
        self.copies.start(self.from_x, self.stage.at[0]).wait()
        add_up(target, [self.own.at[self.place.z, self.place.x], self.stage.at[0]])


def norm_back_rows(grad_ref, input_ref, gain, base_ref, target_ref, low_ref):
    rows = 32

    def body(i, unused):
        at = pl.ds(pl.multiple_of(i * rows, rows), rows)
        inputs = input_ref[at, :].astype(F32)
        back = norm_back(grad_ref[at, :], inputs, rms_scale(inputs), gain)
        total = base_ref[at, :].astype(F32) + back
        if target_ref is not None:
            target_ref[at, :] = total
        low_ref[at, :] = total.astype(BF16)
        return unused

    lax.fori_loop(0, grad_ref.shape[0] // rows, body, 0)


def back_kernel(
    sizes,
    pairs,
    gd_ref,
    hidden_ref,
    wd_ref,
    wg_ref,
    wu_ref,
    gate_ref,
    up_ref,
    gb_ref,
    n1t_ref,
    n2t_ref,
    headst_ref,
    residual_ref,
    qr_ref,
    kvr_ref,
    tables_ref,
    bias_ref,
    wqkv_ref,
    wo_ref,
    x_ref,
    lse_ref,
    gains_ref,
    mixed_out,
    tokens_out,
    down_out,
    out_out,
    gate_own,
    up_own,
    qkv_own,
    x_refs,
    below_refs,
    above_refs,
    send_gate,
    send_up,
    da_all_ref,
    own_refs,
    send_out,
    send_qkv,
    stage_refs,
    core_in_ref,
    far_in_ref,
    mixed_core_in,
    mixed_far_in,
    da_own_ref,
    total_ref,
    send_sems,
    recv_sems,
    copy_sems,
):
    place = Place(sizes)
    ny, nc, nz, nx = sizes
    s, b = place.s, place.b
    n_seq, n_batch = ny * nc, nz * nx
    length, width = x_ref.shape
    total_len = n_seq * length
    ff = wg_ref.shape[3]
    rows = wo_ref.shape[1]
    wires = Wires(send_sems, recv_sems)
    copies = Copies(copy_sems)
    s_down, s_rest, s_gate, s_up, s_out, s_qkv = own_refs

    def reduce(i, stage, x_last=False):
        return LineReduce(
            wires,
            place,
            copies,
            own_refs[i],
            x_refs[i],
            below_refs[i],
            above_refs[i],
            stage_refs[stage],
            x_last,
        )

    down, rest = reduce(0, 0), reduce(1, 1, True)
    gate, up = reduce(2, 2), reduce(3, 2)
    out, qkv = reduce(4, 3), reduce(5, 4)
    row_others = [(dy, dc) for dy in range(ny) for dc in range(nc) if dy or dc]

    late = []
    cut = pl.ds(0, BACK_CUT)
    beyond = pl.ds(BACK_CUT, gd_ref.shape[1] - BACK_CUT)
    own_rest = [
        copies.start(gd_ref.at[zz * nx + x, beyond], s_rest.at[zz, x])
        for zz in range(nz)
        for x in range(nx)
    ]
    own_down = [
        copies.start(gd_ref.at[zz * nx + place.x, cut], s_down.at[zz]) for zz in range(nz)
    ]
    place.enter()
    down.send(lambda zz: gd_ref.at[zz * nx + (place.x + 1) % nx, cut])
    for copy in own_rest:
        copy.wait()
    rest.step(1)

    def weight_rows(flipped_ref, grads, k, dx):
        j = place.batch_at(k, dx)
        pieces = []
        for i in range(n_seq):
            start = pl.multiple_of((i * n_batch + j) * rows, rows)
            pieces.append(flipped_ref[pl.ds(start, rows), :])
        value = product(jnp.concatenate(pieces, axis=0), grads)
        return value.astype(BF16).reshape(n_seq, rows, grads.shape[1])

    def feed_forward(dgate_ref, dup_ref, part_ref):
        row_sum = RowSum(wires, place, part_ref, core_in_ref, far_in_ref)

        def activations(weight1, gate_buf, up_buf, gb_buf):
            load1 = copies.start(wd_ref, weight1)

            base = copies.count
            copies.count += 3

            def load_gb(j):
                return pltpu.make_async_copy(gb_ref.at[j], gb_buf, copy_sems.at[base])

            def load_gate(j):
                at = pl.ds(pl.multiple_of(j * length, length), length)
                return (
                    pltpu.make_async_copy(gate_ref.at[at], gate_buf, copy_sems.at[base + 1]),
                    pltpu.make_async_copy(up_ref.at[at], up_buf, copy_sems.at[base + 2]),
                )

            load_gb(0).start()
            for copy in load_gate(0):
                copy.start()
            load1.wait()

            def rows_back(j, unused):
                load_gb(j).wait()
                grad_hidden = product_cols(gb_buf[...], weight1[...].reshape(ff, width))

                @pl.when(j + 1 < n_seq)
                def _():
                    load_gb(j + 1).start()

                for copy in load_gate(j):
                    copy.wait()
                gate_part, up_part = gate_buf[...], up_buf[...]
                sigma = jax.nn.sigmoid(gate_part)
                activated = gate_part * sigma
                dgate_ref[j] = (
                    grad_hidden * up_part * sigma * (1.0 + gate_part * (1.0 - sigma))
                ).astype(BF16)
                dup_ref[j] = (grad_hidden * activated).astype(BF16)

                @pl.when(j + 1 < n_seq)
                def _():
                    for copy in load_gate(j + 1):
                        copy.start()

                return unused

            def rows_and_sums(j, unused):
                rows_back(j, unused)

                @pl.when(j == 2)
                def _():
                    rest.step(2)

                return unused

            lax.fori_loop(0, n_seq, rows_and_sums, 0)
            for copy in own_down:
                copy.wait()

        pl.run_scoped(
            activations,
            pltpu.VMEM(wd_ref.shape, BF16),
            pltpu.VMEM((length, ff), F32),
            pltpu.VMEM((length, ff), F32),
            pltpu.VMEM((length, width), BF16),
        )

        def rows_of(reduce, flipped, staging, grads_ref, send_ref):
            copies.start(n2t_ref, flipped).wait()
            chunk = lambda zz: send_ref.at[zz]
            reduce.plan(chunk)
            turns = Rotating(copies)

            def body(i, unused):
                zz = reduce.any_target(i)
                k = (zz - place.z + nz) % nz
                grads = grads_ref[...].reshape(total_len, ff)
                staging[i % 2] = weight_rows(flipped, grads, k, 1)
                turns.copy(i, staging.at[i % 2], chunk(zz)).start()
                reduce.own[zz] = weight_rows(flipped, grads, k, 0)
                turns.copy(i, staging.at[i % 2], chunk(zz)).wait()
                reduce.send_one(i, chunk)
                return unused

            lax.fori_loop(0, nz, body, 0)

        def gate_grads(flipped, staging):
            rows_of(gate, flipped, staging, dgate_ref, send_gate)

        def up_grads(flipped, staging):
            rows_of(up, flipped, staging, dup_ref, send_up)

        grad_buffers = (pltpu.VMEM(n2t_ref.shape, BF16), pltpu.VMEM((2, n_seq, rows, ff), BF16))
        pl.run_scoped(gate_grads, *grad_buffers)

        def inputs(weight1, weight2):
            loads = [copies.start(wg_ref, weight1), copies.start(wu_ref, weight2)]
            for load in loads:
                load.wait()

            def input_part(j):
                return product_cols(
                    dgate_ref[j], weight1[...].reshape(width, ff)
                ) + product_cols(dup_ref[j], weight2[...].reshape(width, ff))

            row_sum.compute(input_part)

        pl.run_scoped(inputs, pltpu.VMEM(wg_ref.shape, BF16), pltpu.VMEM(wg_ref.shape, BF16))
        rest.step(3)
        down.add(0)
        down.step(1)
        down.add(1)
        down.step(2)
        pl.run_scoped(up_grads, *grad_buffers)
        down.add(2)
        down.step(3)
        down.add(3)

        def normed(residual_buf, gb_buf):
            loads = [
                copies.start(residual_ref, residual_buf),
                copies.start(gb_ref.at[s], gb_buf),
            ]
            for copy in loads:
                copy.wait()
            row_sum.finish(total_ref)
            norm_back_rows(
                total_ref, residual_buf, gains_ref[1:2, :], gb_buf, total_ref, da_own_ref
            )
            da.start()
            row_sum.sent()

        pl.run_scoped(normed, pltpu.VMEM((length, width), F32), pltpu.VMEM((length, width), BF16))
        gate.add(0)
        gate.step(1)
        gate.add(1)
        gate.step(2)
        rest.change()
        gate.add(2)
        gate.step(3)

    own_da = []
    da = Gather(
        wires,
        lambda j: da_all_ref.at[j],
        lambda: da_own_ref,
        ny,
        nc,
        place.seq_at,
        lambda j: (j, b),
    )
    pl.run_scoped(
        feed_forward,
        pltpu.VMEM((n_seq, length, ff), BF16),
        pltpu.VMEM((n_seq, length, ff), BF16),
        pltpu.VMEM((n_seq, length, width), BF16),
    )
    own_da.append(copies.start(da_own_ref, da_all_ref.at[s]))
    for k in range(1, ny):
        da.pass_on(k)

    def attention(
        da_buf,
        wo_buf,
        wqkv_buf,
        qr_buf,
        headst_buf,
        do_buf,
        kvr_buf,
        tables_buf,
        bias_buf,
        dqkv_buf,
        n1t_buf,
        dq_buf,
        dk_buf,
        dv_buf,
        part_ref,
    ):
        loads = [
            copies.start(source, target)
            for source, target in [
                (wo_ref, wo_buf),
                (headst_ref, headst_buf),
                (qr_ref, qr_buf),
                (kvr_ref, kvr_buf),
                (tables_ref, tables_buf),
                (bias_ref, bias_buf),
                (n1t_ref, n1t_buf),
                (wqkv_ref, wqkv_buf),
            ]
        ]
        gate.add(3)
        da.finish()
        own_da[0].wait()
        copies.start(da_all_ref, da_buf).wait()
        for load in loads:
            load.wait()
        out_weights = wo_buf[...].reshape(n_batch * rows, width)

        def heads_back(j, unused):
            at = pl.ds(pl.multiple_of(j * length, length), length)
            do_buf[at, :] = product_cols(da_buf[j], out_weights).astype(BF16)
            return unused

        lax.fori_loop(0, n_seq, heads_back, 0)
        branch = da_buf[...].reshape(total_len, width)

        def out_rows(dx):
            pieces = []
            for zz in range(nz):
                start = pl.multiple_of((zz * nx + (place.x + dx) % nx) * rows, rows)
                pieces.append(headst_buf[pl.ds(start, rows), :])
            value = product(jnp.concatenate(pieces, axis=0), branch)
            return value.astype(BF16).reshape(nz, rows, width)

        send_out[...] = out_rows(1)
        out.send(lambda zz: send_out.at[zz])
        s_out[...] = out_rows(0)
        dk_buf[...] = jnp.zeros_like(dk_buf)
        dv_buf[...] = jnp.zeros_like(dv_buf)

        def pair_back(pair, unused):
            at = pl.ds(pl.multiple_of(pair * 128, 128), 128)
            low = (qr_buf[:, at] * SCALE).astype(BF16)
            grads_pair = do_buf[:, at]
            for start in range(0, total_len, length):
                stop = start + length
                outs = []
                for head in range(2):
                    lanes = slice(head * HEAD_DIM, (head + 1) * HEAD_DIM)
                    queries = low[start:stop, lanes]
                    grads = grads_pair[start:stop, lanes]
                    keys = kvr_buf[:stop, :HEAD_DIM]
                    values = kvr_buf[:stop, HEAD_DIM:]
                    scores = product_cols(keys, queries)
                    scores = scores + bias_buf[:stop, start:stop].astype(F32)
                    probs = jnp.exp(scores - lse_ref[pair, head : head + 1, start:stop])
                    dprobs = product_cols(values, grads)
                    delta = jnp.sum(probs * dprobs, axis=0, keepdims=True)
                    dscores = (probs * (dprobs - delta)).astype(BF16)
                    dv_buf[:stop, :] += product(probs.astype(BF16), grads)
                    dk_buf[:stop, :] += product(dscores, queries)
                    outs.append(product_rows(dscores, keys) * SCALE)
                dq_buf[start:stop, :] = jnp.concatenate(outs, axis=1)
            dq = dq_buf[...]
            turned = rotate_lanes(dq * tables_buf[1], -1.0)
            dqkv_buf[:, at] = (dq * tables_buf[0] + turned).astype(BF16)
            return unused

        def pair_and_sums(pair, unused):
            pair_back(pair, unused)

            @pl.when(pair == 1)
            def _():
                up.add(0)
                up.step(1)

            return unused

        lax.fori_loop(0, pairs, pair_and_sums, 0)
        grads = jnp.concatenate([dk_buf[...], dv_buf[...]], axis=1)
        back = grads * tables_buf[0] + rotate_lanes(grads * tables_buf[1], -1.0)
        lane = lax.broadcasted_iota(jnp.int32, grads.shape, 1)
        dqkv_buf[:, pairs * 128 :] = jnp.where(lane < HEAD_DIM, back, grads).astype(BF16)

        row_sum = RowSum(wires, place, part_ref, core_in_ref, far_in_ref)
        in_weights = wqkv_buf[...].reshape(width, wqkv_ref.shape[3])

        def input_part(j):
            at = pl.ds(pl.multiple_of(j * length, length), length)
            return product_cols(dqkv_buf[at, :], in_weights)

        row_sum.compute(input_part)

        def qkv_rows(zz, unused):
            k = (zz - place.z + nz) % nz
            send_qkv[zz] = weight_rows(n1t_buf, dqkv_buf[...], k, 1)
            s_qkv[zz] = weight_rows(n1t_buf, dqkv_buf[...], k, 0)
            return unused

        lax.fori_loop(0, nz, qkv_rows, 0)
        qkv.send(lambda zz: send_qkv.at[zz])
        up.add(1)
        up.step(2)
        up.add(2)
        up.step(3)
        up.add(3)
        out.add(0)
        out.step(1)

        def last(grad_ref, x_buf, tokens_ref):
            load = copies.start(x_ref, x_buf)
            row_sum.finish(grad_ref)
            load.wait()
            norm_back_rows(grad_ref, x_buf, gains_ref[0:1, :], total_ref, None, tokens_ref)
            copies.start(tokens_ref, tokens_out).wait()

        row = pltpu.VMEM((length, width), BF16)
        pl.run_scoped(last, pltpu.VMEM((length, width), F32), row, row)
        row_sum.sent()

    pl.run_scoped(
        attention,
        pltpu.VMEM((n_seq, length, width), BF16),
        pltpu.VMEM(wo_ref.shape, BF16),
        pltpu.VMEM(wqkv_ref.shape, BF16),
        pltpu.VMEM(qr_ref.shape, BF16),
        pltpu.VMEM(headst_ref.shape, BF16),
        pltpu.VMEM(qr_ref.shape, BF16),
        pltpu.VMEM(kvr_ref.shape, BF16),
        pltpu.VMEM(tables_ref.shape, F32),
        pltpu.VMEM(bias_ref.shape, BF16),
        pltpu.VMEM((total_len, (pairs + 1) * 128), BF16),
        pltpu.VMEM(n1t_ref.shape, BF16),
        pltpu.VMEM((total_len, 128), F32),
        pltpu.VMEM((total_len, HEAD_DIM), F32),
        pltpu.VMEM((total_len, HEAD_DIM), F32),
        pltpu.VMEM((n_seq, length, width), BF16),
    )

    exchanges = []

    def exchange(reduce, target):
        mine = reduce.finish()
        copy = copies.start(mine.at[s], target.at[s])
        tickets = {}
        for away in row_others:
            tickets[away] = wires.push(
                lambda away=away: reduce.own.at[place.z, place.seq_at(*away)],
                lambda: target.at[s],
                lambda away=away: (place.seq_at(*away), b),
            )
        exchanges.append((copy, target, tickets))

    def layer_out(weight_buf, hidden_buf, part_ref, mixed_total, mixed_ref, down_own, out_own):
        loads = [
            copies.start(wd_ref, weight_buf),
            copies.start(hidden_ref, hidden_buf),
            copies.start(residual_ref, mixed_total),
        ]
        out.add(1)
        out.step(2)
        for load in loads:
            load.wait()

        def mixed_part(j):
            at = pl.ds(pl.multiple_of(j * length, length), length)
            return product(hidden_buf[at, :], weight_buf[...].reshape(ff, width))

        row_sum = RowSum(wires, place, part_ref, mixed_core_in, mixed_far_in)
        row_sum.compute(mixed_part)
        out.add(2)
        out.step(3)
        out.add(3)
        qkv.add(0)
        qkv.step(1)
        exchange(gate, gate_own)
        down.finish(down_own.at[cut])
        rest.close(down_own.at[beyond])
        late.append(copies.start(down_own, down_out))
        qkv.add(1)
        qkv.step(2)
        exchange(up, up_own)
        out.finish(out_own)
        late.append(copies.start(out_own, out_out))
        qkv.add(2)
        qkv.step(3)
        qkv.add(3)
        row_sum.finish(mixed_ref, [mixed_total])
        late.append(copies.start(mixed_ref, mixed_out))
        exchange(qkv, qkv_own)
        row_sum.sent()
        for copy in late:
            copy.wait()

    pl.run_scoped(
        layer_out,
        pltpu.VMEM(wd_ref.shape, BF16),
        pltpu.VMEM(hidden_ref.shape, BF16),
        pltpu.VMEM((n_seq, length, width), BF16),
        pltpu.VMEM((length, width), F32),
        pltpu.VMEM((length, width), BF16),
        pltpu.VMEM(gd_ref.shape[1:], F32),
        pltpu.VMEM((rows, width), F32),
    )

    for copy, target, tickets in exchanges:
        copy.wait()
        for (dy, dc), ticket in tickets.items():
            wires.wait(ticket, target.at[place.seq_at(-dy, -dc)])
    wires.close()


def grouped_back_kernel(sizes, pairs, *refs):
    refs = list(refs)
    groups = []
    at = 21 + 7
    for count in (6, 6, 6):
        groups.append(refs[at : at + count])
        at += count
    singles = refs[at : at + 3]
    at += 3
    own = refs[at : at + 6]
    at += 6
    sends = refs[at : at + 2]
    at += 2
    stages = refs[at : at + 5]
    at += 5
    back_kernel(
        sizes, pairs, *refs[:28], *groups, *singles, own, *sends, stages, *refs[at:]
    )


def back(sizes, gd, hidden, wd, wg, wu, gate, up, gb, n1t, n2t, headst, residual, qr, kvr, tables, bias, wqkv, wo, x, lse, gains):
    ny, nc, nz, nx = sizes
    n_seq, n_batch = ny * nc, nz * nx
    length, width = x.shape
    ff = wg.shape[3]
    rows = wo.shape[1]
    pairs = qr.shape[1] // 128
    chunk_down = (BACK_CUT, width)
    chunk_rest = (gd.shape[1] - BACK_CUT, width)
    chunk_gate = (n_seq, rows, ff)
    chunk_out = (rows, width)
    chunk_qkv = (n_seq, rows, wqkv.shape[3])
    pair_rest = (nx,) + chunk_rest
    chunks = [chunk_down, pair_rest, chunk_gate, chunk_gate, chunk_out, chunk_qkv]
    results = [
        (HBM, shape_of((length, width), BF16)),
        (HBM, shape_of((length, width), BF16)),
        (HBM, shape_of(gd.shape[1:], F32)),
        (HBM, shape_of(chunk_out, F32)),
        (HBM, shape_of(chunk_gate, BF16)),
        (HBM, shape_of(chunk_gate, BF16)),
        (HBM, shape_of(chunk_qkv, BF16)),
    ]
    landings = [
        [shape_of((nz,) + chunk, BF16) for chunk in chunks],
        [shape_of((nz - 1,) + chunk, BF16) for chunk in chunks],
        [shape_of((nz - 1,) + chunk, BF16) for chunk in chunks],
    ]
    landings[0][1] = shape_of(chunk_rest, BF16)
    for group in landings:
        results += [(HBM, kind) for kind in group]
    results += [(HBM, shape_of((nz,) + chunk_gate, BF16))] * 2
    results += [(HBM, shape_of((n_seq, length, width), BF16))]
    wires = len(chunks) * (nz + 2 * (nz - 1)) + 3 * 3 + 3 + 3 * (n_seq - 1)
    row = pltpu.VMEM((length, width), BF16)
    return pl.pallas_call(
        functools.partial(grouped_back_kernel, sizes, pairs),
        in_specs=[HBM] * 19 + [VMEM] * 2,
        out_specs=[spec for spec, unused in results],
        out_shape=[kind for unused, kind in results],
        scratch_shapes=[pltpu.VMEM((nz,) + chunk, BF16) for chunk in chunks]
        + [
            pltpu.VMEM((nz,) + chunk_out, BF16),
            pltpu.VMEM((nz,) + chunk_qkv, BF16),
            pltpu.VMEM(chunk_down, BF16),
            pltpu.VMEM(pair_rest, BF16),
            pltpu.VMEM(chunk_gate, BF16),
            pltpu.VMEM(chunk_out, BF16),
            pltpu.VMEM(chunk_qkv, BF16),
            pltpu.VMEM((ny, length, width), BF16),
            row,
            pltpu.VMEM((ny, length, width), BF16),
            row,
            row,
            pltpu.VMEM((length, width), F32),
            pltpu.SemaphoreType.DMA((wires,)),
            pltpu.SemaphoreType.DMA((wires,)),
            pltpu.SemaphoreType.DMA((140,)),
        ],
        compiler_params=pltpu.CompilerParams(
            collective_id=1, has_side_effects=True, vmem_limit_bytes=VMEM_BYTES
        ),
        cost_estimate=pl.CostEstimate(
            flops=12 * n_seq * length * width * ff,
            bytes_accessed=100 * 1024 * 1024,
            transcendentals=pairs * (n_seq * length) ** 2,
        ),
    )(gd, hidden, wd, wg, wu, gate, up, gb, n1t, n2t, headst, residual, qr, kvr, tables, bias, wqkv, wo, x, lse, gains)


def by_permutes(
    tokens,
    cotangent,
    selection,
    segments,
    positions,
    gain_attn,
    w_query,
    w_key,
    w_value,
    w_out,
    gain_mlp,
    w_gate,
    w_up,
    w_down,
):
    seq = Axis("seq", 2)
    batch = Axis("batch", lax.axis_size("batch") // 4)
    n_seq, n_batch = seq.size, batch.size
    length, width = tokens.shape[1], tokens.shape[2]
    total_len = length * n_seq
    rows = w_query.shape[0]
    ff = w_gate.shape[1]
    q_cols = w_query.shape[1] // n_seq
    sharers = n_seq // KV_HEADS

    query_parts = w_query.reshape(rows, n_seq, q_cols)
    key_parts = jnp.repeat(w_key.reshape(rows, KV_HEADS, HEAD_DIM), sharers, axis=1)
    value_parts = jnp.repeat(w_value.reshape(rows, KV_HEADS, HEAD_DIM), sharers, axis=1)
    qkv_parts = jnp.concatenate([query_parts, key_parts, value_parts], axis=2).transpose(1, 0, 2)

    def spread(parts):
        mine = seq.exchange(parts)
        return batch.gather(mine, 1).reshape(n_seq * n_batch * rows, parts.shape[2])

    def collect(grad):
        parts = grad.astype(BF16).reshape(n_seq, n_batch, rows, grad.shape[1])
        return seq.exchange(batch.scatter_sum(parts, 1).astype(BF16)).astype(F32)

    def by_columns(weight):
        return weight.reshape(rows, n_seq, weight.shape[1] // n_seq).transpose(1, 0, 2)

    places = seq.gather(jnp.stack([segments[0], positions[0]]), 1)
    seg_all = places[0].reshape(total_len)
    pos_all = places[1].reshape(total_len)
    gains = batch.gather(seq.gather(jnp.stack([gain_attn, gain_mlp]), 1), 2)
    gain_one = gains[0].reshape(1, width).astype(F32)
    gain_two = gains[1].reshape(1, width).astype(F32)
    x_all = seq.gather(tokens[0], 0).reshape(total_len, width).astype(F32)
    w_qkv = spread(qkv_parts)
    wo = batch.gather(w_out, 0).reshape(n_batch * rows, width)
    wg = spread(by_columns(w_gate))
    wu = spread(by_columns(w_up))
    wd = batch.gather(w_down, 0).reshape(n_batch * w_down.shape[0], width)

    grad_out_row = cotangent[0].astype(F32) * selection[0].astype(F32)[:, None]
    grad_low = seq.gather(grad_out_row.astype(BF16), 0).reshape(total_len, width)

    row_input = tokens[0].astype(F32)
    inv_attn = rms_scale(row_input)
    normed1 = (x_all * rms_scale(x_all) * gain_one).astype(BF16)
    qkv = product(normed1, w_qkv)
    frequency = 10000.0 ** (-(jnp.arange(HALF, dtype=F32) * 2.0 / HEAD_DIM))
    angles = pos_all.astype(F32)[:, None] * jnp.tile(frequency, 4)[None, :]
    cosine, sine = jnp.cos(angles), jnp.sin(angles)
    seg_row, seg_col = seg_all[None, :], seg_all[:, None]
    heads_out, query_rot, kv_rot, lse = attend(qkv, cosine, sine, seg_row, seg_col)
    attn_part = product(heads_out, wo).astype(BF16).reshape(n_seq, length, width)
    residual = row_input + seq.scatter_sum(attn_part, 0)

    inv_mlp = rms_scale(residual)
    normed2_own = (residual * inv_mlp * gain_two).astype(BF16)
    normed2 = seq.gather(normed2_own, 0).reshape(total_len, width)
    gate_proj = product(normed2, wg)
    up_proj = product(normed2, wu)
    sigma = jax.nn.sigmoid(gate_proj)
    activated = gate_proj * sigma
    hidden = (activated * up_proj).astype(BF16)
    mixed_part = product(hidden, wd).astype(BF16).reshape(n_seq, length, width)
    mixed = (residual + seq.scatter_sum(mixed_part, 0)).astype(BF16)[None]

    grad_down = product_rows(hidden, grad_low)
    grad_hidden = product_cols(grad_low, wd)
    grad_gate_act = (
        grad_hidden * up_proj * sigma * (1.0 + gate_proj * (1.0 - sigma))
    ).astype(BF16)
    grad_up_act = (grad_hidden * activated).astype(BF16)
    grad_gate = product_rows(normed2, grad_gate_act)
    grad_up = product_rows(normed2, grad_up_act)
    normed_part = product_cols(grad_gate_act, wg) + product_cols(grad_up_act, wu)
    normed_terms = seq.scatter_sum(normed_part.astype(BF16).reshape(n_seq, length, width), 0)
    grad_resid = grad_out_row + norm_back(normed_terms, residual, inv_mlp, gain_two)

    down_own = batch.scatter_sum(
        grad_down.astype(BF16).reshape(n_batch, w_down.shape[0], width), 0
    )
    gate_own = collect(grad_gate).transpose(1, 0, 2).reshape(rows, ff)
    up_own = collect(grad_up).transpose(1, 0, 2).reshape(rows, ff)

    grad_branch = seq.gather(grad_resid.astype(BF16), 0).reshape(total_len, width)
    grad_wout = product_rows(heads_out, grad_branch)
    grad_heads = product_cols(grad_branch, wo).astype(BF16)
    grad_qkv_act = attend_back(
        query_rot, kv_rot, grad_heads, lse, cosine, sine, seg_row, seg_col
    )
    grad_wqkv = product_rows(normed1, grad_qkv_act)
    input_part = product_cols(grad_qkv_act, w_qkv).astype(BF16).reshape(n_seq, length, width)
    grad_normed1 = seq.scatter_sum(input_part, 0)
    tokens_grad = (
        grad_resid + norm_back(grad_normed1, row_input, inv_attn, gain_one)
    ).astype(BF16)[None]
    out_own = batch.scatter_sum(grad_wout.astype(BF16).reshape(n_batch, rows, width), 0)
    qkv_own = collect(grad_wqkv)
    query_own = qkv_own[:, :, :q_cols].transpose(1, 0, 2).reshape(rows, n_seq * q_cols)

    def shared(columns):
        heads = columns.reshape(KV_HEADS, sharers, rows, HEAD_DIM).sum(axis=1)
        return heads.transpose(1, 0, 2).reshape(rows, KV_HEADS * HEAD_DIM)

    key_own = shared(qkv_own[:, :, q_cols : q_cols + HEAD_DIM])
    value_own = shared(qkv_own[:, :, q_cols + HEAD_DIM :])

    def along(weight, grad):
        return jnp.sum(weight.astype(F32) * grad, axis=1)

    gain1_own = (
        along(w_query, query_own) + along(w_key, key_own) + along(w_value, value_own)
    ) / gain_attn.astype(F32)
    gain2_own = (along(w_gate, gate_own) + along(w_up, up_own)) / gain_mlp.astype(F32)
    return (
        mixed,
        tokens_grad,
        query_own,
        key_own,
        value_own,
        out_own,
        gate_own,
        up_own,
        down_own,
        gain1_own,
        gain2_own,
    )


def by_kernels(
    tokens,
    cotangent,
    selection,
    segments,
    positions,
    gain_attn,
    w_query,
    w_key,
    w_value,
    w_out,
    gain_mlp,
    w_gate,
    w_up,
    w_down,
):
    sizes = mesh_sizes()
    n_seq, n_batch = sizes[0] * sizes[1], sizes[2] * sizes[3]
    length, width = tokens.shape[1], tokens.shape[2]
    rows, ff = w_gate.shape
    q_cols = w_query.shape[1] // n_seq

    def by_columns(weight):
        return weight.reshape(rows, n_seq, weight.shape[1] // n_seq).transpose(1, 0, 2)

    qkv_parts = jnp.concatenate([by_columns(w) for w in (w_query, w_key, w_value)], axis=2)
    grad_low = (cotangent[0].astype(F32) * selection[0].astype(F32)[:, None]).astype(BF16)
    frequency = 10000.0 ** (-(jnp.arange(HALF, dtype=F32) * 2.0 / HEAD_DIM))
    angles = positions[0].astype(F32)[:, None] * frequency[None, :]
    documents = jnp.broadcast_to(segments[0].astype(F32)[:, None], (length, 128 - HEAD_DIM))
    table = jnp.concatenate([jnp.cos(angles), jnp.sin(angles), documents], axis=1)
    gain_tile = jnp.pad(
        jnp.stack([gain_attn, gain_mlp]).astype(F32), ((0, 6), (0, 128 - gain_attn.shape[0]))
    )
    (
        w_qkv,
        wo,
        wg,
        wu,
        wd,
        gb_all,
        n1t,
        n2t,
        residual,
        headst,
        query_rot,
        kv_rot,
        lse,
        rotary,
        gains,
        bias,
        gate_proj,
        up_proj,
        grad_down,
        hidden,
    ) = front(
        sizes,
        tokens[0],
        grad_low,
        table,
        gain_tile,
        qkv_parts,
        w_out,
        by_columns(w_gate),
        by_columns(w_up),
        w_down,
    )
    mixed, tokens_grad, down_own, out_own, gate_part, up_part, qkv_part = back(
        sizes,
        grad_down.reshape(n_batch, w_down.shape[0], width),
        hidden,
        wd,
        wg,
        wu,
        gate_proj,
        up_proj,
        gb_all,
        n1t,
        n2t,
        headst,
        residual,
        query_rot,
        kv_rot,
        rotary,
        bias,
        w_qkv,
        wo,
        tokens[0],
        lse,
        gains,
    )[:7]

    def by_rows(part):
        return part.astype(F32).transpose(1, 0, 2).reshape(rows, n_seq * part.shape[2])

    query_own = by_rows(qkv_part[:, :, :q_cols])
    key_own = by_rows(qkv_part[:, :, q_cols : q_cols + HEAD_DIM])
    value_own = by_rows(qkv_part[:, :, q_cols + HEAD_DIM :])
    gate_own, up_own = by_rows(gate_part), by_rows(up_part)

    def along(weight, grad):
        return jnp.sum(weight.astype(F32) * grad, axis=1)

    gain1_own = (
        along(w_query, query_own) + along(w_key, key_own) + along(w_value, value_own)
    ) / gain_attn.astype(F32)
    gain2_own = (along(w_gate, gate_own) + along(w_up, up_own)) / gain_mlp.astype(F32)
    return (
        mixed[None],
        tokens_grad[None],
        query_own,
        key_own,
        value_own,
        out_own,
        gate_own,
        up_own,
        down_own,
        gain1_own,
        gain2_own,
    )


def mesh_sizes():
    return (lax.axis_size("seq") // 2, 2, 4, lax.axis_size("batch") // 4)


def per_device(*args):
    fits = mesh_sizes() == (2, 2, 4, 2) and args[0].shape[1:] == (256, 2048)
    return (by_kernels if fits else by_permutes)(*args)


def solution(mesh):
    both = ("seq", "batch")
    tokens = P("batch", "seq", None)
    flags = P("batch", "seq")
    matrix = P(both, None)
    vector = P(both)
    in_specs = (
        (tokens, tokens, flags, flags, flags)
        + (vector, matrix, matrix, matrix, matrix)
        + (vector, matrix, matrix, matrix)
    )
    out_specs = (tokens, tokens) + (matrix,) * 7 + (vector, vector)
    return jax.shard_map(
        per_device, mesh=mesh, in_specs=in_specs, out_specs=out_specs, check_vma=False
    )
```

```python
import functools

import jax
import jax.numpy as jnp
from jax import lax
from jax.experimental import pallas as pl
from jax.experimental.pallas import tpu as pltpu
from jax.sharding import PartitionSpec as P

HEADS = 32
KV_HEADS = 4
HEAD_DIM = 64
HALF = HEAD_DIM // 2

EPSILON = 1e-05
MASKED_SCORE = -1e30
SCALE = HEAD_DIM ** (-0.5)
CONTRACT_ROWS = (((0,), (0,)), ((), ()))
CONTRACT_COLS = (((1,), (1,)), ((), ()))
BF16 = jnp.bfloat16
F32 = jnp.float32


def product(left, right):
    return jnp.dot(left, right, preferred_element_type=F32)


def product_rows(left, right):
    return lax.dot_general(left, right, CONTRACT_ROWS, preferred_element_type=F32)


def product_cols(left, right):
    return lax.dot_general(left, right, CONTRACT_COLS, preferred_element_type=F32)


def rms_scale(inputs):
    return lax.rsqrt(jnp.mean(inputs * inputs, axis=-1, keepdims=True) + EPSILON)


def norm_back(grad_normed, inputs, inverse, gain):
    scaled = gain * grad_normed
    cubed = inverse * inverse * inverse
    return inverse * scaled - inputs * cubed * jnp.mean(scaled * inputs, axis=-1, keepdims=True)


class Axis:
    def __init__(self, name, inner):
        self.name = name
        self.size = lax.axis_size(name)
        self.inner = inner
        self.outer = self.size // inner
        index = lax.axis_index(name)
        self.index = index
        self.o = index // inner
        self.i = index % inner

    def shift(self, value, outer_by, inner_by):
        pairs = []
        for o in range(self.outer):
            for i in range(self.inner):
                target = ((o + outer_by) % self.outer) * self.inner + (i + inner_by) % self.inner
                pairs.append((o * self.inner + i, target))
        return lax.ppermute(value, self.name, pairs)

    def before(self, outer_by, inner_by):
        o = lax.rem(self.o + self.outer - outer_by, self.outer)
        i = lax.rem(self.i + self.inner - inner_by, self.inner)
        return o * self.inner + i

    def after(self, outer_by, inner_by):
        o = lax.rem(self.o + outer_by, self.outer)
        i = lax.rem(self.i + inner_by, self.inner)
        return o * self.inner + i

    def gather(self, block, dim=0):
        shape = block.shape[:dim] + (self.size,) + block.shape[dim:]
        out = jnp.zeros(shape, block.dtype)
        for k in range(self.outer):
            got = block if k == 0 else self.shift(block, k, 0)
            for m in range(self.inner):
                piece = got if m == 0 else self.shift(got, 0, m)
                out = lax.dynamic_update_slice_in_dim(
                    out, jnp.expand_dims(piece, dim), self.before(k, m), dim
                )
        return out

    def scatter_sum(self, parts, dim=0):
        shape = parts.shape[:dim] + (self.outer, self.inner) + parts.shape[dim + 1 :]
        grid = parts.reshape(shape)

        def inner_part(i):
            return lax.squeeze(lax.dynamic_slice_in_dim(grid, i, 1, dim + 1), (dim + 1,))

        total = inner_part(self.i).astype(F32)
        for m in range(1, self.inner):
            mine = inner_part(lax.rem(self.i + m, self.inner))
            total = total + self.shift(mine, 0, m).astype(F32)
        low = total.astype(BF16)

        def outer_part(o):
            return lax.squeeze(lax.dynamic_slice_in_dim(low, o, 1, dim), (dim,))

        out = outer_part(self.o).astype(F32)
        for k in range(1, self.outer):
            out = out + self.shift(outer_part(lax.rem(self.o + k, self.outer)), k, 0).astype(F32)
        return out

    def exchange(self, parts):
        out = jnp.zeros(parts.shape, parts.dtype)
        for k in range(self.outer):
            for m in range(self.inner):
                part = lax.dynamic_slice_in_dim(parts, self.after(k, m), 1, 0)
                got = part if (k, m) == (0, 0) else self.shift(part, k, m)
                out = lax.dynamic_update_slice_in_dim(out, got, self.before(k, m), 0)
        return out


def rotate_lanes(value, sign):
    lane = lax.broadcasted_iota(jnp.int32, value.shape, 1) % HEAD_DIM
    first = lane < HALF
    width = value.shape[1]
    up = pltpu.roll(value, width - HALF, 1)
    down = pltpu.roll(value, HALF, 1)
    return jnp.where(first, -sign * up, sign * down)


def mask_bias(bias_ref, seg_row_ref, seg_col_ref, length):
    rows = 256
    for start in range(0, length, rows):
        keys = seg_col_ref[start : start + rows, :]
        queries = seg_row_ref[:, :]
        key_pos = start + lax.broadcasted_iota(jnp.int32, (rows, length), 0)
        query_pos = lax.broadcasted_iota(jnp.int32, (rows, length), 1)
        allowed = (keys == queries) & (key_pos <= query_pos)
        bias_ref[start : start + rows, :] = jnp.where(allowed, 0.0, MASKED_SCORE)


def attend_kernel(
    qblock,
    q_ref,
    kv_ref,
    cos_ref,
    sin_ref,
    seg_row_ref,
    seg_col_ref,
    o_ref,
    qr_ref,
    kvr_ref,
    lse_ref,
    bias_ref,
):
    length = q_ref.shape[0]
    cosine = cos_ref[...]
    sine = sin_ref[...]

    @pl.when(pl.program_id(0) == 0)
    def _():
        mask_bias(bias_ref, seg_row_ref, seg_col_ref, length)
        kv = kv_ref[...]
        rotated = kv * cosine + rotate_lanes(kv, 1.0) * sine
        lane = lax.broadcasted_iota(jnp.int32, kv.shape, 1)
        kvr_ref[...] = jnp.where(lane < HEAD_DIM, rotated, kv).astype(BF16)

    q = q_ref[...]
    qr_ref[...] = (q * cosine + rotate_lanes(q, 1.0) * sine).astype(BF16)
    for start in range(0, length, qblock):
        stop = start + qblock
        keys = kvr_ref[:stop, :HEAD_DIM]
        values = kvr_ref[:stop, HEAD_DIM:]
        for head in range(2):
            lanes = slice(head * HEAD_DIM, (head + 1) * HEAD_DIM)
            queries = qr_ref[start:stop, lanes] * SCALE
            scores = product_cols(keys, queries.astype(BF16)) + bias_ref[:stop, start:stop]
            top = jnp.max(scores, axis=0, keepdims=True)
            grown = jnp.exp(scores - top)
            total = jnp.sum(grown, axis=0, keepdims=True)
            probs = (grown * (1.0 / total)).astype(BF16)
            lse_ref[0, head : head + 1, start:stop] = top + jnp.log(total)
            o_ref[start:stop, lanes] = product_rows(probs, values).astype(BF16)


def attend_back_kernel(
    qblock,
    qr_ref,
    kvr_ref,
    do_ref,
    lse_ref,
    cos_ref,
    sin_ref,
    seg_row_ref,
    seg_col_ref,
    dqkv_ref,
    bias_ref,
    dq_ref,
    dk_ref,
    dv_ref,
):
    length = qr_ref.shape[0]
    cosine = cos_ref[...]
    sine = sin_ref[...]
    pair = pl.program_id(0)

    @pl.when(pair == 0)
    def _():
        mask_bias(bias_ref, seg_row_ref, seg_col_ref, length)
        dk_ref[...] = jnp.zeros_like(dk_ref)
        dv_ref[...] = jnp.zeros_like(dv_ref)

    for start in range(0, length, qblock):
        stop = start + qblock
        keys = kvr_ref[:stop, :HEAD_DIM]
        values = kvr_ref[:stop, HEAD_DIM:]
        for head in range(2):
            lanes = slice(head * HEAD_DIM, (head + 1) * HEAD_DIM)
            queries = (qr_ref[start:stop, lanes] * SCALE).astype(BF16)
            grads = do_ref[start:stop, lanes]
            scores = product_cols(keys, queries) + bias_ref[:stop, start:stop]
            probs = jnp.exp(scores - lse_ref[0, head : head + 1, start:stop])
            dprobs = product_cols(values, grads)
            delta = jnp.sum(probs * dprobs, axis=0, keepdims=True)
            dscores = (probs * (dprobs - delta)).astype(BF16)
            dv_ref[:stop, :] += product(probs.astype(BF16), grads)
            dk_ref[:stop, :] += product(dscores, queries)
            dq_ref[start:stop, lanes] = product_rows(dscores, keys) * SCALE

    dq = dq_ref[...]
    turned = rotate_lanes(dq * sine, -1.0)
    columns = pl.ds(pl.multiple_of(pair * 128, 128), 128)
    dqkv_ref[:, columns] = (dq * cosine + turned).astype(BF16)

    @pl.when(pair == pl.num_programs(0) - 1)
    def _():
        grads = jnp.concatenate([dk_ref[...], dv_ref[...]], axis=1)
        back = grads * cosine + rotate_lanes(grads * sine, -1.0)
        lane = lax.broadcasted_iota(jnp.int32, grads.shape, 1)
        width = dqkv_ref.shape[1]
        dqkv_ref[:, width - 128 :] = jnp.where(lane < HEAD_DIM, back, grads).astype(BF16)


def whole_spec(shape):
    return pl.BlockSpec(shape, lambda j: (0,) * len(shape))


def attend(qkv, cosine, sine, seg_row, seg_col):
    length, width = qkv.shape
    pairs = width // 128 - 1
    qblock = min(256, length)
    return pl.pallas_call(
        functools.partial(attend_kernel, qblock),
        grid=(pairs,),
        in_specs=[
            pl.BlockSpec((length, 128), lambda j: (0, j)),
            pl.BlockSpec((length, 128), lambda j: (0, pairs)),
            whole_spec((length, 128)),
            whole_spec((length, 128)),
            whole_spec((1, length)),
            whole_spec((length, 1)),
        ],
        out_specs=[
            pl.BlockSpec((length, 128), lambda j: (0, j)),
            pl.BlockSpec((length, 128), lambda j: (0, j)),
            whole_spec((length, 128)),
            pl.BlockSpec((1, 2, length), lambda j: (j, 0, 0)),
        ],
        out_shape=[
            jax.ShapeDtypeStruct((length, pairs * 128), BF16),
            jax.ShapeDtypeStruct((length, pairs * 128), BF16),
            jax.ShapeDtypeStruct((length, 128), BF16),
            jax.ShapeDtypeStruct((pairs, 2, length), F32),
        ],
        scratch_shapes=[pltpu.VMEM((length, length), F32)],
        compiler_params=pltpu.CompilerParams(vmem_limit_bytes=48 * 1024 * 1024),
        cost_estimate=pl.CostEstimate(
            flops=pairs * 2 * length * length * HEAD_DIM * 2,
            bytes_accessed=8 * length * width,
            transcendentals=pairs * length * length,
        ),
    )(qkv, qkv, cosine, sine, seg_row, seg_col)


def attend_back(qr, kvr, grads, lse, cosine, sine, seg_row, seg_col):
    length = qr.shape[0]
    pairs = qr.shape[1] // 128
    qblock = min(256, length)
    return pl.pallas_call(
        functools.partial(attend_back_kernel, qblock),
        grid=(pairs,),
        in_specs=[
            pl.BlockSpec((length, 128), lambda j: (0, j)),
            whole_spec((length, 128)),
            pl.BlockSpec((length, 128), lambda j: (0, j)),
            pl.BlockSpec((1, 2, length), lambda j: (j, 0, 0)),
            whole_spec((length, 128)),
            whole_spec((length, 128)),
            whole_spec((1, length)),
            whole_spec((length, 1)),
        ],
        out_specs=whole_spec((length, (pairs + 1) * 128)),
        out_shape=jax.ShapeDtypeStruct((length, (pairs + 1) * 128), BF16),
        scratch_shapes=[
            pltpu.VMEM((length, length), F32),
            pltpu.VMEM((length, 128), F32),
            pltpu.VMEM((length, HEAD_DIM), F32),
            pltpu.VMEM((length, HEAD_DIM), F32),
        ],
        compiler_params=pltpu.CompilerParams(vmem_limit_bytes=48 * 1024 * 1024),
        cost_estimate=pl.CostEstimate(
            flops=pairs * 5 * length * length * HEAD_DIM * 2,
            bytes_accessed=12 * length * qr.shape[1],
            transcendentals=pairs * length * length,
        ),
    )(qr, kvr, grads, lse, cosine, sine, seg_row, seg_col)


MESH = pl.DeviceIdType.MESH
HBM = pl.BlockSpec(memory_space=pl.ANY)
VMEM = pl.BlockSpec(memory_space=pltpu.VMEM)
VMEM_BYTES = 62 * 1024 * 1024
STEP = 16
DOWN_CUT = 64
BACK_CUT = 96


class Place:
    def __init__(self, sizes):
        self.ny, self.nc, self.nz, self.nx = sizes
        self.s = lax.axis_index("seq")
        self.b = lax.axis_index("batch")
        self.y, self.c = self.s // self.nc, self.s % self.nc
        self.z, self.x = self.b // self.nx, self.b % self.nx

    def seq_at(self, dy, dc):
        return (self.y + dy + self.ny) % self.ny * self.nc + (self.c + dc + self.nc) % self.nc

    def z_at(self, dz):
        return (self.z + dz + self.nz) % self.nz

    def batch_at(self, dz, dx):
        return self.z_at(dz) * self.nx + (self.x + dx + self.nx) % self.nx

    def enter(self):
        peers = [
            (self.seq_at(dy, dc), self.b)
            for dy in range(self.ny)
            for dc in range(self.nc)
            if (dy, dc) != (0, 0)
        ]
        peers += [(self.s, self.batch_at(k, 0)) for k in range(1, self.nz)]
        peers += [(self.s, self.batch_at(0, m)) for m in range(1, self.nx)]
        barrier = pltpu.get_barrier_semaphore()
        for peer in peers:
            pl.semaphore_signal(barrier, inc=1, device_id=peer, device_id_type=MESH)
        pl.semaphore_wait(barrier, len(peers))


def only(when, action):
    if when is None:
        action()
    else:
        pl.when(when())(action)


class Wires:
    def __init__(self, send_sems, recv_sems):
        self.send_sems, self.recv_sems = send_sems, recv_sems
        self.ends = []
        self.open = []

    def describe(self, index, source, target, step=0):
        return pltpu.make_async_remote_copy(
            src_ref=source,
            dst_ref=target,
            send_sem=self.send_sems.at[index + step],
            recv_sem=self.recv_sems.at[index + step],
            device_id=self.ends[index][2](),
            device_id_type=MESH,
        )

    def plan(self, source, target, device, when=None):
        index = len(self.ends)
        self.ends.append((source, target, device, when))
        self.open.append(index)
        return index

    def push(self, source, target, device, when=None):
        index = self.plan(source, target, device, when)
        only(when, lambda: self.describe(index, source(), target()).start())
        return index

    def wait(self, index, landed):
        self.describe(index, landed, landed).wait_recv()

    def sent(self, index):
        self.open.remove(index)
        source, target, unused, when = self.ends[index]
        only(when, lambda: self.describe(index, source(), target()).wait_send())

    def close(self):
        for index in list(self.open):
            self.sent(index)


class Copies:
    def __init__(self, sems):
        self.sems = sems
        self.count = 0

    def start(self, source, target):
        copy = Copy(self, self.count, source, target)
        self.count += 1
        copy.describe().start()
        return copy


class Copy:
    def __init__(self, copies, index, source, target):
        self.copies, self.index, self.source, self.target = copies, index, source, target

    def describe(self):
        sem = self.copies.sems.at[self.index]
        return pltpu.make_async_copy(self.source, self.target, sem)

    def wait(self):
        self.describe().wait()


class Through:
    def __init__(self, copies, source, buffer, target):
        self.copies, self.buffer, self.target = copies, buffer, target
        self.copy = copies.start(source, buffer)

    def turn(self):
        self.copy.wait()
        self.copy = self.copies.start(self.buffer, self.target)

    def wait(self):
        self.copy.wait()


class Gather:
    def __init__(self, wires, slot, own, outer, inner, at, device):
        self.wires, self.slot, self.own = wires, slot, own
        self.outer, self.inner, self.at, self.device = outer, inner, at, device
        self.first, self.second = {}, {}

    def push(self, source, target, k, m):
        return self.wires.push(source, target, lambda: self.device(self.at(k, m)))

    def start(self):
        mine = lambda: self.slot(self.at(0, 0))
        for k in range(1, self.outer):
            self.first[k] = self.push(self.own, mine, k, 0)
        for m in range(1, self.inner):
            self.second[0, m] = self.push(self.own, mine, 0, m)

    def pass_on(self, k):
        came = lambda: self.slot(self.at(-k, 0))
        self.wires.wait(self.first[k], came())
        for m in range(1, self.inner):
            self.second[k, m] = self.push(came, came, 0, m)

    def finish(self):
        for (k, m), ticket in self.second.items():
            self.wires.wait(ticket, self.slot(self.at(-k, -m)))


class LineGather:
    def __init__(self, wires, place, slot, own, x_first=False):
        self.wires, self.place, self.slot, self.own, self.x_first = wires, place, slot, own, x_first
        self.up, self.down, self.across = {}, {}, {}

    def at(self, dz, dx):
        place = self.place
        zz = jnp.clip(place.z + dz, 0, place.nz - 1)
        return self.slot(zz * place.nx + (place.x + dx) % place.nx)

    def below(self, k):
        return self.place.z >= k

    def above(self, k):
        return self.place.z + k < self.place.nz

    def push(self, source, dz, dx, when=None):
        place = self.place
        return self.wires.push(
            source[0],
            source[1],
            lambda: (
                place.s,
                jnp.clip(place.z + dz, 0, place.nz - 1) * place.nx + (place.x + dx) % place.nx,
            ),
            when,
        )

    def spread(self, source, dx):
        self.up[dx, 1] = self.push(source, 1, 0, lambda: self.above(1))
        self.down[dx, 1] = self.push(source, -1, 0, lambda: self.below(1))

    def start_x(self):
        self.across[0] = self.push((self.own, lambda: self.at(0, 0)), 0, 1)

    def start_z(self):
        self.spread((self.own, lambda: self.at(0, 0)), 0)

    def cross(self):
        came = lambda: self.at(0, 1)
        self.wires.wait(self.across[0], came())
        self.spread((came, came), 1)

    def relay(self, k):
        last = k + 1 == self.place.nz
        for dx in (0, 1) if self.x_first else (0,):
            for side, table, here, on in (
                (-1, self.up, self.below, self.above),
                (1, self.down, self.above, self.below),
            ):
                pl.when(here(k))(
                    lambda: self.wires.wait(table[dx, k], self.at(side * k, dx))
                )
                if not last:
                    table[dx, k + 1] = self.push(
                        self.fixed(side * k, dx),
                        -side,
                        0,
                        lambda here=here, on=on: here(k) & on(1),
                    )
                if not self.x_first:
                    self.across[side * k] = self.push(
                        self.fixed(side * k, dx), 0, 1, lambda here=here: here(k)
                    )

    def fixed(self, dz, dx):
        came = lambda: self.at(dz, dx)
        return came, came

    def finish(self):
        if self.x_first:
            return
        self.wires.wait(self.across[0], self.at(0, 1))
        for k in range(1, self.place.nz):
            pl.when(self.below(k))(
                lambda: self.wires.wait(self.across[-k], self.at(-k, 1))
            )
            pl.when(self.above(k))(
                lambda: self.wires.wait(self.across[k], self.at(k, 1))
            )


class RowSum:
    def __init__(self, wires, place, part_ref, core_in, far_in):
        self.wires, self.place = wires, place
        self.part_ref, self.core_in, self.far_in = part_ref, core_in, far_in
        self.tickets = {}

    def slot(self, t):
        return self.place.seq_at((3 - t) // 2, (t + 1) % 2)

    def push(self, t, source, target, dy, dc):
        self.tickets[t] = self.wires.push(
            lambda: self.part_ref.at[source],
            lambda: target(),
            lambda: (self.place.seq_at(dy, dc), self.place.b),
        )

    def half(self, h):
        rows = self.far_in.shape[0] // 2
        return pl.ds(h * rows, rows)

    def push_half(self, h):
        self.tickets[1, h] = self.wires.push(
            lambda: self.part_ref.at[1, self.half(h)],
            lambda: self.far_in.at[self.half(h)],
            lambda: (self.place.seq_at(1, 0), self.place.b),
        )

    def compute(self, part):
        def body(t, unused):
            self.part_ref[t] = part(self.slot(t)).astype(BF16)

            @pl.when(t == 0)
            def _():
                self.push(0, 0, lambda: self.core_in.at[1], 0, 1)

            @pl.when(t == 1)
            def _():
                self.wires.wait(self.tickets[0], self.core_in.at[1])
                mine = self.part_ref.at[1]
                add_up(mine, [mine, self.core_in.at[1]])
                for h in range(2):
                    self.push_half(h)

            @pl.when(t == 2)
            def _():
                self.push(2, 2, lambda: self.core_in.at[0], 0, 1)

            return unused

        lax.fori_loop(0, 4, body, 0)

    def finish_half(self, h, target):
        if h == 0:
            self.wires.wait(self.tickets[2], self.core_in.at[0])
        at = self.half(h)
        self.wires.wait(self.tickets[1, h], self.far_in.at[at])
        add_up(
            target.at[at], [self.part_ref.at[3, at], self.core_in.at[0, at], self.far_in.at[at]]
        )

    def finish(self, target, extra=()):
        self.wires.wait(self.tickets[2], self.core_in.at[0])
        for h in range(2):
            self.wires.wait(self.tickets[1, h], self.far_in.at[self.half(h)])
        add_up(target, [self.part_ref.at[3], self.core_in.at[0], self.far_in] + list(extra))

    def sent(self):
        for ticket in self.tickets.values():
            self.wires.sent(ticket)


class Rotating:
    def __init__(self, copies):
        self.sems, self.base = copies.sems, copies.count
        copies.count += 2

    def copy(self, i, source, target):
        return pltpu.make_async_copy(source, target, self.sems.at[self.base + i % 2])


def add_up(target, sources):
    shape = target.shape
    rows = 2 * STEP if shape[-2] % (2 * STEP) == 0 else STEP
    steps = shape[-2] // rows
    low = len(sources) == 2 and all(ref.dtype == BF16 for ref in [target] + sources)

    def body(i, unused):
        at = pl.ds(pl.multiple_of(i % steps * rows, rows), rows)
        where = (at, slice(None)) if len(shape) == 2 else (i // steps, at, slice(None))
        if low:
            target[where] = sources[0][where] + sources[1][where]
        else:
            total = sources[0][where].astype(F32)
            for source in sources[1:]:
                total = total + source[where].astype(F32)
            target[where] = total.astype(target.dtype)
        return unused

    lax.fori_loop(0, steps * (1 if len(shape) == 2 else shape[0]), body, 0)


def front_kernel(
    sizes,
    pairs,
    x_ref,
    gb_ref,
    table_ref,
    gain_ref,
    qkv_ref,
    out_ref,
    gate_ref,
    up_ref,
    down_ref,
    wqkv_out,
    wo_out,
    wg_ref,
    wu_ref,
    wd_ref,
    gb_all_ref,
    n1t_out,
    n2t_out,
    residual_out,
    headst_out,
    qr_out,
    kvr_out,
    lse_ref,
    tables_out,
    gains_ref,
    bias_out,
    gate_proj_ref,
    up_proj_ref,
    grad_down_ref,
    hidden_out_ref,
    wqkv_ref,
    wo_ref,
    n1t_ref,
    n2t_ref,
    residual_ref,
    headst_ref,
    qr_ref,
    kvr_ref,
    tables_ref,
    bias_ref,
    x_all_ref,
    table_all_ref,
    gain_all_ref,
    core_in_ref,
    far_in_ref,
    own_gb_ref,
    n2_ref,
    own_down_ref,
    own_gate_ref,
    send_sems,
    recv_sems,
    copy_sems,
):
    place = Place(sizes)
    ny, nc, nz, nx = sizes
    s, b = place.s, place.b
    n_seq, n_batch = ny * nc, nz * nx
    length, width = x_ref.shape
    total_len = n_seq * length
    ff = gate_ref.shape[2]
    wires = Wires(send_sems, recv_sems)
    copies = Copies(copy_sems)
    row_others = [(dy, dc) for dy in range(ny) for dc in range(nc) if dy or dc]

    def over_batch(slot, own, x_first=False):
        return LineGather(wires, place, slot, own, x_first)

    def over_seq(slot, own):
        return Gather(wires, slot, own, ny, nc, place.seq_at, lambda j: (j, b))

    def columns(ref):
        return lambda j: ref.at[:, j]

    def blocks(ref):
        return lambda j: ref.at[j]

    class Exchange:
        def __init__(self, parts, target, many=True, own=None):
            self.target = target
            part = (lambda j: parts.at[j]) if many else (lambda j: parts)
            self.copy = own or copies.start(part(s), target.at[s, b])
            self.tickets = {}
            for away in row_others:
                self.tickets[away] = wires.push(
                    lambda away=away: part(place.seq_at(*away)),
                    lambda: target.at[s, b],
                    lambda away=away: (place.seq_at(*away), b),
                )

        def finish(self):
            self.copy.wait()
            for (dy, dc), ticket in self.tickets.items():
                wires.wait(ticket, self.target.at[place.seq_at(-dy, -dc), b])

    late = []

    def keep(source, target):
        late.append(copies.start(source, target))

    own_gb = Through(copies, gb_ref, own_gb_ref, gb_all_ref.at[s])
    own_down = Through(copies, down_ref, own_down_ref, wd_ref.at[b])
    own_gate = Through(copies, gate_ref.at[s], own_gate_ref.at[0], wg_ref.at[s, b])
    own_up = Through(copies, up_ref.at[s], own_gate_ref.at[1], wu_ref.at[s, b])
    own_table = copies.start(table_ref, table_all_ref.at[s])
    own_x = copies.start(x_ref, x_all_ref.at[s])
    own_out = copies.start(out_ref, wo_ref.at[b])
    place.enter()
    qkv_parts = Exchange(qkv_ref, wqkv_ref)
    gain_parts = Exchange(gain_ref, gain_all_ref, many=False)
    for copy in (own_gate, own_up, own_down, own_gb):
        copy.turn()
    wo = over_batch(blocks(wo_ref), lambda: out_ref)
    wo.start_x()
    wo.start_z()
    table_all = over_seq(blocks(table_all_ref), lambda: table_ref)
    table_all.start()
    gate_parts = Exchange(gate_ref, wg_ref, own=own_gate)
    x_all = over_seq(blocks(x_all_ref), lambda: x_ref)
    x_all.start()
    up_parts = Exchange(up_ref, wu_ref, own=own_up)
    wqkv = over_batch(columns(wqkv_ref), lambda: wqkv_ref.at[:, b])
    gains = over_batch(columns(gain_all_ref), lambda: gain_all_ref.at[:, b])
    wg = over_batch(columns(wg_ref), lambda: wg_ref.at[:, b])
    wu = over_batch(columns(wu_ref), lambda: wu_ref.at[:, b])
    cut = pl.ds(0, DOWN_CUT)
    rest = pl.ds(DOWN_CUT, down_ref.shape[0] - DOWN_CUT)
    wd1 = over_batch(lambda j: wd_ref.at[j, cut], lambda: down_ref.at[cut])
    wd2 = over_batch(lambda j: wd_ref.at[j, rest], lambda: down_ref.at[rest], True)
    gb_all = over_seq(blocks(gb_all_ref), lambda: gb_ref)

    qkv_parts.finish()
    wqkv.start_x()
    wqkv.start_z()
    gain_parts.finish()
    gains.start_x()
    gains.start_z()
    wo.relay(1)
    gains.relay(1)
    gate_parts.finish()
    wg.start_x()
    wqkv.relay(1)
    wg.start_z()
    wo.relay(2)
    gains.relay(2)
    wqkv.relay(2)
    for k in range(1, ny):
        table_all.pass_on(k)
        x_all.pass_on(k)
    wo.relay(3)
    gains.relay(3)
    wqkv.relay(3)
    up_parts.finish()
    wu.start_x()
    wd2.start_x()
    wu.start_z()
    gb_all.start()

    def attention(n1_ref, qkv_proj_ref, part_ref):
        own_table.wait()
        table_all.finish()
        own_x.wait()
        x_all.finish()
        gains.finish()
        rows = width // (n_seq * n_batch)
        for g in range(2):
            gains_ref[g : g + 1, :] = jnp.concatenate(
                [gain_all_ref[i, j, g : g + 1, :rows] for i in range(n_seq) for j in range(n_batch)],
                axis=1,
            )
        gain_one = gains_ref[0:1, :]
        half = length // 2

        def norm_rows(i, unused):
            part = x_all_ref[i // 2, pl.ds(i % 2 * half, half), :].astype(F32)
            at = pl.ds(pl.multiple_of(i * half, half), half)
            n1_ref[at, :] = (part * rms_scale(part) * gain_one).astype(BF16)
            return unused

        lax.fori_loop(0, 2 * n_seq, norm_rows, 0)
        for j in range(n_seq):
            at = slice(j * length, (j + 1) * length)
            table = table_all_ref[j]
            cos_part, sin_part = table[:, :HALF], table[:, HALF:HEAD_DIM]
            tables_ref[0, at, :] = jnp.concatenate([cos_part] * 4, axis=1)
            tables_ref[1, at, :] = jnp.concatenate([sin_part] * 4, axis=1)
        flipped = [
            jnp.transpose(table_all_ref[j])[HEAD_DIM : HEAD_DIM + 1, :] for j in range(n_seq)
        ]
        query_seg = jnp.concatenate(flipped, axis=1)
        for j in range(n_seq):
            key_seg = table_all_ref[j][:, HEAD_DIM : HEAD_DIM + 1]
            key_pos = j * length + lax.broadcasted_iota(jnp.int32, (length, total_len), 0)
            query_pos = lax.broadcasted_iota(jnp.int32, (length, total_len), 1)
            allowed = (key_seg == query_seg) & (key_pos <= query_pos)
            bias_ref[j * length : (j + 1) * length, :] = jnp.where(
                allowed, 0.0, MASKED_SCORE
            ).astype(BF16)
        keep(tables_ref, tables_out)
        keep(bias_ref, bias_out)

        wqkv.finish()
        keep(wqkv_ref, wqkv_out)
        weights = wqkv_ref[...].reshape(width, wqkv_ref.shape[3])

        def project(i, unused):
            at = pl.ds(pl.multiple_of(i * length, length), length)
            qkv_proj_ref[at, :] = product(n1_ref[at, :], weights)
            return unused

        lax.fori_loop(0, n_seq, project, 0)
        kv = qkv_proj_ref[:, pairs * 128 :]
        lane = lax.broadcasted_iota(jnp.int32, kv.shape, 1)
        rotated = kv * tables_ref[0] + rotate_lanes(kv, 1.0) * tables_ref[1]
        kvr_ref[...] = jnp.where(lane < HEAD_DIM, rotated, kv).astype(BF16)

        def attend_pair(pair, unused):
            at = pl.ds(pl.multiple_of(pair * 128, 128), 128)
            q = qkv_proj_ref[:, at]
            qr = (q * tables_ref[0] + rotate_lanes(q, 1.0) * tables_ref[1]).astype(BF16)
            qr_ref[:, at] = qr
            low = (qr * SCALE).astype(BF16)
            for start in range(0, total_len, length):
                stop = start + length
                outs = []
                for head in range(2):
                    queries = low[start:stop, head * HEAD_DIM : (head + 1) * HEAD_DIM]
                    scores = product_cols(kvr_ref[:stop, :HEAD_DIM], queries)
                    scores = scores + bias_ref[:stop, start:stop].astype(F32)
                    top = jnp.max(scores, axis=0, keepdims=True)
                    grown = jnp.exp(scores - top)
                    total = jnp.sum(grown, axis=0, keepdims=True)
                    probs = (grown * (1.0 / total)).astype(BF16)
                    lse_ref[pair, head : head + 1, start:stop] = top + jnp.log(total)
                    outs.append(product_rows(probs, kvr_ref[:stop, HEAD_DIM:]))
                headst_ref[at, start:stop] = jnp.transpose(
                    jnp.concatenate(outs, axis=1).astype(BF16)
                )
            return unused

        wg.relay(1)
        lax.fori_loop(0, pairs, attend_pair, 0)
        wg.relay(2)

        keep(headst_ref, headst_out)
        keep(qr_ref, qr_out)
        keep(kvr_ref, kvr_out)

        own_out.wait()
        wo.finish()
        keep(wo_ref, wo_out)
        out_weights = wo_ref[...].reshape(n_batch * wo_ref.shape[1], width)

        def out_part(j):
            at = pl.ds(pl.multiple_of(j * length, length), length)
            return product_rows(headst_ref[:, at], out_weights)

        row_sum = RowSum(wires, place, part_ref, core_in_ref, far_in_ref)
        row_sum.compute(out_part)
        wg.relay(3)

        def flip_rows(i, unused):
            at = pl.ds(pl.multiple_of(i * length, length), length)
            n1t_ref[:, at] = jnp.transpose(n1_ref[at, :])
            return unused

        lax.fori_loop(0, n_seq, flip_rows, 0)
        keep(n1t_ref, n1t_out)
        wu.relay(1)
        wd1.start_z()
        wd2.start_z()
        wd2.cross()
        row_sum.finish(residual_ref, [x_all_ref.at[s]])
        keep(residual_ref, residual_out)

        def norm_own(i, unused):
            at = pl.ds(pl.multiple_of(i * 32, 32), 32)
            total = residual_ref[at, :]
            normed = (total * rms_scale(total) * gains_ref[1:2, :]).astype(BF16)
            n2_ref[s, at, :] = normed
            return unused

        lax.fori_loop(0, length // 32, norm_own, 0)
        row_sum.sent()

    pl.run_scoped(
        attention,
        pltpu.VMEM((total_len, width), BF16),
        pltpu.VMEM((total_len, wqkv_ref.shape[3]), F32),
        pltpu.VMEM((n_seq, length, width), BF16),
    )
    n2 = over_seq(blocks(n2_ref), lambda: n2_ref.at[s])
    n2.start()
    wu.relay(2)
    wd1.start_x()
    for k in range(1, ny):
        n2.pass_on(k)
        gb_all.pass_on(k)
    wu.relay(3)

    def feed_forward(weight_ref, gate_buf, up_buf, hidden_ref, gb_buf, grad_buf):
        n2.finish()
        for j in range(n_seq):
            n2t_ref[:, j * length : (j + 1) * length] = jnp.transpose(n2_ref[j])
        keep(n2t_ref, n2t_out)
        wd1.relay(1)
        wd1.relay(2)
        wg.finish()
        copies.start(wg_ref, weight_ref).wait()
        weights = (width, ff)

        def gate_rows(j, unused):
            at = pl.ds(pl.multiple_of(j * length, length), length)
            gate_buf[at, :] = product(n2_ref[j], weight_ref[...].reshape(weights))
            return unused

        lax.fori_loop(0, n_seq, gate_rows, 0)
        outs = [copies.start(gate_buf, gate_proj_ref)]
        wd1.relay(3)
        wd2.relay(1)
        own_gb.wait()
        gb_all.finish()
        gb_in = copies.start(gb_all_ref, gb_buf)
        wu.finish()
        copies.start(wu_ref, weight_ref).wait()
        up_out = Rotating(copies)

        def up_copy(j):
            at = pl.ds(pl.multiple_of(j * length, length), length)
            return up_out.copy(j, up_buf.at[j % 2], up_proj_ref.at[at])

        def up_rows(j, unused):
            at = pl.ds(pl.multiple_of(j * length, length), length)

            @pl.when(j >= 2)
            def _():
                up_copy(j - 2).wait()

            up = product(n2_ref[j], weight_ref[...].reshape(weights))
            up_buf[j % 2] = up
            up_copy(j).start()
            gate = gate_buf[at, :]
            hidden_ref[at, :] = (gate * jax.nn.sigmoid(gate) * up).astype(BF16)
            return unused

        lax.fori_loop(0, n_seq, up_rows, 0)
        outs.append(copies.start(hidden_ref, hidden_out_ref))
        gb_in.wait()
        wd2.relay(2)
        grads = gb_buf[...].reshape(total_len, width)
        grad_out = Rotating(copies)

        def grad_copy(i):
            at = pl.ds(pl.multiple_of(i * 256, 256), 256)
            return grad_out.copy(i, grad_buf.at[i % 2], grad_down_ref.at[at])

        def grad_rows(i, unused):
            at = pl.ds(pl.multiple_of(i * 256, 256), 256)

            @pl.when(i >= 2)
            def _():
                grad_copy(i - 2).wait()

            grad_buf[i % 2] = product_rows(hidden_ref[:, at], grads).astype(BF16)
            grad_copy(i).start()
            return unused

        whole = ff // 256
        lax.fori_loop(0, whole, grad_rows, 0)
        up_copy(n_seq - 2).wait()
        up_copy(n_seq - 1).wait()
        grad_copy(whole - 2).wait()
        grad_copy(whole - 1).wait()
        rest = ff - whole * 256
        if rest:
            grad_buf[0, :rest] = product_rows(hidden_ref[:, whole * 256 :], grads).astype(BF16)
            outs.append(
                copies.start(grad_buf.at[0, :rest], grad_down_ref.at[pl.ds(whole * 256, rest)])
            )
        for copy in outs:
            copy.wait()

    pl.run_scoped(
        feed_forward,
        pltpu.VMEM(wg_ref.shape, BF16),
        pltpu.VMEM((total_len, ff), F32),
        pltpu.VMEM((2, length, ff), F32),
        pltpu.VMEM((total_len, ff), BF16),
        pltpu.VMEM((n_seq, length, width), BF16),
        pltpu.VMEM((2, 256, width), BF16),
    )
    wd2.relay(3)
    wd1.finish()
    wd2.finish()
    own_down.wait()
    for copy in late:
        copy.wait()
    wires.close()


def shape_of(dims, kind):
    return jax.ShapeDtypeStruct(dims, kind)


def front(sizes, x, gb, table, gain, qkv, w_out, gate, up, down):
    ny, nc, nz, nx = sizes
    n_seq, n_batch = ny * nc, nz * nx
    length, width = x.shape
    total_len = n_seq * length
    pairs = qkv.shape[2] // 128 - 1
    rows = w_out.shape[0]
    ff = gate.shape[2]
    held = [
        ((n_seq, n_batch, rows, qkv.shape[2]), BF16),
        ((n_batch, rows, width), BF16),
        ((width, total_len), BF16),
        ((width, total_len), BF16),
        ((length, width), F32),
        ((pairs * 128, total_len), BF16),
        ((total_len, pairs * 128), BF16),
        ((total_len, 128), BF16),
        ((2, total_len, 128), F32),
        ((total_len, total_len), BF16),
    ]
    kept = [(HBM, shape_of(*item)) for item in held]
    results = kept[:2]
    results += [
        (HBM, shape_of((n_seq, n_batch, rows, ff), BF16)),
        (HBM, shape_of((n_seq, n_batch, rows, ff), BF16)),
        (HBM, shape_of((n_batch,) + down.shape, BF16)),
        (HBM, shape_of((n_seq, length, width), BF16)),
    ]
    results += kept[2:8]
    results += [(VMEM, shape_of((pairs, 2, total_len), F32))]
    results += kept[8:9]
    results += [(VMEM, shape_of((2, width), F32))]
    results += kept[9:]
    results += [
        (HBM, shape_of((total_len, ff), F32)),
        (HBM, shape_of((total_len, ff), F32)),
        (HBM, shape_of((ff, width), BF16)),
        (HBM, shape_of((total_len, ff), BF16)),
    ]
    seq_copies = ny - 1 + (nc - 1) * ny
    wires = 4 * (n_seq - 1) + 5 * seq_copies + 7 * 16
    return pl.pallas_call(
        functools.partial(front_kernel, sizes, pairs),
        in_specs=[HBM] * 9,
        out_specs=[spec for spec, unused in results],
        out_shape=[kind for unused, kind in results],
        scratch_shapes=[pltpu.VMEM(*item) for item in held]
        + [
            pltpu.VMEM((n_seq, length, width), BF16),
            pltpu.VMEM((n_seq, length, 128), F32),
            pltpu.VMEM((n_seq, n_batch, 8, 128), F32),
            pltpu.VMEM((ny, length, width), BF16),
            pltpu.VMEM((length, width), BF16),
            pltpu.VMEM((length, width), BF16),
            pltpu.VMEM((n_seq, length, width), BF16),
            pltpu.VMEM(down.shape, BF16),
            pltpu.VMEM((2, rows, ff), BF16),
            pltpu.SemaphoreType.DMA((wires,)),
            pltpu.SemaphoreType.DMA((wires,)),
            pltpu.SemaphoreType.DMA((40,)),
        ],
        compiler_params=pltpu.CompilerParams(
            collective_id=0, has_side_effects=True, vmem_limit_bytes=VMEM_BYTES
        ),
        cost_estimate=pl.CostEstimate(
            flops=2 * total_len * width * (qkv.shape[2] + rows * n_batch + 3 * ff),
            bytes_accessed=100 * 1024 * 1024,
            transcendentals=pairs * total_len * total_len,
        ),
    )(x, gb, table, gain, qkv, w_out, gate, up, down)


class LineReduce:
    def __init__(self, wires, place, copies, own, from_x, below, above, stage, x_last=False):
        self.wires, self.place, self.copies, self.own = wires, place, copies, own
        self.from_x, self.below, self.above, self.stage = from_x, below, above, stage
        self.x_last = x_last
        self.x_tickets, self.up, self.down = {}, {}, {}

    def target(self, i):
        z, last = self.place.z, self.place.nz - 1
        low = z < self.place.nz // 2
        return [
            jnp.where(low, last, 0),
            jnp.where(low, last - 1, 1),
            z + 1 - 2 * (z % 2),
            z,
        ][i]

    def across(self):
        return self.place.s, self.place.batch_at(0, 1)

    def send(self, chunk):
        for i in range(self.place.nz):
            self.x_tickets[i] = self.wires.push(
                lambda i=i: chunk(self.target(i)),
                lambda i=i: self.from_x.at[self.target(i)],
                self.across,
            )

    def plan(self, chunk):
        for i in range(self.place.nz):
            self.x_tickets[i] = self.wires.plan(
                lambda i=i: chunk(self.target(i)),
                lambda i=i: self.from_x.at[self.target(i)],
                self.across,
            )

    def any_target(self, i):
        chosen = self.target(0)
        for j in range(1, self.place.nz):
            chosen = jnp.where(i == j, self.target(j), chosen)
        return chosen

    def send_one(self, i, chunk):
        zz = self.any_target(i)
        self.wires.describe(self.x_tickets[0], chunk(zz), self.from_x.at[zz], i).start()

    def take(self, landed, mine):
        self.copies.start(landed, self.stage).wait()
        add_up(mine, [mine, self.stage])

    def add(self, i):
        zz = self.target(i)
        self.wires.wait(self.x_tickets[i], self.from_x.at[zz])
        self.take(self.from_x.at[zz], self.own.at[zz])

    def step(self, k):
        place = self.place
        nz = place.nz
        for side, tickets, landing in ((1, self.up, self.below), (-1, self.down, self.above)):

            def moves(side=side):
                return (place.z <= k - 1) if side > 0 else (place.z >= nz - k)

            def away(side=side):
                return jnp.clip(place.z + side * (nz - k), 0, nz - 1)

            if k > 1:
                behind = (place.z > 0) if side > 0 else (place.z < nz - 1)

                @pl.when(moves() & behind)
                def _():
                    landed = landing.at[k - 2]
                    self.wires.wait(tickets[k - 1], landed)
                    self.take(landed, self.own.at[away()])

            tickets[k] = self.wires.push(
                lambda away=away: self.own.at[away()],
                lambda landing=landing: landing.at[k - 1],
                lambda side=side: (
                    place.s,
                    jnp.clip(place.z + side, 0, nz - 1) * place.nx + place.x,
                ),
                moves,
            )

    def gather_z(self, target):
        place, last = self.place, self.place.nz - 1
        mine = self.own.at[place.z]

        def body(stages):
            def load(ticket, landed, stage):
                self.wires.wait(ticket, landed)
                self.copies.start(landed, stage).wait()

            @pl.when(place.z > 0)
            def _():
                load(self.up[last], self.below.at[last - 1], stages.at[0])

            @pl.when(place.z < last)
            def _():
                load(self.down[last], self.above.at[last - 1], stages.at[1])

            @pl.when(place.z == 0)
            def _():
                add_up(target, [mine, stages.at[1]])

            @pl.when(place.z == last)
            def _():
                add_up(target, [mine, stages.at[0]])

            @pl.when((place.z > 0) & (place.z < last))
            def _():
                add_up(target, [mine, stages.at[0], stages.at[1]])

        pl.run_scoped(body, pltpu.VMEM((2,) + self.stage.shape, BF16))

    def finish(self, target=None):
        mine = self.own.at[self.place.z]
        self.gather_z(mine if target is None else target)
        return mine

    def change(self):
        mine = self.own.at[self.place.z]
        self.gather_z(mine)
        self.x_tickets[0] = self.wires.push(
            lambda: self.own.at[self.place.z, (self.place.x + 1) % 2],
            lambda: self.from_x,
            self.across,
        )

    def close(self, target):
        self.wires.wait(self.x_tickets[0], self.from_x)
        self.copies.start(self.from_x, self.stage.at[0]).wait()
        add_up(target, [self.own.at[self.place.z, self.place.x], self.stage.at[0]])


def norm_back_rows(grad_ref, input_ref, gain, base_ref, target_ref, low_ref):
    rows = 32

    def body(i, unused):
        at = pl.ds(pl.multiple_of(i * rows, rows), rows)
        inputs = input_ref[at, :].astype(F32)
        back = norm_back(grad_ref[at, :], inputs, rms_scale(inputs), gain)
        total = base_ref[at, :].astype(F32) + back
        if target_ref is not None:
            target_ref[at, :] = total
        low_ref[at, :] = total.astype(BF16)
        return unused

    lax.fori_loop(0, grad_ref.shape[0] // rows, body, 0)


def back_kernel(
    sizes,
    pairs,
    gd_ref,
    hidden_ref,
    wd_ref,
    wg_ref,
    wu_ref,
    gate_ref,
    up_ref,
    gb_ref,
    n1t_ref,
    n2t_ref,
    headst_ref,
    residual_ref,
    qr_ref,
    kvr_ref,
    tables_ref,
    bias_ref,
    wqkv_ref,
    wo_ref,
    x_ref,
    lse_ref,
    gains_ref,
    mixed_out,
    tokens_out,
    down_out,
    out_out,
    gate_own,
    up_own,
    qkv_own,
    x_refs,
    below_refs,
    above_refs,
    send_gate,
    send_up,
    da_all_ref,
    own_refs,
    send_out,
    send_qkv,
    stage_refs,
    core_in_ref,
    far_in_ref,
    mixed_core_in,
    mixed_far_in,
    da_own_ref,
    total_ref,
    send_sems,
    recv_sems,
    copy_sems,
):
    place = Place(sizes)
    ny, nc, nz, nx = sizes
    s, b = place.s, place.b
    n_seq, n_batch = ny * nc, nz * nx
    length, width = x_ref.shape
    total_len = n_seq * length
    ff = wg_ref.shape[3]
    rows = wo_ref.shape[1]
    wires = Wires(send_sems, recv_sems)
    copies = Copies(copy_sems)
    s_down, s_rest, s_gate, s_up, s_out, s_qkv = own_refs

    def reduce(i, stage, x_last=False):
        return LineReduce(
            wires,
            place,
            copies,
            own_refs[i],
            x_refs[i],
            below_refs[i],
            above_refs[i],
            stage_refs[stage],
            x_last,
        )

    down, rest = reduce(0, 0), reduce(1, 1, True)
    gate, up = reduce(2, 2), reduce(3, 2)
    out, qkv = reduce(4, 3), reduce(5, 4)
    row_others = [(dy, dc) for dy in range(ny) for dc in range(nc) if dy or dc]

    late = []
    cut = pl.ds(0, BACK_CUT)
    beyond = pl.ds(BACK_CUT, gd_ref.shape[1] - BACK_CUT)
    own_rest = [
        copies.start(gd_ref.at[zz * nx + x, beyond], s_rest.at[zz, x])
        for zz in range(nz)
        for x in range(nx)
    ]
    own_down = [
        copies.start(gd_ref.at[zz * nx + place.x, cut], s_down.at[zz]) for zz in range(nz)
    ]
    place.enter()
    down.send(lambda zz: gd_ref.at[zz * nx + (place.x + 1) % nx, cut])
    for copy in own_rest:
        copy.wait()
    rest.step(1)

    def weight_rows(flipped_ref, grads, k, dx):
        j = place.batch_at(k, dx)
        pieces = []
        for i in range(n_seq):
            start = pl.multiple_of((i * n_batch + j) * rows, rows)
            pieces.append(flipped_ref[pl.ds(start, rows), :])
        value = product(jnp.concatenate(pieces, axis=0), grads)
        return value.astype(BF16).reshape(n_seq, rows, grads.shape[1])

    def feed_forward(dgate_ref, dup_ref, part_ref, flipped, staging):
        flip = copies.start(n2t_ref, flipped)
        row_sum = RowSum(wires, place, part_ref, core_in_ref, far_in_ref)

        def activations(weight1, gate_buf, up_buf, gb_buf):
            load1 = copies.start(wd_ref, weight1)

            base = copies.count
            copies.count += 3

            def load_gb(j):
                return pltpu.make_async_copy(gb_ref.at[j], gb_buf, copy_sems.at[base])

            def load_gate(j):
                at = pl.ds(pl.multiple_of(j * length, length), length)
                return (
                    pltpu.make_async_copy(gate_ref.at[at], gate_buf, copy_sems.at[base + 1]),
                    pltpu.make_async_copy(up_ref.at[at], up_buf, copy_sems.at[base + 2]),
                )

            load_gb(0).start()
            for copy in load_gate(0):
                copy.start()
            load1.wait()

            def rows_back(j, unused):
                load_gb(j).wait()
                grad_hidden = product_cols(gb_buf[...], weight1[...].reshape(ff, width))

                @pl.when(j + 1 < n_seq)
                def _():
                    load_gb(j + 1).start()

                for copy in load_gate(j):
                    copy.wait()
                gate_part, up_part = gate_buf[...], up_buf[...]
                sigma = jax.nn.sigmoid(gate_part)
                activated = gate_part * sigma
                dgate_ref[j] = (
                    grad_hidden * up_part * sigma * (1.0 + gate_part * (1.0 - sigma))
                ).astype(BF16)
                dup_ref[j] = (grad_hidden * activated).astype(BF16)

                @pl.when(j + 1 < n_seq)
                def _():
                    for copy in load_gate(j + 1):
                        copy.start()

                return unused

            lax.fori_loop(0, n_seq, rows_back, 0)
            for copy in own_down:
                copy.wait()

        pl.run_scoped(
            activations,
            pltpu.VMEM(wd_ref.shape, BF16),
            pltpu.VMEM((length, ff), F32),
            pltpu.VMEM((length, ff), F32),
            pltpu.VMEM((length, width), BF16),
        )

        def rows_of(reduce, grads_ref, send_ref):
            chunk = lambda zz: send_ref.at[zz]
            reduce.plan(chunk)
            turns = Rotating(copies)

            def body(i, unused):
                zz = reduce.any_target(i)
                k = (zz - place.z + nz) % nz
                grads = grads_ref[...].reshape(total_len, ff)
                staging[i % 2] = weight_rows(flipped, grads, k, 1)
                turns.copy(i, staging.at[i % 2], chunk(zz)).start()
                reduce.own[zz] = weight_rows(flipped, grads, k, 0)
                turns.copy(i, staging.at[i % 2], chunk(zz)).wait()
                reduce.send_one(i, chunk)
                return unused

            lax.fori_loop(0, nz, body, 0)

        def inputs(weight1, weight2):
            loads = [copies.start(wg_ref, weight1), copies.start(wu_ref, weight2)]
            flip.wait()
            rows_of(gate, dgate_ref, send_gate)
            rest.step(2)
            down.add(0)
            down.step(1)
            for load in loads:
                load.wait()

            def input_part(j):
                return product_cols(
                    dgate_ref[j], weight1[...].reshape(width, ff)
                ) + product_cols(dup_ref[j], weight2[...].reshape(width, ff))

            row_sum.compute(input_part)

        pl.run_scoped(inputs, pltpu.VMEM(wg_ref.shape, BF16), pltpu.VMEM(wg_ref.shape, BF16))
        rest.step(3)
        down.add(1)
        down.step(2)
        rows_of(up, dup_ref, send_up)
        down.add(2)
        down.step(3)
        down.add(3)

        def normed(residual_buf, gb_buf):
            loads = [
                copies.start(residual_ref, residual_buf),
                copies.start(gb_ref.at[s], gb_buf),
            ]
            for copy in loads:
                copy.wait()
            for h in range(2):
                at = row_sum.half(h)
                row_sum.finish_half(h, total_ref)
                norm_back_rows(
                    total_ref.at[at],
                    residual_buf.at[at],
                    gains_ref[1:2, :],
                    gb_buf.at[at],
                    total_ref.at[at],
                    da_own_ref.at[at],
                )
                da[h].start()
            row_sum.sent()

        pl.run_scoped(normed, pltpu.VMEM((length, width), F32), pltpu.VMEM((length, width), BF16))
        gate.add(0)
        gate.step(1)
        gate.add(1)
        gate.step(2)
        rest.change()
        gate.add(2)
        gate.step(3)

    own_da = []
    half = length // 2

    def da_gather(h):
        at = pl.ds(h * half, half)
        return Gather(
            wires,
            lambda j: da_all_ref.at[j, at],
            lambda: da_own_ref.at[at],
            ny,
            nc,
            place.seq_at,
            lambda j: (j, b),
        )

    da = [da_gather(0), da_gather(1)]
    pl.run_scoped(
        feed_forward,
        pltpu.VMEM((n_seq, length, ff), BF16),
        pltpu.VMEM((n_seq, length, ff), BF16),
        pltpu.VMEM((n_seq, length, width), BF16),
        pltpu.VMEM(n2t_ref.shape, BF16),
        pltpu.VMEM((2, n_seq, rows, ff), BF16),
    )
    own_da.append(copies.start(da_own_ref, da_all_ref.at[s]))
    for k in range(1, ny):
        for piece in da:
            piece.pass_on(k)

    def attention(
        da_buf,
        wo_buf,
        wqkv_buf,
        qr_buf,
        headst_buf,
        do_buf,
        kvr_buf,
        tables_buf,
        bias_buf,
        dqkv_buf,
        n1t_buf,
        dq_buf,
        dk_buf,
        dv_buf,
        part_ref,
    ):
        loads = [
            copies.start(source, target)
            for source, target in [
                (wo_ref, wo_buf),
                (headst_ref, headst_buf),
                (qr_ref, qr_buf),
                (kvr_ref, kvr_buf),
                (tables_ref, tables_buf),
                (bias_ref, bias_buf),
                (n1t_ref, n1t_buf),
                (wqkv_ref, wqkv_buf),
            ]
        ]
        gate.add(3)
        for piece in da:
            piece.finish()
        own_da[0].wait()
        copies.start(da_all_ref, da_buf).wait()
        for load in loads:
            load.wait()
        out_weights = wo_buf[...].reshape(n_batch * rows, width)

        def heads_back(j, unused):
            at = pl.ds(pl.multiple_of(j * length, length), length)
            do_buf[at, :] = product_cols(da_buf[j], out_weights).astype(BF16)
            return unused

        lax.fori_loop(0, n_seq, heads_back, 0)
        branch = da_buf[...].reshape(total_len, width)

        def out_rows(dx):
            pieces = []
            for zz in range(nz):
                start = pl.multiple_of((zz * nx + (place.x + dx) % nx) * rows, rows)
                pieces.append(headst_buf[pl.ds(start, rows), :])
            value = product(jnp.concatenate(pieces, axis=0), branch)
            return value.astype(BF16).reshape(nz, rows, width)

        send_out[...] = out_rows(1)
        out.send(lambda zz: send_out.at[zz])
        s_out[...] = out_rows(0)
        dk_buf[...] = jnp.zeros_like(dk_buf)
        dv_buf[...] = jnp.zeros_like(dv_buf)

        def pair_back(pair, unused):
            at = pl.ds(pl.multiple_of(pair * 128, 128), 128)
            low = (qr_buf[:, at] * SCALE).astype(BF16)
            grads_pair = do_buf[:, at]
            for start in range(0, total_len, length):
                stop = start + length
                outs = []
                for head in range(2):
                    lanes = slice(head * HEAD_DIM, (head + 1) * HEAD_DIM)
                    queries = low[start:stop, lanes]
                    grads = grads_pair[start:stop, lanes]
                    keys = kvr_buf[:stop, :HEAD_DIM]
                    values = kvr_buf[:stop, HEAD_DIM:]
                    scores = product_cols(keys, queries)
                    scores = scores + bias_buf[:stop, start:stop].astype(F32)
                    probs = jnp.exp(scores - lse_ref[pair, head : head + 1, start:stop])
                    dprobs = product_cols(values, grads)
                    delta = jnp.sum(probs * dprobs, axis=0, keepdims=True)
                    dscores = (probs * (dprobs - delta)).astype(BF16)
                    dv_buf[:stop, :] += product(probs.astype(BF16), grads)
                    dk_buf[:stop, :] += product(dscores, queries)
                    outs.append(product_rows(dscores, keys) * SCALE)
                dq_buf[start:stop, :] = jnp.concatenate(outs, axis=1)
            dq = dq_buf[...]
            turned = rotate_lanes(dq * tables_buf[1], -1.0)
            dqkv_buf[:, at] = (dq * tables_buf[0] + turned).astype(BF16)
            return unused

        def pair_and_sums(pair, unused):
            pair_back(pair, unused)

            @pl.when(pair == 0)
            def _():
                up.add(0)
                up.step(1)

            @pl.when(pair == 2)
            def _():
                up.add(1)
                up.step(2)

            return unused

        lax.fori_loop(0, pairs, pair_and_sums, 0)
        grads = jnp.concatenate([dk_buf[...], dv_buf[...]], axis=1)
        back = grads * tables_buf[0] + rotate_lanes(grads * tables_buf[1], -1.0)
        lane = lax.broadcasted_iota(jnp.int32, grads.shape, 1)
        dqkv_buf[:, pairs * 128 :] = jnp.where(lane < HEAD_DIM, back, grads).astype(BF16)

        row_sum = RowSum(wires, place, part_ref, core_in_ref, far_in_ref)
        in_weights = wqkv_buf[...].reshape(width, wqkv_ref.shape[3])

        def input_part(j):
            at = pl.ds(pl.multiple_of(j * length, length), length)
            return product_cols(dqkv_buf[at, :], in_weights)

        row_sum.compute(input_part)

        def qkv_rows(zz, unused):
            k = (zz - place.z + nz) % nz
            send_qkv[zz] = weight_rows(n1t_buf, dqkv_buf[...], k, 1)
            s_qkv[zz] = weight_rows(n1t_buf, dqkv_buf[...], k, 0)
            return unused

        lax.fori_loop(0, nz, qkv_rows, 0)
        qkv.send(lambda zz: send_qkv.at[zz])
        up.add(2)
        up.step(3)
        up.add(3)
        out.add(0)
        out.step(1)

        def last(grad_ref, x_buf, tokens_ref):
            load = copies.start(x_ref, x_buf)
            row_sum.finish(grad_ref)
            load.wait()
            norm_back_rows(grad_ref, x_buf, gains_ref[0:1, :], total_ref, None, tokens_ref)
            copies.start(tokens_ref, tokens_out).wait()

        row = pltpu.VMEM((length, width), BF16)
        pl.run_scoped(last, pltpu.VMEM((length, width), F32), row, row)
        row_sum.sent()

    pl.run_scoped(
        attention,
        pltpu.VMEM((n_seq, length, width), BF16),
        pltpu.VMEM(wo_ref.shape, BF16),
        pltpu.VMEM(wqkv_ref.shape, BF16),
        pltpu.VMEM(qr_ref.shape, BF16),
        pltpu.VMEM(headst_ref.shape, BF16),
        pltpu.VMEM(qr_ref.shape, BF16),
        pltpu.VMEM(kvr_ref.shape, BF16),
        pltpu.VMEM(tables_ref.shape, F32),
        pltpu.VMEM(bias_ref.shape, BF16),
        pltpu.VMEM((total_len, (pairs + 1) * 128), BF16),
        pltpu.VMEM(n1t_ref.shape, BF16),
        pltpu.VMEM((total_len, 128), F32),
        pltpu.VMEM((total_len, HEAD_DIM), F32),
        pltpu.VMEM((total_len, HEAD_DIM), F32),
        pltpu.VMEM((n_seq, length, width), BF16),
    )

    exchanges = []

    def exchange(reduce, target):
        mine = reduce.finish()
        copy = copies.start(mine.at[s], target.at[s])
        tickets = {}
        for away in row_others:
            tickets[away] = wires.push(
                lambda away=away: reduce.own.at[place.z, place.seq_at(*away)],
                lambda: target.at[s],
                lambda away=away: (place.seq_at(*away), b),
            )
        exchanges.append((copy, target, tickets))

    def layer_out(weight_buf, hidden_buf, part_ref, mixed_total, mixed_ref, down_own, out_own):
        loads = [
            copies.start(wd_ref, weight_buf),
            copies.start(hidden_ref, hidden_buf),
            copies.start(residual_ref, mixed_total),
        ]
        out.add(1)
        out.step(2)
        for load in loads:
            load.wait()

        def mixed_part(j):
            at = pl.ds(pl.multiple_of(j * length, length), length)
            return product(hidden_buf[at, :], weight_buf[...].reshape(ff, width))

        row_sum = RowSum(wires, place, part_ref, mixed_core_in, mixed_far_in)
        row_sum.compute(mixed_part)
        out.add(2)
        out.step(3)
        out.add(3)
        qkv.add(0)
        qkv.step(1)
        exchange(gate, gate_own)
        down.finish(down_own.at[cut])
        rest.close(down_own.at[beyond])
        late.append(copies.start(down_own, down_out))
        qkv.add(1)
        qkv.step(2)
        exchange(up, up_own)
        out.finish(out_own)
        late.append(copies.start(out_own, out_out))
        qkv.add(2)
        qkv.step(3)
        qkv.add(3)
        row_sum.finish(mixed_ref, [mixed_total])
        late.append(copies.start(mixed_ref, mixed_out))
        exchange(qkv, qkv_own)
        row_sum.sent()
        for copy in late:
            copy.wait()

    pl.run_scoped(
        layer_out,
        pltpu.VMEM(wd_ref.shape, BF16),
        pltpu.VMEM(hidden_ref.shape, BF16),
        pltpu.VMEM((n_seq, length, width), BF16),
        pltpu.VMEM((length, width), F32),
        pltpu.VMEM((length, width), BF16),
        pltpu.VMEM(gd_ref.shape[1:], F32),
        pltpu.VMEM((rows, width), F32),
    )

    for copy, target, tickets in exchanges:
        copy.wait()
        for (dy, dc), ticket in tickets.items():
            wires.wait(ticket, target.at[place.seq_at(-dy, -dc)])
    wires.close()


def grouped_back_kernel(sizes, pairs, *refs):
    refs = list(refs)
    groups = []
    at = 21 + 7
    for count in (6, 6, 6):
        groups.append(refs[at : at + count])
        at += count
    singles = refs[at : at + 3]
    at += 3
    own = refs[at : at + 6]
    at += 6
    sends = refs[at : at + 2]
    at += 2
    stages = refs[at : at + 5]
    at += 5
    back_kernel(
        sizes, pairs, *refs[:28], *groups, *singles, own, *sends, stages, *refs[at:]
    )


def back(sizes, gd, hidden, wd, wg, wu, gate, up, gb, n1t, n2t, headst, residual, qr, kvr, tables, bias, wqkv, wo, x, lse, gains):
    ny, nc, nz, nx = sizes
    n_seq, n_batch = ny * nc, nz * nx
    length, width = x.shape
    ff = wg.shape[3]
    rows = wo.shape[1]
    pairs = qr.shape[1] // 128
    chunk_down = (BACK_CUT, width)
    chunk_rest = (gd.shape[1] - BACK_CUT, width)
    chunk_gate = (n_seq, rows, ff)
    chunk_out = (rows, width)
    chunk_qkv = (n_seq, rows, wqkv.shape[3])
    pair_rest = (nx,) + chunk_rest
    chunks = [chunk_down, pair_rest, chunk_gate, chunk_gate, chunk_out, chunk_qkv]
    results = [
        (HBM, shape_of((length, width), BF16)),
        (HBM, shape_of((length, width), BF16)),
        (HBM, shape_of(gd.shape[1:], F32)),
        (HBM, shape_of(chunk_out, F32)),
        (HBM, shape_of(chunk_gate, BF16)),
        (HBM, shape_of(chunk_gate, BF16)),
        (HBM, shape_of(chunk_qkv, BF16)),
    ]
    landings = [
        [shape_of((nz,) + chunk, BF16) for chunk in chunks],
        [shape_of((nz - 1,) + chunk, BF16) for chunk in chunks],
        [shape_of((nz - 1,) + chunk, BF16) for chunk in chunks],
    ]
    landings[0][1] = shape_of(chunk_rest, BF16)
    for group in landings:
        results += [(HBM, kind) for kind in group]
    results += [(HBM, shape_of((nz,) + chunk_gate, BF16))] * 2
    results += [(HBM, shape_of((n_seq, length, width), BF16))]
    wires = len(chunks) * (nz + 2 * (nz - 1)) + 3 * 4 + 6 + 3 * (n_seq - 1)
    row = pltpu.VMEM((length, width), BF16)
    return pl.pallas_call(
        functools.partial(grouped_back_kernel, sizes, pairs),
        in_specs=[HBM] * 19 + [VMEM] * 2,
        out_specs=[spec for spec, unused in results],
        out_shape=[kind for unused, kind in results],
        scratch_shapes=[pltpu.VMEM((nz,) + chunk, BF16) for chunk in chunks]
        + [
            pltpu.VMEM((nz,) + chunk_out, BF16),
            pltpu.VMEM((nz,) + chunk_qkv, BF16),
            pltpu.VMEM(chunk_down, BF16),
            pltpu.VMEM(pair_rest, BF16),
            pltpu.VMEM(chunk_gate, BF16),
            pltpu.VMEM(chunk_out, BF16),
            pltpu.VMEM(chunk_qkv, BF16),
            pltpu.VMEM((ny, length, width), BF16),
            row,
            pltpu.VMEM((ny, length, width), BF16),
            row,
            row,
            pltpu.VMEM((length, width), F32),
            pltpu.SemaphoreType.DMA((wires,)),
            pltpu.SemaphoreType.DMA((wires,)),
            pltpu.SemaphoreType.DMA((140,)),
        ],
        compiler_params=pltpu.CompilerParams(
            collective_id=1, has_side_effects=True, vmem_limit_bytes=VMEM_BYTES
        ),
        cost_estimate=pl.CostEstimate(
            flops=12 * n_seq * length * width * ff,
            bytes_accessed=100 * 1024 * 1024,
            transcendentals=pairs * (n_seq * length) ** 2,
        ),
    )(gd, hidden, wd, wg, wu, gate, up, gb, n1t, n2t, headst, residual, qr, kvr, tables, bias, wqkv, wo, x, lse, gains)


def by_permutes(
    tokens,
    cotangent,
    selection,
    segments,
    positions,
    gain_attn,
    w_query,
    w_key,
    w_value,
    w_out,
    gain_mlp,
    w_gate,
    w_up,
    w_down,
):
    seq = Axis("seq", 2)
    batch = Axis("batch", lax.axis_size("batch") // 4)
    n_seq, n_batch = seq.size, batch.size
    length, width = tokens.shape[1], tokens.shape[2]
    total_len = length * n_seq
    rows = w_query.shape[0]
    ff = w_gate.shape[1]
    q_cols = w_query.shape[1] // n_seq
    sharers = n_seq // KV_HEADS

    query_parts = w_query.reshape(rows, n_seq, q_cols)
    key_parts = jnp.repeat(w_key.reshape(rows, KV_HEADS, HEAD_DIM), sharers, axis=1)
    value_parts = jnp.repeat(w_value.reshape(rows, KV_HEADS, HEAD_DIM), sharers, axis=1)
    qkv_parts = jnp.concatenate([query_parts, key_parts, value_parts], axis=2).transpose(1, 0, 2)

    def spread(parts):
        mine = seq.exchange(parts)
        return batch.gather(mine, 1).reshape(n_seq * n_batch * rows, parts.shape[2])

    def collect(grad):
        parts = grad.astype(BF16).reshape(n_seq, n_batch, rows, grad.shape[1])
        return seq.exchange(batch.scatter_sum(parts, 1).astype(BF16)).astype(F32)

    def by_columns(weight):
        return weight.reshape(rows, n_seq, weight.shape[1] // n_seq).transpose(1, 0, 2)

    places = seq.gather(jnp.stack([segments[0], positions[0]]), 1)
    seg_all = places[0].reshape(total_len)
    pos_all = places[1].reshape(total_len)
    gains = batch.gather(seq.gather(jnp.stack([gain_attn, gain_mlp]), 1), 2)
    gain_one = gains[0].reshape(1, width).astype(F32)
    gain_two = gains[1].reshape(1, width).astype(F32)
    x_all = seq.gather(tokens[0], 0).reshape(total_len, width).astype(F32)
    w_qkv = spread(qkv_parts)
    wo = batch.gather(w_out, 0).reshape(n_batch * rows, width)
    wg = spread(by_columns(w_gate))
    wu = spread(by_columns(w_up))
    wd = batch.gather(w_down, 0).reshape(n_batch * w_down.shape[0], width)

    grad_out_row = cotangent[0].astype(F32) * selection[0].astype(F32)[:, None]
    grad_low = seq.gather(grad_out_row.astype(BF16), 0).reshape(total_len, width)

    row_input = tokens[0].astype(F32)
    inv_attn = rms_scale(row_input)
    normed1 = (x_all * rms_scale(x_all) * gain_one).astype(BF16)
    qkv = product(normed1, w_qkv)
    frequency = 10000.0 ** (-(jnp.arange(HALF, dtype=F32) * 2.0 / HEAD_DIM))
    angles = pos_all.astype(F32)[:, None] * jnp.tile(frequency, 4)[None, :]
    cosine, sine = jnp.cos(angles), jnp.sin(angles)
    seg_row, seg_col = seg_all[None, :], seg_all[:, None]
    heads_out, query_rot, kv_rot, lse = attend(qkv, cosine, sine, seg_row, seg_col)
    attn_part = product(heads_out, wo).astype(BF16).reshape(n_seq, length, width)
    residual = row_input + seq.scatter_sum(attn_part, 0)

    inv_mlp = rms_scale(residual)
    normed2_own = (residual * inv_mlp * gain_two).astype(BF16)
    normed2 = seq.gather(normed2_own, 0).reshape(total_len, width)
    gate_proj = product(normed2, wg)
    up_proj = product(normed2, wu)
    sigma = jax.nn.sigmoid(gate_proj)
    activated = gate_proj * sigma
    hidden = (activated * up_proj).astype(BF16)
    mixed_part = product(hidden, wd).astype(BF16).reshape(n_seq, length, width)
    mixed = (residual + seq.scatter_sum(mixed_part, 0)).astype(BF16)[None]

    grad_down = product_rows(hidden, grad_low)
    grad_hidden = product_cols(grad_low, wd)
    grad_gate_act = (
        grad_hidden * up_proj * sigma * (1.0 + gate_proj * (1.0 - sigma))
    ).astype(BF16)
    grad_up_act = (grad_hidden * activated).astype(BF16)
    grad_gate = product_rows(normed2, grad_gate_act)
    grad_up = product_rows(normed2, grad_up_act)
    normed_part = product_cols(grad_gate_act, wg) + product_cols(grad_up_act, wu)
    normed_terms = seq.scatter_sum(normed_part.astype(BF16).reshape(n_seq, length, width), 0)
    grad_resid = grad_out_row + norm_back(normed_terms, residual, inv_mlp, gain_two)

    down_own = batch.scatter_sum(
        grad_down.astype(BF16).reshape(n_batch, w_down.shape[0], width), 0
    )
    gate_own = collect(grad_gate).transpose(1, 0, 2).reshape(rows, ff)
    up_own = collect(grad_up).transpose(1, 0, 2).reshape(rows, ff)

    grad_branch = seq.gather(grad_resid.astype(BF16), 0).reshape(total_len, width)
    grad_wout = product_rows(heads_out, grad_branch)
    grad_heads = product_cols(grad_branch, wo).astype(BF16)
    grad_qkv_act = attend_back(
        query_rot, kv_rot, grad_heads, lse, cosine, sine, seg_row, seg_col
    )
    grad_wqkv = product_rows(normed1, grad_qkv_act)
    input_part = product_cols(grad_qkv_act, w_qkv).astype(BF16).reshape(n_seq, length, width)
    grad_normed1 = seq.scatter_sum(input_part, 0)
    tokens_grad = (
        grad_resid + norm_back(grad_normed1, row_input, inv_attn, gain_one)
    ).astype(BF16)[None]
    out_own = batch.scatter_sum(grad_wout.astype(BF16).reshape(n_batch, rows, width), 0)
    qkv_own = collect(grad_wqkv)
    query_own = qkv_own[:, :, :q_cols].transpose(1, 0, 2).reshape(rows, n_seq * q_cols)

    def shared(columns):
        heads = columns.reshape(KV_HEADS, sharers, rows, HEAD_DIM).sum(axis=1)
        return heads.transpose(1, 0, 2).reshape(rows, KV_HEADS * HEAD_DIM)

    key_own = shared(qkv_own[:, :, q_cols : q_cols + HEAD_DIM])
    value_own = shared(qkv_own[:, :, q_cols + HEAD_DIM :])

    def along(weight, grad):
        return jnp.sum(weight.astype(F32) * grad, axis=1)

    gain1_own = (
        along(w_query, query_own) + along(w_key, key_own) + along(w_value, value_own)
    ) / gain_attn.astype(F32)
    gain2_own = (along(w_gate, gate_own) + along(w_up, up_own)) / gain_mlp.astype(F32)
    return (
        mixed,
        tokens_grad,
        query_own,
        key_own,
        value_own,
        out_own,
        gate_own,
        up_own,
        down_own,
        gain1_own,
        gain2_own,
    )


def by_kernels(
    tokens,
    cotangent,
    selection,
    segments,
    positions,
    gain_attn,
    w_query,
    w_key,
    w_value,
    w_out,
    gain_mlp,
    w_gate,
    w_up,
    w_down,
):
    sizes = mesh_sizes()
    n_seq, n_batch = sizes[0] * sizes[1], sizes[2] * sizes[3]
    length, width = tokens.shape[1], tokens.shape[2]
    rows, ff = w_gate.shape
    q_cols = w_query.shape[1] // n_seq

    def by_columns(weight):
        return weight.reshape(rows, n_seq, weight.shape[1] // n_seq).transpose(1, 0, 2)

    qkv_parts = jnp.concatenate([by_columns(w) for w in (w_query, w_key, w_value)], axis=2)
    grad_low = (cotangent[0].astype(F32) * selection[0].astype(F32)[:, None]).astype(BF16)
    frequency = 10000.0 ** (-(jnp.arange(HALF, dtype=F32) * 2.0 / HEAD_DIM))
    angles = positions[0].astype(F32)[:, None] * frequency[None, :]
    documents = jnp.broadcast_to(segments[0].astype(F32)[:, None], (length, 128 - HEAD_DIM))
    table = jnp.concatenate([jnp.cos(angles), jnp.sin(angles), documents], axis=1)
    gain_tile = jnp.pad(
        jnp.stack([gain_attn, gain_mlp]).astype(F32), ((0, 6), (0, 128 - gain_attn.shape[0]))
    )
    (
        w_qkv,
        wo,
        wg,
        wu,
        wd,
        gb_all,
        n1t,
        n2t,
        residual,
        headst,
        query_rot,
        kv_rot,
        lse,
        rotary,
        gains,
        bias,
        gate_proj,
        up_proj,
        grad_down,
        hidden,
    ) = front(
        sizes,
        tokens[0],
        grad_low,
        table,
        gain_tile,
        qkv_parts,
        w_out,
        by_columns(w_gate),
        by_columns(w_up),
        w_down,
    )
    mixed, tokens_grad, down_own, out_own, gate_part, up_part, qkv_part = back(
        sizes,
        grad_down.reshape(n_batch, w_down.shape[0], width),
        hidden,
        wd,
        wg,
        wu,
        gate_proj,
        up_proj,
        gb_all,
        n1t,
        n2t,
        headst,
        residual,
        query_rot,
        kv_rot,
        rotary,
        bias,
        w_qkv,
        wo,
        tokens[0],
        lse,
        gains,
    )[:7]

    def by_rows(part):
        return part.astype(F32).transpose(1, 0, 2).reshape(rows, n_seq * part.shape[2])

    query_own = by_rows(qkv_part[:, :, :q_cols])
    key_own = by_rows(qkv_part[:, :, q_cols : q_cols + HEAD_DIM])
    value_own = by_rows(qkv_part[:, :, q_cols + HEAD_DIM :])
    gate_own, up_own = by_rows(gate_part), by_rows(up_part)

    def along(weight, grad):
        return jnp.sum(weight.astype(F32) * grad, axis=1)

    gain1_own = (
        along(w_query, query_own) + along(w_key, key_own) + along(w_value, value_own)
    ) / gain_attn.astype(F32)
    gain2_own = (along(w_gate, gate_own) + along(w_up, up_own)) / gain_mlp.astype(F32)
    return (
        mixed[None],
        tokens_grad[None],
        query_own,
        key_own,
        value_own,
        out_own,
        gate_own,
        up_own,
        down_own,
        gain1_own,
        gain2_own,
    )


def mesh_sizes():
    return (lax.axis_size("seq") // 2, 2, 4, lax.axis_size("batch") // 4)


def per_device(*args):
    fits = mesh_sizes() == (2, 2, 4, 2) and args[0].shape[1:] == (256, 2048)
    return (by_kernels if fits else by_permutes)(*args)


def solution(mesh):
    both = ("seq", "batch")
    tokens = P("batch", "seq", None)
    flags = P("batch", "seq")
    matrix = P(both, None)
    vector = P(both)
    in_specs = (
        (tokens, tokens, flags, flags, flags)
        + (vector, matrix, matrix, matrix, matrix)
        + (vector, matrix, matrix, matrix)
    )
    out_specs = (tokens, tokens) + (matrix,) * 7 + (vector, vector)
    return jax.shard_map(
        per_device, mesh=mesh, in_specs=in_specs, out_specs=out_specs, check_vma=False
    )
```

```python
import functools

import jax
import jax.numpy as jnp
from jax import lax
from jax.experimental import pallas as pl
from jax.experimental.pallas import tpu as pltpu
from jax.sharding import PartitionSpec as P

HEADS = 32
KV_HEADS = 4
HEAD_DIM = 64
HALF = HEAD_DIM // 2

EPSILON = 1e-05
MASKED_SCORE = -1e30
SCALE = HEAD_DIM ** (-0.5)
CONTRACT_ROWS = (((0,), (0,)), ((), ()))
CONTRACT_COLS = (((1,), (1,)), ((), ()))
BF16 = jnp.bfloat16
F32 = jnp.float32


def product(left, right):
    return jnp.dot(left, right, preferred_element_type=F32)


def product_rows(left, right):
    return lax.dot_general(left, right, CONTRACT_ROWS, preferred_element_type=F32)


def product_cols(left, right):
    return lax.dot_general(left, right, CONTRACT_COLS, preferred_element_type=F32)


def rms_scale(inputs):
    return lax.rsqrt(jnp.mean(inputs * inputs, axis=-1, keepdims=True) + EPSILON)


def norm_back(grad_normed, inputs, inverse, gain):
    scaled = gain * grad_normed
    cubed = inverse * inverse * inverse
    return inverse * scaled - inputs * cubed * jnp.mean(scaled * inputs, axis=-1, keepdims=True)


class Axis:
    def __init__(self, name, inner):
        self.name = name
        self.size = lax.axis_size(name)
        self.inner = inner
        self.outer = self.size // inner
        index = lax.axis_index(name)
        self.index = index
        self.o = index // inner
        self.i = index % inner

    def shift(self, value, outer_by, inner_by):
        pairs = []
        for o in range(self.outer):
            for i in range(self.inner):
                target = ((o + outer_by) % self.outer) * self.inner + (i + inner_by) % self.inner
                pairs.append((o * self.inner + i, target))
        return lax.ppermute(value, self.name, pairs)

    def before(self, outer_by, inner_by):
        o = lax.rem(self.o + self.outer - outer_by, self.outer)
        i = lax.rem(self.i + self.inner - inner_by, self.inner)
        return o * self.inner + i

    def after(self, outer_by, inner_by):
        o = lax.rem(self.o + outer_by, self.outer)
        i = lax.rem(self.i + inner_by, self.inner)
        return o * self.inner + i

    def gather(self, block, dim=0):
        shape = block.shape[:dim] + (self.size,) + block.shape[dim:]
        out = jnp.zeros(shape, block.dtype)
        for k in range(self.outer):
            got = block if k == 0 else self.shift(block, k, 0)
            for m in range(self.inner):
                piece = got if m == 0 else self.shift(got, 0, m)
                out = lax.dynamic_update_slice_in_dim(
                    out, jnp.expand_dims(piece, dim), self.before(k, m), dim
                )
        return out

    def scatter_sum(self, parts, dim=0):
        shape = parts.shape[:dim] + (self.outer, self.inner) + parts.shape[dim + 1 :]
        grid = parts.reshape(shape)

        def inner_part(i):
            return lax.squeeze(lax.dynamic_slice_in_dim(grid, i, 1, dim + 1), (dim + 1,))

        total = inner_part(self.i).astype(F32)
        for m in range(1, self.inner):
            mine = inner_part(lax.rem(self.i + m, self.inner))
            total = total + self.shift(mine, 0, m).astype(F32)
        low = total.astype(BF16)

        def outer_part(o):
            return lax.squeeze(lax.dynamic_slice_in_dim(low, o, 1, dim), (dim,))

        out = outer_part(self.o).astype(F32)
        for k in range(1, self.outer):
            out = out + self.shift(outer_part(lax.rem(self.o + k, self.outer)), k, 0).astype(F32)
        return out

    def exchange(self, parts):
        out = jnp.zeros(parts.shape, parts.dtype)
        for k in range(self.outer):
            for m in range(self.inner):
                part = lax.dynamic_slice_in_dim(parts, self.after(k, m), 1, 0)
                got = part if (k, m) == (0, 0) else self.shift(part, k, m)
                out = lax.dynamic_update_slice_in_dim(out, got, self.before(k, m), 0)
        return out


def rotate_lanes(value, sign):
    lane = lax.broadcasted_iota(jnp.int32, value.shape, 1) % HEAD_DIM
    first = lane < HALF
    width = value.shape[1]
    up = pltpu.roll(value, width - HALF, 1)
    down = pltpu.roll(value, HALF, 1)
    return jnp.where(first, -sign * up, sign * down)


def mask_bias(bias_ref, seg_row_ref, seg_col_ref, length):
    rows = 256
    for start in range(0, length, rows):
        keys = seg_col_ref[start : start + rows, :]
        queries = seg_row_ref[:, :]
        key_pos = start + lax.broadcasted_iota(jnp.int32, (rows, length), 0)
        query_pos = lax.broadcasted_iota(jnp.int32, (rows, length), 1)
        allowed = (keys == queries) & (key_pos <= query_pos)
        bias_ref[start : start + rows, :] = jnp.where(allowed, 0.0, MASKED_SCORE)


def attend_kernel(
    qblock,
    q_ref,
    kv_ref,
    cos_ref,
    sin_ref,
    seg_row_ref,
    seg_col_ref,
    o_ref,
    qr_ref,
    kvr_ref,
    lse_ref,
    bias_ref,
):
    length = q_ref.shape[0]
    cosine = cos_ref[...]
    sine = sin_ref[...]

    @pl.when(pl.program_id(0) == 0)
    def _():
        mask_bias(bias_ref, seg_row_ref, seg_col_ref, length)
        kv = kv_ref[...]
        rotated = kv * cosine + rotate_lanes(kv, 1.0) * sine
        lane = lax.broadcasted_iota(jnp.int32, kv.shape, 1)
        kvr_ref[...] = jnp.where(lane < HEAD_DIM, rotated, kv).astype(BF16)

    q = q_ref[...]
    qr_ref[...] = (q * cosine + rotate_lanes(q, 1.0) * sine).astype(BF16)
    for start in range(0, length, qblock):
        stop = start + qblock
        keys = kvr_ref[:stop, :HEAD_DIM]
        values = kvr_ref[:stop, HEAD_DIM:]
        for head in range(2):
            lanes = slice(head * HEAD_DIM, (head + 1) * HEAD_DIM)
            queries = qr_ref[start:stop, lanes] * SCALE
            scores = product_cols(keys, queries.astype(BF16)) + bias_ref[:stop, start:stop]
            top = jnp.max(scores, axis=0, keepdims=True)
            grown = jnp.exp(scores - top)
            total = jnp.sum(grown, axis=0, keepdims=True)
            probs = (grown * (1.0 / total)).astype(BF16)
            lse_ref[0, head : head + 1, start:stop] = top + jnp.log(total)
            o_ref[start:stop, lanes] = product_rows(probs, values).astype(BF16)


def attend_back_kernel(
    qblock,
    qr_ref,
    kvr_ref,
    do_ref,
    lse_ref,
    cos_ref,
    sin_ref,
    seg_row_ref,
    seg_col_ref,
    dqkv_ref,
    bias_ref,
    dq_ref,
    dk_ref,
    dv_ref,
):
    length = qr_ref.shape[0]
    cosine = cos_ref[...]
    sine = sin_ref[...]
    pair = pl.program_id(0)

    @pl.when(pair == 0)
    def _():
        mask_bias(bias_ref, seg_row_ref, seg_col_ref, length)
        dk_ref[...] = jnp.zeros_like(dk_ref)
        dv_ref[...] = jnp.zeros_like(dv_ref)

    for start in range(0, length, qblock):
        stop = start + qblock
        keys = kvr_ref[:stop, :HEAD_DIM]
        values = kvr_ref[:stop, HEAD_DIM:]
        for head in range(2):
            lanes = slice(head * HEAD_DIM, (head + 1) * HEAD_DIM)
            queries = (qr_ref[start:stop, lanes] * SCALE).astype(BF16)
            grads = do_ref[start:stop, lanes]
            scores = product_cols(keys, queries) + bias_ref[:stop, start:stop]
            probs = jnp.exp(scores - lse_ref[0, head : head + 1, start:stop])
            dprobs = product_cols(values, grads)
            delta = jnp.sum(probs * dprobs, axis=0, keepdims=True)
            dscores = (probs * (dprobs - delta)).astype(BF16)
            dv_ref[:stop, :] += product(probs.astype(BF16), grads)
            dk_ref[:stop, :] += product(dscores, queries)
            dq_ref[start:stop, lanes] = product_rows(dscores, keys) * SCALE

    dq = dq_ref[...]
    turned = rotate_lanes(dq * sine, -1.0)
    columns = pl.ds(pl.multiple_of(pair * 128, 128), 128)
    dqkv_ref[:, columns] = (dq * cosine + turned).astype(BF16)

    @pl.when(pair == pl.num_programs(0) - 1)
    def _():
        grads = jnp.concatenate([dk_ref[...], dv_ref[...]], axis=1)
        back = grads * cosine + rotate_lanes(grads * sine, -1.0)
        lane = lax.broadcasted_iota(jnp.int32, grads.shape, 1)
        width = dqkv_ref.shape[1]
        dqkv_ref[:, width - 128 :] = jnp.where(lane < HEAD_DIM, back, grads).astype(BF16)


def whole_spec(shape):
    return pl.BlockSpec(shape, lambda j: (0,) * len(shape))


def attend(qkv, cosine, sine, seg_row, seg_col):
    length, width = qkv.shape
    pairs = width // 128 - 1
    qblock = min(256, length)
    return pl.pallas_call(
        functools.partial(attend_kernel, qblock),
        grid=(pairs,),
        in_specs=[
            pl.BlockSpec((length, 128), lambda j: (0, j)),
            pl.BlockSpec((length, 128), lambda j: (0, pairs)),
            whole_spec((length, 128)),
            whole_spec((length, 128)),
            whole_spec((1, length)),
            whole_spec((length, 1)),
        ],
        out_specs=[
            pl.BlockSpec((length, 128), lambda j: (0, j)),
            pl.BlockSpec((length, 128), lambda j: (0, j)),
            whole_spec((length, 128)),
            pl.BlockSpec((1, 2, length), lambda j: (j, 0, 0)),
        ],
        out_shape=[
            jax.ShapeDtypeStruct((length, pairs * 128), BF16),
            jax.ShapeDtypeStruct((length, pairs * 128), BF16),
            jax.ShapeDtypeStruct((length, 128), BF16),
            jax.ShapeDtypeStruct((pairs, 2, length), F32),
        ],
        scratch_shapes=[pltpu.VMEM((length, length), F32)],
        compiler_params=pltpu.CompilerParams(vmem_limit_bytes=48 * 1024 * 1024),
        cost_estimate=pl.CostEstimate(
            flops=pairs * 2 * length * length * HEAD_DIM * 2,
            bytes_accessed=8 * length * width,
            transcendentals=pairs * length * length,
        ),
    )(qkv, qkv, cosine, sine, seg_row, seg_col)


def attend_back(qr, kvr, grads, lse, cosine, sine, seg_row, seg_col):
    length = qr.shape[0]
    pairs = qr.shape[1] // 128
    qblock = min(256, length)
    return pl.pallas_call(
        functools.partial(attend_back_kernel, qblock),
        grid=(pairs,),
        in_specs=[
            pl.BlockSpec((length, 128), lambda j: (0, j)),
            whole_spec((length, 128)),
            pl.BlockSpec((length, 128), lambda j: (0, j)),
            pl.BlockSpec((1, 2, length), lambda j: (j, 0, 0)),
            whole_spec((length, 128)),
            whole_spec((length, 128)),
            whole_spec((1, length)),
            whole_spec((length, 1)),
        ],
        out_specs=whole_spec((length, (pairs + 1) * 128)),
        out_shape=jax.ShapeDtypeStruct((length, (pairs + 1) * 128), BF16),
        scratch_shapes=[
            pltpu.VMEM((length, length), F32),
            pltpu.VMEM((length, 128), F32),
            pltpu.VMEM((length, HEAD_DIM), F32),
            pltpu.VMEM((length, HEAD_DIM), F32),
        ],
        compiler_params=pltpu.CompilerParams(vmem_limit_bytes=48 * 1024 * 1024),
        cost_estimate=pl.CostEstimate(
            flops=pairs * 5 * length * length * HEAD_DIM * 2,
            bytes_accessed=12 * length * qr.shape[1],
            transcendentals=pairs * length * length,
        ),
    )(qr, kvr, grads, lse, cosine, sine, seg_row, seg_col)


MESH = pl.DeviceIdType.MESH
HBM = pl.BlockSpec(memory_space=pl.ANY)
VMEM = pl.BlockSpec(memory_space=pltpu.VMEM)
VMEM_BYTES = 62 * 1024 * 1024
STEP = 16
DOWN_CUT = 64
BACK_CUT = 96


class Place:
    def __init__(self, sizes):
        self.ny, self.nc, self.nz, self.nx = sizes
        self.s = lax.axis_index("seq")
        self.b = lax.axis_index("batch")
        self.y, self.c = self.s // self.nc, self.s % self.nc
        self.z, self.x = self.b // self.nx, self.b % self.nx

    def seq_at(self, dy, dc):
        return (self.y + dy + self.ny) % self.ny * self.nc + (self.c + dc + self.nc) % self.nc

    def z_at(self, dz):
        return (self.z + dz + self.nz) % self.nz

    def batch_at(self, dz, dx):
        return self.z_at(dz) * self.nx + (self.x + dx + self.nx) % self.nx

    def enter(self):
        peers = [
            (self.seq_at(dy, dc), self.b)
            for dy in range(self.ny)
            for dc in range(self.nc)
            if (dy, dc) != (0, 0)
        ]
        peers += [(self.s, self.batch_at(k, 0)) for k in range(1, self.nz)]
        peers += [(self.s, self.batch_at(0, m)) for m in range(1, self.nx)]
        barrier = pltpu.get_barrier_semaphore()
        for peer in peers:
            pl.semaphore_signal(barrier, inc=1, device_id=peer, device_id_type=MESH)
        pl.semaphore_wait(barrier, len(peers))


def only(when, action):
    if when is None:
        action()
    else:
        pl.when(when())(action)


class Wires:
    def __init__(self, send_sems, recv_sems):
        self.send_sems, self.recv_sems = send_sems, recv_sems
        self.ends = []
        self.open = []

    def describe(self, index, source, target, step=0):
        return pltpu.make_async_remote_copy(
            src_ref=source,
            dst_ref=target,
            send_sem=self.send_sems.at[index + step],
            recv_sem=self.recv_sems.at[index + step],
            device_id=self.ends[index][2](),
            device_id_type=MESH,
        )

    def plan(self, source, target, device, when=None):
        index = len(self.ends)
        self.ends.append((source, target, device, when))
        self.open.append(index)
        return index

    def push(self, source, target, device, when=None):
        index = self.plan(source, target, device, when)
        only(when, lambda: self.describe(index, source(), target()).start())
        return index

    def wait(self, index, landed):
        self.describe(index, landed, landed).wait_recv()

    def sent(self, index):
        self.open.remove(index)
        source, target, unused, when = self.ends[index]
        only(when, lambda: self.describe(index, source(), target()).wait_send())

    def close(self):
        for index in list(self.open):
            self.sent(index)


class Copies:
    def __init__(self, sems):
        self.sems = sems
        self.count = 0

    def start(self, source, target):
        copy = Copy(self, self.count, source, target)
        self.count += 1
        copy.describe().start()
        return copy


class Copy:
    def __init__(self, copies, index, source, target):
        self.copies, self.index, self.source, self.target = copies, index, source, target

    def describe(self):
        sem = self.copies.sems.at[self.index]
        return pltpu.make_async_copy(self.source, self.target, sem)

    def wait(self):
        self.describe().wait()


class Through:
    def __init__(self, copies, source, buffer, target):
        self.copies, self.buffer, self.target = copies, buffer, target
        self.copy = copies.start(source, buffer)

    def turn(self):
        self.copy.wait()
        self.copy = self.copies.start(self.buffer, self.target)

    def wait(self):
        self.copy.wait()


class Gather:
    def __init__(self, wires, slot, own, outer, inner, at, device):
        self.wires, self.slot, self.own = wires, slot, own
        self.outer, self.inner, self.at, self.device = outer, inner, at, device
        self.first, self.second = {}, {}

    def push(self, source, target, k, m):
        return self.wires.push(source, target, lambda: self.device(self.at(k, m)))

    def start(self):
        mine = lambda: self.slot(self.at(0, 0))
        for k in range(1, self.outer):
            self.first[k] = self.push(self.own, mine, k, 0)
        for m in range(1, self.inner):
            self.second[0, m] = self.push(self.own, mine, 0, m)

    def pass_on(self, k):
        came = lambda: self.slot(self.at(-k, 0))
        self.wires.wait(self.first[k], came())
        for m in range(1, self.inner):
            self.second[k, m] = self.push(came, came, 0, m)

    def finish(self):
        for (k, m), ticket in self.second.items():
            self.wires.wait(ticket, self.slot(self.at(-k, -m)))


class LineGather:
    def __init__(self, wires, place, slot, own, x_first=False):
        self.wires, self.place, self.slot, self.own, self.x_first = wires, place, slot, own, x_first
        self.up, self.down, self.across = {}, {}, {}

    def at(self, dz, dx):
        place = self.place
        zz = jnp.clip(place.z + dz, 0, place.nz - 1)
        return self.slot(zz * place.nx + (place.x + dx) % place.nx)

    def below(self, k):
        return self.place.z >= k

    def above(self, k):
        return self.place.z + k < self.place.nz

    def push(self, source, dz, dx, when=None):
        place = self.place
        return self.wires.push(
            source[0],
            source[1],
            lambda: (
                place.s,
                jnp.clip(place.z + dz, 0, place.nz - 1) * place.nx + (place.x + dx) % place.nx,
            ),
            when,
        )

    def spread(self, source, dx):
        self.up[dx, 1] = self.push(source, 1, 0, lambda: self.above(1))
        self.down[dx, 1] = self.push(source, -1, 0, lambda: self.below(1))

    def start_x(self):
        self.across[0] = self.push((self.own, lambda: self.at(0, 0)), 0, 1)

    def start_z(self):
        self.spread((self.own, lambda: self.at(0, 0)), 0)

    def cross(self):
        came = lambda: self.at(0, 1)
        self.wires.wait(self.across[0], came())
        self.spread((came, came), 1)

    def relay(self, k):
        last = k + 1 == self.place.nz
        for dx in (0, 1) if self.x_first else (0,):
            for side, table, here, on in (
                (-1, self.up, self.below, self.above),
                (1, self.down, self.above, self.below),
            ):
                pl.when(here(k))(
                    lambda: self.wires.wait(table[dx, k], self.at(side * k, dx))
                )
                if not last:
                    table[dx, k + 1] = self.push(
                        self.fixed(side * k, dx),
                        -side,
                        0,
                        lambda here=here, on=on: here(k) & on(1),
                    )
                if not self.x_first:
                    self.across[side * k] = self.push(
                        self.fixed(side * k, dx), 0, 1, lambda here=here: here(k)
                    )

    def fixed(self, dz, dx):
        came = lambda: self.at(dz, dx)
        return came, came

    def finish(self):
        if self.x_first:
            return
        self.wires.wait(self.across[0], self.at(0, 1))
        for k in range(1, self.place.nz):
            pl.when(self.below(k))(
                lambda: self.wires.wait(self.across[-k], self.at(-k, 1))
            )
            pl.when(self.above(k))(
                lambda: self.wires.wait(self.across[k], self.at(k, 1))
            )


class RowSum:
    def __init__(self, wires, place, part_ref, core_in, far_in):
        self.wires, self.place = wires, place
        self.part_ref, self.core_in, self.far_in = part_ref, core_in, far_in
        self.tickets = {}

    def slot(self, t):
        return self.place.seq_at((3 - t) // 2, (t + 1) % 2)

    def push(self, t, source, target, dy, dc):
        self.tickets[t] = self.wires.push(
            lambda: self.part_ref.at[source],
            lambda: target(),
            lambda: (self.place.seq_at(dy, dc), self.place.b),
        )

    def half(self, h):
        rows = self.far_in.shape[0] // 2
        return pl.ds(h * rows, rows)

    def push_half(self, h):
        self.tickets[1, h] = self.wires.push(
            lambda: self.part_ref.at[1, self.half(h)],
            lambda: self.far_in.at[self.half(h)],
            lambda: (self.place.seq_at(1, 0), self.place.b),
        )

    def compute(self, part):
        def body(t, unused):
            self.part_ref[t] = part(self.slot(t)).astype(BF16)

            @pl.when(t == 0)
            def _():
                self.push(0, 0, lambda: self.core_in.at[1], 0, 1)

            @pl.when(t == 1)
            def _():
                self.wires.wait(self.tickets[0], self.core_in.at[1])
                mine = self.part_ref.at[1]
                add_up(mine, [mine, self.core_in.at[1]])
                for h in range(2):
                    self.push_half(h)

            @pl.when(t == 2)
            def _():
                self.push(2, 2, lambda: self.core_in.at[0], 0, 1)

            return unused

        lax.fori_loop(0, 4, body, 0)

    def finish_half(self, h, target):
        if h == 0:
            self.wires.wait(self.tickets[2], self.core_in.at[0])
        at = self.half(h)
        self.wires.wait(self.tickets[1, h], self.far_in.at[at])
        add_up(
            target.at[at], [self.part_ref.at[3, at], self.core_in.at[0, at], self.far_in.at[at]]
        )

    def finish(self, target, extra=()):
        self.wires.wait(self.tickets[2], self.core_in.at[0])
        for h in range(2):
            self.wires.wait(self.tickets[1, h], self.far_in.at[self.half(h)])
        add_up(target, [self.part_ref.at[3], self.core_in.at[0], self.far_in] + list(extra))

    def sent(self):
        for ticket in self.tickets.values():
            self.wires.sent(ticket)


class Rotating:
    def __init__(self, copies):
        self.sems, self.base = copies.sems, copies.count
        copies.count += 2

    def copy(self, i, source, target):
        return pltpu.make_async_copy(source, target, self.sems.at[self.base + i % 2])


def add_up(target, sources):
    shape = target.shape
    rows = 2 * STEP if shape[-2] % (2 * STEP) == 0 else STEP
    steps = shape[-2] // rows
    low = len(sources) == 2 and all(ref.dtype == BF16 for ref in [target] + sources)

    def body(i, unused):
        at = pl.ds(pl.multiple_of(i % steps * rows, rows), rows)
        where = (at, slice(None)) if len(shape) == 2 else (i // steps, at, slice(None))
        if low:
            target[where] = sources[0][where] + sources[1][where]
        else:
            total = sources[0][where].astype(F32)
            for source in sources[1:]:
                total = total + source[where].astype(F32)
            target[where] = total.astype(target.dtype)
        return unused

    lax.fori_loop(0, steps * (1 if len(shape) == 2 else shape[0]), body, 0)


def front_kernel(
    sizes,
    pairs,
    x_ref,
    gb_ref,
    table_ref,
    gain_ref,
    qkv_ref,
    out_ref,
    gate_ref,
    up_ref,
    down_ref,
    wqkv_out,
    wo_out,
    wg_ref,
    wu_ref,
    wd_ref,
    gb_all_ref,
    n1t_out,
    n2t_out,
    residual_out,
    headst_out,
    qr_out,
    kvr_out,
    lse_ref,
    tables_out,
    gains_ref,
    bias_out,
    gate_proj_ref,
    up_proj_ref,
    grad_down_ref,
    hidden_out_ref,
    wqkv_ref,
    wo_ref,
    n1t_ref,
    n2t_ref,
    residual_ref,
    headst_ref,
    qr_ref,
    kvr_ref,
    tables_ref,
    bias_ref,
    x_all_ref,
    table_all_ref,
    gain_all_ref,
    core_in_ref,
    far_in_ref,
    own_gb_ref,
    n2_ref,
    own_down_ref,
    own_gate_ref,
    send_sems,
    recv_sems,
    copy_sems,
):
    place = Place(sizes)
    ny, nc, nz, nx = sizes
    s, b = place.s, place.b
    n_seq, n_batch = ny * nc, nz * nx
    length, width = x_ref.shape
    total_len = n_seq * length
    ff = gate_ref.shape[2]
    wires = Wires(send_sems, recv_sems)
    copies = Copies(copy_sems)
    row_others = [(dy, dc) for dy in range(ny) for dc in range(nc) if dy or dc]

    def over_batch(slot, own, x_first=False):
        return LineGather(wires, place, slot, own, x_first)

    def over_seq(slot, own):
        return Gather(wires, slot, own, ny, nc, place.seq_at, lambda j: (j, b))

    def columns(ref):
        return lambda j: ref.at[:, j]

    def blocks(ref):
        return lambda j: ref.at[j]

    class Exchange:
        def __init__(self, parts, target, many=True, own=None):
            self.target = target
            part = (lambda j: parts.at[j]) if many else (lambda j: parts)
            self.copy = own or copies.start(part(s), target.at[s, b])
            self.tickets = {}
            for away in row_others:
                self.tickets[away] = wires.push(
                    lambda away=away: part(place.seq_at(*away)),
                    lambda: target.at[s, b],
                    lambda away=away: (place.seq_at(*away), b),
                )

        def finish(self):
            self.copy.wait()
            for (dy, dc), ticket in self.tickets.items():
                wires.wait(ticket, self.target.at[place.seq_at(-dy, -dc), b])

    late = []

    def keep(source, target):
        late.append(copies.start(source, target))

    own_gb = Through(copies, gb_ref, own_gb_ref, gb_all_ref.at[s])
    own_down = Through(copies, down_ref, own_down_ref, wd_ref.at[b])
    own_gate = Through(copies, gate_ref.at[s], own_gate_ref.at[0], wg_ref.at[s, b])
    own_up = Through(copies, up_ref.at[s], own_gate_ref.at[1], wu_ref.at[s, b])
    own_table = copies.start(table_ref, table_all_ref.at[s])
    own_x = copies.start(x_ref, x_all_ref.at[s])
    own_out = copies.start(out_ref, wo_ref.at[b])
    place.enter()
    qkv_parts = Exchange(qkv_ref, wqkv_ref)
    gain_parts = Exchange(gain_ref, gain_all_ref, many=False)
    for copy in (own_gate, own_up, own_down, own_gb):
        copy.turn()
    wo = over_batch(blocks(wo_ref), lambda: out_ref)
    wo.start_x()
    wo.start_z()
    table_all = over_seq(blocks(table_all_ref), lambda: table_ref)
    table_all.start()
    gate_parts = Exchange(gate_ref, wg_ref, own=own_gate)
    x_all = over_seq(blocks(x_all_ref), lambda: x_ref)
    x_all.start()
    up_parts = Exchange(up_ref, wu_ref, own=own_up)
    wqkv = over_batch(columns(wqkv_ref), lambda: wqkv_ref.at[:, b])
    gains = over_batch(columns(gain_all_ref), lambda: gain_all_ref.at[:, b])
    wg = over_batch(columns(wg_ref), lambda: wg_ref.at[:, b])
    wu = over_batch(columns(wu_ref), lambda: wu_ref.at[:, b])
    cut = pl.ds(0, DOWN_CUT)
    rest = pl.ds(DOWN_CUT, down_ref.shape[0] - DOWN_CUT)
    wd1 = over_batch(lambda j: wd_ref.at[j, cut], lambda: down_ref.at[cut])
    wd2 = over_batch(lambda j: wd_ref.at[j, rest], lambda: down_ref.at[rest], True)
    gb_all = over_seq(blocks(gb_all_ref), lambda: gb_ref)

    qkv_parts.finish()
    wqkv.start_x()
    wqkv.start_z()
    gain_parts.finish()
    gains.start_x()
    gains.start_z()
    wo.relay(1)
    gains.relay(1)
    gate_parts.finish()
    wg.start_x()
    wqkv.relay(1)
    wg.start_z()
    wo.relay(2)
    gains.relay(2)
    wqkv.relay(2)
    for k in range(1, ny):
        table_all.pass_on(k)
        x_all.pass_on(k)
    wo.relay(3)
    gains.relay(3)
    wqkv.relay(3)
    up_parts.finish()
    wu.start_x()
    wd2.start_x()
    wu.start_z()
    gb_all.start()

    def attention(n1_ref, qkv_proj_ref, part_ref):
        own_table.wait()
        table_all.finish()
        own_x.wait()
        x_all.finish()
        gains.finish()
        rows = width // (n_seq * n_batch)
        for g in range(2):
            gains_ref[g : g + 1, :] = jnp.concatenate(
                [gain_all_ref[i, j, g : g + 1, :rows] for i in range(n_seq) for j in range(n_batch)],
                axis=1,
            )
        gain_one = gains_ref[0:1, :]
        half = length // 2

        def norm_rows(i, unused):
            part = x_all_ref[i // 2, pl.ds(i % 2 * half, half), :].astype(F32)
            at = pl.ds(pl.multiple_of(i * half, half), half)
            n1_ref[at, :] = (part * rms_scale(part) * gain_one).astype(BF16)
            return unused

        lax.fori_loop(0, 2 * n_seq, norm_rows, 0)
        for j in range(n_seq):
            at = slice(j * length, (j + 1) * length)
            table = table_all_ref[j]
            cos_part, sin_part = table[:, :HALF], table[:, HALF:HEAD_DIM]
            tables_ref[0, at, :] = jnp.concatenate([cos_part] * 4, axis=1)
            tables_ref[1, at, :] = jnp.concatenate([sin_part] * 4, axis=1)
        flipped = [
            jnp.transpose(table_all_ref[j])[HEAD_DIM : HEAD_DIM + 1, :] for j in range(n_seq)
        ]
        query_seg = jnp.concatenate(flipped, axis=1)
        for j in range(n_seq):
            key_seg = table_all_ref[j][:, HEAD_DIM : HEAD_DIM + 1]
            key_pos = j * length + lax.broadcasted_iota(jnp.int32, (length, total_len), 0)
            query_pos = lax.broadcasted_iota(jnp.int32, (length, total_len), 1)
            allowed = (key_seg == query_seg) & (key_pos <= query_pos)
            bias_ref[j * length : (j + 1) * length, :] = jnp.where(
                allowed, 0.0, MASKED_SCORE
            ).astype(BF16)
        keep(tables_ref, tables_out)
        keep(bias_ref, bias_out)

        wqkv.finish()
        keep(wqkv_ref, wqkv_out)
        weights = wqkv_ref[...].reshape(width, wqkv_ref.shape[3])

        def project(i, unused):
            at = pl.ds(pl.multiple_of(i * length, length), length)
            qkv_proj_ref[at, :] = product(n1_ref[at, :], weights)
            return unused

        lax.fori_loop(0, n_seq, project, 0)
        kv = qkv_proj_ref[:, pairs * 128 :]
        lane = lax.broadcasted_iota(jnp.int32, kv.shape, 1)
        rotated = kv * tables_ref[0] + rotate_lanes(kv, 1.0) * tables_ref[1]
        kvr_ref[...] = jnp.where(lane < HEAD_DIM, rotated, kv).astype(BF16)

        def attend_pair(pair, unused):
            at = pl.ds(pl.multiple_of(pair * 128, 128), 128)
            q = qkv_proj_ref[:, at]
            qr = (q * tables_ref[0] + rotate_lanes(q, 1.0) * tables_ref[1]).astype(BF16)
            qr_ref[:, at] = qr
            low = (qr * SCALE).astype(BF16)
            for start in range(0, total_len, length):
                stop = start + length
                outs = []
                for head in range(2):
                    queries = low[start:stop, head * HEAD_DIM : (head + 1) * HEAD_DIM]
                    scores = product_cols(kvr_ref[:stop, :HEAD_DIM], queries)
                    scores = scores + bias_ref[:stop, start:stop].astype(F32)
                    top = jnp.max(scores, axis=0, keepdims=True)
                    grown = jnp.exp(scores - top)
                    total = jnp.sum(grown, axis=0, keepdims=True)
                    probs = (grown * (1.0 / total)).astype(BF16)
                    lse_ref[pair, head : head + 1, start:stop] = top + jnp.log(total)
                    outs.append(product_rows(probs, kvr_ref[:stop, HEAD_DIM:]))
                headst_ref[at, start:stop] = jnp.transpose(
                    jnp.concatenate(outs, axis=1).astype(BF16)
                )
            return unused

        wg.relay(1)

        def attend_and_relay(pair, unused):
            attend_pair(pair, unused)

            @pl.when(pair == 2)
            def _():
                wg.relay(2)

            return unused

        lax.fori_loop(0, pairs, attend_and_relay, 0)

        keep(headst_ref, headst_out)
        keep(qr_ref, qr_out)
        keep(kvr_ref, kvr_out)

        own_out.wait()
        wo.finish()
        keep(wo_ref, wo_out)
        out_weights = wo_ref[...].reshape(n_batch * wo_ref.shape[1], width)

        def out_part(j):
            at = pl.ds(pl.multiple_of(j * length, length), length)
            return product_rows(headst_ref[:, at], out_weights)

        row_sum = RowSum(wires, place, part_ref, core_in_ref, far_in_ref)
        row_sum.compute(out_part)
        wg.relay(3)

        def flip_rows(i, unused):
            at = pl.ds(pl.multiple_of(i * length, length), length)
            n1t_ref[:, at] = jnp.transpose(n1_ref[at, :])
            return unused

        lax.fori_loop(0, n_seq, flip_rows, 0)
        keep(n1t_ref, n1t_out)
        wu.relay(1)
        wd1.start_z()
        wd2.start_z()
        wd2.cross()
        row_sum.finish(residual_ref, [x_all_ref.at[s]])
        keep(residual_ref, residual_out)

        def norm_own(i, unused):
            at = pl.ds(pl.multiple_of(i * 32, 32), 32)
            total = residual_ref[at, :]
            normed = (total * rms_scale(total) * gains_ref[1:2, :]).astype(BF16)
            n2_ref[s, at, :] = normed
            return unused

        lax.fori_loop(0, length // 32, norm_own, 0)
        row_sum.sent()

    pl.run_scoped(
        attention,
        pltpu.VMEM((total_len, width), BF16),
        pltpu.VMEM((total_len, wqkv_ref.shape[3]), F32),
        pltpu.VMEM((n_seq, length, width), BF16),
    )
    n2 = over_seq(blocks(n2_ref), lambda: n2_ref.at[s])
    n2.start()
    wu.relay(2)
    wd1.start_x()
    for k in range(1, ny):
        n2.pass_on(k)
        gb_all.pass_on(k)
    wu.relay(3)

    def feed_forward(weight_ref, gate_buf, up_buf, hidden_ref, gb_buf, grad_buf):
        n2.finish()
        for j in range(n_seq):
            n2t_ref[:, j * length : (j + 1) * length] = jnp.transpose(n2_ref[j])
        keep(n2t_ref, n2t_out)
        wd1.relay(1)
        wd1.relay(2)
        wg.finish()
        copies.start(wg_ref, weight_ref).wait()
        weights = (width, ff)

        def gate_rows(j, unused):
            at = pl.ds(pl.multiple_of(j * length, length), length)
            gate_buf[at, :] = product(n2_ref[j], weight_ref[...].reshape(weights))
            return unused

        lax.fori_loop(0, n_seq, gate_rows, 0)
        outs = [copies.start(gate_buf, gate_proj_ref)]
        wd1.relay(3)
        wd2.relay(1)
        own_gb.wait()
        gb_all.finish()
        gb_in = copies.start(gb_all_ref, gb_buf)
        wu.finish()
        copies.start(wu_ref, weight_ref).wait()
        up_out = Rotating(copies)

        def up_copy(j):
            at = pl.ds(pl.multiple_of(j * length, length), length)
            return up_out.copy(j, up_buf.at[j % 2], up_proj_ref.at[at])

        def up_rows(j, unused):
            at = pl.ds(pl.multiple_of(j * length, length), length)

            @pl.when(j >= 2)
            def _():
                up_copy(j - 2).wait()

            up = product(n2_ref[j], weight_ref[...].reshape(weights))
            up_buf[j % 2] = up
            up_copy(j).start()
            gate = gate_buf[at, :]
            hidden_ref[at, :] = (gate * jax.nn.sigmoid(gate) * up).astype(BF16)
            return unused

        lax.fori_loop(0, n_seq, up_rows, 0)
        outs.append(copies.start(hidden_ref, hidden_out_ref))
        gb_in.wait()
        wd2.relay(2)
        grads = gb_buf[...].reshape(total_len, width)
        grad_out = Rotating(copies)

        def grad_copy(i):
            at = pl.ds(pl.multiple_of(i * 256, 256), 256)
            return grad_out.copy(i, grad_buf.at[i % 2], grad_down_ref.at[at])

        def grad_rows(i, unused):
            at = pl.ds(pl.multiple_of(i * 256, 256), 256)

            @pl.when(i >= 2)
            def _():
                grad_copy(i - 2).wait()

            grad_buf[i % 2] = product_rows(hidden_ref[:, at], grads).astype(BF16)
            grad_copy(i).start()
            return unused

        whole = ff // 256
        lax.fori_loop(0, whole, grad_rows, 0)
        up_copy(n_seq - 2).wait()
        up_copy(n_seq - 1).wait()
        grad_copy(whole - 2).wait()
        grad_copy(whole - 1).wait()
        rest = ff - whole * 256
        if rest:
            grad_buf[0, :rest] = product_rows(hidden_ref[:, whole * 256 :], grads).astype(BF16)
            outs.append(
                copies.start(grad_buf.at[0, :rest], grad_down_ref.at[pl.ds(whole * 256, rest)])
            )
        for copy in outs:
            copy.wait()

    pl.run_scoped(
        feed_forward,
        pltpu.VMEM(wg_ref.shape, BF16),
        pltpu.VMEM((total_len, ff), F32),
        pltpu.VMEM((2, length, ff), F32),
        pltpu.VMEM((total_len, ff), BF16),
        pltpu.VMEM((n_seq, length, width), BF16),
        pltpu.VMEM((2, 256, width), BF16),
    )
    wd2.relay(3)
    wd1.finish()
    wd2.finish()
    own_down.wait()
    for copy in late:
        copy.wait()
    wires.close()


def shape_of(dims, kind):
    return jax.ShapeDtypeStruct(dims, kind)


def front(sizes, x, gb, table, gain, qkv, w_out, gate, up, down):
    ny, nc, nz, nx = sizes
    n_seq, n_batch = ny * nc, nz * nx
    length, width = x.shape
    total_len = n_seq * length
    pairs = qkv.shape[2] // 128 - 1
    rows = w_out.shape[0]
    ff = gate.shape[2]
    held = [
        ((n_seq, n_batch, rows, qkv.shape[2]), BF16),
        ((n_batch, rows, width), BF16),
        ((width, total_len), BF16),
        ((width, total_len), BF16),
        ((length, width), F32),
        ((pairs * 128, total_len), BF16),
        ((total_len, pairs * 128), BF16),
        ((total_len, 128), BF16),
        ((2, total_len, 128), F32),
        ((total_len, total_len), BF16),
    ]
    kept = [(HBM, shape_of(*item)) for item in held]
    results = kept[:2]
    results += [
        (HBM, shape_of((n_seq, n_batch, rows, ff), BF16)),
        (HBM, shape_of((n_seq, n_batch, rows, ff), BF16)),
        (HBM, shape_of((n_batch,) + down.shape, BF16)),
        (HBM, shape_of((n_seq, length, width), BF16)),
    ]
    results += kept[2:8]
    results += [(VMEM, shape_of((pairs, 2, total_len), F32))]
    results += kept[8:9]
    results += [(VMEM, shape_of((2, width), F32))]
    results += kept[9:]
    results += [
        (HBM, shape_of((total_len, ff), F32)),
        (HBM, shape_of((total_len, ff), F32)),
        (HBM, shape_of((ff, width), BF16)),
        (HBM, shape_of((total_len, ff), BF16)),
    ]
    seq_copies = ny - 1 + (nc - 1) * ny
    wires = 4 * (n_seq - 1) + 5 * seq_copies + 7 * 16
    return pl.pallas_call(
        functools.partial(front_kernel, sizes, pairs),
        in_specs=[HBM] * 9,
        out_specs=[spec for spec, unused in results],
        out_shape=[kind for unused, kind in results],
        scratch_shapes=[pltpu.VMEM(*item) for item in held]
        + [
            pltpu.VMEM((n_seq, length, width), BF16),
            pltpu.VMEM((n_seq, length, 128), F32),
            pltpu.VMEM((n_seq, n_batch, 8, 128), F32),
            pltpu.VMEM((ny, length, width), BF16),
            pltpu.VMEM((length, width), BF16),
            pltpu.VMEM((length, width), BF16),
            pltpu.VMEM((n_seq, length, width), BF16),
            pltpu.VMEM(down.shape, BF16),
            pltpu.VMEM((2, rows, ff), BF16),
            pltpu.SemaphoreType.DMA((wires,)),
            pltpu.SemaphoreType.DMA((wires,)),
            pltpu.SemaphoreType.DMA((40,)),
        ],
        compiler_params=pltpu.CompilerParams(
            collective_id=0, has_side_effects=True, vmem_limit_bytes=VMEM_BYTES
        ),
        cost_estimate=pl.CostEstimate(
            flops=2 * total_len * width * (qkv.shape[2] + rows * n_batch + 3 * ff),
            bytes_accessed=100 * 1024 * 1024,
            transcendentals=pairs * total_len * total_len,
        ),
    )(x, gb, table, gain, qkv, w_out, gate, up, down)


class LineReduce:
    def __init__(self, wires, place, copies, own, from_x, below, above, stage, x_last=False):
        self.wires, self.place, self.copies, self.own = wires, place, copies, own
        self.from_x, self.below, self.above, self.stage = from_x, below, above, stage
        self.x_last = x_last
        self.x_tickets, self.up, self.down = {}, {}, {}

    def target(self, i):
        z, last = self.place.z, self.place.nz - 1
        low = z < self.place.nz // 2
        return [
            jnp.where(low, last, 0),
            jnp.where(low, last - 1, 1),
            z + 1 - 2 * (z % 2),
            z,
        ][i]

    def across(self):
        return self.place.s, self.place.batch_at(0, 1)

    def send(self, chunk):
        for i in range(self.place.nz):
            self.x_tickets[i] = self.wires.push(
                lambda i=i: chunk(self.target(i)),
                lambda i=i: self.from_x.at[self.target(i)],
                self.across,
            )

    def plan(self, chunk):
        for i in range(self.place.nz):
            self.x_tickets[i] = self.wires.plan(
                lambda i=i: chunk(self.target(i)),
                lambda i=i: self.from_x.at[self.target(i)],
                self.across,
            )

    def any_target(self, i):
        chosen = self.target(0)
        for j in range(1, self.place.nz):
            chosen = jnp.where(i == j, self.target(j), chosen)
        return chosen

    def send_one(self, i, chunk):
        zz = self.any_target(i)
        self.wires.describe(self.x_tickets[0], chunk(zz), self.from_x.at[zz], i).start()

    def take(self, landed, mine):
        self.copies.start(landed, self.stage).wait()
        add_up(mine, [mine, self.stage])

    def add(self, i):
        zz = self.target(i)
        self.wires.wait(self.x_tickets[i], self.from_x.at[zz])
        self.take(self.from_x.at[zz], self.own.at[zz])

    def step(self, k):
        place = self.place
        nz = place.nz
        for side, tickets, landing in ((1, self.up, self.below), (-1, self.down, self.above)):

            def moves(side=side):
                return (place.z <= k - 1) if side > 0 else (place.z >= nz - k)

            def away(side=side):
                return jnp.clip(place.z + side * (nz - k), 0, nz - 1)

            if k > 1:
                behind = (place.z > 0) if side > 0 else (place.z < nz - 1)

                @pl.when(moves() & behind)
                def _():
                    landed = landing.at[k - 2]
                    self.wires.wait(tickets[k - 1], landed)
                    self.take(landed, self.own.at[away()])

            tickets[k] = self.wires.push(
                lambda away=away: self.own.at[away()],
                lambda landing=landing: landing.at[k - 1],
                lambda side=side: (
                    place.s,
                    jnp.clip(place.z + side, 0, nz - 1) * place.nx + place.x,
                ),
                moves,
            )

    def gather_z(self, target):
        place, last = self.place, self.place.nz - 1
        mine = self.own.at[place.z]

        def body(stages):
            def load(ticket, landed, stage):
                self.wires.wait(ticket, landed)
                self.copies.start(landed, stage).wait()

            @pl.when(place.z > 0)
            def _():
                load(self.up[last], self.below.at[last - 1], stages.at[0])

            @pl.when(place.z < last)
            def _():
                load(self.down[last], self.above.at[last - 1], stages.at[1])

            @pl.when(place.z == 0)
            def _():
                add_up(target, [mine, stages.at[1]])

            @pl.when(place.z == last)
            def _():
                add_up(target, [mine, stages.at[0]])

            @pl.when((place.z > 0) & (place.z < last))
            def _():
                add_up(target, [mine, stages.at[0], stages.at[1]])

        pl.run_scoped(body, pltpu.VMEM((2,) + self.stage.shape, BF16))

    def finish(self, target=None):
        mine = self.own.at[self.place.z]
        self.gather_z(mine if target is None else target)
        return mine

    def change(self):
        mine = self.own.at[self.place.z]
        self.gather_z(mine)
        self.x_tickets[0] = self.wires.push(
            lambda: self.own.at[self.place.z, (self.place.x + 1) % 2],
            lambda: self.from_x,
            self.across,
        )

    def close(self, target):
        self.wires.wait(self.x_tickets[0], self.from_x)
        self.copies.start(self.from_x, self.stage.at[0]).wait()
        add_up(target, [self.own.at[self.place.z, self.place.x], self.stage.at[0]])


def norm_back_rows(grad_ref, input_ref, gain, base_ref, target_ref, low_ref):
    rows = 32

    def body(i, unused):
        at = pl.ds(pl.multiple_of(i * rows, rows), rows)
        inputs = input_ref[at, :].astype(F32)
        back = norm_back(grad_ref[at, :], inputs, rms_scale(inputs), gain)
        total = base_ref[at, :].astype(F32) + back
        if target_ref is not None:
            target_ref[at, :] = total
        low_ref[at, :] = total.astype(BF16)
        return unused

    lax.fori_loop(0, grad_ref.shape[0] // rows, body, 0)


def back_kernel(
    sizes,
    pairs,
    gd_ref,
    hidden_ref,
    wd_ref,
    wg_ref,
    wu_ref,
    gate_ref,
    up_ref,
    gb_ref,
    n1t_ref,
    n2t_ref,
    headst_ref,
    residual_ref,
    qr_ref,
    kvr_ref,
    tables_ref,
    bias_ref,
    wqkv_ref,
    wo_ref,
    x_ref,
    lse_ref,
    gains_ref,
    mixed_out,
    tokens_out,
    down_out,
    out_out,
    gate_own,
    up_own,
    qkv_own,
    x_refs,
    below_refs,
    above_refs,
    send_gate,
    send_up,
    da_all_ref,
    own_refs,
    send_out,
    send_qkv,
    stage_refs,
    core_in_ref,
    far_in_ref,
    mixed_core_in,
    mixed_far_in,
    da_own_ref,
    total_ref,
    send_sems,
    recv_sems,
    copy_sems,
):
    place = Place(sizes)
    ny, nc, nz, nx = sizes
    s, b = place.s, place.b
    n_seq, n_batch = ny * nc, nz * nx
    length, width = x_ref.shape
    total_len = n_seq * length
    ff = wg_ref.shape[3]
    rows = wo_ref.shape[1]
    wires = Wires(send_sems, recv_sems)
    copies = Copies(copy_sems)
    s_down, s_rest, s_gate, s_up, s_out, s_qkv = own_refs

    def reduce(i, stage, x_last=False):
        return LineReduce(
            wires,
            place,
            copies,
            own_refs[i],
            x_refs[i],
            below_refs[i],
            above_refs[i],
            stage_refs[stage],
            x_last,
        )

    down, rest = reduce(0, 0), reduce(1, 1, True)
    gate, up = reduce(2, 2), reduce(3, 2)
    out, qkv = reduce(4, 3), reduce(5, 4)
    row_others = [(dy, dc) for dy in range(ny) for dc in range(nc) if dy or dc]

    late = []
    cut = pl.ds(0, BACK_CUT)
    beyond = pl.ds(BACK_CUT, gd_ref.shape[1] - BACK_CUT)
    own_rest = [
        copies.start(gd_ref.at[zz * nx + x, beyond], s_rest.at[zz, x])
        for zz in range(nz)
        for x in range(nx)
    ]
    own_down = [
        copies.start(gd_ref.at[zz * nx + place.x, cut], s_down.at[zz]) for zz in range(nz)
    ]
    place.enter()
    down.send(lambda zz: gd_ref.at[zz * nx + (place.x + 1) % nx, cut])
    for copy in own_rest:
        copy.wait()
    rest.step(1)

    def weight_rows(flipped_ref, grads, k, dx):
        j = place.batch_at(k, dx)
        pieces = []
        for i in range(n_seq):
            start = pl.multiple_of((i * n_batch + j) * rows, rows)
            pieces.append(flipped_ref[pl.ds(start, rows), :])
        value = product(jnp.concatenate(pieces, axis=0), grads)
        return value.astype(BF16).reshape(n_seq, rows, grads.shape[1])

    def feed_forward(dgate_ref, dup_ref, part_ref, flipped, staging):
        flip = copies.start(n2t_ref, flipped)
        row_sum = RowSum(wires, place, part_ref, core_in_ref, far_in_ref)

        def activations(weight1, gate_buf, up_buf, gb_buf):
            load1 = copies.start(wd_ref, weight1)

            base = copies.count
            copies.count += 3

            def load_gb(j):
                return pltpu.make_async_copy(gb_ref.at[j], gb_buf, copy_sems.at[base])

            def load_gate(j):
                at = pl.ds(pl.multiple_of(j * length, length), length)
                return (
                    pltpu.make_async_copy(gate_ref.at[at], gate_buf, copy_sems.at[base + 1]),
                    pltpu.make_async_copy(up_ref.at[at], up_buf, copy_sems.at[base + 2]),
                )

            load_gb(0).start()
            for copy in load_gate(0):
                copy.start()
            load1.wait()

            def rows_back(j, unused):
                load_gb(j).wait()
                grad_hidden = product_cols(gb_buf[...], weight1[...].reshape(ff, width))

                @pl.when(j + 1 < n_seq)
                def _():
                    load_gb(j + 1).start()

                for copy in load_gate(j):
                    copy.wait()
                gate_part, up_part = gate_buf[...], up_buf[...]
                sigma = jax.nn.sigmoid(gate_part)
                activated = gate_part * sigma
                dgate_ref[j] = (
                    grad_hidden * up_part * sigma * (1.0 + gate_part * (1.0 - sigma))
                ).astype(BF16)
                dup_ref[j] = (grad_hidden * activated).astype(BF16)

                @pl.when(j + 1 < n_seq)
                def _():
                    for copy in load_gate(j + 1):
                        copy.start()

                return unused

            lax.fori_loop(0, n_seq, rows_back, 0)
            for copy in own_down:
                copy.wait()

        pl.run_scoped(
            activations,
            pltpu.VMEM(wd_ref.shape, BF16),
            pltpu.VMEM((length, ff), F32),
            pltpu.VMEM((length, ff), F32),
            pltpu.VMEM((length, width), BF16),
        )

        def rows_of(reduce, grads_ref, send_ref):
            chunk = lambda zz: send_ref.at[zz]
            reduce.plan(chunk)
            turns = Rotating(copies)

            def body(i, unused):
                zz = reduce.any_target(i)
                k = (zz - place.z + nz) % nz
                grads = grads_ref[...].reshape(total_len, ff)
                staging[i % 2] = weight_rows(flipped, grads, k, 1)
                turns.copy(i, staging.at[i % 2], chunk(zz)).start()
                reduce.own[zz] = weight_rows(flipped, grads, k, 0)
                turns.copy(i, staging.at[i % 2], chunk(zz)).wait()
                reduce.send_one(i, chunk)
                return unused

            lax.fori_loop(0, nz, body, 0)

        def inputs(weight1, weight2):
            loads = [copies.start(wg_ref, weight1), copies.start(wu_ref, weight2)]
            flip.wait()
            rows_of(gate, dgate_ref, send_gate)
            rest.step(2)
            down.add(0)
            down.step(1)
            for load in loads:
                load.wait()

            def input_part(j):
                return product_cols(
                    dgate_ref[j], weight1[...].reshape(width, ff)
                ) + product_cols(dup_ref[j], weight2[...].reshape(width, ff))

            row_sum.compute(input_part)

        pl.run_scoped(inputs, pltpu.VMEM(wg_ref.shape, BF16), pltpu.VMEM(wg_ref.shape, BF16))
        rest.step(3)
        down.add(1)
        down.step(2)
        rows_of(up, dup_ref, send_up)
        down.add(2)
        down.step(3)
        down.add(3)

        def normed(residual_buf, gb_buf):
            loads = [
                copies.start(residual_ref, residual_buf),
                copies.start(gb_ref.at[s], gb_buf),
            ]
            for copy in loads:
                copy.wait()
            for h in range(2):
                at = row_sum.half(h)
                row_sum.finish_half(h, total_ref)
                norm_back_rows(
                    total_ref.at[at],
                    residual_buf.at[at],
                    gains_ref[1:2, :],
                    gb_buf.at[at],
                    total_ref.at[at],
                    da_own_ref.at[at],
                )
                da[h].start()
            row_sum.sent()

        pl.run_scoped(normed, pltpu.VMEM((length, width), F32), pltpu.VMEM((length, width), BF16))
        gate.add(0)
        gate.step(1)
        gate.add(1)
        gate.step(2)
        rest.change()
        gate.add(2)
        gate.step(3)

    own_da = []
    half = length // 2

    def da_gather(h):
        at = pl.ds(h * half, half)
        return Gather(
            wires,
            lambda j: da_all_ref.at[j, at],
            lambda: da_own_ref.at[at],
            ny,
            nc,
            place.seq_at,
            lambda j: (j, b),
        )

    da = [da_gather(0), da_gather(1)]
    pl.run_scoped(
        feed_forward,
        pltpu.VMEM((n_seq, length, ff), BF16),
        pltpu.VMEM((n_seq, length, ff), BF16),
        pltpu.VMEM((n_seq, length, width), BF16),
        pltpu.VMEM(n2t_ref.shape, BF16),
        pltpu.VMEM((2, n_seq, rows, ff), BF16),
    )
    own_da.append(copies.start(da_own_ref, da_all_ref.at[s]))
    for k in range(1, ny):
        for piece in da:
            piece.pass_on(k)

    def attention(
        da_buf,
        wo_buf,
        wqkv_buf,
        qr_buf,
        headst_buf,
        do_buf,
        kvr_buf,
        tables_buf,
        bias_buf,
        dqkv_buf,
        n1t_buf,
        dq_buf,
        dk_buf,
        dv_buf,
        part_ref,
    ):
        loads = [
            copies.start(source, target)
            for source, target in [
                (wo_ref, wo_buf),
                (headst_ref, headst_buf),
                (qr_ref, qr_buf),
                (kvr_ref, kvr_buf),
                (tables_ref, tables_buf),
                (bias_ref, bias_buf),
                (n1t_ref, n1t_buf),
                (wqkv_ref, wqkv_buf),
            ]
        ]
        gate.add(3)
        for piece in da:
            piece.finish()
        own_da[0].wait()
        copies.start(da_all_ref, da_buf).wait()
        for load in loads:
            load.wait()
        out_weights = wo_buf[...].reshape(n_batch * rows, width)

        def heads_back(j, unused):
            at = pl.ds(pl.multiple_of(j * length, length), length)
            do_buf[at, :] = product_cols(da_buf[j], out_weights).astype(BF16)
            return unused

        lax.fori_loop(0, n_seq, heads_back, 0)
        branch = da_buf[...].reshape(total_len, width)

        def out_rows(dx):
            pieces = []
            for zz in range(nz):
                start = pl.multiple_of((zz * nx + (place.x + dx) % nx) * rows, rows)
                pieces.append(headst_buf[pl.ds(start, rows), :])
            value = product(jnp.concatenate(pieces, axis=0), branch)
            return value.astype(BF16).reshape(nz, rows, width)

        send_out[...] = out_rows(1)
        out.send(lambda zz: send_out.at[zz])
        s_out[...] = out_rows(0)
        dk_buf[...] = jnp.zeros_like(dk_buf)
        dv_buf[...] = jnp.zeros_like(dv_buf)

        def pair_back(pair, unused):
            at = pl.ds(pl.multiple_of(pair * 128, 128), 128)
            low = (qr_buf[:, at] * SCALE).astype(BF16)
            grads_pair = do_buf[:, at]
            for start in range(0, total_len, length):
                stop = start + length
                outs = []
                for head in range(2):
                    lanes = slice(head * HEAD_DIM, (head + 1) * HEAD_DIM)
                    queries = low[start:stop, lanes]
                    grads = grads_pair[start:stop, lanes]
                    keys = kvr_buf[:stop, :HEAD_DIM]
                    values = kvr_buf[:stop, HEAD_DIM:]
                    scores = product_cols(keys, queries)
                    scores = scores + bias_buf[:stop, start:stop].astype(F32)
                    probs = jnp.exp(scores - lse_ref[pair, head : head + 1, start:stop])
                    dprobs = product_cols(values, grads)
                    delta = jnp.sum(probs * dprobs, axis=0, keepdims=True)
                    dscores = (probs * (dprobs - delta)).astype(BF16)
                    dv_buf[:stop, :] += product(probs.astype(BF16), grads)
                    dk_buf[:stop, :] += product(dscores, queries)
                    outs.append(product_rows(dscores, keys) * SCALE)
                dq_buf[start:stop, :] = jnp.concatenate(outs, axis=1)
            dq = dq_buf[...]
            turned = rotate_lanes(dq * tables_buf[1], -1.0)
            dqkv_buf[:, at] = (dq * tables_buf[0] + turned).astype(BF16)
            return unused

        def pair_and_sums(pair, unused):
            pair_back(pair, unused)

            @pl.when(pair == 0)
            def _():
                up.add(0)
                up.step(1)

            @pl.when(pair == 2)
            def _():
                up.add(1)
                up.step(2)

            return unused

        lax.fori_loop(0, pairs, pair_and_sums, 0)
        grads = jnp.concatenate([dk_buf[...], dv_buf[...]], axis=1)
        back = grads * tables_buf[0] + rotate_lanes(grads * tables_buf[1], -1.0)
        lane = lax.broadcasted_iota(jnp.int32, grads.shape, 1)
        dqkv_buf[:, pairs * 128 :] = jnp.where(lane < HEAD_DIM, back, grads).astype(BF16)

        row_sum = RowSum(wires, place, part_ref, core_in_ref, far_in_ref)
        in_weights = wqkv_buf[...].reshape(width, wqkv_ref.shape[3])

        def input_part(j):
            at = pl.ds(pl.multiple_of(j * length, length), length)
            return product_cols(dqkv_buf[at, :], in_weights)

        row_sum.compute(input_part)

        def qkv_rows(zz, unused):
            k = (zz - place.z + nz) % nz
            send_qkv[zz] = weight_rows(n1t_buf, dqkv_buf[...], k, 1)
            s_qkv[zz] = weight_rows(n1t_buf, dqkv_buf[...], k, 0)
            return unused

        lax.fori_loop(0, nz, qkv_rows, 0)
        qkv.send(lambda zz: send_qkv.at[zz])
        up.add(2)
        up.step(3)
        up.add(3)
        out.add(0)
        out.step(1)

        def last(grad_ref, x_buf, tokens_ref):
            load = copies.start(x_ref, x_buf)
            row_sum.finish(grad_ref)
            load.wait()
            norm_back_rows(grad_ref, x_buf, gains_ref[0:1, :], total_ref, None, tokens_ref)
            copies.start(tokens_ref, tokens_out).wait()

        row = pltpu.VMEM((length, width), BF16)
        pl.run_scoped(last, pltpu.VMEM((length, width), F32), row, row)
        row_sum.sent()

    pl.run_scoped(
        attention,
        pltpu.VMEM((n_seq, length, width), BF16),
        pltpu.VMEM(wo_ref.shape, BF16),
        pltpu.VMEM(wqkv_ref.shape, BF16),
        pltpu.VMEM(qr_ref.shape, BF16),
        pltpu.VMEM(headst_ref.shape, BF16),
        pltpu.VMEM(qr_ref.shape, BF16),
        pltpu.VMEM(kvr_ref.shape, BF16),
        pltpu.VMEM(tables_ref.shape, F32),
        pltpu.VMEM(bias_ref.shape, BF16),
        pltpu.VMEM((total_len, (pairs + 1) * 128), BF16),
        pltpu.VMEM(n1t_ref.shape, BF16),
        pltpu.VMEM((total_len, 128), F32),
        pltpu.VMEM((total_len, HEAD_DIM), F32),
        pltpu.VMEM((total_len, HEAD_DIM), F32),
        pltpu.VMEM((n_seq, length, width), BF16),
    )

    exchanges = []

    def exchange(reduce, target):
        mine = reduce.finish()
        copy = copies.start(mine.at[s], target.at[s])
        tickets = {}
        for away in row_others:
            tickets[away] = wires.push(
                lambda away=away: reduce.own.at[place.z, place.seq_at(*away)],
                lambda: target.at[s],
                lambda away=away: (place.seq_at(*away), b),
            )
        exchanges.append((copy, target, tickets))

    def layer_out(weight_buf, hidden_buf, part_ref, mixed_total, mixed_ref, down_own, out_own):
        loads = [
            copies.start(wd_ref, weight_buf),
            copies.start(hidden_ref, hidden_buf),
            copies.start(residual_ref, mixed_total),
        ]
        out.add(1)
        out.step(2)
        for load in loads:
            load.wait()

        def mixed_part(j):
            at = pl.ds(pl.multiple_of(j * length, length), length)
            return product(hidden_buf[at, :], weight_buf[...].reshape(ff, width))

        row_sum = RowSum(wires, place, part_ref, mixed_core_in, mixed_far_in)
        row_sum.compute(mixed_part)
        out.add(2)
        out.step(3)
        out.add(3)
        qkv.add(0)
        qkv.step(1)
        exchange(gate, gate_own)
        down.finish(down_own.at[cut])
        rest.close(down_own.at[beyond])
        late.append(copies.start(down_own, down_out))
        qkv.add(1)
        qkv.step(2)
        exchange(up, up_own)
        out.finish(out_own)
        late.append(copies.start(out_own, out_out))
        qkv.add(2)
        qkv.step(3)
        qkv.add(3)
        row_sum.finish(mixed_ref, [mixed_total])
        late.append(copies.start(mixed_ref, mixed_out))
        exchange(qkv, qkv_own)
        row_sum.sent()
        for copy in late:
            copy.wait()

    pl.run_scoped(
        layer_out,
        pltpu.VMEM(wd_ref.shape, BF16),
        pltpu.VMEM(hidden_ref.shape, BF16),
        pltpu.VMEM((n_seq, length, width), BF16),
        pltpu.VMEM((length, width), F32),
        pltpu.VMEM((length, width), BF16),
        pltpu.VMEM(gd_ref.shape[1:], F32),
        pltpu.VMEM((rows, width), F32),
    )

    for copy, target, tickets in exchanges:
        copy.wait()
        for (dy, dc), ticket in tickets.items():
            wires.wait(ticket, target.at[place.seq_at(-dy, -dc)])
    wires.close()


def grouped_back_kernel(sizes, pairs, *refs):
    refs = list(refs)
    groups = []
    at = 21 + 7
    for count in (6, 6, 6):
        groups.append(refs[at : at + count])
        at += count
    singles = refs[at : at + 3]
    at += 3
    own = refs[at : at + 6]
    at += 6
    sends = refs[at : at + 2]
    at += 2
    stages = refs[at : at + 5]
    at += 5
    back_kernel(
        sizes, pairs, *refs[:28], *groups, *singles, own, *sends, stages, *refs[at:]
    )


def back(sizes, gd, hidden, wd, wg, wu, gate, up, gb, n1t, n2t, headst, residual, qr, kvr, tables, bias, wqkv, wo, x, lse, gains):
    ny, nc, nz, nx = sizes
    n_seq, n_batch = ny * nc, nz * nx
    length, width = x.shape
    ff = wg.shape[3]
    rows = wo.shape[1]
    pairs = qr.shape[1] // 128
    chunk_down = (BACK_CUT, width)
    chunk_rest = (gd.shape[1] - BACK_CUT, width)
    chunk_gate = (n_seq, rows, ff)
    chunk_out = (rows, width)
    chunk_qkv = (n_seq, rows, wqkv.shape[3])
    pair_rest = (nx,) + chunk_rest
    chunks = [chunk_down, pair_rest, chunk_gate, chunk_gate, chunk_out, chunk_qkv]
    results = [
        (HBM, shape_of((length, width), BF16)),
        (HBM, shape_of((length, width), BF16)),
        (HBM, shape_of(gd.shape[1:], F32)),
        (HBM, shape_of(chunk_out, F32)),
        (HBM, shape_of(chunk_gate, BF16)),
        (HBM, shape_of(chunk_gate, BF16)),
        (HBM, shape_of(chunk_qkv, BF16)),
    ]
    landings = [
        [shape_of((nz,) + chunk, BF16) for chunk in chunks],
        [shape_of((nz - 1,) + chunk, BF16) for chunk in chunks],
        [shape_of((nz - 1,) + chunk, BF16) for chunk in chunks],
    ]
    landings[0][1] = shape_of(chunk_rest, BF16)
    for group in landings:
        results += [(HBM, kind) for kind in group]
    results += [(HBM, shape_of((nz,) + chunk_gate, BF16))] * 2
    results += [(HBM, shape_of((n_seq, length, width), BF16))]
    wires = len(chunks) * (nz + 2 * (nz - 1)) + 3 * 4 + 6 + 3 * (n_seq - 1)
    row = pltpu.VMEM((length, width), BF16)
    return pl.pallas_call(
        functools.partial(grouped_back_kernel, sizes, pairs),
        in_specs=[HBM] * 19 + [VMEM] * 2,
        out_specs=[spec for spec, unused in results],
        out_shape=[kind for unused, kind in results],
        scratch_shapes=[pltpu.VMEM((nz,) + chunk, BF16) for chunk in chunks]
        + [
            pltpu.VMEM((nz,) + chunk_out, BF16),
            pltpu.VMEM((nz,) + chunk_qkv, BF16),
            pltpu.VMEM(chunk_down, BF16),
            pltpu.VMEM(pair_rest, BF16),
            pltpu.VMEM(chunk_gate, BF16),
            pltpu.VMEM(chunk_out, BF16),
            pltpu.VMEM(chunk_qkv, BF16),
            pltpu.VMEM((ny, length, width), BF16),
            row,
            pltpu.VMEM((ny, length, width), BF16),
            row,
            row,
            pltpu.VMEM((length, width), F32),
            pltpu.SemaphoreType.DMA((wires,)),
            pltpu.SemaphoreType.DMA((wires,)),
            pltpu.SemaphoreType.DMA((140,)),
        ],
        compiler_params=pltpu.CompilerParams(
            collective_id=1, has_side_effects=True, vmem_limit_bytes=VMEM_BYTES
        ),
        cost_estimate=pl.CostEstimate(
            flops=12 * n_seq * length * width * ff,
            bytes_accessed=100 * 1024 * 1024,
            transcendentals=pairs * (n_seq * length) ** 2,
        ),
    )(gd, hidden, wd, wg, wu, gate, up, gb, n1t, n2t, headst, residual, qr, kvr, tables, bias, wqkv, wo, x, lse, gains)


def by_permutes(
    tokens,
    cotangent,
    selection,
    segments,
    positions,
    gain_attn,
    w_query,
    w_key,
    w_value,
    w_out,
    gain_mlp,
    w_gate,
    w_up,
    w_down,
):
    seq = Axis("seq", 2)
    batch = Axis("batch", lax.axis_size("batch") // 4)
    n_seq, n_batch = seq.size, batch.size
    length, width = tokens.shape[1], tokens.shape[2]
    total_len = length * n_seq
    rows = w_query.shape[0]
    ff = w_gate.shape[1]
    q_cols = w_query.shape[1] // n_seq
    sharers = n_seq // KV_HEADS

    query_parts = w_query.reshape(rows, n_seq, q_cols)
    key_parts = jnp.repeat(w_key.reshape(rows, KV_HEADS, HEAD_DIM), sharers, axis=1)
    value_parts = jnp.repeat(w_value.reshape(rows, KV_HEADS, HEAD_DIM), sharers, axis=1)
    qkv_parts = jnp.concatenate([query_parts, key_parts, value_parts], axis=2).transpose(1, 0, 2)

    def spread(parts):
        mine = seq.exchange(parts)
        return batch.gather(mine, 1).reshape(n_seq * n_batch * rows, parts.shape[2])

    def collect(grad):
        parts = grad.astype(BF16).reshape(n_seq, n_batch, rows, grad.shape[1])
        return seq.exchange(batch.scatter_sum(parts, 1).astype(BF16)).astype(F32)

    def by_columns(weight):
        return weight.reshape(rows, n_seq, weight.shape[1] // n_seq).transpose(1, 0, 2)

    places = seq.gather(jnp.stack([segments[0], positions[0]]), 1)
    seg_all = places[0].reshape(total_len)
    pos_all = places[1].reshape(total_len)
    gains = batch.gather(seq.gather(jnp.stack([gain_attn, gain_mlp]), 1), 2)
    gain_one = gains[0].reshape(1, width).astype(F32)
    gain_two = gains[1].reshape(1, width).astype(F32)
    x_all = seq.gather(tokens[0], 0).reshape(total_len, width).astype(F32)
    w_qkv = spread(qkv_parts)
    wo = batch.gather(w_out, 0).reshape(n_batch * rows, width)
    wg = spread(by_columns(w_gate))
    wu = spread(by_columns(w_up))
    wd = batch.gather(w_down, 0).reshape(n_batch * w_down.shape[0], width)

    grad_out_row = cotangent[0].astype(F32) * selection[0].astype(F32)[:, None]
    grad_low = seq.gather(grad_out_row.astype(BF16), 0).reshape(total_len, width)

    row_input = tokens[0].astype(F32)
    inv_attn = rms_scale(row_input)
    normed1 = (x_all * rms_scale(x_all) * gain_one).astype(BF16)
    qkv = product(normed1, w_qkv)
    frequency = 10000.0 ** (-(jnp.arange(HALF, dtype=F32) * 2.0 / HEAD_DIM))
    angles = pos_all.astype(F32)[:, None] * jnp.tile(frequency, 4)[None, :]
    cosine, sine = jnp.cos(angles), jnp.sin(angles)
    seg_row, seg_col = seg_all[None, :], seg_all[:, None]
    heads_out, query_rot, kv_rot, lse = attend(qkv, cosine, sine, seg_row, seg_col)
    attn_part = product(heads_out, wo).astype(BF16).reshape(n_seq, length, width)
    residual = row_input + seq.scatter_sum(attn_part, 0)

    inv_mlp = rms_scale(residual)
    normed2_own = (residual * inv_mlp * gain_two).astype(BF16)
    normed2 = seq.gather(normed2_own, 0).reshape(total_len, width)
    gate_proj = product(normed2, wg)
    up_proj = product(normed2, wu)
    sigma = jax.nn.sigmoid(gate_proj)
    activated = gate_proj * sigma
    hidden = (activated * up_proj).astype(BF16)
    mixed_part = product(hidden, wd).astype(BF16).reshape(n_seq, length, width)
    mixed = (residual + seq.scatter_sum(mixed_part, 0)).astype(BF16)[None]

    grad_down = product_rows(hidden, grad_low)
    grad_hidden = product_cols(grad_low, wd)
    grad_gate_act = (
        grad_hidden * up_proj * sigma * (1.0 + gate_proj * (1.0 - sigma))
    ).astype(BF16)
    grad_up_act = (grad_hidden * activated).astype(BF16)
    grad_gate = product_rows(normed2, grad_gate_act)
    grad_up = product_rows(normed2, grad_up_act)
    normed_part = product_cols(grad_gate_act, wg) + product_cols(grad_up_act, wu)
    normed_terms = seq.scatter_sum(normed_part.astype(BF16).reshape(n_seq, length, width), 0)
    grad_resid = grad_out_row + norm_back(normed_terms, residual, inv_mlp, gain_two)

    down_own = batch.scatter_sum(
        grad_down.astype(BF16).reshape(n_batch, w_down.shape[0], width), 0
    )
    gate_own = collect(grad_gate).transpose(1, 0, 2).reshape(rows, ff)
    up_own = collect(grad_up).transpose(1, 0, 2).reshape(rows, ff)

    grad_branch = seq.gather(grad_resid.astype(BF16), 0).reshape(total_len, width)
    grad_wout = product_rows(heads_out, grad_branch)
    grad_heads = product_cols(grad_branch, wo).astype(BF16)
    grad_qkv_act = attend_back(
        query_rot, kv_rot, grad_heads, lse, cosine, sine, seg_row, seg_col
    )
    grad_wqkv = product_rows(normed1, grad_qkv_act)
    input_part = product_cols(grad_qkv_act, w_qkv).astype(BF16).reshape(n_seq, length, width)
    grad_normed1 = seq.scatter_sum(input_part, 0)
    tokens_grad = (
        grad_resid + norm_back(grad_normed1, row_input, inv_attn, gain_one)
    ).astype(BF16)[None]
    out_own = batch.scatter_sum(grad_wout.astype(BF16).reshape(n_batch, rows, width), 0)
    qkv_own = collect(grad_wqkv)
    query_own = qkv_own[:, :, :q_cols].transpose(1, 0, 2).reshape(rows, n_seq * q_cols)

    def shared(columns):
        heads = columns.reshape(KV_HEADS, sharers, rows, HEAD_DIM).sum(axis=1)
        return heads.transpose(1, 0, 2).reshape(rows, KV_HEADS * HEAD_DIM)

    key_own = shared(qkv_own[:, :, q_cols : q_cols + HEAD_DIM])
    value_own = shared(qkv_own[:, :, q_cols + HEAD_DIM :])

    def along(weight, grad):
        return jnp.sum(weight.astype(F32) * grad, axis=1)

    gain1_own = (
        along(w_query, query_own) + along(w_key, key_own) + along(w_value, value_own)
    ) / gain_attn.astype(F32)
    gain2_own = (along(w_gate, gate_own) + along(w_up, up_own)) / gain_mlp.astype(F32)
    return (
        mixed,
        tokens_grad,
        query_own,
        key_own,
        value_own,
        out_own,
        gate_own,
        up_own,
        down_own,
        gain1_own,
        gain2_own,
    )


def by_kernels(
    tokens,
    cotangent,
    selection,
    segments,
    positions,
    gain_attn,
    w_query,
    w_key,
    w_value,
    w_out,
    gain_mlp,
    w_gate,
    w_up,
    w_down,
):
    sizes = mesh_sizes()
    n_seq, n_batch = sizes[0] * sizes[1], sizes[2] * sizes[3]
    length, width = tokens.shape[1], tokens.shape[2]
    rows, ff = w_gate.shape
    q_cols = w_query.shape[1] // n_seq

    def by_columns(weight):
        return weight.reshape(rows, n_seq, weight.shape[1] // n_seq).transpose(1, 0, 2)

    qkv_parts = jnp.concatenate([by_columns(w) for w in (w_query, w_key, w_value)], axis=2)
    grad_low = (cotangent[0].astype(F32) * selection[0].astype(F32)[:, None]).astype(BF16)
    frequency = 10000.0 ** (-(jnp.arange(HALF, dtype=F32) * 2.0 / HEAD_DIM))
    angles = positions[0].astype(F32)[:, None] * frequency[None, :]
    documents = jnp.broadcast_to(segments[0].astype(F32)[:, None], (length, 128 - HEAD_DIM))
    table = jnp.concatenate([jnp.cos(angles), jnp.sin(angles), documents], axis=1)
    gain_tile = jnp.pad(
        jnp.stack([gain_attn, gain_mlp]).astype(F32), ((0, 6), (0, 128 - gain_attn.shape[0]))
    )
    (
        w_qkv,
        wo,
        wg,
        wu,
        wd,
        gb_all,
        n1t,
        n2t,
        residual,
        headst,
        query_rot,
        kv_rot,
        lse,
        rotary,
        gains,
        bias,
        gate_proj,
        up_proj,
        grad_down,
        hidden,
    ) = front(
        sizes,
        tokens[0],
        grad_low,
        table,
        gain_tile,
        qkv_parts,
        w_out,
        by_columns(w_gate),
        by_columns(w_up),
        w_down,
    )
    mixed, tokens_grad, down_own, out_own, gate_part, up_part, qkv_part = back(
        sizes,
        grad_down.reshape(n_batch, w_down.shape[0], width),
        hidden,
        wd,
        wg,
        wu,
        gate_proj,
        up_proj,
        gb_all,
        n1t,
        n2t,
        headst,
        residual,
        query_rot,
        kv_rot,
        rotary,
        bias,
        w_qkv,
        wo,
        tokens[0],
        lse,
        gains,
    )[:7]

    def by_rows(part):
        return part.astype(F32).transpose(1, 0, 2).reshape(rows, n_seq * part.shape[2])

    query_own = by_rows(qkv_part[:, :, :q_cols])
    key_own = by_rows(qkv_part[:, :, q_cols : q_cols + HEAD_DIM])
    value_own = by_rows(qkv_part[:, :, q_cols + HEAD_DIM :])
    gate_own, up_own = by_rows(gate_part), by_rows(up_part)

    def along(weight, grad):
        return jnp.sum(weight.astype(F32) * grad, axis=1)

    gain1_own = (
        along(w_query, query_own) + along(w_key, key_own) + along(w_value, value_own)
    ) / gain_attn.astype(F32)
    gain2_own = (along(w_gate, gate_own) + along(w_up, up_own)) / gain_mlp.astype(F32)
    return (
        mixed[None],
        tokens_grad[None],
        query_own,
        key_own,
        value_own,
        out_own,
        gate_own,
        up_own,
        down_own,
        gain1_own,
        gain2_own,
    )


def mesh_sizes():
    return (lax.axis_size("seq") // 2, 2, 4, lax.axis_size("batch") // 4)


def per_device(*args):
    fits = mesh_sizes() == (2, 2, 4, 2) and args[0].shape[1:] == (256, 2048)
    return (by_kernels if fits else by_permutes)(*args)


def solution(mesh):
    both = ("seq", "batch")
    tokens = P("batch", "seq", None)
    flags = P("batch", "seq")
    matrix = P(both, None)
    vector = P(both)
    in_specs = (
        (tokens, tokens, flags, flags, flags)
        + (vector, matrix, matrix, matrix, matrix)
        + (vector, matrix, matrix, matrix)
    )
    out_specs = (tokens, tokens) + (matrix,) * 7 + (vector, vector)
    return jax.shard_map(
        per_device, mesh=mesh, in_specs=in_specs, out_specs=out_specs, check_vma=False
    )
```
